32 devices in a mesh: seq: 8 (over z, y), head: 4 (over x, core).
Axes of the slice: x: 2, y: 2, z: 4, core: 2. Of those that a mesh axis runs over, the one named last changes fastest.
Arguments:
- tokens_in: bfloat16 [2048, 1536], P('seq'), may hold values from -6 to 6
- cotangent: bfloat16 [2048, 1536], P('seq'), may hold values from -6 to 6
- document_ids: int32 [2048], replicated, may hold values from 0 to 2, as said below
- expert_routes: int32 [2048, 2], P('seq'), may hold values from 0 to 3, all different within a row; in each aligned block of 256 rows (0 to 255, 256 to 511, ...) at most 160 rows name the same one
- norm_mixer: bfloat16 [1536], replicated, may hold values from 0.5 to 1.5
- mixer_inner: bfloat16 [1536, 3072], P(None, 'head'), may hold values from -0.15625 to 0.15625
- mixer_gate: bfloat16 [1536, 3072], P(None, 'head'), may hold values from -0.15625 to 0.15625
- conv_taps: bfloat16 [4, 3072], P(None, 'head'), may hold values from -5 to 5
- conv_bias: bfloat16 [3072], P('head'), may hold values from -3 to 3
- state_proj: bfloat16 [3072, 128], P('head'), may hold values from -0.109375 to 0.109375
- step_proj: bfloat16 [96, 3072], P(None, 'head'), may hold values from -0.625 to 0.625
- step_bias: bfloat16 [3072], P('head'), may hold values from -10 to -3
- decay_log: bfloat16 [3072, 16], P('head'), may hold values from -1 to 1
- skip_gain: bfloat16 [3072], P('head'), may hold values from 0.5 to 1.5
- mixer_out: bfloat16 [3072, 1536], P('head'), may hold values from -0.3125 to 0.3125
- norm_ffn: bfloat16 [1536], replicated, may hold values from 0.5 to 1.5
- ffn_gate: bfloat16 [1536, 4096], P(None, 'head'), may hold values from -0.15625 to 0.15625
- ffn_up: bfloat16 [1536, 4096], P(None, 'head'), may hold values from -0.15625 to 0.15625
- ffn_down: bfloat16 [4096, 1536], P('head'), may hold values from -0.125 to 0.125
- norm_attn: bfloat16 [1536], replicated, may hold values from 0.5 to 1.5
- attn_query: bfloat16 [1536, 1536], P(None, 'head'), may hold values from -0.15625 to 0.15625
- attn_key: bfloat16 [1536, 512], P(None, 'head'), may hold values from -0.15625 to 0.15625
- attn_value: bfloat16 [1536, 512], P(None, 'head'), may hold values from -0.15625 to 0.15625
- attn_output: bfloat16 [1536, 1536], P('head'), may hold values from -1.25 to 1.25
- norm_moe: bfloat16 [1536], replicated, may hold values from 0.5 to 1.5
- router: bfloat16 [1536, 4], replicated, may hold values from -0.15625 to 0.15625
- expert_gate: bfloat16 [4, 1536, 1024], P(None, None, 'head'), may hold values from -0.15625 to 0.15625
- expert_up: bfloat16 [4, 1536, 1024], P(None, None, 'head'), may hold values from -0.15625 to 0.15625
- expert_down: bfloat16 [4, 1024, 1536], P(None, 'head'), may hold values from -0.25 to 0.25
Outputs:
- mixed_out: bfloat16 [2048, 1536], P('seq')
- grad_tokens: float32 [2048, 1536], P('seq')
- grad_norm_mixer: float32 [1536], P('seq')
- grad_mixer_inner: float32 [1536, 3072], P('seq', 'head')
- grad_mixer_gate: float32 [1536, 3072], P('seq', 'head')
- grad_conv_taps: float32 [4, 3072], P(None, ('head', 'seq'))
- grad_conv_bias: float32 [3072], P(('head', 'seq'))
- grad_state_proj: float32 [3072, 128], P(('head', 'seq'))
- grad_step_proj: float32 [96, 3072], P(None, ('head', 'seq'))
- grad_step_bias: float32 [3072], P(('head', 'seq'))
- grad_decay_log: float32 [3072, 16], P(('head', 'seq'))
- grad_skip_gain: float32 [3072], P(('head', 'seq'))
- grad_mixer_out: float32 [3072, 1536], P('head', 'seq')
- grad_norm_ffn: float32 [1536], P('seq')
- grad_ffn_gate: float32 [1536, 4096], P('seq', 'head')
- grad_ffn_up: float32 [1536, 4096], P('seq', 'head')
- grad_ffn_down: float32 [4096, 1536], P('head', 'seq')
- grad_norm_attn: float32 [1536], P('seq')
- grad_attn_query: float32 [1536, 1536], P('seq', 'head')
- grad_attn_key: float32 [1536, 512], P('seq', 'head')
- grad_attn_value: float32 [1536, 512], P('seq', 'head')
- grad_attn_output: float32 [1536, 1536], P('head', 'seq')
- grad_norm_moe: float32 [1536], P('seq')
- grad_router: float32 [1536, 4], P('seq')
- grad_expert_gate: float32 [4, 1536, 1024], P(None, 'seq', 'head')
- grad_expert_up: float32 [4, 1536, 1024], P(None, 'seq', 'head')
- grad_expert_down: float32 [4, 1024, 1536], P(None, 'head', 'seq')
The draws below stay inside these ranges and needn't reach their ends.
Inputs may be any that keep to these rules, and one draw needn't show every extreme that they name: `document_ids`: document ids never fall along the tokens; document 1 starts within the first 256 tokens and ends within the last 256 tokens. `expert_routes`: A token's two experts differ; among the tokens of one index of seq no expert is named more than 160 times.
All inputs are finite; a program needn't handle non-finite values.
Results may differ from the reference program's by a relative error of at most 0.03.
Values may be sent and summed in bfloat16 or wider, within the bound.
A program may use at most 256 MiB of HBM per device.

```python
import math
import jax
import jax.numpy as jnp
import numpy as np
from jax import lax

D = 1536
INNER = 3072
STATE = 16
CONV = 4
RANK = 96
FF = 4096
HEADS = 24
KV_HEADS = 8
HEAD_DIM = 64
EFF = 1024
EXPERTS = 4
TOK_DEV = 256
CAP = 160
TOKENS = 2048


def draw_document_ids(key, part):
    key = jax.random.fold_in(key, 11)
    first_key, second_key = jax.random.split(key)
    opening = jax.random.randint(first_key, (), 1, TOK_DEV)
    closing = jax.random.randint(second_key, (), TOKENS - TOK_DEV + 1, TOKENS)
    position = jnp.arange(TOKENS, dtype=jnp.int32)
    return (position >= opening).astype(jnp.int32) + (position >= closing).astype(jnp.int32)


def block_scale(rng, dims, cuts, smallest, high):
    factor_of, own = 1.0, jax.random.fold_in(rng, 6)
    for dim, shards_of in cuts:
        steps = jnp.exp(jax.random.uniform(jax.random.fold_in(own, dim), (shards_of,), jnp.float32, smallest / len(cuts), high / len(cuts)))
        factor_of = factor_of * jnp.repeat(steps, dims[dim] // shards_of).reshape([-1 if axis == dim else 1 for axis in range(len(dims))])
    return factor_of


def shared_out(key, own, number, rows, count, top, reach, lean):
    ranking = jax.random.permutation(key, count)
    heavy_load, usual = portions_of(count, rows * top, reach, lean, True), portions_of(count, rows * top, reach, lean, False)
    places = jnp.arange(count)

    def named(tallies, turn):
        used = int((tallies > 0).sum())
        fixed = max(1, used // 4)
        passed = fixed + (places - fixed + turn * (used - fixed)) % max(1, count - fixed)
        return jnp.zeros((count,), jnp.int32).at[ranking[jnp.where(places < fixed, places, passed)]].set(jnp.asarray(tallies, jnp.int32))

    tallies = jnp.where(number % 4 == 0, named(heavy_load, number // 4), named(usual, number - number // 4 - 1))
    mixed = jax.random.permutation(jax.random.fold_in(own, 3), count)
    giver, taker = mixed[0:count // 2 * 2:2], mixed[1:count // 2 * 2:2]
    slack = jnp.minimum(tallies[giver] - 1, reach - tallies[taker]) // 2
    slack = jnp.where((giver == ranking[0]) | (taker == ranking[0]) | (tallies[taker] == 0), 0, jnp.maximum(slack, 0))
    passed = jax.random.randint(jax.random.fold_in(own, 4), (count // 2,), 0, 1 << 20) % (slack + 1)
    tallies = tallies.at[giver].add(-passed).at[taker].add(passed)
    labels = jnp.searchsorted(jnp.cumsum(tallies), jnp.arange(rows * top), side="right").astype(jnp.int32)
    grid = labels.reshape(top, rows).T
    grid = grid[jax.random.permutation(jax.random.fold_in(own, 1), rows)]
    turn = jax.random.randint(jax.random.fold_in(own, 2), (rows, 1), 0, top)
    return jnp.take_along_axis(grid, (jnp.arange(top)[None, :] + turn) % top, axis=1)


def portions_of(amount, total, bound, skew, full):
    loads = [(1 << 20) // math.isqrt(standing ** skew) + 1 for standing in range(1, amount + 1)]
    largest = bound if full else min(bound, max(-(-total // amount), total * loads[0] // sum(loads)))
    least = 1 if total - largest >= amount - 1 else 0
    counts, spare = [largest] + [least] * (amount - 1), total - largest - least * (amount - 1)
    while spare > 0:
        movable = [i for i in range(1, amount) if counts[i] < largest] or [i for i in range(1, amount) if counts[i] < bound]
        mass, remaining = sum([loads[i] for i in movable]), spare
        for i in movable:
            extra = min(bound - counts[i], max(1, remaining * loads[i] // mass), spare)
            counts[i] = counts[i] + extra
            spare = spare - extra
    return np.array(counts)


def scatter_about(own_key, extent, deviation, bound, shards=(), kind=jnp.bfloat16):
    array = jax.random.normal(own_key, extent, jnp.float32) * deviation
    if len(shards) > 0:
        array = block_scale(own_key, extent, shards, -0.22, 0.18) * array
    return jnp.clip(array, min=-bound, max=bound).astype(kind)


def setup_inputs(seed: int = 0) -> dict:
    streams_of = jax.random.split(jax.random.key(seed), 30)
    tokens_in = scatter_about(streams_of[0], (TOKENS, D), 1.0, 6.0, ((0, 8),))
    cotangent = scatter_about(streams_of[1], (TOKENS, D), 1.0, 6.0, ((0, 8),))
    document_ids = draw_document_ids(jax.random.fold_in(streams_of[29], 71), 0)
    expert_routes_keys = jax.random.split(jax.random.fold_in(streams_of[3], 1), TOKENS // TOK_DEV)
    expert_routes_turns = jax.random.permutation(jax.random.fold_in(streams_of[3], 3), TOKENS // TOK_DEV)
    expert_routes = jax.vmap(lambda own, number: shared_out(jax.random.fold_in(streams_of[3], 2), own, number, TOK_DEV, EXPERTS, 2, CAP, 1))(expert_routes_keys, expert_routes_turns).reshape((TOKENS, 2))
    norm_mixer = jnp.clip(1.0 + 0.1 * jax.random.normal(streams_of[4], (D,), jnp.float32), 0.5, 1.5).astype(jnp.bfloat16)
    mixer_inner = scatter_about(streams_of[5], (D, INNER), D ** -0.5, 0.15625, ((1, 4),))
    mixer_gate = scatter_about(streams_of[6], (D, INNER), D ** -0.5, 0.15625, ((1, 4),))
    conv_taps = scatter_about(streams_of[7], (CONV, INNER), 1.25, 5.0, ((1, 4),))
    conv_bias = scatter_about(streams_of[8], (INNER,), 0.5, 3.0, ((0, 4),))
    state_proj = scatter_about(streams_of[9], (INNER, RANK + 2 * STATE), INNER ** -0.5, 0.109375, ((0, 4),))
    step_proj = scatter_about(streams_of[10], (RANK, INNER), RANK ** -0.5, 0.625, ((1, 4),))
    step_bias = jnp.clip(-10.0 + 7.0 * jax.random.uniform(streams_of[11], (INNER,), jnp.float32) ** block_scale(streams_of[11], (INNER,), ((0, 4),), -0.2, 0.2), -10.0, -3.0).astype(jnp.bfloat16)
    decay_log = jnp.clip(jax.random.uniform(streams_of[12], (INNER, STATE), jnp.float32, -1.0, 1.0) * block_scale(streams_of[12], (INNER, STATE), ((0, 4),), -0.4, 0.0), -1.0, 1.0).astype(jnp.bfloat16)
    skip_gain = jnp.clip(1.0 + 0.1 * jax.random.normal(streams_of[13], (INNER,), jnp.float32), 0.5, 1.5).astype(jnp.bfloat16)
    mixer_out = scatter_about(streams_of[14], (INNER, D), (INNER // 8) ** -0.5, 0.3125, ((0, 4),))
    norm_ffn = jnp.clip(1.0 + 0.1 * jax.random.normal(streams_of[15], (D,), jnp.float32), 0.5, 1.5).astype(jnp.bfloat16)
    ffn_gate = scatter_about(streams_of[16], (D, FF), D ** -0.5, 0.15625, ((1, 4),))
    ffn_up = scatter_about(streams_of[17], (D, FF), D ** -0.5, 0.15625, ((1, 4),))
    ffn_down = scatter_about(streams_of[18], (FF, D), (FF // 2) ** -0.5, 0.125, ((0, 4),))
    norm_attn = jnp.clip(1.0 + 0.1 * jax.random.normal(streams_of[19], (D,), jnp.float32), 0.5, 1.5).astype(jnp.bfloat16)
    attn_query = scatter_about(streams_of[20], (D, HEADS * HEAD_DIM), D ** -0.5, 0.15625, ((1, 4),))
    attn_key = scatter_about(streams_of[21], (D, KV_HEADS * HEAD_DIM), D ** -0.5, 0.15625, ((1, 4),))
    attn_value = scatter_about(streams_of[22], (D, KV_HEADS * HEAD_DIM), D ** -0.5, 0.15625, ((1, 4),))
    attn_output = scatter_about(streams_of[23], (HEADS * HEAD_DIM, D), (HEADS * HEAD_DIM // 64) ** -0.5, 1.25, ((0, 4),))
    norm_moe = jnp.clip(1.0 + 0.1 * jax.random.normal(streams_of[24], (D,), jnp.float32), 0.5, 1.5).astype(jnp.bfloat16)
    router = scatter_about(streams_of[25], (D, EXPERTS), D ** -0.5, 0.15625)
    expert_gate = scatter_about(streams_of[26], (EXPERTS, D, EFF), D ** -0.5, 0.15625, ((2, 4),))
    expert_up = scatter_about(streams_of[27], (EXPERTS, D, EFF), D ** -0.5, 0.15625, ((2, 4),))
    expert_down = scatter_about(streams_of[28], (EXPERTS, EFF, D), (EFF // 2) ** -0.5, 0.25, ((1, 4),))
    return {"tokens_in": tokens_in, "cotangent": cotangent, "document_ids": document_ids, "expert_routes": expert_routes, "norm_mixer": norm_mixer, "mixer_inner": mixer_inner, "mixer_gate": mixer_gate, "conv_taps": conv_taps, "conv_bias": conv_bias, "state_proj": state_proj, "step_proj": step_proj, "step_bias": step_bias, "decay_log": decay_log, "skip_gain": skip_gain, "mixer_out": mixer_out, "norm_ffn": norm_ffn, "ffn_gate": ffn_gate, "ffn_up": ffn_up, "ffn_down": ffn_down, "norm_attn": norm_attn, "attn_query": attn_query, "attn_key": attn_key, "attn_value": attn_value, "attn_output": attn_output, "norm_moe": norm_moe, "router": router, "expert_gate": expert_gate, "expert_up": expert_up, "expert_down": expert_down}


highest = lax.Precision.HIGHEST
epsilon = 1e-05
masked_score = -1e+30

@jax.custom_vjp
def low(v):
    return lax.optimization_barrier(v.astype(jnp.bfloat16)).astype(jnp.float32)

@jax.custom_vjp
def low_back(v):
    return v

def low_keep(v):
    return (low(v), None)

def low_pass(kept, grad):
    return (grad,)

def back_keep(v):
    return (v, None)

def back_low(kept, grad):
    return (low(grad),)
low.defvjp(low_keep, low_pass)
low_back.defvjp(back_keep, back_low)

def rounded(values):
    return low(low_back(values))

def matmul(left, right):
    return jnp.dot(left, right, precision=highest, preferred_element_type=jnp.float32)

def rms_scale(values, gain):
    return values * lax.rsqrt(lax.optimization_barrier(jnp.mean(values * values, axis=-1, keepdims=True)) + epsilon) * gain

def mixer_scan(step_dt, inputs, inject, readout, retain, decay_rate):
    row_total = step_dt.shape[0]
    length = math.gcd(row_total, 64)
    blocks = row_total // length

    def advance(carried, pieces):
        step_row, input_row, inject_row, readout_row, retain_row = pieces
        carried = carried * (jnp.exp(-step_row[:, None] * decay_rate) * retain_row) + (step_row * input_row)[:, None] * inject_row[None, :]
        return (carried, lax.optimization_barrier(jnp.sum(carried * readout_row[None, :], axis=1)))

    def run_block(carried, pieces):
        return lax.scan(advance, carried, pieces)

    def shaped(values):
        return values.reshape((blocks, length) + values.shape[1:])
    initial = jnp.zeros(decay_rate.shape, jnp.float32)
    unused, outputs = lax.scan(jax.checkpoint(run_block), initial, (shaped(step_dt), shaped(inputs), shaped(inject), shaped(readout), shaped(retain)))
    return outputs.reshape(step_dt.shape)

def attention(queries, keys_rows, values_rows, document_ids):
    group_size = queries.shape[1] // keys_rows.shape[1]
    keys_all = jnp.repeat(keys_rows, group_size, axis=1)
    values_all = jnp.repeat(values_rows, group_size, axis=1)
    token_count = queries.shape[0]
    block_rows = math.gcd(token_count, 128)
    positions = jnp.arange(token_count, dtype=jnp.int32)

    def one_block(block_index):
        offset = (block_index * block_rows).astype(jnp.int32)
        query_block = lax.dynamic_slice_in_dim(queries, offset, block_rows, 0)
        scores = low_back(jnp.einsum('qhd,khd->hqk', query_block, keys_all, precision=highest) * 0.125)
        query_pos = offset + jnp.arange(block_rows, dtype=jnp.int32)
        query_docs = lax.dynamic_slice_in_dim(document_ids, offset, block_rows, 0)
        allowed = (positions[None, :] <= query_pos[:, None]) & (document_ids[None, :] == query_docs[:, None])
        weights = jax.nn.softmax(jnp.where(allowed[None], scores, masked_score), axis=-1)
        return jnp.einsum('hqk,khd->qhd', low(weights), values_all, precision=highest)
    outputs = lax.map(jax.checkpoint(one_block), jnp.arange(token_count // block_rows, dtype=jnp.int32))
    return outputs.reshape(queries.shape)

def slot_index(expert_routes):
    token_count = expert_routes.shape[0]
    blocks = token_count // TOK_DEV
    route_rows = expert_routes.reshape(blocks, TOK_DEV * 2)
    one_hot = (route_rows[:, :, None] == jnp.arange(EXPERTS, dtype=jnp.int32)).astype(jnp.int32)
    earlier = jnp.cumsum(one_hot, axis=1) - one_hot
    within = lax.optimization_barrier(jnp.sum(earlier * one_hot, axis=2))
    block_base = (jnp.arange(blocks, dtype=jnp.int32) * (EXPERTS * CAP))[:, None]
    return (block_base + route_rows * CAP + within).reshape(token_count, 2).astype(jnp.int32)

def forward(tokens, params, document_ids, expert_routes):
    norm_mixer, mixer_inner, mixer_gate, conv_taps, conv_bias, state_proj, step_proj, step_bias, decay_log, skip_gain, mixer_out, norm_ffn, ffn_gate, ffn_up, ffn_down, norm_attn, attn_query, attn_key, attn_value, attn_output, norm_moe, router, expert_gate, expert_up, expert_down = params
    token_count = tokens.shape[0]
    previous_docs = jnp.concatenate([document_ids[:1], document_ids[:-1]])
    retain = (document_ids == previous_docs).astype(jnp.float32)
    normed_one = low(rms_scale(tokens, norm_mixer))
    conv_in = rounded(matmul(normed_one, mixer_inner))
    gate_in = low_back(matmul(normed_one, mixer_gate))
    conv_reach = conv_taps.shape[0] - 1
    padded = jnp.concatenate([jnp.zeros((conv_reach, conv_in.shape[1]), jnp.float32), conv_in])
    padded_docs = jnp.concatenate([jnp.full((conv_reach,), -1, jnp.int32), document_ids])
    conv_sum = conv_bias[None, :]
    for offset in range(conv_reach + 1):
        same_doc = (padded_docs[offset:offset + token_count] == document_ids).astype(jnp.float32)[:, None]
        conv_sum = conv_sum + conv_taps[offset] * padded[offset:offset + token_count] * same_doc
    activated = jax.nn.silu(conv_sum)
    projected = low_back(matmul(low(activated), state_proj))
    rank_size = step_proj.shape[0]
    state_size = decay_log.shape[1]
    step_pre = low_back(matmul(low(projected[:, :rank_size]), step_proj)) + step_bias
    step_dt = jax.nn.softplus(step_pre)
    scanned = mixer_scan(step_dt, activated, projected[:, rank_size:rank_size + state_size], projected[:, rank_size + state_size:], retain, jnp.exp(decay_log))
    gated = rounded((scanned + skip_gain * activated) * jax.nn.silu(gate_in))
    hidden_one = tokens + low_back(matmul(gated, mixer_out))
    normed_two = low(rms_scale(hidden_one, norm_ffn))
    gate_two = low_back(matmul(normed_two, ffn_gate))
    up_two = low_back(matmul(normed_two, ffn_up))
    ffn_act = rounded(jax.nn.silu(gate_two) * up_two)
    hidden_two = hidden_one + low_back(matmul(ffn_act, ffn_down))
    normed_three = low(rms_scale(hidden_two, norm_attn))
    queries = rounded(matmul(normed_three, attn_query)).reshape(token_count, HEADS, HEAD_DIM)
    keys_rows = rounded(matmul(normed_three, attn_key)).reshape(token_count, KV_HEADS, HEAD_DIM)
    values_rows = rounded(matmul(normed_three, attn_value)).reshape(token_count, KV_HEADS, HEAD_DIM)
    attended = rounded(attention(queries, keys_rows, values_rows, document_ids).reshape(token_count, HEADS * HEAD_DIM))
    hidden_three = hidden_two + low_back(matmul(attended, attn_output))
    normed_four = low(rms_scale(hidden_three, norm_moe))
    logits = matmul(normed_four, router)
    chosen = jnp.take_along_axis(logits, expert_routes, axis=1)
    gate_weights = jax.nn.softmax(chosen, axis=1)
    flat_slots = slot_index(expert_routes).reshape(-1)
    slot_total = token_count // TOK_DEV * EXPERTS * CAP
    dispatched = jnp.zeros((slot_total, D), jnp.float32).at[flat_slots].add(jnp.repeat(normed_four, 2, axis=0))
    expert_in = dispatched.reshape(-1, EXPERTS, CAP, D)
    gate_four = low_back(jnp.einsum('becd,edf->becf', expert_in, expert_gate, precision=highest))
    up_four = low_back(jnp.einsum('becd,edf->becf', expert_in, expert_up, precision=highest))
    acted = rounded(jax.nn.silu(gate_four) * up_four)
    expert_res = low_back(jnp.einsum('becf,efd->becd', acted, expert_down, precision=highest)).reshape(slot_total, D)
    picked = jnp.take(expert_res, flat_slots, axis=0).reshape(token_count, 2, D)
    return hidden_three + lax.optimization_barrier(jnp.sum(gate_weights[:, :, None] * picked, axis=1))

def reference(tokens_in, cotangent, document_ids, expert_routes, norm_mixer, mixer_inner, mixer_gate, conv_taps, conv_bias, state_proj, step_proj, step_bias, decay_log, skip_gain, mixer_out, norm_ffn, ffn_gate, ffn_up, ffn_down, norm_attn, attn_query, attn_key, attn_value, attn_output, norm_moe, router, expert_gate, expert_up, expert_down):
    weights = tuple((weight_in.astype(jnp.float32) for weight_in in (norm_mixer, mixer_inner, mixer_gate, conv_taps, conv_bias, state_proj, step_proj, step_bias, decay_log, skip_gain, mixer_out, norm_ffn, ffn_gate, ffn_up, ffn_down, norm_attn, attn_query, attn_key, attn_value, attn_output, norm_moe, router, expert_gate, expert_up, expert_down)))

    def apply_layers(tokens_wide, params):
        return forward(tokens_wide, params, document_ids, expert_routes)
    primal, pullback = jax.vjp(apply_layers, tokens_in.astype(jnp.float32), weights)
    grad_tokens, weight_grads = pullback(cotangent.astype(jnp.float32))
    return (primal.astype(jnp.bfloat16), grad_tokens, weight_grads[0], weight_grads[1], weight_grads[2], weight_grads[3], weight_grads[4], weight_grads[5], weight_grads[6], weight_grads[7], weight_grads[8], weight_grads[9], weight_grads[10], weight_grads[11], weight_grads[12], weight_grads[13], weight_grads[14], weight_grads[15], weight_grads[16], weight_grads[17], weight_grads[18], weight_grads[19], weight_grads[20], weight_grads[21], weight_grads[22], weight_grads[23], weight_grads[24])
```

```python
import math

import jax
import jax.numpy as jnp
from jax import lax
from jax.sharding import PartitionSpec as P

HEAD_DIM = 64
CAP = 160


highest = lax.Precision.HIGHEST
epsilon = 1e-05
masked_score = -1e30


def from_behind(block, axis, distance):
    devices = range(lax.axis_size(axis))
    route = [(i - distance, i) for i in devices if i - distance in devices]
    return lax.ppermute(block, axis, route)


def to_low(values):
    return values.astype(jnp.bfloat16)


def product(left, right):
    return jnp.dot(left, right, preferred_element_type=jnp.float32)


def exact_product(left, right):
    return jnp.dot(left, right, precision=highest, preferred_element_type=jnp.float32)


def rms_scale(values, gain):
    return values * lax.rsqrt(jnp.mean(values * values, axis=-1, keepdims=True) + epsilon) * gain


def rms_back(values, gain, upstream):
    unused, pullback = jax.vjp(rms_scale, values, gain)
    return pullback(upstream)


def silu_slope(values):
    logistic = jax.nn.sigmoid(values)
    return logistic * (1.0 + values * (1.0 - logistic))


def head_total(values):
    return lax.psum(values, "head")


def block_shape(row_total):
    length = math.gcd(row_total, 32)
    return (length, row_total // length)


def state_sweep(initial, step_dt, inputs, inject, readout, retain, decay_rate, collect):
    length, count = block_shape(step_dt.shape[0])

    def reshaped(values):
        return values.reshape((count, length) + values.shape[1:])

    def advance(carried, pieces):
        step_rows, input_rows, inject_rows, readout_rows, retain_rows = pieces
        decays = jnp.exp(-step_rows[:, :, None] * decay_rate[None]) * retain_rows[:, None, None]
        drives = (step_rows * input_rows)[:, :, None] * inject_rows[:, None, :]
        begin = carried
        outputs = []
        for offset in range(length):
            carried = carried * decays[offset] + drives[offset]
            if collect:
                outputs.append(jnp.sum(carried * readout_rows[offset][None, :], axis=1))
        if collect:
            return (carried, (jnp.stack(outputs), begin))
        return (carried, begin)

    return lax.scan(
        advance,
        initial,
        (
            reshaped(step_dt),
            reshaped(inputs),
            reshaped(inject),
            reshaped(readout),
            reshaped(retain),
        ),
    )


def adjoint_summary(step_dt, readout, upstream, retain, decay_rate):
    length, count = block_shape(step_dt.shape[0])

    def reshaped(values):
        return values.reshape((count, length) + values.shape[1:])

    def retreat(carried, pieces):
        step_rows, readout_rows, upstream_rows, retain_rows = pieces
        decays = jnp.exp(-step_rows[:, :, None] * decay_rate[None]) * retain_rows[:, None, None]
        for offset in reversed(range(length)):
            adjoint = readout_rows[offset][None, :] * upstream_rows[offset][:, None] + carried
            carried = decays[offset] * adjoint
        return (carried, None)

    initial = jnp.zeros(decay_rate.shape, jnp.float32)
    final, unused = lax.scan(
        retreat,
        initial,
        (reshaped(step_dt), reshaped(readout), reshaped(upstream), reshaped(retain)),
        reverse=True,
    )
    return final


def adjoint_sweep(incoming, starts, step_dt, inputs, inject, readout, upstream, retain, decay_rate):
    row_total = step_dt.shape[0]
    length, count = block_shape(row_total)

    def reshaped(values):
        return values.reshape((count, length) + values.shape[1:])

    def retreat(carried, pieces):
        adjoint_in, rate_grad = carried
        begin, step_rows, input_rows, inject_rows, readout_rows, upstream_rows, retain_rows = pieces
        decays = jnp.exp(-step_rows[:, :, None] * decay_rate[None]) * retain_rows[:, None, None]
        drives = (step_rows * input_rows)[:, :, None] * inject_rows[:, None, :]
        states = []
        running = begin
        for offset in range(length):
            running = running * decays[offset] + drives[offset]
            states.append(running)
        step_list = [None] * length
        input_list = [None] * length
        inject_list = [None] * length
        readout_list = [None] * length
        for offset in reversed(range(length)):
            previous = states[offset - 1] if offset > 0 else begin
            adjoint = readout_rows[offset][None, :] * upstream_rows[offset][:, None] + adjoint_in
            readout_list[offset] = jnp.sum(upstream_rows[offset][:, None] * states[offset], axis=0)
            through = adjoint * previous * decays[offset]
            rate_grad = rate_grad - through * step_rows[offset][:, None]
            injected = jnp.sum(adjoint * inject_rows[offset][None, :], axis=1)
            step_list[offset] = (
                -jnp.sum(through * decay_rate, axis=1) + input_rows[offset] * injected
            )
            input_list[offset] = step_rows[offset] * injected
            inject_list[offset] = jnp.sum(
                adjoint * (step_rows[offset] * input_rows[offset])[:, None], axis=0
            )
            adjoint_in = decays[offset] * adjoint
        return (
            (adjoint_in, rate_grad),
            (
                jnp.stack(step_list),
                jnp.stack(input_list),
                jnp.stack(inject_list),
                jnp.stack(readout_list),
            ),
        )

    initial = (incoming, jnp.zeros(decay_rate.shape, jnp.float32))
    carried, stacked = lax.scan(
        retreat,
        initial,
        (
            starts,
            reshaped(step_dt),
            reshaped(inputs),
            reshaped(inject),
            reshaped(readout),
            reshaped(upstream),
            reshaped(retain),
        ),
        reverse=True,
    )
    step_grad = stacked[0].reshape(row_total, -1)
    input_grad = stacked[1].reshape(row_total, -1)
    inject_grad = stacked[2].reshape(row_total, -1)
    readout_grad = stacked[3].reshape(row_total, -1)
    return (carried[1], step_grad, input_grad, inject_grad, readout_grad)


def body(
    tokens_in,
    cotangent,
    document_ids,
    expert_routes,
    norm_mixer,
    mixer_inner,
    mixer_gate,
    conv_taps,
    conv_bias,
    state_proj,
    step_proj,
    step_bias,
    decay_log,
    skip_gain,
    mixer_out,
    norm_ffn,
    ffn_gate,
    ffn_up,
    ffn_down,
    norm_attn,
    attn_query,
    attn_key,
    attn_value,
    attn_output,
    norm_moe,
    router,
    expert_gate,
    expert_up,
    expert_down,
):
    seq_count = lax.axis_size("seq")
    row_count = tokens_in.shape[0]
    total_rows = seq_count * row_count
    first_row = lax.axis_index("seq") * row_count
    last_row = first_row + row_count - 1
    local_docs = lax.dynamic_slice_in_dim(document_ids, first_row, row_count)
    reach = conv_taps.shape[0] - 1
    border = jnp.arange(reach, dtype=jnp.int32)
    docs_before = jnp.take(document_ids, jnp.maximum(first_row - reach + border, 0))
    docs_after = jnp.take(document_ids, jnp.minimum(first_row + row_count + border, total_rows - 1))
    docs_prior = jnp.concatenate([docs_before[reach - 1 :], local_docs[:-1]])
    retain = (local_docs == docs_prior).astype(jnp.float32)
    tokens = tokens_in.astype(jnp.float32)
    gain_mixer = norm_mixer.astype(jnp.float32)
    normed_one = to_low(rms_scale(tokens, gain_mixer))
    conv_in = to_low(product(normed_one, mixer_inner))
    gate_in = product(normed_one, mixer_gate)
    conv_edge = from_behind(conv_in[row_count - reach :], "seq", 1)
    extended = jnp.concatenate([conv_edge, conv_in]).astype(jnp.float32)
    docs_ext = jnp.concatenate([docs_before, local_docs])
    taps = conv_taps.astype(jnp.float32)
    conv_sum = conv_bias.astype(jnp.float32)[None, :]
    masks = []
    for offset in range(reach + 1):
        same_doc = (docs_ext[offset : offset + row_count] == local_docs).astype(jnp.float32)[
            :, None
        ]
        masks.append(same_doc)
        conv_sum = conv_sum + taps[offset] * extended[offset : offset + row_count] * same_doc
    activated = jax.nn.silu(conv_sum)
    act_low = to_low(activated)
    projected = head_total(product(act_low, state_proj))
    rank_size = step_proj.shape[0]
    state_size = decay_log.shape[1]
    step_low = to_low(projected[:, :rank_size])
    inject = projected[:, rank_size : rank_size + state_size]
    readout = projected[:, rank_size + state_size :]
    step_pre = product(step_low, step_proj) + step_bias.astype(jnp.float32)
    step_dt = jax.nn.softplus(step_pre)
    decay_rate = jnp.exp(decay_log.astype(jnp.float32))
    zero_state = jnp.zeros(decay_rate.shape, jnp.float32)
    whole_decay = jnp.exp(-decay_rate * jnp.sum(step_dt, axis=0)[:, None]) * jnp.prod(retain)
    local_last, unused = state_sweep(
        zero_state, step_dt, activated, inject, readout, retain, decay_rate, False
    )

    def hop_forward(position, incoming):
        return from_behind(
            (whole_decay * incoming + local_last).astype(jnp.bfloat16), "seq", 1
        ).astype(jnp.float32)

    state_in = lax.fori_loop(0, seq_count - 1, hop_forward, zero_state)
    state_out, collected = state_sweep(
        state_in, step_dt, activated, inject, readout, retain, decay_rate, True
    )
    scanned = collected[0].reshape(row_count, -1)
    starts = collected[1]
    skipping = skip_gain.astype(jnp.float32)
    mixed_state = scanned + skipping * activated
    gate_act = jax.nn.silu(gate_in)
    gated = to_low(mixed_state * gate_act)
    hidden_one = tokens + head_total(product(gated, mixer_out))
    gain_ffn = norm_ffn.astype(jnp.float32)
    normed_two = to_low(rms_scale(hidden_one, gain_ffn))
    gate_two = product(normed_two, ffn_gate)
    up_two = product(normed_two, ffn_up)
    ffn_act = to_low(jax.nn.silu(gate_two) * up_two)
    hidden_two = hidden_one + head_total(product(ffn_act, ffn_down))
    gain_attn = norm_attn.astype(jnp.float32)
    normed_three = to_low(rms_scale(hidden_two, gain_attn))
    queries = to_low(product(normed_three, attn_query))
    key_rows = to_low(product(normed_three, attn_key))
    value_rows = to_low(product(normed_three, attn_value))
    shared_heads = attn_key.shape[1] // HEAD_DIM
    group_size = attn_query.shape[1] // attn_key.shape[1]
    query_heads = queries.reshape(row_count, shared_heads, group_size, HEAD_DIM)
    query_pos = first_row + jnp.arange(row_count, dtype=jnp.int32)

    def visible(offset, block_rows):
        key_pos = offset + jnp.arange(block_rows, dtype=jnp.int32)
        key_docs = lax.dynamic_slice_in_dim(document_ids, offset, block_rows)
        return (key_pos[None, :] <= query_pos[:, None]) & (key_docs[None, :] == local_docs[:, None])

    def split_blocks(pieces, begin_row):
        key_piece, value_piece = pieces
        piece_rows = key_piece.shape[0]
        block_rows = math.gcd(piece_rows, 512)
        block_count = piece_rows // block_rows
        key_blocks = key_piece.reshape(block_count, block_rows, shared_heads, HEAD_DIM)
        value_blocks = value_piece.reshape(block_count, block_rows, shared_heads, HEAD_DIM)
        offsets = begin_row + block_rows * jnp.arange(block_count, dtype=jnp.int32)
        return (block_rows, (key_blocks, value_blocks, offsets))

    start_max = jnp.full((shared_heads, group_size, row_count), masked_score, jnp.float32)
    block_rows, blocked = split_blocks(
        (
            lax.all_gather(key_rows, "seq", axis=0, tiled=True),
            lax.all_gather(value_rows, "seq", axis=0, tiled=True),
        ),
        jnp.int32(0),
    )

    def visit_block(running, element):
        key_block, value_block, offset = element

        def compute(current):
            row_max, row_sum, weighted = current
            scores = (
                jnp.einsum(
                    "qgrd,kgd->grqk", query_heads, key_block, preferred_element_type=jnp.float32
                )
                * 0.125
            )
            allowed = visible(offset, block_rows)
            masked = jnp.where(allowed, scores, masked_score)
            new_max = jnp.maximum(row_max, jnp.max(masked, axis=-1))
            weights = jnp.where(allowed, jnp.exp(masked - new_max[..., None]), 0.0)
            factor = jnp.exp(row_max - new_max)
            row_sum = row_sum * factor + jnp.sum(weights, axis=-1)
            weighted = weighted * factor[..., None] + jnp.einsum(
                "grqk,kgd->grqd", to_low(weights), value_block, preferred_element_type=jnp.float32
            )
            return (new_max, row_sum, weighted)

        return (lax.cond(offset <= last_row, compute, lambda untouched: untouched, running), None)

    result, unused_out = lax.scan(
        visit_block,
        (
            start_max,
            jnp.zeros_like(start_max),
            jnp.zeros((shared_heads, group_size, row_count, HEAD_DIM), jnp.float32),
        ),
        blocked,
    )
    folded = result
    attended = folded[2] / folded[1][..., None]
    log_sum = folded[0] + jnp.log(folded[1])
    attended_low = to_low(attended.transpose(2, 0, 1, 3).reshape(row_count, -1))
    hidden_three = hidden_two + head_total(product(attended_low, attn_output))
    gain_moe = norm_moe.astype(jnp.float32)
    normed_four = to_low(rms_scale(hidden_three, gain_moe))
    router_wide = router.astype(jnp.float32)
    logits = exact_product(normed_four.astype(jnp.float32), router_wide)
    chosen = jnp.take_along_axis(logits, expert_routes, axis=1)
    gate_weights = jax.nn.softmax(chosen, axis=1)
    expert_count = router.shape[1]
    route_flat = expert_routes.reshape(-1)
    pair_order = jnp.arange(route_flat.shape[0], dtype=jnp.int32)
    earlier = (pair_order[None, :] < pair_order[:, None]) & (
        route_flat[None, :] == route_flat[:, None]
    )
    within = jnp.sum(earlier.astype(jnp.int32), axis=1)
    slot_index = route_flat * CAP + within
    pair_count = route_flat.shape[0]
    slot_pairs = (
        jnp.zeros((expert_count * CAP,), jnp.int32)
        .at[slot_index]
        .set(jnp.arange(pair_count, dtype=jnp.int32))
    )
    filled = jnp.zeros((expert_count * CAP,), jnp.float32).at[slot_index].set(1.0)
    expert_in = (jnp.take(normed_four, slot_pairs // 2, axis=0) * to_low(filled)[:, None]).reshape(
        expert_count, CAP, -1
    )
    gate_four = jnp.einsum(
        "ecd,edf->ecf", expert_in, expert_gate, preferred_element_type=jnp.float32
    )
    up_four = jnp.einsum("ecd,edf->ecf", expert_in, expert_up, preferred_element_type=jnp.float32)
    expert_act = to_low(jax.nn.silu(gate_four) * up_four)
    expert_res = jnp.einsum(
        "ecf,efd->ecd", expert_act, expert_down, preferred_element_type=jnp.float32
    ).reshape(expert_count * CAP, -1)
    picked = jnp.take(expert_res, slot_index, axis=0).reshape(row_count, 2, -1)
    hidden_four = hidden_three + head_total(jnp.sum(gate_weights[:, :, None] * picked, axis=1))
    mixed_out = to_low(hidden_four)
    upstream = cotangent.astype(jnp.float32)
    pair_grads = (gate_weights[:, :, None] * upstream[:, None, :]).reshape(pair_count, -1)
    res_grad = to_low(jnp.take(pair_grads, slot_pairs, axis=0) * filled[:, None]).reshape(
        expert_count, CAP, -1
    )
    dots_part = jnp.sum(picked * upstream[:, None, :], axis=2)
    act_back = to_low(
        jnp.einsum("ecd,efd->ecf", res_grad, expert_down, preferred_element_type=jnp.float32)
    ).astype(jnp.float32)
    gating_grad = to_low(act_back * up_four * silu_slope(gate_four))
    upward_grad = to_low(act_back * jax.nn.silu(gate_four))
    grad_expert_down = jnp.einsum(
        "ecf,ecd->efd", expert_act, res_grad, preferred_element_type=jnp.float32
    )
    grad_expert_gate = jnp.einsum(
        "ecd,ecf->edf", expert_in, gating_grad, preferred_element_type=jnp.float32
    )
    grad_expert_up = jnp.einsum(
        "ecd,ecf->edf", expert_in, upward_grad, preferred_element_type=jnp.float32
    )
    slot_grads = (
        jnp.einsum("ecf,edf->ecd", gating_grad, expert_gate, preferred_element_type=jnp.float32)
        + jnp.einsum("ecf,edf->ecd", upward_grad, expert_up, preferred_element_type=jnp.float32)
    ).reshape(expert_count * CAP, -1)
    token_part = jnp.sum(jnp.take(slot_grads, slot_index, axis=0).reshape(row_count, 2, -1), axis=1)
    normed_grad, dots = (
        lax.psum(token_part.astype(jnp.bfloat16), "head").astype(jnp.float32),
        lax.psum(dots_part.astype(jnp.bfloat16), "head").astype(jnp.float32),
    )
    chosen_grad = gate_weights * (dots - jnp.sum(gate_weights * dots, axis=1, keepdims=True))
    logit_grad = jnp.sum(
        (expert_routes[:, :, None] == jnp.arange(expert_count, dtype=jnp.int32)).astype(jnp.float32)
        * chosen_grad[:, :, None],
        axis=1,
    )
    grad_router = exact_product(normed_four.astype(jnp.float32).T, logit_grad)
    normed_grad = normed_grad + exact_product(logit_grad, router_wide.T)
    hidden_grad, grad_norm_moe = rms_back(hidden_three, gain_moe, normed_grad)
    three_grad = upstream + hidden_grad
    branch_grad = to_low(three_grad)
    grad_attn_output = product(attended_low.T, branch_grad)
    attended_grad = to_low(product(branch_grad, attn_output.T))
    out_heads = attended_grad.reshape(row_count, shared_heads, group_size, HEAD_DIM).transpose(
        1, 2, 0, 3
    )
    delta = jnp.sum(out_heads.astype(jnp.float32) * attended, axis=-1)
    key_width = key_rows.shape[1]
    initial = (
        jnp.zeros((shared_heads, group_size, row_count, HEAD_DIM), jnp.float32),
        jnp.zeros((total_rows, key_width), jnp.float32),
        jnp.zeros((total_rows, key_width), jnp.float32),
    )
    attend_block_rows, blocked = split_blocks(
        (
            lax.all_gather(key_rows, "seq", axis=0, tiled=True),
            lax.all_gather(value_rows, "seq", axis=0, tiled=True),
        ),
        jnp.int32(0),
    )

    def visit_back(running, element):
        key_block, value_block, offset = element

        def compute(current):
            query_acc, key_acc, value_acc = current
            scores = (
                jnp.einsum(
                    "qgrd,kgd->grqk", query_heads, key_block, preferred_element_type=jnp.float32
                )
                * 0.125
            )
            allowed = visible(offset, attend_block_rows)
            probs = jnp.where(allowed, jnp.exp(scores - log_sum[..., None]), 0.0)
            value_part = jnp.einsum(
                "grqk,grqd->kgd", to_low(probs), out_heads, preferred_element_type=jnp.float32
            )
            prob_grad = jnp.einsum(
                "grqd,kgd->grqk", out_heads, value_block, preferred_element_type=jnp.float32
            )
            score_grad = to_low(probs * (prob_grad - delta[..., None]))
            query_acc = (
                query_acc
                + jnp.einsum(
                    "grqk,kgd->grqd", score_grad, key_block, preferred_element_type=jnp.float32
                )
                * 0.125
            )
            key_part = (
                jnp.einsum(
                    "grqk,qgrd->kgd", score_grad, query_heads, preferred_element_type=jnp.float32
                )
                * 0.125
            )
            key_acc = lax.dynamic_update_slice_in_dim(
                key_acc,
                lax.dynamic_slice_in_dim(key_acc, offset, attend_block_rows, 0)
                + key_part.reshape(attend_block_rows, -1),
                offset,
                0,
            )
            value_acc = lax.dynamic_update_slice_in_dim(
                value_acc,
                lax.dynamic_slice_in_dim(value_acc, offset, attend_block_rows, 0)
                + value_part.reshape(attend_block_rows, -1),
                offset,
                0,
            )
            return (query_acc, key_acc, value_acc)

        return (lax.cond(offset <= last_row, compute, lambda untouched: untouched, running), None)

    result, unused_out = lax.scan(visit_back, initial, blocked)
    query_acc, key_acc, value_acc = result
    key_sum, value_sum = (
        lax.psum_scatter(
            key_acc.astype(jnp.bfloat16), "seq", scatter_dimension=0, tiled=True
        ).astype(jnp.float32),
        lax.psum_scatter(
            value_acc.astype(jnp.bfloat16), "seq", scatter_dimension=0, tiled=True
        ).astype(jnp.float32),
    )
    query_grad = to_low(query_acc.transpose(2, 0, 1, 3).reshape(row_count, -1))
    key_grad = to_low(key_sum)
    value_grad = to_low(value_sum)
    grad_attn_query = product(normed_three.T, query_grad)
    grad_attn_key = product(normed_three.T, key_grad)
    grad_attn_value = product(normed_three.T, value_grad)
    normed_grad = head_total(
        product(query_grad, attn_query.T)
        + product(key_grad, attn_key.T)
        + product(value_grad, attn_value.T)
    )
    hidden_grad, grad_norm_attn = rms_back(hidden_two, gain_attn, normed_grad)
    two_grad = three_grad + hidden_grad
    branch_grad = to_low(two_grad)
    grad_ffn_down = product(ffn_act.T, branch_grad)
    ffn_back = to_low(product(branch_grad, ffn_down.T)).astype(jnp.float32)
    feed_gate_grad = to_low(ffn_back * up_two * silu_slope(gate_two))
    feed_up_grad = to_low(ffn_back * jax.nn.silu(gate_two))
    grad_ffn_gate = product(normed_two.T, feed_gate_grad)
    grad_ffn_up = product(normed_two.T, feed_up_grad)
    normed_grad = head_total(product(feed_gate_grad, ffn_gate.T) + product(feed_up_grad, ffn_up.T))
    hidden_grad, grad_norm_ffn = rms_back(hidden_one, gain_ffn, normed_grad)
    one_grad = two_grad + hidden_grad
    branch_grad = to_low(one_grad)
    grad_mixer_out = product(gated.T, branch_grad)
    gated_grad = to_low(product(branch_grad, mixer_out.T)).astype(jnp.float32)
    scan_grad = gated_grad * gate_act
    gate_in_grad = to_low(gated_grad * mixed_state * silu_slope(gate_in))
    grad_skip_gain = jnp.sum(scan_grad * activated, axis=0)
    local_back = adjoint_summary(step_dt, readout, scan_grad, retain, decay_rate)

    def hop_backward(position, incoming):
        return from_behind(
            (whole_decay * incoming + local_back).astype(jnp.bfloat16), "seq", -1
        ).astype(jnp.float32)

    state_after = lax.fori_loop(0, seq_count - 1, hop_backward, zero_state)
    rate_grad, step_grad, input_grad, inject_grad, readout_grad = adjoint_sweep(
        state_after, starts, step_dt, activated, inject, readout, scan_grad, retain, decay_rate
    )
    grad_decay_log = rate_grad * decay_rate
    pre_grad = step_grad * jax.nn.sigmoid(step_pre)
    grad_step_bias = jnp.sum(pre_grad, axis=0)
    pre_low = to_low(pre_grad)
    grad_step_proj = product(step_low.T, pre_low)
    proj_part = jnp.concatenate([product(pre_low, step_proj.T), inject_grad, readout_grad], axis=1)
    proj_low = to_low(head_total(proj_part))
    grad_state_proj = product(act_low.T, proj_low)
    act_total = input_grad + skipping * scan_grad + product(proj_low, state_proj.T)
    conv_grad = act_total * silu_slope(conv_sum)
    grad_conv_bias = jnp.sum(conv_grad, axis=0)
    after_edge = from_behind(conv_grad[:reach], "seq", -1)
    grad_ext = jnp.concatenate([conv_grad, after_edge])
    docs_next = jnp.concatenate([local_docs, docs_after])
    conv_in_grad = jnp.zeros_like(conv_grad)
    tap_rows = []
    for offset in range(reach + 1):
        tap_rows.append(
            jnp.sum(conv_grad * extended[offset : offset + row_count] * masks[offset], axis=0)
        )
        lead = reach - offset
        same_next = (docs_next[lead : lead + row_count] == local_docs).astype(jnp.float32)[:, None]
        conv_in_grad = conv_in_grad + taps[offset] * grad_ext[lead : lead + row_count] * same_next
    grad_conv_taps = jnp.stack(tap_rows)
    conv_low = to_low(conv_in_grad)
    grad_mixer_inner = product(normed_one.T, conv_low)
    grad_mixer_gate = product(normed_one.T, gate_in_grad)
    normed_grad = head_total(product(conv_low, mixer_inner.T) + product(gate_in_grad, mixer_gate.T))
    hidden_grad, grad_norm_mixer = rms_back(tokens, gain_mixer, normed_grad)
    grad_tokens = one_grad + hidden_grad
    summed = (
        lax.psum_scatter(
            grad_norm_mixer.astype(jnp.bfloat16), "seq", scatter_dimension=0, tiled=True
        ).astype(jnp.float32),
        lax.psum_scatter(
            grad_mixer_inner.astype(jnp.bfloat16), "seq", scatter_dimension=0, tiled=True
        ).astype(jnp.float32),
        lax.psum_scatter(
            grad_mixer_gate.astype(jnp.bfloat16), "seq", scatter_dimension=0, tiled=True
        ).astype(jnp.float32),
        lax.psum_scatter(
            grad_conv_taps.astype(jnp.bfloat16), "seq", scatter_dimension=1, tiled=True
        ).astype(jnp.float32),
        lax.psum_scatter(
            grad_conv_bias.astype(jnp.bfloat16), "seq", scatter_dimension=0, tiled=True
        ).astype(jnp.float32),
        lax.psum_scatter(
            grad_state_proj.astype(jnp.bfloat16), "seq", scatter_dimension=0, tiled=True
        ).astype(jnp.float32),
        lax.psum_scatter(
            grad_step_proj.astype(jnp.bfloat16), "seq", scatter_dimension=1, tiled=True
        ).astype(jnp.float32),
        lax.psum_scatter(
            grad_step_bias.astype(jnp.bfloat16), "seq", scatter_dimension=0, tiled=True
        ).astype(jnp.float32),
        lax.psum_scatter(
            grad_decay_log.astype(jnp.bfloat16), "seq", scatter_dimension=0, tiled=True
        ).astype(jnp.float32),
        lax.psum_scatter(
            grad_skip_gain.astype(jnp.bfloat16), "seq", scatter_dimension=0, tiled=True
        ).astype(jnp.float32),
        lax.psum_scatter(
            grad_mixer_out.astype(jnp.bfloat16), "seq", scatter_dimension=1, tiled=True
        ).astype(jnp.float32),
        lax.psum_scatter(
            grad_norm_ffn.astype(jnp.bfloat16), "seq", scatter_dimension=0, tiled=True
        ).astype(jnp.float32),
        lax.psum_scatter(
            grad_ffn_gate.astype(jnp.bfloat16), "seq", scatter_dimension=0, tiled=True
        ).astype(jnp.float32),
        lax.psum_scatter(
            grad_ffn_up.astype(jnp.bfloat16), "seq", scatter_dimension=0, tiled=True
        ).astype(jnp.float32),
        lax.psum_scatter(
            grad_ffn_down.astype(jnp.bfloat16), "seq", scatter_dimension=1, tiled=True
        ).astype(jnp.float32),
        lax.psum_scatter(
            grad_norm_attn.astype(jnp.bfloat16), "seq", scatter_dimension=0, tiled=True
        ).astype(jnp.float32),
        lax.psum_scatter(
            grad_attn_query.astype(jnp.bfloat16), "seq", scatter_dimension=0, tiled=True
        ).astype(jnp.float32),
        lax.psum_scatter(
            grad_attn_key.astype(jnp.bfloat16), "seq", scatter_dimension=0, tiled=True
        ).astype(jnp.float32),
        lax.psum_scatter(
            grad_attn_value.astype(jnp.bfloat16), "seq", scatter_dimension=0, tiled=True
        ).astype(jnp.float32),
        lax.psum_scatter(
            grad_attn_output.astype(jnp.bfloat16), "seq", scatter_dimension=1, tiled=True
        ).astype(jnp.float32),
        lax.psum_scatter(
            grad_norm_moe.astype(jnp.bfloat16), "seq", scatter_dimension=0, tiled=True
        ).astype(jnp.float32),
        lax.psum_scatter(
            grad_router.astype(jnp.bfloat16), "seq", scatter_dimension=0, tiled=True
        ).astype(jnp.float32),
        lax.psum_scatter(
            grad_expert_gate.astype(jnp.bfloat16), "seq", scatter_dimension=1, tiled=True
        ).astype(jnp.float32),
        lax.psum_scatter(
            grad_expert_up.astype(jnp.bfloat16), "seq", scatter_dimension=1, tiled=True
        ).astype(jnp.float32),
        lax.psum_scatter(
            grad_expert_down.astype(jnp.bfloat16), "seq", scatter_dimension=2, tiled=True
        ).astype(jnp.float32),
    )
    return (
        mixed_out,
        grad_tokens,
        summed[0],
        summed[1],
        summed[2],
        summed[3],
        summed[4],
        summed[5],
        summed[6],
        summed[7],
        summed[8],
        summed[9],
        summed[10],
        summed[11],
        summed[12],
        summed[13],
        summed[14],
        summed[15],
        summed[16],
        summed[17],
        summed[18],
        summed[19],
        summed[20],
        summed[21],
        summed[22],
        summed[23],
        summed[24],
    )


def solution(mesh):
    in_specs = (
        P("seq", None),
        P("seq", None),
        P(),
        P("seq", None),
        P(),
        P(None, "head"),
        P(None, "head"),
        P(None, "head"),
        P("head"),
        P("head", None),
        P(None, "head"),
        P("head"),
        P("head", None),
        P("head"),
        P("head", None),
        P(),
        P(None, "head"),
        P(None, "head"),
        P("head", None),
        P(),
        P(None, "head"),
        P(None, "head"),
        P(None, "head"),
        P("head", None),
        P(),
        P(),
        P(None, None, "head"),
        P(None, None, "head"),
        P(None, "head", None),
    )
    out_specs = (
        P("seq", None),
        P("seq", None),
        P("seq"),
        P("seq", "head"),
        P("seq", "head"),
        P(None, ("head", "seq")),
        P(("head", "seq")),
        P(("head", "seq"), None),
        P(None, ("head", "seq")),
        P(("head", "seq")),
        P(("head", "seq"), None),
        P(("head", "seq")),
        P("head", "seq"),
        P("seq"),
        P("seq", "head"),
        P("seq", "head"),
        P("head", "seq"),
        P("seq"),
        P("seq", "head"),
        P("seq", "head"),
        P("seq", "head"),
        P("head", "seq"),
        P("seq"),
        P("seq", None),
        P(None, "seq", "head"),
        P(None, "seq", "head"),
        P(None, "head", "seq"),
    )
    return jax.shard_map(body, mesh=mesh, in_specs=in_specs, out_specs=out_specs, check_vma=False)
```

```python
import itertools
import math

import jax
import jax.numpy as jnp
from jax import lax
from jax.experimental import pallas as pl
from jax.experimental.pallas import tpu as pltpu
from jax.sharding import PartitionSpec as P

HEAD_DIM = 64
CAP = 160
LANES = 128
LOG2E = 1.4426950408889634
LN2 = 0.6931471805599453
NEVER = 1e30
LIMIT = 56 * 1024 * 1024
MESH = pl.DeviceIdType.MESH
VMEM = pl.BlockSpec(memory_space=pltpu.VMEM)
ANY = pl.BlockSpec(memory_space=pl.ANY)


highest = lax.Precision.HIGHEST
epsilon = 1e-05
masked_score = -1e30


def from_behind(block, axis, distance):
    devices = range(lax.axis_size(axis))
    route = [(i - distance, i) for i in devices if i - distance in devices]
    return lax.ppermute(block, axis, route)


def to_low(values):
    return values.astype(jnp.bfloat16)


def product(left, right):
    return jnp.dot(left, right, preferred_element_type=jnp.float32)


def exact_product(left, right):
    return jnp.dot(left, right, precision=highest, preferred_element_type=jnp.float32)


def rms_scale(values, gain):
    return values * lax.rsqrt(jnp.mean(values * values, axis=-1, keepdims=True) + epsilon) * gain


def rms_back(values, gain, upstream):
    unused, pullback = jax.vjp(rms_scale, values, gain)
    return pullback(upstream)


def silu_slope(values):
    logistic = jax.nn.sigmoid(values)
    return logistic * (1.0 + values * (1.0 - logistic))


def meet(peers):
    barrier = pltpu.get_barrier_semaphore()
    for peer in peers:
        pl.semaphore_signal(barrier, inc=1, device_id=peer, device_id_type=MESH)
    pl.semaphore_wait(barrier, len(peers))


def send_to(source, target, send_sem, recv_sem, peer):
    return pltpu.make_async_remote_copy(
        src_ref=source,
        dst_ref=target,
        send_sem=send_sem,
        recv_sem=recv_sem,
        device_id=peer,
        device_id_type=MESH,
    )


def talking(number):
    return pltpu.CompilerParams(
        collective_id=number, has_side_effects=True, vmem_limit_bytes=LIMIT
    )


def head_sum(values, number, wire, pieces):
    rows, width = values.shape
    half = rows // 2
    step = half // pieces

    def kernel(x_ref, o_ref, near_out, near_in, far_out, far_in, send, recv):
        seq = lax.axis_index("seq")
        head = lax.axis_index("head")
        core = head % 2
        near = (seq, head + 1 - 2 * core)
        far = (seq, (head + 2) % 4)
        meet([near, far])

        def rows_of(side, piece):
            return pl.ds(pl.multiple_of(side * half + piece * step, 8), step)

        copies = []
        for piece in range(pieces):
            local = pl.ds(piece * step, step)
            near_out[local] = x_ref[rows_of(1 - core, piece)].astype(wire)
            copy = send_to(
                near_out.at[local], near_in.at[local], send.at[0, piece], recv.at[0, piece], near
            )
            copy.start()
            copies.append(copy)
        second = []
        for piece in range(pieces):
            local = pl.ds(piece * step, step)
            copies[piece].wait_recv()
            total = x_ref[rows_of(core, piece)] + near_in[local].astype(jnp.float32)
            far_out[local] = total.astype(wire)
            copy = send_to(
                far_out.at[local], far_in.at[local], send.at[1, piece], recv.at[1, piece], far
            )
            copy.start()
            second.append(copy)
        third = []
        for piece in range(pieces):
            local = pl.ds(piece * step, step)
            second[piece].wait_recv()
            whole = far_out[local].astype(jnp.float32) + far_in[local].astype(jnp.float32)
            o_ref[rows_of(core, piece)] = whole
            copy = send_to(
                o_ref.at[rows_of(core, piece)],
                o_ref.at[rows_of(core, piece)],
                send.at[2, piece],
                recv.at[2, piece],
                near,
            )
            copy.start()
            third.append(copy)
        for copy in third:
            copy.wait_recv()
        for copy in copies + second + third:
            copy.wait_send()

    return pl.pallas_call(
        kernel,
        out_shape=jax.ShapeDtypeStruct((rows, width), jnp.float32),
        in_specs=[VMEM],
        out_specs=VMEM,
        scratch_shapes=[pltpu.VMEM((half, width), wire)] * 4
        + [pltpu.SemaphoreType.DMA((3, pieces))] * 2,
        compiler_params=talking(number),
        name="head_sum",
    )(values)


def seq_gather(block, number):
    rows, width = block.shape
    seq_count = lax.axis_size("seq")
    pairs = seq_count // 2

    def kernel(x_ref, o_ref, send, recv, pass_send, pass_recv, own_sem):
        seq = lax.axis_index("seq")
        head = lax.axis_index("head")
        place = seq % 2
        pair = seq // 2
        partner = (seq + 1 - 2 * place, head)
        others = [(((pair + k) % pairs) * 2 + place, head) for k in range(1, pairs)]
        meet([partner] + others)
        own = pltpu.make_async_copy(x_ref, o_ref.at[seq], own_sem)
        own.start()
        first = [
            send_to(x_ref, o_ref.at[seq], send.at[k], recv.at[k], others[k])
            for k in range(pairs - 1)
        ]
        passed = [send_to(x_ref, o_ref.at[seq], pass_send.at[0], pass_recv.at[0], partner)]
        passed[0].start()
        for copy in first:
            copy.start()
        for k in range(1, pairs):
            first[k - 1].wait_recv()
            origin = ((pair - k + pairs) % pairs) * 2 + place
            copy = send_to(
                o_ref.at[origin], o_ref.at[origin], pass_send.at[k], pass_recv.at[k], partner
            )
            copy.start()
            passed.append(copy)
        for copy in passed:
            copy.wait_recv()
        for copy in first + passed:
            copy.wait_send()
        own.wait()

    out = pl.pallas_call(
        kernel,
        out_shape=jax.ShapeDtypeStruct((seq_count, rows, width), block.dtype),
        in_specs=[VMEM],
        out_specs=VMEM,
        scratch_shapes=[pltpu.SemaphoreType.DMA((pairs,))] * 4 + [pltpu.SemaphoreType.DMA],
        compiler_params=talking(number),
        name="seq_gather",
    )(block)
    return out.reshape(seq_count * rows, width)


def seq_scatter(arrays, number):
    seq_count = lax.axis_size("seq")
    pairs = seq_count // 2
    count = len(arrays)
    shapes = [(a.shape[0] // seq_count, a.shape[1]) for a in arrays]
    blocks = [
        a.reshape(pairs, 2, shape[0], shape[1]) for a, shape in zip(arrays, shapes, strict=True)
    ]

    def kernel(*refs):
        takes, gives = refs[:count], refs[count : 2 * count]
        own, near = refs[2 * count : 3 * count], refs[3 * count : 4 * count]
        far = refs[4 * count : 5 * count]
        own_sem, near_send, near_recv, far_send, far_recv = refs[5 * count :]
        seq = lax.axis_index("seq")
        head = lax.axis_index("head")
        place = seq % 2
        pair = seq // 2
        partner = (seq + 1 - 2 * place, head)
        owners = [(pair + k) % pairs for k in range(1, pairs)]
        others = [(owner * 2 + place, head) for owner in owners]
        meet([partner] + others)
        loads = [
            pltpu.make_async_copy(takes[i].at[:, place], own[i], own_sem.at[i])
            for i in range(count)
        ]
        halves = [
            send_to(takes[i].at[:, 1 - place], near[i], near_send.at[i], near_recv.at[i], partner)
            for i in range(count)
        ]

        def launch(i):
            if i < count:
                halves[i].start()
                loads[i].start()

        sums = []

        def finish(i):
            rows = shapes[i][0]
            for copy in sums[i]:
                copy.wait_recv()

            @pl.loop(0, rows // 16)
            def add(step):
                part = pl.ds(pl.multiple_of(step * 16, 16), 16)
                total = own[i][pair, part].astype(jnp.float32)
                for k in range(pairs - 1):
                    total = total + far[i][k, part].astype(jnp.float32)
                gives[i][part] = total

        launch(0)
        launch(1)
        for i in range(count):
            rows = shapes[i][0]
            halves[i].wait_recv()
            loads[i].wait()
            launch(i + 2)

            @pl.loop(0, pairs)
            def merge(block):
                @pl.loop(0, rows // 16)
                def add(step):
                    part = pl.ds(pl.multiple_of(step * 16, 16), 16)
                    total = own[i][block, part].astype(jnp.float32) + near[i][block, part].astype(
                        jnp.float32
                    )
                    own[i][block, part] = total.astype(jnp.bfloat16)

            sums.append(
                [
                    send_to(
                        own[i].at[owners[k]],
                        far[i].at[k],
                        far_send.at[i, k],
                        far_recv.at[i, k],
                        others[k],
                    )
                    for k in range(pairs - 1)
                ]
            )
            for copy in sums[i]:
                copy.start()
            if i > 0:
                finish(i - 1)
        finish(count - 1)
        for copy in halves:
            copy.wait_send()
        for group in sums:
            for copy in group:
                copy.wait_send()

    return pl.pallas_call(
        kernel,
        out_shape=[jax.ShapeDtypeStruct(shape, jnp.float32) for shape in shapes],
        in_specs=[ANY] * count,
        out_specs=[VMEM] * count,
        scratch_shapes=[pltpu.VMEM((pairs,) + shape, jnp.bfloat16) for shape in shapes] * 2
        + [pltpu.VMEM((pairs - 1,) + shape, jnp.bfloat16) for shape in shapes]
        + [pltpu.SemaphoreType.DMA((count,))] * 3
        + [pltpu.SemaphoreType.DMA((count, pairs - 1))] * 2,
        compiler_params=talking(number),
        name="seq_scatter",
    )(*blocks)


def widen(column_block, width):
    return jnp.concatenate([column_block] * (width // LANES), axis=-1)


def narrow(wide):
    width = wide.shape[-1]
    total = wide[:, :LANES]
    for place in range(1, width // LANES):
        total = total + wide[:, place * LANES : (place + 1) * LANES]
    return total


def spread(columns):
    return jnp.broadcast_to(columns[:, :, None], columns.shape + (LANES,))


def run_summary(steps, drives, coefficients, slopes, number, forward):
    rows, width = steps.shape
    entries = slopes.shape[0]
    seq_count = lax.axis_size("seq")
    group = math.gcd(rows, 8)

    def kernel(step_ref, drive_ref, coef_ref, slope_ref, o_ref, outgoing, incoming, send, recv):
        seq = lax.axis_index("seq")
        head = lax.axis_index("head")
        peers = [((seq + k) % seq_count, head) for k in range(1, seq_count)]
        meet(peers)
        slope = slope_ref[...]

        def advance(position, state):
            for offset in range(group):
                t = position * group + offset
                t = t if forward else rows - 1 - t
                decays = jnp.exp2(step_ref[pl.ds(t, 1), :] * slope)
                drive = drive_ref[pl.ds(t, 1), :] * widen(coef_ref[t], width)
                state = state * decays + drive if forward else (state + drive) * decays
            return state

        state = lax.fori_loop(0, rows // group, advance, jnp.zeros((entries, width), jnp.float32))
        whole = jnp.exp2(jnp.sum(step_ref[...], axis=0, keepdims=True) * slope)
        outgoing[:entries] = state.astype(jnp.bfloat16)
        outgoing[entries:] = whole.astype(jnp.bfloat16)
        copies = [
            send_to(outgoing, incoming.at[k], send.at[k], recv.at[k], peers[k])
            for k in range(seq_count - 1)
        ]
        for copy in copies:
            copy.start()
        for copy in copies:
            copy.wait_recv()
        carried = jnp.zeros((entries, width), jnp.float32)
        order = range(seq_count - 1, 0, -1) if forward else range(1, seq_count)
        for k in order:
            known = seq - k >= 0 if forward else seq - k < 0
            block = incoming[k - 1].astype(jnp.float32)
            carried = jnp.where(known, block[entries:] * carried + block[:entries], 0.0)
        o_ref[...] = carried
        for copy in copies:
            copy.wait_send()

    return pl.pallas_call(
        kernel,
        out_shape=jax.ShapeDtypeStruct((entries, width), jnp.float32),
        in_specs=[VMEM] * 4,
        out_specs=VMEM,
        scratch_shapes=[
            pltpu.VMEM((2 * entries, width), jnp.bfloat16),
            pltpu.VMEM((seq_count - 1, 2 * entries, width), jnp.bfloat16),
            pltpu.SemaphoreType.DMA((seq_count - 1,)),
            pltpu.SemaphoreType.DMA((seq_count - 1,)),
        ],
        compiler_params=talking(number),
        name="run_summary",
    )(steps, drives, coefficients, slopes)


def state_sweep(initial, steps, drives, inject, readout, slopes):
    rows, width = steps.shape
    entries = slopes.shape[0]
    length = math.gcd(rows, 32)
    group = math.gcd(length, 8)

    def kernel(
        init_ref, step_ref, drive_ref, inject_ref, read_ref, slope_ref, y_ref, before_ref, end_ref
    ):
        @pl.when(pl.program_id(0) == 0)
        def begin():
            end_ref[...] = init_ref[...]

        slope = slope_ref[...]

        def advance(position, state):
            for offset in range(group):
                t = position * group + offset
                before_ref[t] = state
                decays = jnp.exp2(step_ref[pl.ds(t, 1), :] * slope)
                drive = drive_ref[pl.ds(t, 1), :] * widen(inject_ref[t], width)
                state = state * decays + drive
                y_ref[pl.ds(t, 1), :] = jnp.sum(
                    state * widen(read_ref[t], width), axis=0, keepdims=True
                )
            return state

        end_ref[...] = lax.fori_loop(0, length // group, advance, end_ref[...])

    row_spec = pl.BlockSpec((length, width), lambda i: (i, 0))
    entry_spec = pl.BlockSpec((length, entries, LANES), lambda i: (i, 0, 0))
    fixed = pl.BlockSpec((entries, width), lambda i: (0, 0))
    return pl.pallas_call(
        kernel,
        grid=(rows // length,),
        out_shape=(
            jax.ShapeDtypeStruct((rows, width), jnp.float32),
            jax.ShapeDtypeStruct((rows, entries, width), jnp.float32),
            jax.ShapeDtypeStruct((entries, width), jnp.float32),
        ),
        in_specs=[fixed, row_spec, row_spec, entry_spec, entry_spec, fixed],
        out_specs=(
            row_spec,
            pl.BlockSpec((length, entries, width), lambda i: (i, 0, 0)),
            fixed,
        ),
        compiler_params=pltpu.CompilerParams(vmem_limit_bytes=LIMIT),
        name="state_sweep",
    )(initial, steps, drives, inject, readout, slopes)


def adjoint_sweep(incoming, last_state, befores, steps, drives, inject, readout, upstream, slopes):
    rows, width = steps.shape
    entries = slopes.shape[0]
    length = math.gcd(rows, 32)
    group = math.gcd(length, 8)
    blocks = rows // length

    def kernel(
        in_ref,
        last_ref,
        before_ref,
        step_ref,
        drive_ref,
        inject_ref,
        read_ref,
        up_ref,
        slope_ref,
        through_ref,
        injected_ref,
        inject_out,
        read_out,
        rate_ref,
        adjoint_ref,
        state_ref,
    ):
        @pl.when(pl.program_id(0) == 0)
        def begin():
            adjoint_ref[...] = in_ref[...]
            state_ref[...] = last_ref[...]
            rate_ref[...] = jnp.zeros_like(rate_ref)

        slope = slope_ref[...]

        def retreat(position, carried):
            adjoint_in, rate = carried
            for offset in range(group):
                t = length - 1 - (position * group + offset)
                upper = up_ref[pl.ds(t, 1), :]
                step = step_ref[pl.ds(t, 1), :]
                adjoint = widen(read_ref[t], width) * upper + adjoint_in
                state = state_ref[...] if offset == 0 else before_ref[t + 1]
                read_out[t] = narrow(upper * state)
                adjoint_in = jnp.exp2(step * slope) * adjoint
                before = before_ref[t]
                through = adjoint_in * before
                rate = rate + through * step
                through_ref[pl.ds(t, 1), :] = jnp.sum(through * slope, axis=0, keepdims=True)
                injected_ref[pl.ds(t, 1), :] = jnp.sum(
                    adjoint * widen(inject_ref[t], width), axis=0, keepdims=True
                )
                inject_out[t] = narrow(adjoint * drive_ref[pl.ds(t, 1), :])
            state_ref[...] = before_ref[length - (position + 1) * group]
            return (adjoint_in, rate)

        adjoint_end, rate_end = lax.fori_loop(
            0, length // group, retreat, (adjoint_ref[...], rate_ref[...])
        )
        adjoint_ref[...] = adjoint_end
        rate_ref[...] = rate_end

    row_spec = pl.BlockSpec((length, width), lambda i: (blocks - 1 - i, 0))
    entry_spec = pl.BlockSpec((length, entries, LANES), lambda i: (blocks - 1 - i, 0, 0))
    fixed = pl.BlockSpec((entries, width), lambda i: (0, 0))
    wide = jax.ShapeDtypeStruct((rows, width), jnp.float32)
    partial = jax.ShapeDtypeStruct((rows, entries, LANES), jnp.float32)
    return pl.pallas_call(
        kernel,
        grid=(blocks,),
        out_shape=(
            wide,
            wide,
            partial,
            partial,
            jax.ShapeDtypeStruct((entries, width), jnp.float32),
        ),
        in_specs=[
            fixed,
            fixed,
            pl.BlockSpec((length, entries, width), lambda i: (blocks - 1 - i, 0, 0)),
            row_spec,
            row_spec,
            entry_spec,
            entry_spec,
            row_spec,
            fixed,
        ],
        out_specs=(row_spec, row_spec, entry_spec, entry_spec, fixed),
        scratch_shapes=[pltpu.VMEM((entries, width), jnp.float32)] * 2,
        compiler_params=pltpu.CompilerParams(vmem_limit_bytes=LIMIT),
        name="adjoint_sweep",
    )(incoming, last_state, befores, steps, drives, inject, readout, upstream, slopes)


def body(
    tokens_in,
    cotangent,
    document_ids,
    expert_routes,
    norm_mixer,
    mixer_inner,
    mixer_gate,
    conv_taps,
    conv_bias,
    state_proj,
    step_proj,
    step_bias,
    decay_log,
    skip_gain,
    mixer_out,
    norm_ffn,
    ffn_gate,
    ffn_up,
    ffn_down,
    norm_attn,
    attn_query,
    attn_key,
    attn_value,
    attn_output,
    norm_moe,
    router,
    expert_gate,
    expert_up,
    expert_down,
):
    numbers = itertools.count()
    seq_count = lax.axis_size("seq")
    row_count = tokens_in.shape[0]
    total_rows = seq_count * row_count
    first_row = lax.axis_index("seq") * row_count
    last_row = first_row + row_count - 1

    def by_model_rows(pattern, left, right):
        blocks = to_low(jnp.einsum(pattern, left, right, preferred_element_type=jnp.float32))
        return blocks.transpose(1, 0, 2).reshape(blocks.shape[1], -1)

    def branch_sum(values):
        return head_sum(values, next(numbers), jnp.bfloat16, 4)

    local_docs = lax.dynamic_slice_in_dim(document_ids, first_row, row_count)
    reach = conv_taps.shape[0] - 1
    border = jnp.arange(reach, dtype=jnp.int32)
    docs_before = jnp.take(document_ids, jnp.maximum(first_row - reach + border, 0))
    docs_after = jnp.take(document_ids, jnp.minimum(first_row + row_count + border, total_rows - 1))
    docs_prior = jnp.concatenate([docs_before[reach - 1 :], local_docs[:-1]])
    retain = (local_docs == docs_prior).astype(jnp.float32)
    tokens = tokens_in.astype(jnp.float32)
    gain_mixer = norm_mixer.astype(jnp.float32)
    normed_one = to_low(rms_scale(tokens, gain_mixer))
    conv_in = to_low(product(normed_one, mixer_inner))
    gate_in = product(normed_one, mixer_gate)
    conv_edge = from_behind(conv_in[row_count - reach :], "seq", 1)
    extended = jnp.concatenate([conv_edge, conv_in]).astype(jnp.float32)
    docs_ext = jnp.concatenate([docs_before, local_docs])
    taps = conv_taps.astype(jnp.float32)
    conv_sum = conv_bias.astype(jnp.float32)[None, :]
    masks = []
    for offset in range(reach + 1):
        same_doc = (docs_ext[offset : offset + row_count] == local_docs).astype(jnp.float32)[
            :, None
        ]
        masks.append(same_doc)
        conv_sum = conv_sum + taps[offset] * extended[offset : offset + row_count] * same_doc
    activated = jax.nn.silu(conv_sum)
    act_low = to_low(activated)
    projected = head_sum(product(act_low, state_proj), next(numbers), jnp.float32, 1)
    rank_size = step_proj.shape[0]
    state_size = decay_log.shape[1]
    step_low = to_low(projected[:, :rank_size])
    inject = projected[:, rank_size : rank_size + state_size]
    readout = projected[:, rank_size + state_size :]
    step_pre = product(step_low, step_proj) + step_bias.astype(jnp.float32)
    step_dt = jax.nn.softplus(step_pre)
    decay_rate = jnp.exp(decay_log.astype(jnp.float32)).T
    slopes = -LOG2E * decay_rate
    steps = jnp.where(retain[:, None] > 0.0, step_dt, NEVER)
    drives = step_dt * activated
    inject_wide = spread(inject)
    readout_wide = spread(readout)
    state_in = run_summary(steps, drives, inject_wide, slopes, next(numbers), True)
    scanned, befores, state_out = state_sweep(
        state_in, steps, drives, inject_wide, readout_wide, slopes
    )
    skipping = skip_gain.astype(jnp.float32)
    mixed_state = scanned + skipping * activated
    gate_act = jax.nn.silu(gate_in)
    gated = to_low(mixed_state * gate_act)
    hidden_one = tokens + branch_sum(product(gated, mixer_out))
    gain_ffn = norm_ffn.astype(jnp.float32)
    normed_two = to_low(rms_scale(hidden_one, gain_ffn))
    gate_two = product(normed_two, ffn_gate)
    up_two = product(normed_two, ffn_up)
    ffn_act = to_low(jax.nn.silu(gate_two) * up_two)
    hidden_two = hidden_one + branch_sum(product(ffn_act, ffn_down))
    gain_attn = norm_attn.astype(jnp.float32)
    normed_three = to_low(rms_scale(hidden_two, gain_attn))
    queries = to_low(product(normed_three, attn_query))
    key_rows = to_low(product(normed_three, attn_key))
    value_rows = to_low(product(normed_three, attn_value))
    shared_heads = attn_key.shape[1] // HEAD_DIM
    group_size = attn_query.shape[1] // attn_key.shape[1]
    query_heads = queries.reshape(row_count, shared_heads, group_size, HEAD_DIM)
    query_pos = first_row + jnp.arange(row_count, dtype=jnp.int32)

    def visible(offset, block_rows):
        key_pos = offset + jnp.arange(block_rows, dtype=jnp.int32)
        key_docs = lax.dynamic_slice_in_dim(document_ids, offset, block_rows)
        return (key_pos[None, :] <= query_pos[:, None]) & (key_docs[None, :] == local_docs[:, None])

    def split_blocks(pieces, begin_row):
        key_piece, value_piece = pieces
        piece_rows = key_piece.shape[0]
        block_rows = math.gcd(piece_rows, 512)
        block_count = piece_rows // block_rows
        key_blocks = key_piece.reshape(block_count, block_rows, shared_heads, HEAD_DIM)
        value_blocks = value_piece.reshape(block_count, block_rows, shared_heads, HEAD_DIM)
        offsets = begin_row + block_rows * jnp.arange(block_count, dtype=jnp.int32)
        return (block_rows, (key_blocks, value_blocks, offsets))

    both_rows = seq_gather(jnp.concatenate([key_rows, value_rows], axis=1), next(numbers))
    key_width = key_rows.shape[1]
    gathered = (both_rows[:, :key_width], both_rows[:, key_width:])
    start_max = jnp.full((shared_heads, group_size, row_count), masked_score, jnp.float32)
    block_rows, blocked = split_blocks(
        gathered,
        jnp.int32(0),
    )

    def visit_block(running, element):
        key_block, value_block, offset = element

        def compute(current):
            row_max, row_sum, weighted = current
            scores = (
                jnp.einsum(
                    "qgrd,kgd->grqk", query_heads, key_block, preferred_element_type=jnp.float32
                )
                * 0.125
            )
            allowed = visible(offset, block_rows)
            masked = jnp.where(allowed, scores, masked_score)
            new_max = jnp.maximum(row_max, jnp.max(masked, axis=-1))
            weights = jnp.where(allowed, jnp.exp(masked - new_max[..., None]), 0.0)
            factor = jnp.exp(row_max - new_max)
            row_sum = row_sum * factor + jnp.sum(weights, axis=-1)
            weighted = weighted * factor[..., None] + jnp.einsum(
                "grqk,kgd->grqd", to_low(weights), value_block, preferred_element_type=jnp.float32
            )
            return (new_max, row_sum, weighted)

        return (lax.cond(offset <= last_row, compute, lambda untouched: untouched, running), None)

    result, unused_out = lax.scan(
        visit_block,
        (
            start_max,
            jnp.zeros_like(start_max),
            jnp.zeros((shared_heads, group_size, row_count, HEAD_DIM), jnp.float32),
        ),
        blocked,
    )
    folded = result
    attended = folded[2] / folded[1][..., None]
    log_sum = folded[0] + jnp.log(folded[1])
    attended_low = to_low(attended.transpose(2, 0, 1, 3).reshape(row_count, -1))
    hidden_three = hidden_two + branch_sum(product(attended_low, attn_output))
    gain_moe = norm_moe.astype(jnp.float32)
    normed_four = to_low(rms_scale(hidden_three, gain_moe))
    logits = product(normed_four, router)
    expert_count = router.shape[1]
    experts = jnp.arange(expert_count, dtype=jnp.int32)
    named = (expert_routes[:, :, None] == experts).astype(jnp.float32)
    gate_weights = jax.nn.softmax(jnp.sum(named * logits[:, None, :], axis=2), axis=1)
    route_flat = expert_routes.reshape(-1)
    pair_count = route_flat.shape[0]
    pair_order = jnp.arange(pair_count, dtype=jnp.int32)
    earlier = (pair_order[None, :] < pair_order[:, None]) & (
        route_flat[None, :] == route_flat[:, None]
    )
    within = jnp.sum(earlier.astype(jnp.int32), axis=1)
    slot_index = (route_flat * CAP + within).reshape(row_count, 2)
    slots = jnp.arange(expert_count * CAP, dtype=jnp.int32)
    first_hit = slot_index[:, 0][None, :] == slots[:, None]
    second_hit = slot_index[:, 1][None, :] == slots[:, None]
    placing = (first_hit | second_hit).astype(jnp.bfloat16)
    slot_gates = jnp.sum(
        jnp.where(first_hit, gate_weights[:, 0][None, :], 0.0)
        + jnp.where(second_hit, gate_weights[:, 1][None, :], 0.0),
        axis=1,
    )
    expert_in = to_low(product(placing, normed_four)).reshape(expert_count, CAP, -1)
    slot_upstream = product(placing, cotangent)
    res_grad = to_low(slot_gates[:, None] * slot_upstream).reshape(expert_count, CAP, -1)
    gate_four = jnp.einsum(
        "ecd,edf->ecf", expert_in, expert_gate, preferred_element_type=jnp.float32
    )
    up_four = jnp.einsum("ecd,edf->ecf", expert_in, expert_up, preferred_element_type=jnp.float32)
    expert_act = to_low(jax.nn.silu(gate_four) * up_four)
    expert_res = jnp.einsum(
        "ecf,efd->ecd", expert_act, expert_down, preferred_element_type=jnp.float32
    ).reshape(expert_count * CAP, -1)
    upstream = cotangent.astype(jnp.float32)
    slot_dots = jnp.sum(expert_res * slot_upstream, axis=1)
    dots_part = jnp.stack(
        [
            jnp.sum(jnp.where(first_hit, slot_dots[:, None], 0.0), axis=0),
            jnp.sum(jnp.where(second_hit, slot_dots[:, None], 0.0), axis=0),
        ],
        axis=1,
    )
    combined = product(placing.T, to_low(slot_gates[:, None] * expert_res))
    act_back = to_low(
        jnp.einsum("ecd,efd->ecf", res_grad, expert_down, preferred_element_type=jnp.float32)
    ).astype(jnp.float32)
    gating_grad = to_low(act_back * up_four * silu_slope(gate_four))
    upward_grad = to_low(act_back * jax.nn.silu(gate_four))
    grad_expert_down = by_model_rows("ecd,ecf->edf", res_grad, expert_act)
    grad_expert_gate = by_model_rows("ecd,ecf->edf", expert_in, gating_grad)
    grad_expert_up = by_model_rows("ecd,ecf->edf", expert_in, upward_grad)
    slot_grads = (
        jnp.einsum("ecf,edf->ecd", gating_grad, expert_gate, preferred_element_type=jnp.float32)
        + jnp.einsum("ecf,edf->ecd", upward_grad, expert_up, preferred_element_type=jnp.float32)
    ).reshape(expert_count * CAP, -1)
    token_part = product(placing.T, to_low(slot_grads))
    model_width = tokens.shape[1]
    expert_sums = branch_sum(
        jnp.concatenate(
            [combined, token_part, jnp.pad(dots_part, ((0, 0), (0, LANES - 2)))], axis=1
        )
    )
    mixed_out = to_low(hidden_three + expert_sums[:, :model_width])
    normed_grad = expert_sums[:, model_width : 2 * model_width]
    dots = expert_sums[:, 2 * model_width : 2 * model_width + 2]
    chosen_grad = gate_weights * (dots - jnp.sum(gate_weights * dots, axis=1, keepdims=True))
    logit_grad = jnp.sum(named * chosen_grad[:, :, None], axis=1)
    grad_router = exact_product(normed_four.astype(jnp.float32).T, logit_grad)
    normed_grad = normed_grad + exact_product(logit_grad, router.astype(jnp.float32).T)
    hidden_grad, grad_norm_moe = rms_back(hidden_three, gain_moe, normed_grad)
    three_grad = upstream + hidden_grad
    branch_grad = to_low(three_grad)
    grad_attn_output = to_low(product(branch_grad.T, attended_low))
    attended_grad = to_low(product(branch_grad, attn_output.T))
    out_heads = attended_grad.reshape(row_count, shared_heads, group_size, HEAD_DIM).transpose(
        1, 2, 0, 3
    )
    delta = jnp.sum(out_heads.astype(jnp.float32) * attended, axis=-1)
    initial = (
        jnp.zeros((shared_heads, group_size, row_count, HEAD_DIM), jnp.float32),
        jnp.zeros((total_rows, key_width), jnp.float32),
        jnp.zeros((total_rows, key_width), jnp.float32),
    )
    attend_block_rows, blocked = split_blocks(
        gathered,
        jnp.int32(0),
    )

    def visit_back(running, element):
        key_block, value_block, offset = element

        def compute(current):
            query_acc, key_acc, value_acc = current
            scores = (
                jnp.einsum(
                    "qgrd,kgd->grqk", query_heads, key_block, preferred_element_type=jnp.float32
                )
                * 0.125
            )
            allowed = visible(offset, attend_block_rows)
            probs = jnp.where(allowed, jnp.exp(scores - log_sum[..., None]), 0.0)
            value_part = jnp.einsum(
                "grqk,grqd->kgd", to_low(probs), out_heads, preferred_element_type=jnp.float32
            )
            prob_grad = jnp.einsum(
                "grqd,kgd->grqk", out_heads, value_block, preferred_element_type=jnp.float32
            )
            score_grad = to_low(probs * (prob_grad - delta[..., None]))
            query_acc = (
                query_acc
                + jnp.einsum(
                    "grqk,kgd->grqd", score_grad, key_block, preferred_element_type=jnp.float32
                )
                * 0.125
            )
            key_part = (
                jnp.einsum(
                    "grqk,qgrd->kgd", score_grad, query_heads, preferred_element_type=jnp.float32
                )
                * 0.125
            )
            key_acc = lax.dynamic_update_slice_in_dim(
                key_acc,
                lax.dynamic_slice_in_dim(key_acc, offset, attend_block_rows, 0)
                + key_part.reshape(attend_block_rows, -1),
                offset,
                0,
            )
            value_acc = lax.dynamic_update_slice_in_dim(
                value_acc,
                lax.dynamic_slice_in_dim(value_acc, offset, attend_block_rows, 0)
                + value_part.reshape(attend_block_rows, -1),
                offset,
                0,
            )
            return (query_acc, key_acc, value_acc)

        return (lax.cond(offset <= last_row, compute, lambda untouched: untouched, running), None)

    result, unused_out = lax.scan(visit_back, initial, blocked)
    query_acc, key_acc, value_acc = result
    (both_sums,) = seq_scatter(
        [to_low(jnp.concatenate([key_acc, value_acc], axis=1))], next(numbers)
    )
    key_sum, value_sum = both_sums[:, :key_width], both_sums[:, key_width:]
    query_grad = to_low(query_acc.transpose(2, 0, 1, 3).reshape(row_count, -1))
    key_grad = to_low(key_sum)
    value_grad = to_low(value_sum)
    grad_attn_in = to_low(
        product(normed_three.T, jnp.concatenate([query_grad, key_grad, value_grad], axis=1))
    )
    normed_grad = branch_sum(
        product(query_grad, attn_query.T)
        + product(key_grad, attn_key.T)
        + product(value_grad, attn_value.T)
    )
    hidden_grad, grad_norm_attn = rms_back(hidden_two, gain_attn, normed_grad)
    two_grad = three_grad + hidden_grad
    branch_grad = to_low(two_grad)
    grad_ffn_down = to_low(product(branch_grad.T, ffn_act))
    ffn_back = to_low(product(branch_grad, ffn_down.T)).astype(jnp.float32)
    feed_gate_grad = to_low(ffn_back * up_two * silu_slope(gate_two))
    feed_up_grad = to_low(ffn_back * jax.nn.silu(gate_two))
    grad_ffn_gate = to_low(product(normed_two.T, feed_gate_grad))
    grad_ffn_up = to_low(product(normed_two.T, feed_up_grad))
    normed_grad = branch_sum(product(feed_gate_grad, ffn_gate.T) + product(feed_up_grad, ffn_up.T))
    hidden_grad, grad_norm_ffn = rms_back(hidden_one, gain_ffn, normed_grad)
    one_grad = two_grad + hidden_grad
    branch_grad = to_low(one_grad)
    grad_mixer_out = to_low(product(branch_grad.T, gated))
    gated_grad = to_low(product(branch_grad, mixer_out.T)).astype(jnp.float32)
    scan_grad = gated_grad * gate_act
    gate_in_grad = to_low(gated_grad * mixed_state * silu_slope(gate_in))
    grad_skip_gain = jnp.sum(scan_grad * activated, axis=0)
    state_after = run_summary(steps, scan_grad, readout_wide, slopes, next(numbers), False)
    through_sum, injected, inject_part, readout_part, rate_sum = adjoint_sweep(
        state_after,
        state_out,
        befores,
        steps,
        drives,
        inject_wide,
        readout_wide,
        scan_grad,
        slopes,
    )
    step_grad = LN2 * through_sum + activated * injected
    input_grad = step_dt * injected
    inject_grad = jnp.sum(inject_part, axis=2)
    readout_grad = jnp.sum(readout_part, axis=2)
    grad_decay_log = -rate_sum * decay_rate
    pre_grad = step_grad * jax.nn.sigmoid(step_pre)
    grad_step_bias = jnp.sum(pre_grad, axis=0)
    pre_low = to_low(pre_grad)
    grad_step_proj = product(step_low.T, pre_low)
    proj_part = jnp.concatenate([product(pre_low, step_proj.T), inject_grad, readout_grad], axis=1)
    proj_low = to_low(head_sum(proj_part, next(numbers), jnp.float32, 1))
    grad_state_proj = product(act_low.T, proj_low)
    act_total = input_grad + skipping * scan_grad + product(proj_low, state_proj.T)
    conv_grad = act_total * silu_slope(conv_sum)
    grad_conv_bias = jnp.sum(conv_grad, axis=0)
    after_edge = from_behind(conv_grad[:reach], "seq", -1)
    grad_ext = jnp.concatenate([conv_grad, after_edge])
    docs_next = jnp.concatenate([local_docs, docs_after])
    conv_in_grad = jnp.zeros_like(conv_grad)
    tap_rows = []
    for offset in range(reach + 1):
        tap_rows.append(
            jnp.sum(conv_grad * extended[offset : offset + row_count] * masks[offset], axis=0)
        )
        lead = reach - offset
        same_next = (docs_next[lead : lead + row_count] == local_docs).astype(jnp.float32)[:, None]
        conv_in_grad = conv_in_grad + taps[offset] * grad_ext[lead : lead + row_count] * same_next
    grad_conv_taps = jnp.stack(tap_rows)
    conv_low = to_low(conv_in_grad)
    grad_mixer_inner = to_low(product(normed_one.T, conv_low))
    grad_mixer_gate = to_low(product(normed_one.T, gate_in_grad))
    normed_grad = branch_sum(product(conv_low, mixer_inner.T) + product(gate_in_grad, mixer_gate.T))
    hidden_grad, grad_norm_mixer = rms_back(tokens, gain_mixer, normed_grad)
    grad_tokens = one_grad + hidden_grad
    own_channels = grad_conv_bias.shape[0] // seq_count

    def cut(values, axis):
        values = jnp.moveaxis(values, axis, 0)
        return values.reshape(seq_count, -1)

    packed = jnp.concatenate(
        [
            cut(grad_norm_mixer, 0),
            cut(grad_norm_ffn, 0),
            cut(grad_norm_attn, 0),
            cut(grad_norm_moe, 0),
            cut(grad_router, 0),
            cut(grad_conv_taps, 1),
            cut(grad_conv_bias, 0),
            cut(grad_state_proj, 0),
            cut(grad_step_proj, 1),
            cut(grad_step_bias, 0),
            cut(grad_decay_log, 1),
            cut(grad_skip_gain, 0),
        ],
        axis=1,
    )
    spare = -packed.shape[1] % (16 * LANES)
    packed = to_low(jnp.pad(packed, ((0, 0), (0, spare)))).reshape(-1, LANES)
    (
        sum_expert_gate,
        sum_expert_up,
        sum_expert_down,
        sum_ffn_gate,
        sum_ffn_up,
        sum_ffn_down,
        sum_attn_in,
        sum_attn_output,
        sum_mixer_out,
        sum_mixer_inner,
        sum_mixer_gate,
        sum_packed,
    ) = seq_scatter(
        [
            grad_expert_gate,
            grad_expert_up,
            grad_expert_down,
            grad_ffn_gate,
            grad_ffn_up,
            grad_ffn_down,
            grad_attn_in,
            grad_attn_output,
            grad_mixer_out,
            grad_mixer_inner,
            grad_mixer_gate,
            packed,
        ],
        next(numbers),
    )
    sum_packed = sum_packed.reshape(-1)
    own_rows = model_width // seq_count
    taken = itertools.accumulate(
        [0]
        + [own_rows] * 4
        + [own_rows * expert_count]
        + [own_channels * (reach + 1), own_channels, own_channels * state_proj.shape[1]]
        + [own_channels * rank_size, own_channels, own_channels * state_size, own_channels]
    )
    bounds = list(taken)
    pieces = [sum_packed[low:high] for low, high in itertools.pairwise(bounds)]
    query_width = attn_query.shape[1]

    def by_expert(values):
        return values.reshape(values.shape[0], expert_count, -1)

    return (
        mixed_out,
        grad_tokens,
        pieces[0],
        sum_mixer_inner,
        sum_mixer_gate,
        pieces[5].reshape(own_channels, -1).T,
        pieces[6],
        pieces[7].reshape(own_channels, -1),
        pieces[8].reshape(own_channels, -1).T,
        pieces[9],
        pieces[10].reshape(own_channels, -1),
        pieces[11],
        sum_mixer_out.T,
        pieces[1],
        sum_ffn_gate,
        sum_ffn_up,
        sum_ffn_down.T,
        pieces[2],
        sum_attn_in[:, :query_width],
        sum_attn_in[:, query_width : query_width + key_width],
        sum_attn_in[:, query_width + key_width :],
        sum_attn_output.T,
        pieces[3],
        pieces[4].reshape(own_rows, -1),
        by_expert(sum_expert_gate).transpose(1, 0, 2),
        by_expert(sum_expert_up).transpose(1, 0, 2),
        by_expert(sum_expert_down).transpose(1, 2, 0),
    )


def solution(mesh):
    in_specs = (
        P("seq", None),
        P("seq", None),
        P(),
        P("seq", None),
        P(),
        P(None, "head"),
        P(None, "head"),
        P(None, "head"),
        P("head"),
        P("head", None),
        P(None, "head"),
        P("head"),
        P("head", None),
        P("head"),
        P("head", None),
        P(),
        P(None, "head"),
        P(None, "head"),
        P("head", None),
        P(),
        P(None, "head"),
        P(None, "head"),
        P(None, "head"),
        P("head", None),
        P(),
        P(),
        P(None, None, "head"),
        P(None, None, "head"),
        P(None, "head", None),
    )
    out_specs = (
        P("seq", None),
        P("seq", None),
        P("seq"),
        P("seq", "head"),
        P("seq", "head"),
        P(None, ("head", "seq")),
        P(("head", "seq")),
        P(("head", "seq"), None),
        P(None, ("head", "seq")),
        P(("head", "seq")),
        P(("head", "seq"), None),
        P(("head", "seq")),
        P("head", "seq"),
        P("seq"),
        P("seq", "head"),
        P("seq", "head"),
        P("head", "seq"),
        P("seq"),
        P("seq", "head"),
        P("seq", "head"),
        P("seq", "head"),
        P("head", "seq"),
        P("seq"),
        P("seq", None),
        P(None, "seq", "head"),
        P(None, "seq", "head"),
        P(None, "head", "seq"),
    )
    return jax.shard_map(body, mesh=mesh, in_specs=in_specs, out_specs=out_specs, check_vma=False)
```

```python
import itertools
import math

import jax
import jax.numpy as jnp
from jax import lax
from jax.experimental import pallas as pl
from jax.experimental.pallas import tpu as pltpu
from jax.sharding import PartitionSpec as P

HEAD_DIM = 64
CAP = 160
LANES = 128
LOG2E = 1.4426950408889634
LN2 = 0.6931471805599453
NEVER = 1e30
LIMIT = 56 * 1024 * 1024
MESH = pl.DeviceIdType.MESH
VMEM = pl.BlockSpec(memory_space=pltpu.VMEM)
ANY = pl.BlockSpec(memory_space=pl.ANY)


highest = lax.Precision.HIGHEST
epsilon = 1e-05
masked_score = -1e30


def from_behind(block, axis, distance):
    devices = range(lax.axis_size(axis))
    route = [(i - distance, i) for i in devices if i - distance in devices]
    return lax.ppermute(block, axis, route)


def to_low(values):
    return values.astype(jnp.bfloat16)


def product(left, right):
    return jnp.dot(left, right, preferred_element_type=jnp.float32)


def exact_product(left, right):
    return jnp.dot(left, right, precision=highest, preferred_element_type=jnp.float32)


def rms_scale(values, gain):
    return values * lax.rsqrt(jnp.mean(values * values, axis=-1, keepdims=True) + epsilon) * gain


def rms_back(values, gain, upstream):
    unused, pullback = jax.vjp(rms_scale, values, gain)
    return pullback(upstream)


def silu_slope(values):
    logistic = jax.nn.sigmoid(values)
    return logistic * (1.0 + values * (1.0 - logistic))


def meet(peers):
    barrier = pltpu.get_barrier_semaphore()
    for peer in peers:
        pl.semaphore_signal(barrier, inc=1, device_id=peer, device_id_type=MESH)
    pl.semaphore_wait(barrier, len(peers))


def send_to(source, target, send_sem, recv_sem, peer):
    return pltpu.make_async_remote_copy(
        src_ref=source,
        dst_ref=target,
        send_sem=send_sem,
        recv_sem=recv_sem,
        device_id=peer,
        device_id_type=MESH,
    )


def lasting(microseconds):
    return pl.CostEstimate(
        flops=int(microseconds * 1e3),
        bytes_accessed=int(microseconds * 1e3),
        transcendentals=0,
    )


def talking(number):
    return pltpu.CompilerParams(
        collective_id=number, has_side_effects=True, vmem_limit_bytes=LIMIT
    )


def head_sum(values, number, wire, pieces):
    rows, width = values.shape
    half = rows // 2
    step = half // pieces

    def kernel(x_ref, o_ref, near_out, near_in, far_out, far_in, send, recv):
        seq = lax.axis_index("seq")
        head = lax.axis_index("head")
        core = head % 2
        near = (seq, head + 1 - 2 * core)
        far = (seq, (head + 2) % 4)
        meet([near, far])

        def rows_of(side, piece):
            return pl.ds(pl.multiple_of(side * half + piece * step, 8), step)

        copies = []
        for piece in range(pieces):
            local = pl.ds(piece * step, step)
            near_out[local] = x_ref[rows_of(1 - core, piece)].astype(wire)
            copy = send_to(
                near_out.at[local], near_in.at[local], send.at[0, piece], recv.at[0, piece], near
            )
            copy.start()
            copies.append(copy)
        second = []
        for piece in range(pieces):
            local = pl.ds(piece * step, step)
            copies[piece].wait_recv()
            total = x_ref[rows_of(core, piece)] + near_in[local].astype(jnp.float32)
            far_out[local] = total.astype(wire)
            copy = send_to(
                far_out.at[local], far_in.at[local], send.at[1, piece], recv.at[1, piece], far
            )
            copy.start()
            second.append(copy)
        third = []
        for piece in range(pieces):
            local = pl.ds(piece * step, step)
            second[piece].wait_recv()
            whole = far_out[local].astype(jnp.float32) + far_in[local].astype(jnp.float32)
            o_ref[rows_of(core, piece)] = whole
            copy = send_to(
                o_ref.at[rows_of(core, piece)],
                o_ref.at[rows_of(core, piece)],
                send.at[2, piece],
                recv.at[2, piece],
                near,
            )
            copy.start()
            third.append(copy)
        for copy in third:
            copy.wait_recv()
        for copy in copies + second + third:
            copy.wait_send()

    return pl.pallas_call(
        kernel,
        out_shape=jax.ShapeDtypeStruct((rows, width), jnp.float32),
        in_specs=[VMEM],
        out_specs=VMEM,
        scratch_shapes=[pltpu.VMEM((half, width), wire)] * 4
        + [pltpu.SemaphoreType.DMA((3, pieces))] * 2,
        compiler_params=talking(number),
        cost_estimate=lasting(6 + values.size // 40000),
        name="head_sum",
    )(values)


def seq_gather(block, number):
    rows, width = block.shape
    seq_count = lax.axis_size("seq")
    pairs = seq_count // 2

    def kernel(x_ref, o_ref, send, recv, pass_send, pass_recv, own_sem):
        seq = lax.axis_index("seq")
        head = lax.axis_index("head")
        place = seq % 2
        pair = seq // 2
        partner = (seq + 1 - 2 * place, head)
        others = [(((pair + k) % pairs) * 2 + place, head) for k in range(1, pairs)]
        meet([partner] + others)
        own = pltpu.make_async_copy(x_ref, o_ref.at[seq], own_sem)
        own.start()
        first = [
            send_to(x_ref, o_ref.at[seq], send.at[k], recv.at[k], others[k])
            for k in range(pairs - 1)
        ]
        passed = [send_to(x_ref, o_ref.at[seq], pass_send.at[0], pass_recv.at[0], partner)]
        passed[0].start()
        for copy in first:
            copy.start()
        for k in range(1, pairs):
            first[k - 1].wait_recv()
            origin = ((pair - k + pairs) % pairs) * 2 + place
            copy = send_to(
                o_ref.at[origin], o_ref.at[origin], pass_send.at[k], pass_recv.at[k], partner
            )
            copy.start()
            passed.append(copy)
        for copy in passed:
            copy.wait_recv()
        for copy in first + passed:
            copy.wait_send()
        own.wait()

    out = pl.pallas_call(
        kernel,
        out_shape=jax.ShapeDtypeStruct((seq_count, rows, width), block.dtype),
        in_specs=[VMEM],
        out_specs=VMEM,
        scratch_shapes=[pltpu.SemaphoreType.DMA((pairs,))] * 4 + [pltpu.SemaphoreType.DMA],
        compiler_params=talking(number),
        cost_estimate=lasting(20),
        name="seq_gather",
    )(block)
    return out.reshape(seq_count * rows, width)


def seq_scatter(arrays, number):
    seq_count = lax.axis_size("seq")
    pairs = seq_count // 2
    count = len(arrays)
    shapes = [(a.shape[0] // seq_count, a.shape[1]) for a in arrays]
    blocks = [
        a.reshape(pairs, 2, shape[0], shape[1]) for a, shape in zip(arrays, shapes, strict=True)
    ]

    def kernel(*refs):
        takes, gives = refs[:count], refs[count : 2 * count]
        own, near = refs[2 * count : 3 * count], refs[3 * count : 4 * count]
        far = refs[4 * count : 5 * count]
        own_sem, near_send, near_recv, far_send, far_recv = refs[5 * count :]
        seq = lax.axis_index("seq")
        head = lax.axis_index("head")
        place = seq % 2
        pair = seq // 2
        partner = (seq + 1 - 2 * place, head)
        owners = [(pair + k) % pairs for k in range(1, pairs)]
        others = [(owner * 2 + place, head) for owner in owners]
        meet([partner] + others)
        loads = [
            pltpu.make_async_copy(takes[i].at[:, place], own[i], own_sem.at[i])
            for i in range(count)
        ]
        halves = [
            send_to(takes[i].at[:, 1 - place], near[i], near_send.at[i], near_recv.at[i], partner)
            for i in range(count)
        ]

        def launch(i):
            if i < count:
                halves[i].start()
                loads[i].start()

        sums = []

        def finish(i):
            rows = shapes[i][0]
            for copy in sums[i]:
                copy.wait_recv()

            @pl.loop(0, rows // 16)
            def add(step):
                part = pl.ds(pl.multiple_of(step * 16, 16), 16)
                total = own[i][pair, part].astype(jnp.float32)
                for k in range(pairs - 1):
                    total = total + far[i][k, part].astype(jnp.float32)
                gives[i][part] = total

        launch(0)
        launch(1)
        for i in range(count):
            rows = shapes[i][0]
            halves[i].wait_recv()
            loads[i].wait()
            launch(i + 2)

            @pl.loop(0, pairs)
            def merge(block):
                @pl.loop(0, rows // 16)
                def add(step):
                    part = pl.ds(pl.multiple_of(step * 16, 16), 16)
                    total = own[i][block, part].astype(jnp.float32) + near[i][block, part].astype(
                        jnp.float32
                    )
                    own[i][block, part] = total.astype(jnp.bfloat16)

            sums.append(
                [
                    send_to(
                        own[i].at[owners[k]],
                        far[i].at[k],
                        far_send.at[i, k],
                        far_recv.at[i, k],
                        others[k],
                    )
                    for k in range(pairs - 1)
                ]
            )
            for copy in sums[i]:
                copy.start()
            if i > 0:
                finish(i - 1)
        finish(count - 1)
        for copy in halves:
            copy.wait_send()
        for group in sums:
            for copy in group:
                copy.wait_send()

    return pl.pallas_call(
        kernel,
        out_shape=[jax.ShapeDtypeStruct(shape, jnp.float32) for shape in shapes],
        in_specs=[ANY] * count,
        out_specs=[VMEM] * count,
        scratch_shapes=[pltpu.VMEM((pairs,) + shape, jnp.bfloat16) for shape in shapes] * 2
        + [pltpu.VMEM((pairs - 1,) + shape, jnp.bfloat16) for shape in shapes]
        + [pltpu.SemaphoreType.DMA((count,))] * 3
        + [pltpu.SemaphoreType.DMA((count, pairs - 1))] * 2,
        compiler_params=talking(number),
        cost_estimate=lasting(15 + sum(a.size for a in arrays) // 50000),
        name="seq_scatter",
    )(*blocks)


def widen(column_block, width):
    return jnp.concatenate([column_block] * (width // LANES), axis=-1)


def narrow(wide):
    width = wide.shape[-1]
    total = wide[:, :LANES]
    for place in range(1, width // LANES):
        total = total + wide[:, place * LANES : (place + 1) * LANES]
    return total


def spread(columns):
    return jnp.broadcast_to(columns[:, :, None], columns.shape + (LANES,))


def run_summary(steps, drives, coefficients, slopes, number, forward):
    rows, width = steps.shape
    entries = slopes.shape[0]
    seq_count = lax.axis_size("seq")
    group = math.gcd(rows, 8)

    def kernel(step_ref, drive_ref, coef_ref, slope_ref, o_ref, outgoing, incoming, send, recv):
        seq = lax.axis_index("seq")
        head = lax.axis_index("head")
        peers = [((seq + k) % seq_count, head) for k in range(1, seq_count)]
        meet(peers)
        slope = slope_ref[...]

        def advance(position, state):
            for offset in range(group):
                t = position * group + offset
                t = t if forward else rows - 1 - t
                decays = jnp.exp2(step_ref[pl.ds(t, 1), :] * slope)
                drive = drive_ref[pl.ds(t, 1), :] * widen(coef_ref[t], width)
                state = state * decays + drive if forward else (state + drive) * decays
            return state

        state = lax.fori_loop(0, rows // group, advance, jnp.zeros((entries, width), jnp.float32))
        whole = jnp.exp2(jnp.sum(step_ref[...], axis=0, keepdims=True) * slope)
        outgoing[:entries] = state.astype(jnp.bfloat16)
        outgoing[entries:] = whole.astype(jnp.bfloat16)
        copies = [
            send_to(outgoing, incoming.at[k], send.at[k], recv.at[k], peers[k])
            for k in range(seq_count - 1)
        ]
        for copy in copies:
            copy.start()
        for copy in copies:
            copy.wait_recv()
        carried = jnp.zeros((entries, width), jnp.float32)
        order = range(seq_count - 1, 0, -1) if forward else range(1, seq_count)
        for k in order:
            known = seq - k >= 0 if forward else seq - k < 0
            block = incoming[k - 1].astype(jnp.float32)
            carried = jnp.where(known, block[entries:] * carried + block[:entries], 0.0)
        o_ref[...] = carried
        for copy in copies:
            copy.wait_send()

    return pl.pallas_call(
        kernel,
        out_shape=jax.ShapeDtypeStruct((entries, width), jnp.float32),
        in_specs=[VMEM] * 4,
        out_specs=VMEM,
        scratch_shapes=[
            pltpu.VMEM((2 * entries, width), jnp.bfloat16),
            pltpu.VMEM((seq_count - 1, 2 * entries, width), jnp.bfloat16),
            pltpu.SemaphoreType.DMA((seq_count - 1,)),
            pltpu.SemaphoreType.DMA((seq_count - 1,)),
        ],
        compiler_params=talking(number),
        cost_estimate=lasting(16),
        name="run_summary",
    )(steps, drives, coefficients, slopes)


def state_sweep(initial, steps, drives, inject, readout, slopes):
    rows, width = steps.shape
    entries = slopes.shape[0]
    length = math.gcd(rows, 32)
    group = math.gcd(length, 8)

    def kernel(
        init_ref, step_ref, drive_ref, inject_ref, read_ref, slope_ref, y_ref, before_ref, end_ref
    ):
        @pl.when(pl.program_id(0) == 0)
        def begin():
            end_ref[...] = init_ref[...]

        slope = slope_ref[...]

        def advance(position, state):
            for offset in range(group):
                t = position * group + offset
                before_ref[t] = state
                decays = jnp.exp2(step_ref[pl.ds(t, 1), :] * slope)
                drive = drive_ref[pl.ds(t, 1), :] * widen(inject_ref[t], width)
                state = state * decays + drive
                y_ref[pl.ds(t, 1), :] = jnp.sum(
                    state * widen(read_ref[t], width), axis=0, keepdims=True
                )
            return state

        end_ref[...] = lax.fori_loop(0, length // group, advance, end_ref[...])

    row_spec = pl.BlockSpec((length, width), lambda i: (i, 0))
    entry_spec = pl.BlockSpec((length, entries, LANES), lambda i: (i, 0, 0))
    fixed = pl.BlockSpec((entries, width), lambda i: (0, 0))
    return pl.pallas_call(
        kernel,
        grid=(rows // length,),
        out_shape=(
            jax.ShapeDtypeStruct((rows, width), jnp.float32),
            jax.ShapeDtypeStruct((rows, entries, width), jnp.float32),
            jax.ShapeDtypeStruct((entries, width), jnp.float32),
        ),
        in_specs=[fixed, row_spec, row_spec, entry_spec, entry_spec, fixed],
        out_specs=(
            row_spec,
            pl.BlockSpec((length, entries, width), lambda i: (i, 0, 0)),
            fixed,
        ),
        compiler_params=pltpu.CompilerParams(vmem_limit_bytes=LIMIT),
        cost_estimate=lasting(11),
        name="state_sweep",
    )(initial, steps, drives, inject, readout, slopes)


def adjoint_sweep(incoming, last_state, befores, steps, drives, inject, readout, upstream, slopes):
    rows, width = steps.shape
    entries = slopes.shape[0]
    length = math.gcd(rows, 32)
    group = math.gcd(length, 8)
    blocks = rows // length

    def kernel(
        in_ref,
        last_ref,
        before_ref,
        step_ref,
        drive_ref,
        inject_ref,
        read_ref,
        up_ref,
        slope_ref,
        through_ref,
        injected_ref,
        inject_out,
        read_out,
        rate_ref,
        adjoint_ref,
        state_ref,
    ):
        @pl.when(pl.program_id(0) == 0)
        def begin():
            adjoint_ref[...] = in_ref[...]
            state_ref[...] = last_ref[...]
            rate_ref[...] = jnp.zeros_like(rate_ref)

        slope = slope_ref[...]

        def retreat(position, carried):
            adjoint_in, rate = carried
            for offset in range(group):
                t = length - 1 - (position * group + offset)
                upper = up_ref[pl.ds(t, 1), :]
                step = step_ref[pl.ds(t, 1), :]
                adjoint = widen(read_ref[t], width) * upper + adjoint_in
                state = state_ref[...] if offset == 0 else before_ref[t + 1]
                read_out[t] = narrow(upper * state)
                adjoint_in = jnp.exp2(step * slope) * adjoint
                before = before_ref[t]
                through = adjoint_in * before
                rate = rate + through * step
                through_ref[pl.ds(t, 1), :] = jnp.sum(through * slope, axis=0, keepdims=True)
                injected_ref[pl.ds(t, 1), :] = jnp.sum(
                    adjoint * widen(inject_ref[t], width), axis=0, keepdims=True
                )
                inject_out[t] = narrow(adjoint * drive_ref[pl.ds(t, 1), :])
            state_ref[...] = before_ref[length - (position + 1) * group]
            return (adjoint_in, rate)

        adjoint_end, rate_end = lax.fori_loop(
            0, length // group, retreat, (adjoint_ref[...], rate_ref[...])
        )
        adjoint_ref[...] = adjoint_end
        rate_ref[...] = rate_end

    row_spec = pl.BlockSpec((length, width), lambda i: (blocks - 1 - i, 0))
    entry_spec = pl.BlockSpec((length, entries, LANES), lambda i: (blocks - 1 - i, 0, 0))
    fixed = pl.BlockSpec((entries, width), lambda i: (0, 0))
    wide = jax.ShapeDtypeStruct((rows, width), jnp.float32)
    partial = jax.ShapeDtypeStruct((rows, entries, LANES), jnp.float32)
    return pl.pallas_call(
        kernel,
        grid=(blocks,),
        out_shape=(
            wide,
            wide,
            partial,
            partial,
            jax.ShapeDtypeStruct((entries, width), jnp.float32),
        ),
        in_specs=[
            fixed,
            fixed,
            pl.BlockSpec((length, entries, width), lambda i: (blocks - 1 - i, 0, 0)),
            row_spec,
            row_spec,
            entry_spec,
            entry_spec,
            row_spec,
            fixed,
        ],
        out_specs=(row_spec, row_spec, entry_spec, entry_spec, fixed),
        scratch_shapes=[pltpu.VMEM((entries, width), jnp.float32)] * 2,
        compiler_params=pltpu.CompilerParams(vmem_limit_bytes=LIMIT),
        cost_estimate=lasting(15),
        name="adjoint_sweep",
    )(incoming, last_state, befores, steps, drives, inject, readout, upstream, slopes)


def over_rows(left, right):
    return lax.dot_general(left, right, (((0,), (0,)), ((), ())), preferred_element_type=jnp.float32)


def over_columns(left, right):
    return lax.dot_general(left, right, (((1,), (1,)), ((), ())), preferred_element_type=jnp.float32)


def stand_up(rows, target, shared_heads):
    count, width = rows.shape
    heads = width // HEAD_DIM
    group = heads // shared_heads
    turned = rows.astype(jnp.float32).T.astype(target.dtype)
    target[...] = jnp.zeros_like(target)
    for head in range(heads):
        shared = head // group
        target[shared * HEAD_DIM : (shared + 1) * HEAD_DIM, head * count : (head + 1) * count] = (
            turned[head * HEAD_DIM : (head + 1) * HEAD_DIM]
        )


def lie_down(upright, count, shared_heads):
    heads = upright.shape[1] // count
    group = heads // shared_heads
    blocks = []
    for head in range(heads):
        shared = head // group
        blocks.append(
            upright[
                shared * HEAD_DIM : (shared + 1) * HEAD_DIM, head * count : (head + 1) * count
            ]
        )
    return jnp.concatenate(blocks, axis=0).T


def hidden_bias(key_docs, query_docs, diagonal):
    key_count, query_count = key_docs.shape[0], query_docs.shape[1]
    shape = (key_count, query_count)
    earlier = lax.broadcasted_iota(jnp.int32, shape, 0) <= lax.broadcasted_iota(
        jnp.int32, shape, 1
    )
    bias = jnp.where(key_docs == query_docs, 0.0, masked_score)
    return jnp.where(jnp.logical_or(earlier, jnp.logical_not(diagonal)), bias, masked_score)


def attend(own, queries, both_rows, key_docs, query_docs):
    rows, width = queries.shape
    key_width = both_rows.shape[1] // 2
    shared_heads = key_width // HEAD_DIM
    heads = width // HEAD_DIM
    scale = 0.125 * LOG2E

    def kernel(own_ref, q_ref, kv_ref, kd_ref, qd_ref, low_ref, att_ref, lse_ref, qt_ref, max_ref, sum_ref):
        stand_up(q_ref[...], qt_ref, shared_heads)
        me = own_ref[0]

        def block(step, first):
            begin = pl.multiple_of((me - step) * rows, rows)
            keys = kv_ref[pl.ds(begin, rows), :key_width]
            values = kv_ref[pl.ds(begin, rows), key_width:]
            bias = hidden_bias(kd_ref[pl.ds(begin, rows), :], qd_ref[...], step == 0)
            for head in range(heads):
                columns = slice(head * rows, (head + 1) * rows)
                scores = product(keys, qt_ref[:, columns]) * scale + bias
                top = jnp.max(scores, axis=0, keepdims=True)
                if not first:
                    old = max_ref[:, columns]
                    top = jnp.maximum(top, old)
                weights = jnp.exp2(scores - top)
                total = jnp.sum(weights, axis=0, keepdims=True)
                weighted = over_rows(values, to_low(weights))
                if not first:
                    factor = jnp.exp2(old - top)
                    total = total + sum_ref[:, columns] * factor
                    weighted = weighted + att_ref[:, columns] * factor
                max_ref[:, columns] = top
                sum_ref[:, columns] = total
                att_ref[:, columns] = weighted

        block(0, True)

        @pl.loop(1, me + 1)
        def earlier(step):
            block(step, False)

        att_ref[...] = att_ref[...] / sum_ref[...]
        lse_ref[...] = max_ref[...] + jnp.log2(sum_ref[...])
        low_ref[...] = to_low(lie_down(att_ref, rows, shared_heads))

    return pl.pallas_call(
        kernel,
        out_shape=(
            jax.ShapeDtypeStruct((rows, width), jnp.bfloat16),
            jax.ShapeDtypeStruct((key_width, heads * rows), jnp.float32),
            jax.ShapeDtypeStruct((1, heads * rows), jnp.float32),
        ),
        in_specs=[pl.BlockSpec(memory_space=pltpu.SMEM)] + [VMEM] * 4,
        out_specs=(VMEM,) * 3,
        scratch_shapes=[
            pltpu.VMEM((key_width, heads * rows), jnp.bfloat16),
            pltpu.VMEM((1, heads * rows), jnp.float32),
            pltpu.VMEM((1, heads * rows), jnp.float32),
        ],
        compiler_params=pltpu.CompilerParams(vmem_limit_bytes=LIMIT),
        cost_estimate=lasting(12),
        name="attend",
    )(own, queries, both_rows, key_docs, query_docs)


def attend_back(own, queries, upstream, both_rows, key_docs, query_docs, attended, log_sum):
    rows, width = queries.shape
    total_rows = both_rows.shape[0]
    key_width = both_rows.shape[1] // 2
    shared_heads = key_width // HEAD_DIM
    heads = width // HEAD_DIM
    scale = 0.125 * LOG2E

    def kernel(
        own_ref, q_ref, up_ref, kv_ref, kd_ref, qd_ref, att_ref, lse_ref, qg_ref, kvg_ref, qt_ref, ut_ref, acc_ref
    ):
        stand_up(q_ref[...], qt_ref, shared_heads)
        stand_up(up_ref[...], ut_ref, shared_heads)
        me = own_ref[0]
        delta = jnp.sum(ut_ref[...].astype(jnp.float32) * att_ref[...], axis=0, keepdims=True)
        acc_ref[...] = jnp.zeros_like(acc_ref)

        @pl.loop(me + 1, total_rows // rows)
        def later(position):
            begin = pl.multiple_of(position * rows, rows)
            kvg_ref[pl.ds(begin, rows), :] = jnp.zeros((rows, 2 * key_width), jnp.bfloat16)

        @pl.loop(0, me + 1)
        def block(position):
            begin = pl.multiple_of(position * rows, rows)
            keys = kv_ref[pl.ds(begin, rows), :key_width]
            values = kv_ref[pl.ds(begin, rows), key_width:]
            bias = hidden_bias(kd_ref[pl.ds(begin, rows), :], qd_ref[...], position == me)
            key_grad = jnp.zeros((rows, key_width), jnp.float32)
            value_grad = jnp.zeros((rows, key_width), jnp.float32)
            for head in range(heads):
                columns = slice(head * rows, (head + 1) * rows)
                query = qt_ref[:, columns]
                upper = ut_ref[:, columns]
                probs = jnp.exp2(product(keys, query) * scale + bias - lse_ref[:, columns])
                value_grad = value_grad + over_columns(to_low(probs), upper)
                score_grad = to_low(probs * (product(values, upper) - delta[:, columns]))
                key_grad = key_grad + over_columns(score_grad, query)
                acc_ref[:, columns] += over_rows(keys, score_grad)
            kvg_ref[pl.ds(begin, rows), :key_width] = to_low(key_grad * 0.125)
            kvg_ref[pl.ds(begin, rows), key_width:] = to_low(value_grad)

        qg_ref[...] = to_low(lie_down(acc_ref, rows, shared_heads) * 0.125)

    return pl.pallas_call(
        kernel,
        out_shape=(
            jax.ShapeDtypeStruct((rows, width), jnp.bfloat16),
            jax.ShapeDtypeStruct((total_rows, 2 * key_width), jnp.bfloat16),
        ),
        in_specs=[pl.BlockSpec(memory_space=pltpu.SMEM)] + [VMEM] * 7,
        out_specs=(VMEM,) * 2,
        scratch_shapes=[
            pltpu.VMEM((key_width, heads * rows), jnp.bfloat16),
            pltpu.VMEM((key_width, heads * rows), jnp.bfloat16),
            pltpu.VMEM((key_width, heads * rows), jnp.float32),
        ],
        compiler_params=pltpu.CompilerParams(vmem_limit_bytes=LIMIT),
        cost_estimate=lasting(20),
        name="attend_back",
    )(own, queries, upstream, both_rows, key_docs, query_docs, attended, log_sum)


def body(
    tokens_in,
    cotangent,
    document_ids,
    expert_routes,
    norm_mixer,
    mixer_inner,
    mixer_gate,
    conv_taps,
    conv_bias,
    state_proj,
    step_proj,
    step_bias,
    decay_log,
    skip_gain,
    mixer_out,
    norm_ffn,
    ffn_gate,
    ffn_up,
    ffn_down,
    norm_attn,
    attn_query,
    attn_key,
    attn_value,
    attn_output,
    norm_moe,
    router,
    expert_gate,
    expert_up,
    expert_down,
):
    numbers = itertools.count()
    seq_count = lax.axis_size("seq")
    row_count = tokens_in.shape[0]
    total_rows = seq_count * row_count
    first_row = lax.axis_index("seq") * row_count
    last_row = first_row + row_count - 1

    me = lax.axis_index("seq")
    bit_count = seq_count.bit_length() - 1
    across_first = [0] + list(range(1, bit_count))
    along_first = [1, 0] + list(range(2, bit_count))

    def by_owner(values, bits):
        turned = values.transpose(0, 2, 1)
        own_rows = turned.shape[1] // seq_count
        order = [0]
        for bit in reversed(bits):
            order = order + [j + (1 << bit) for j in order]
        blocks = []
        for j in order:
            owner = me
            for bit in range(bit_count):
                if j >> bit & 1:
                    owner = owner + (1 << bit) * (1 - 2 * ((owner >> bit) & 1))
            blocks.append(lax.dynamic_slice_in_dim(turned, owner * own_rows, own_rows, 1))
        parts = []
        while len(blocks) > 1:
            half = len(blocks) // 2
            parts.append(jnp.concatenate(blocks[half:], axis=1) if half > 1 else blocks[half])
            blocks = blocks[:half]
        return parts + blocks, bits

    def begin_sum(rows, columns):
        flow = {"rows": rows[0], "bits": rows[1], "columns": columns, "got": []}
        settle(flow)
        return flow

    def settle(flow):
        step = len(flow["got"])
        part = flow["rows"][step]
        total = jnp.einsum(
            "bdt,btf->bdf", part, flow["columns"], preferred_element_type=jnp.float32
        )
        first = part.shape[1] if step < len(flow["bits"]) else 0
        for got in flow["got"]:
            total = total + got[:, first : first + part.shape[1]].astype(jnp.float32)
        if step == len(flow["bits"]):
            flow["total"] = total
            return
        bit = flow["bits"][step]
        route = [(i, i ^ (1 << bit)) for i in range(seq_count)]
        flow["got"].append(lax.ppermute(to_low(total), "seq", route))

    def hold(values, *flows):
        if flows:
            tied = lax.optimization_barrier((values, *[flow["got"][-1] for flow in flows]))
            values = tied[0]
            for flow, got in zip(flows, tied[1:], strict=True):
                flow["got"][-1] = got
        return values

    def after(values, *flows):
        values = hold(values, *flows)
        for flow in flows:
            settle(flow)
        return values

    def finished(flow):
        while "total" not in flow:
            settle(flow)
        return flow["total"]

    def branch_sum(values):
        return head_sum(values, next(numbers), jnp.bfloat16, 4)

    local_docs = lax.dynamic_slice_in_dim(document_ids, first_row, row_count)
    reach = conv_taps.shape[0] - 1
    border = jnp.arange(reach, dtype=jnp.int32)
    docs_before = jnp.take(document_ids, jnp.maximum(first_row - reach + border, 0))
    docs_after = jnp.take(document_ids, jnp.minimum(first_row + row_count + border, total_rows - 1))
    docs_prior = jnp.concatenate([docs_before[reach - 1 :], local_docs[:-1]])
    retain = (local_docs == docs_prior).astype(jnp.float32)
    tokens = tokens_in.astype(jnp.float32)
    gain_mixer = norm_mixer.astype(jnp.float32)
    normed_one = to_low(rms_scale(tokens, gain_mixer))
    conv_in = to_low(product(normed_one, mixer_inner))
    gate_in = product(normed_one, mixer_gate)
    conv_edge = from_behind(conv_in[row_count - reach :], "seq", 1)
    extended = jnp.concatenate([conv_edge, conv_in]).astype(jnp.float32)
    docs_ext = jnp.concatenate([docs_before, local_docs])
    taps = conv_taps.astype(jnp.float32)
    conv_sum = conv_bias.astype(jnp.float32)[None, :]
    masks = []
    for offset in range(reach + 1):
        same_doc = (docs_ext[offset : offset + row_count] == local_docs).astype(jnp.float32)[
            :, None
        ]
        masks.append(same_doc)
        conv_sum = conv_sum + taps[offset] * extended[offset : offset + row_count] * same_doc
    activated = jax.nn.silu(conv_sum)
    act_low = to_low(activated)
    projected = head_sum(product(act_low, state_proj), next(numbers), jnp.float32, 1)
    rank_size = step_proj.shape[0]
    state_size = decay_log.shape[1]
    step_low = to_low(projected[:, :rank_size])
    inject = projected[:, rank_size : rank_size + state_size]
    readout = projected[:, rank_size + state_size :]
    step_pre = product(step_low, step_proj) + step_bias.astype(jnp.float32)
    step_dt = jax.nn.softplus(step_pre)
    decay_rate = jnp.exp(decay_log.astype(jnp.float32)).T
    slopes = -LOG2E * decay_rate
    steps = jnp.where(retain[:, None] > 0.0, step_dt, NEVER)
    drives = step_dt * activated
    inject_wide = spread(inject)
    readout_wide = spread(readout)
    state_in = run_summary(steps, drives, inject_wide, slopes, next(numbers), True)
    scanned, befores, state_out = state_sweep(
        state_in, steps, drives, inject_wide, readout_wide, slopes
    )
    skipping = skip_gain.astype(jnp.float32)
    mixed_state = scanned + skipping * activated
    gate_act = jax.nn.silu(gate_in)
    gated = to_low(mixed_state * gate_act)
    hidden_one = tokens + branch_sum(product(gated, mixer_out))
    gain_ffn = norm_ffn.astype(jnp.float32)
    normed_two = to_low(rms_scale(hidden_one, gain_ffn))
    gate_two = product(normed_two, ffn_gate)
    up_two = product(normed_two, ffn_up)
    ffn_act = to_low(jax.nn.silu(gate_two) * up_two)
    hidden_two = hidden_one + branch_sum(product(ffn_act, ffn_down))
    gain_attn = norm_attn.astype(jnp.float32)
    normed_three = to_low(rms_scale(hidden_two, gain_attn))
    queries = to_low(product(normed_three, attn_query))
    key_rows = to_low(product(normed_three, attn_key))
    value_rows = to_low(product(normed_three, attn_value))
    both_rows = seq_gather(jnp.concatenate([key_rows, value_rows], axis=1), next(numbers))
    key_width = key_rows.shape[1]
    own_place = lax.axis_index("seq").reshape(1)
    key_docs = document_ids[:, None]
    query_docs = local_docs[None, :]
    attended_low, attended, log_sum = attend(own_place, queries, both_rows, key_docs, query_docs)
    hidden_three = hidden_two + branch_sum(product(attended_low, attn_output))
    gain_moe = norm_moe.astype(jnp.float32)
    normed_four = to_low(rms_scale(hidden_three, gain_moe))
    logits = product(normed_four, router)
    expert_count = router.shape[1]
    experts = jnp.arange(expert_count, dtype=jnp.int32)
    named = (expert_routes[:, :, None] == experts).astype(jnp.float32)
    gate_weights = jax.nn.softmax(jnp.sum(named * logits[:, None, :], axis=2), axis=1)
    route_flat = expert_routes.reshape(-1)
    pair_count = route_flat.shape[0]
    pair_order = jnp.arange(pair_count, dtype=jnp.int32)
    earlier = (pair_order[None, :] < pair_order[:, None]) & (
        route_flat[None, :] == route_flat[:, None]
    )
    within = jnp.sum(earlier.astype(jnp.int32), axis=1)
    slot_index = (route_flat * CAP + within).reshape(row_count, 2)
    slots = jnp.arange(expert_count * CAP, dtype=jnp.int32)
    first_hit = slot_index[:, 0][None, :] == slots[:, None]
    second_hit = slot_index[:, 1][None, :] == slots[:, None]
    placing = (first_hit | second_hit).astype(jnp.bfloat16)
    slot_gates = jnp.sum(
        jnp.where(first_hit, gate_weights[:, 0][None, :], 0.0)
        + jnp.where(second_hit, gate_weights[:, 1][None, :], 0.0),
        axis=1,
    )
    expert_in = to_low(product(placing, normed_four)).reshape(expert_count, CAP, -1)
    slot_upstream = product(placing, cotangent)
    res_grad = to_low(slot_gates[:, None] * slot_upstream).reshape(expert_count, CAP, -1)
    gate_four = jnp.einsum(
        "ecd,edf->ecf", expert_in, expert_gate, preferred_element_type=jnp.float32
    )
    up_four = jnp.einsum("ecd,edf->ecf", expert_in, expert_up, preferred_element_type=jnp.float32)
    expert_act = to_low(jax.nn.silu(gate_four) * up_four)
    expert_res = jnp.einsum(
        "ecf,efd->ecd", expert_act, expert_down, preferred_element_type=jnp.float32
    ).reshape(expert_count * CAP, -1)
    upstream = cotangent.astype(jnp.float32)
    slot_dots = jnp.sum(expert_res * slot_upstream, axis=1)
    dots_part = jnp.stack(
        [
            jnp.sum(jnp.where(first_hit, slot_dots[:, None], 0.0), axis=0),
            jnp.sum(jnp.where(second_hit, slot_dots[:, None], 0.0), axis=0),
        ],
        axis=1,
    )
    combined = product(placing.T, to_low(slot_gates[:, None] * expert_res))
    act_back = to_low(
        jnp.einsum("ecd,efd->ecf", res_grad, expert_down, preferred_element_type=jnp.float32)
    ).astype(jnp.float32)
    gating_grad = to_low(act_back * up_four * silu_slope(gate_four))
    upward_grad = to_low(act_back * jax.nn.silu(gate_four))
    flow_expert_down = begin_sum(by_owner(res_grad, along_first), expert_act)
    expert_rows = by_owner(expert_in, across_first)
    flow_expert_in = begin_sum(expert_rows, jnp.concatenate([gating_grad, upward_grad], axis=2))
    slot_grads = (
        jnp.einsum("ecf,edf->ecd", gating_grad, expert_gate, preferred_element_type=jnp.float32)
        + jnp.einsum("ecf,edf->ecd", upward_grad, expert_up, preferred_element_type=jnp.float32)
    ).reshape(expert_count * CAP, -1)
    token_part = product(placing.T, to_low(slot_grads))
    model_width = tokens.shape[1]
    expert_sums = branch_sum(
        jnp.concatenate(
            [combined, token_part, jnp.pad(dots_part, ((0, 0), (0, LANES - 2)))], axis=1
        )
    )
    mixed_out = to_low(hidden_three + expert_sums[:, :model_width])
    normed_grad = expert_sums[:, model_width : 2 * model_width]
    dots = expert_sums[:, 2 * model_width : 2 * model_width + 2]
    chosen_grad = gate_weights * (dots - jnp.sum(gate_weights * dots, axis=1, keepdims=True))
    logit_grad = jnp.sum(named * chosen_grad[:, :, None], axis=1)
    grad_router = exact_product(normed_four.astype(jnp.float32).T, logit_grad)
    normed_grad = normed_grad + exact_product(logit_grad, router.astype(jnp.float32).T)
    hidden_grad, grad_norm_moe = rms_back(hidden_three, gain_moe, normed_grad)
    three_grad = upstream + hidden_grad
    branch_grad = to_low(three_grad)
    flow_attn_output = begin_sum(by_owner(branch_grad[None], across_first), attended_low[None])
    attended_grad = to_low(product(branch_grad, attn_output.T))
    attended_grad = after(attended_grad, flow_expert_down)
    query_grad, both_grads = attend_back(
        own_place, queries, attended_grad, both_rows, key_docs, query_docs, attended, log_sum
    )
    both_grads = after(
        both_grads,
        flow_expert_in,
    )
    (both_sums,) = seq_scatter([both_grads], next(numbers))
    key_sum, value_sum = both_sums[:, :key_width], both_sums[:, key_width:]
    key_grad = to_low(key_sum)
    value_grad = to_low(value_sum)
    flow_attn_in = begin_sum(
        by_owner(normed_three[None], across_first),
        jnp.concatenate([query_grad, key_grad, value_grad], axis=1)[None],
    )
    normed_part = (
        product(query_grad, attn_query.T)
        + product(key_grad, attn_key.T)
        + product(value_grad, attn_value.T)
    )
    normed_part = after(normed_part, flow_expert_down, flow_attn_output)
    normed_grad = branch_sum(normed_part)
    hidden_grad, grad_norm_attn = rms_back(hidden_two, gain_attn, normed_grad)
    two_grad = three_grad + hidden_grad
    branch_grad = to_low(two_grad)
    flow_ffn_down = begin_sum(by_owner(branch_grad[None], along_first), ffn_act[None])
    ffn_back = to_low(product(branch_grad, ffn_down.T)).astype(jnp.float32)
    feed_gate_grad = to_low(ffn_back * up_two * silu_slope(gate_two))
    feed_up_grad = to_low(ffn_back * jax.nn.silu(gate_two))
    feed_rows = by_owner(normed_two[None], across_first)
    flow_ffn_in = begin_sum(
        feed_rows, jnp.concatenate([feed_gate_grad, feed_up_grad], axis=1)[None]
    )
    normed_part = product(feed_gate_grad, ffn_gate.T) + product(feed_up_grad, ffn_up.T)
    normed_part = after(
        normed_part, flow_expert_in, flow_expert_down, flow_attn_in, flow_attn_output
    )
    normed_grad = branch_sum(normed_part)
    hidden_grad, grad_norm_ffn = rms_back(hidden_one, gain_ffn, normed_grad)
    one_grad = two_grad + hidden_grad
    branch_grad = to_low(one_grad)
    mixer_out_rows = by_owner(branch_grad[None], across_first)
    gated_grad = to_low(product(branch_grad, mixer_out.T)).astype(jnp.float32)
    scan_grad = gated_grad * gate_act
    gate_in_grad = to_low(gated_grad * mixed_state * silu_slope(gate_in))
    grad_skip_gain = jnp.sum(scan_grad * activated, axis=0)
    scan_grad = hold(
        scan_grad, flow_expert_in, flow_attn_in, flow_attn_output, flow_ffn_down, flow_ffn_in
    )
    state_after = run_summary(steps, scan_grad, readout_wide, slopes, next(numbers), False)
    state_after, gated_late, gate_grad_late = lax.optimization_barrier(
        (state_after, gated, gate_in_grad)
    )
    state_after = after(state_after, flow_attn_in, flow_ffn_down, flow_ffn_in)
    flow_mixer_out = begin_sum(mixer_out_rows, gated_late[None])
    flow_mixer_gate = begin_sum(by_owner(normed_one[None], across_first), gate_grad_late[None])
    through_sum, injected, inject_part, readout_part, rate_sum = adjoint_sweep(
        state_after,
        state_out,
        befores,
        steps,
        drives,
        inject_wide,
        readout_wide,
        scan_grad,
        slopes,
    )
    step_grad = LN2 * through_sum + activated * injected
    input_grad = step_dt * injected
    inject_grad = jnp.sum(inject_part, axis=2)
    readout_grad = jnp.sum(readout_part, axis=2)
    grad_decay_log = -rate_sum * decay_rate
    pre_grad = step_grad * jax.nn.sigmoid(step_pre)
    grad_step_bias = jnp.sum(pre_grad, axis=0)
    pre_low = to_low(pre_grad)
    grad_step_proj = product(step_low.T, pre_low)
    proj_part = jnp.concatenate([product(pre_low, step_proj.T), inject_grad, readout_grad], axis=1)
    proj_part = after(proj_part, flow_attn_in, flow_ffn_down)
    proj_low = to_low(head_sum(proj_part, next(numbers), jnp.float32, 1))
    grad_state_proj = product(act_low.T, proj_low)
    act_total = input_grad + skipping * scan_grad + product(proj_low, state_proj.T)
    conv_grad = act_total * silu_slope(conv_sum)
    grad_conv_bias = jnp.sum(conv_grad, axis=0)
    after_edge = from_behind(conv_grad[:reach], "seq", -1)
    grad_ext = jnp.concatenate([conv_grad, after_edge])
    docs_next = jnp.concatenate([local_docs, docs_after])
    conv_in_grad = jnp.zeros_like(conv_grad)
    tap_rows = []
    for offset in range(reach + 1):
        tap_rows.append(
            jnp.sum(conv_grad * extended[offset : offset + row_count] * masks[offset], axis=0)
        )
        lead = reach - offset
        same_next = (docs_next[lead : lead + row_count] == local_docs).astype(jnp.float32)[:, None]
        conv_in_grad = conv_in_grad + taps[offset] * grad_ext[lead : lead + row_count] * same_next
    grad_conv_taps = jnp.stack(tap_rows)
    conv_low = to_low(conv_in_grad)
    grad_mixer_inner = to_low(product(normed_one.T, conv_low))
    normed_part = product(conv_low, mixer_inner.T) + product(gate_in_grad, mixer_gate.T)
    normed_part = after(normed_part, flow_ffn_in, flow_mixer_out)
    normed_grad = branch_sum(normed_part)
    hidden_grad, grad_norm_mixer = rms_back(tokens, gain_mixer, normed_grad)
    grad_tokens = one_grad + hidden_grad
    own_channels = grad_conv_bias.shape[0] // seq_count

    def cut(values, axis):
        values = jnp.moveaxis(values, axis, 0)
        return values.reshape(seq_count, -1)

    packed = jnp.concatenate(
        [
            cut(grad_norm_mixer, 0),
            cut(grad_norm_ffn, 0),
            cut(grad_norm_attn, 0),
            cut(grad_norm_moe, 0),
            cut(grad_router, 0),
            cut(grad_conv_taps, 1),
            cut(grad_conv_bias, 0),
            cut(grad_state_proj, 0),
            cut(grad_step_proj, 1),
            cut(grad_step_bias, 0),
            cut(grad_decay_log, 1),
            cut(grad_skip_gain, 0),
        ],
        axis=1,
    )
    spare = -packed.shape[1] % (16 * LANES)
    packed = to_low(jnp.pad(packed, ((0, 0), (0, spare)))).reshape(-1, LANES)
    packed = after(packed, flow_mixer_gate, flow_mixer_out, flow_ffn_in)
    inner_half = grad_mixer_inner.shape[1] // 2
    first_inner, second_inner, sum_packed = seq_scatter(
        [grad_mixer_inner[:, :inner_half], grad_mixer_inner[:, inner_half:], packed],
        next(numbers),
    )
    sum_attn_in = finished(flow_attn_in)[0]
    sum_ffn_in = finished(flow_ffn_in)[0]
    sum_expert_in = finished(flow_expert_in)
    expert_width = expert_gate.shape[2]
    feed_width = ffn_gate.shape[1]
    sum_packed = sum_packed.reshape(-1)
    own_rows = model_width // seq_count
    taken = itertools.accumulate(
        [0]
        + [own_rows] * 4
        + [own_rows * expert_count]
        + [own_channels * (reach + 1), own_channels, own_channels * state_proj.shape[1]]
        + [own_channels * rank_size, own_channels, own_channels * state_size, own_channels]
    )
    bounds = list(taken)
    pieces = [sum_packed[low:high] for low, high in itertools.pairwise(bounds)]
    query_width = attn_query.shape[1]

    return (
        mixed_out,
        grad_tokens,
        pieces[0],
        jnp.concatenate([first_inner, second_inner], axis=1),
        finished(flow_mixer_gate)[0],
        pieces[5].reshape(own_channels, -1).T,
        pieces[6],
        pieces[7].reshape(own_channels, -1),
        pieces[8].reshape(own_channels, -1).T,
        pieces[9],
        pieces[10].reshape(own_channels, -1),
        pieces[11],
        finished(flow_mixer_out)[0].T,
        pieces[1],
        sum_ffn_in[:, :feed_width],
        sum_ffn_in[:, feed_width:],
        finished(flow_ffn_down)[0].T,
        pieces[2],
        sum_attn_in[:, :query_width],
        sum_attn_in[:, query_width : query_width + key_width],
        sum_attn_in[:, query_width + key_width :],
        finished(flow_attn_output)[0].T,
        pieces[3],
        pieces[4].reshape(own_rows, -1),
        sum_expert_in[:, :, :expert_width],
        sum_expert_in[:, :, expert_width:],
        finished(flow_expert_down).transpose(0, 2, 1),
    )


def solution(mesh):
    in_specs = (
        P("seq", None),
        P("seq", None),
        P(),
        P("seq", None),
        P(),
        P(None, "head"),
        P(None, "head"),
        P(None, "head"),
        P("head"),
        P("head", None),
        P(None, "head"),
        P("head"),
        P("head", None),
        P("head"),
        P("head", None),
        P(),
        P(None, "head"),
        P(None, "head"),
        P("head", None),
        P(),
        P(None, "head"),
        P(None, "head"),
        P(None, "head"),
        P("head", None),
        P(),
        P(),
        P(None, None, "head"),
        P(None, None, "head"),
        P(None, "head", None),
    )
    out_specs = (
        P("seq", None),
        P("seq", None),
        P("seq"),
        P("seq", "head"),
        P("seq", "head"),
        P(None, ("head", "seq")),
        P(("head", "seq")),
        P(("head", "seq"), None),
        P(None, ("head", "seq")),
        P(("head", "seq")),
        P(("head", "seq"), None),
        P(("head", "seq")),
        P("head", "seq"),
        P("seq"),
        P("seq", "head"),
        P("seq", "head"),
        P("head", "seq"),
        P("seq"),
        P("seq", "head"),
        P("seq", "head"),
        P("seq", "head"),
        P("head", "seq"),
        P("seq"),
        P("seq", None),
        P(None, "seq", "head"),
        P(None, "seq", "head"),
        P(None, "head", "seq"),
    )
    return jax.shard_map(body, mesh=mesh, in_specs=in_specs, out_specs=out_specs, check_vma=False)
```

```python
import itertools
import math

import jax
import jax.numpy as jnp
from jax import lax
from jax.experimental import pallas as pl
from jax.experimental.pallas import tpu as pltpu
from jax.sharding import PartitionSpec as P

HEAD_DIM = 64
CAP = 160
LANES = 128
LOG2E = 1.4426950408889634
LN2 = 0.6931471805599453
NEVER = 1e30
LIMIT = 56 * 1024 * 1024
MESH = pl.DeviceIdType.MESH
VMEM = pl.BlockSpec(memory_space=pltpu.VMEM)
ANY = pl.BlockSpec(memory_space=pl.ANY)


highest = lax.Precision.HIGHEST
epsilon = 1e-05
masked_score = -1e30


def from_behind(block, axis, distance):
    devices = range(lax.axis_size(axis))
    route = [(i - distance, i) for i in devices if i - distance in devices]
    return lax.ppermute(block, axis, route)


def to_low(values):
    return values.astype(jnp.bfloat16)


def product(left, right):
    return jnp.dot(left, right, preferred_element_type=jnp.float32)


def exact_product(left, right):
    return jnp.dot(left, right, precision=highest, preferred_element_type=jnp.float32)


def rms_scale(values, gain):
    return values * lax.rsqrt(jnp.mean(values * values, axis=-1, keepdims=True) + epsilon) * gain


def rms_back(values, gain, upstream):
    unused, pullback = jax.vjp(rms_scale, values, gain)
    return pullback(upstream)


def silu_slope(values):
    logistic = jax.nn.sigmoid(values)
    return logistic * (1.0 + values * (1.0 - logistic))


def meet(peers):
    barrier = pltpu.get_barrier_semaphore()
    for peer in peers:
        pl.semaphore_signal(barrier, inc=1, device_id=peer, device_id_type=MESH)
    pl.semaphore_wait(barrier, len(peers))


def send_to(source, target, send_sem, recv_sem, peer):
    return pltpu.make_async_remote_copy(
        src_ref=source,
        dst_ref=target,
        send_sem=send_sem,
        recv_sem=recv_sem,
        device_id=peer,
        device_id_type=MESH,
    )


def lasting(microseconds):
    return pl.CostEstimate(
        flops=int(microseconds * 1e3),
        bytes_accessed=int(microseconds * 1e3),
        transcendentals=0,
    )


def talking(number):
    return pltpu.CompilerParams(
        collective_id=number, has_side_effects=True, vmem_limit_bytes=LIMIT
    )


def together(*jobs):
    waiting = list(jobs)
    while waiting:
        for job in list(waiting):
            if next(job, waiting) is waiting:
                waiting.remove(job)


def head_peers():
    seq = lax.axis_index("seq")
    head = lax.axis_index("head")
    return [(seq, head + 1 - 2 * (head % 2)), (seq, (head + 2) % 4)]


def head_scratch(rows, width, wire, pieces):
    return [pltpu.VMEM((rows // 2, width), wire)] * 4 + [
        pltpu.SemaphoreType.DMA((3, pieces)),
        pltpu.SemaphoreType.DMA((3, pieces)),
    ]


def head_job(x_ref, o_ref, scratch, wire, pieces):
    near_out, near_in, far_out, far_in, send, recv = scratch
    half = x_ref.shape[0] // 2
    step = half // pieces
    near, far = head_peers()
    core = lax.axis_index("head") % 2

    def rows_of(side, piece):
        return pl.ds(pl.multiple_of(side * half + piece * step, 8), step)

    first, second, third = [], [], []
    for piece in range(pieces):
        local = pl.ds(piece * step, step)
        near_out[local] = x_ref[rows_of(1 - core, piece)].astype(wire)
        first.append(
            send_to(
                near_out.at[local], near_in.at[local], send.at[0, piece], recv.at[0, piece], near
            )
        )
        first[-1].start()
    yield
    for piece in range(pieces):
        local = pl.ds(piece * step, step)
        first[piece].wait_recv()
        total = x_ref[rows_of(core, piece)] + near_in[local].astype(jnp.float32)
        far_out[local] = total.astype(wire)
        second.append(
            send_to(far_out.at[local], far_in.at[local], send.at[1, piece], recv.at[1, piece], far)
        )
        second[-1].start()
    yield
    for piece in range(pieces):
        local = pl.ds(piece * step, step)
        second[piece].wait_recv()
        whole = far_out[local].astype(jnp.float32) + far_in[local].astype(jnp.float32)
        o_ref[rows_of(core, piece)] = whole
        third.append(
            send_to(
                o_ref.at[rows_of(core, piece)],
                o_ref.at[rows_of(core, piece)],
                send.at[2, piece],
                recv.at[2, piece],
                near,
            )
        )
        third[-1].start()
    yield
    for copy in third:
        copy.wait_recv()
    for copy in first + second + third:
        copy.wait_send()


def head_sum(values, number, wire, pieces):
    rows, width = values.shape

    def kernel(x_ref, o_ref, *scratch):
        meet(head_peers())
        together(head_job(x_ref, o_ref, scratch, wire, pieces))

    return pl.pallas_call(
        kernel,
        out_shape=jax.ShapeDtypeStruct((rows, width), jnp.float32),
        in_specs=[VMEM],
        out_specs=VMEM,
        scratch_shapes=head_scratch(rows, width, wire, pieces),
        compiler_params=talking(number),
        cost_estimate=lasting(6 + values.size // 40000),
        name="head_sum",
    )(values)


def pair_peers():
    seq = lax.axis_index("seq")
    head = lax.axis_index("head")
    pairs = lax.axis_size("seq") // 2
    place = seq % 2
    pair = seq // 2
    others = [(((pair + k) % pairs) * 2 + place, head) for k in range(1, pairs)]
    return [(seq + 1 - 2 * place, head)] + others


def scatter_shapes(arrays):
    seq_count = lax.axis_size("seq")
    return [(a.shape[0] // seq_count, a.shape[1]) for a in arrays]


def scatter_blocks(arrays):
    pairs = lax.axis_size("seq") // 2
    return [
        a.reshape(pairs, 2, shape[0], shape[1])
        for a, shape in zip(arrays, scatter_shapes(arrays), strict=True)
    ]


def scatter_scratch(shapes):
    pairs = lax.axis_size("seq") // 2
    count = len(shapes)
    return (
        [pltpu.VMEM((pairs,) + shape, jnp.bfloat16) for shape in shapes] * 2
        + [pltpu.VMEM((pairs - 1,) + shape, jnp.bfloat16) for shape in shapes]
        + [pltpu.SemaphoreType.DMA((count,))] * 3
        + [pltpu.SemaphoreType.DMA((count, pairs - 1))] * 2
    )


def scatter_job(takes, gives, scratch, shapes):
    count = len(takes)
    pairs = lax.axis_size("seq") // 2
    own, near, far = scratch[:count], scratch[count : 2 * count], scratch[2 * count : 3 * count]
    own_sem, near_send, near_recv, far_send, far_recv = scratch[3 * count :]
    seq = lax.axis_index("seq")
    place = seq % 2
    pair = seq // 2
    partner, *others = pair_peers()
    owners = [(pair + k) % pairs for k in range(1, pairs)]
    loads = [
        pltpu.make_async_copy(takes[i].at[:, place], own[i], own_sem.at[i]) for i in range(count)
    ]
    halves = [
        send_to(takes[i].at[:, 1 - place], near[i], near_send.at[i], near_recv.at[i], partner)
        for i in range(count)
    ]

    def launch(i):
        if i < count:
            halves[i].start()
            loads[i].start()

    sums = []

    def finish(i):
        for copy in sums[i]:
            copy.wait_recv()

        @pl.loop(0, shapes[i][0] // 16)
        def add(step):
            part = pl.ds(pl.multiple_of(step * 16, 16), 16)
            total = own[i][pair, part].astype(jnp.float32)
            for k in range(pairs - 1):
                total = total + far[i][k, part].astype(jnp.float32)
            gives[i][part] = total

    launch(0)
    launch(1)
    for i in range(count):
        yield
        halves[i].wait_recv()
        loads[i].wait()
        launch(i + 2)

        @pl.loop(0, pairs)
        def merge(block):
            @pl.loop(0, shapes[i][0] // 16)
            def add(step):
                part = pl.ds(pl.multiple_of(step * 16, 16), 16)
                total = own[i][block, part].astype(jnp.float32) + near[i][block, part].astype(
                    jnp.float32
                )
                own[i][block, part] = total.astype(jnp.bfloat16)

        sums.append(
            [
                send_to(
                    own[i].at[owners[k]],
                    far[i].at[k],
                    far_send.at[i, k],
                    far_recv.at[i, k],
                    others[k],
                )
                for k in range(pairs - 1)
            ]
        )
        for copy in sums[i]:
            copy.start()
        if i > 0:
            finish(i - 1)
    yield
    finish(count - 1)
    for copy in halves:
        copy.wait_send()
    for group in sums:
        for copy in group:
            copy.wait_send()


def scatter_and_head_sum(arrays, values, number):
    count = len(arrays)
    shapes = scatter_shapes(arrays)
    rows, width = values.shape
    spaces = scatter_scratch(shapes)

    def kernel(*refs):
        takes, x_ref = refs[:count], refs[count]
        gives, o_ref = refs[count + 1 : 2 * count + 1], refs[2 * count + 1]
        scratch = refs[2 * count + 2 :]
        meet(pair_peers() + head_peers())
        together(
            scatter_job(takes, gives, scratch[: len(spaces)], shapes),
            head_job(x_ref, o_ref, scratch[len(spaces) :], jnp.bfloat16, 4),
        )

    return pl.pallas_call(
        kernel,
        out_shape=[jax.ShapeDtypeStruct(shape, jnp.float32) for shape in shapes]
        + [jax.ShapeDtypeStruct((rows, width), jnp.float32)],
        in_specs=[ANY] * count + [VMEM],
        out_specs=[VMEM] * (count + 1),
        scratch_shapes=spaces + head_scratch(rows, width, jnp.bfloat16, 4),
        compiler_params=talking(number),
        cost_estimate=lasting(20),
        name="scatter_and_head_sum",
    )(*scatter_blocks(arrays), values)


def last_sums(arrays, values, tokens, gain, upstream, number):
    count = len(arrays)
    shapes = scatter_shapes(arrays)
    rows, width = values.shape
    seq_count = lax.axis_size("seq")
    spaces = scatter_scratch(shapes)
    step = 16

    def kernel(*refs):
        takes = refs[:count]
        x_ref, token_ref, gain_ref, up_ref = refs[count : count + 4]
        gives = refs[count + 4 : 2 * count + 4]
        grad_ref, gain_out = refs[2 * count + 4 : 2 * count + 6]
        scratch = refs[2 * count + 6 :]
        total_ref, part_out, part_in, part_send, part_recv = scratch[-5:]
        seq = lax.axis_index("seq")
        head = lax.axis_index("head")
        peers = [((seq + k) % seq_count, head) for k in range(1, seq_count)]
        meet(peers + head_peers())

        def norm_job():
            yield from head_job(x_ref, total_ref, scratch[len(spaces) : -5], jnp.bfloat16, 4)

            def back(position, gained):
                part = pl.ds(pl.multiple_of(position * step, step), step)
                token = token_ref[part].astype(jnp.float32)
                scale = lax.rsqrt(jnp.mean(token * token, axis=1, keepdims=True) + epsilon)
                unit = token * scale
                given = total_ref[part]
                scaled = given * gain_ref[...]
                pull = jnp.mean(scaled * unit, axis=1, keepdims=True)
                grad_ref[part] = up_ref[part] + scale * (scaled - unit * pull)
                product_rows = given * unit
                return gained + product_rows[:8] + product_rows[8:]

            gained = lax.fori_loop(0, rows // step, back, jnp.zeros((8, width), jnp.float32))
            part_out[...] = jnp.sum(gained, axis=0, keepdims=True)
            copies = [
                send_to(part_out, part_in.at[k], part_send.at[k], part_recv.at[k], peers[k])
                for k in range(seq_count - 1)
            ]
            for copy in copies:
                copy.start()
            yield
            for copy in copies:
                copy.wait_recv()
            whole = part_out[...]
            for k in range(seq_count - 1):
                whole = whole + part_in[k]
            gain_out[...] = whole
            for copy in copies:
                copy.wait_send()

        together(norm_job(), scatter_job(takes, gives, scratch[: len(spaces)], shapes))

    return pl.pallas_call(
        kernel,
        out_shape=[jax.ShapeDtypeStruct(shape, jnp.float32) for shape in shapes]
        + [
            jax.ShapeDtypeStruct((rows, width), jnp.float32),
            jax.ShapeDtypeStruct((1, width), jnp.float32),
        ],
        in_specs=[ANY] * count + [VMEM] * 4,
        out_specs=[VMEM] * (count + 2),
        scratch_shapes=spaces
        + head_scratch(rows, width, jnp.bfloat16, 4)
        + [
            pltpu.VMEM((rows, width), jnp.float32),
            pltpu.VMEM((1, width), jnp.float32),
            pltpu.VMEM((seq_count - 1, 1, width), jnp.float32),
            pltpu.SemaphoreType.DMA((seq_count - 1,)),
            pltpu.SemaphoreType.DMA((seq_count - 1,)),
        ],
        compiler_params=talking(number),
        cost_estimate=lasting(20),
        name="last_sums",
    )(*scatter_blocks(arrays), values, tokens, gain, upstream)


def widen(column_block, width):
    return jnp.concatenate([column_block] * (width // LANES), axis=-1)


def narrow(wide):
    width = wide.shape[-1]
    total = wide[:, :LANES]
    for place in range(1, width // LANES):
        total = total + wide[:, place * LANES : (place + 1) * LANES]
    return total


def spread(columns):
    return jnp.broadcast_to(columns[:, :, None], columns.shape + (LANES,))


def run_summary(steps, drives, coefficients, slopes, number, forward):
    rows, width = steps.shape
    entries = slopes.shape[0]
    seq_count = lax.axis_size("seq")
    group = math.gcd(rows, 8)

    def kernel(
        step_ref,
        drive_ref,
        coef_ref,
        slope_ref,
        o_ref,
        outgoing,
        incoming,
        span_out,
        span_in,
        send,
        recv,
    ):
        seq = lax.axis_index("seq")
        head = lax.axis_index("head")
        peers = [((seq + k) % seq_count, head) for k in range(1, seq_count)]
        meet(peers)
        slope = slope_ref[...]
        span_out[...] = jnp.broadcast_to(
            jnp.sum(step_ref[...], axis=0, keepdims=True), span_out.shape
        )
        spans = [
            send_to(span_out, span_in.at[k], send.at[1, k], recv.at[1, k], peers[k])
            for k in range(seq_count - 1)
        ]
        for copy in spans:
            copy.start()

        def advance(position, state):
            for offset in range(group):
                t = position * group + offset
                t = t if forward else rows - 1 - t
                decays = jnp.exp2(step_ref[pl.ds(t, 1), :] * slope)
                drive = drive_ref[pl.ds(t, 1), :] * widen(coef_ref[t], width)
                state = state * decays + drive if forward else (state + drive) * decays
            return state

        state = lax.fori_loop(0, rows // group, advance, jnp.zeros((entries, width), jnp.float32))
        outgoing[...] = state.astype(jnp.bfloat16)
        copies = [
            send_to(outgoing, incoming.at[k], send.at[0, k], recv.at[0, k], peers[k])
            for k in range(seq_count - 1)
        ]
        for copy in copies:
            copy.start()
        for copy in spans:
            copy.wait_recv()
        for copy in copies:
            copy.wait_recv()
        carried = jnp.zeros((entries, width), jnp.float32)
        order = range(seq_count - 1, 0, -1) if forward else range(1, seq_count)
        for k in order:
            known = seq - k >= 0 if forward else seq - k < 0
            whole = jnp.exp2(span_in[k - 1][:1] * slope)
            carried = jnp.where(known, whole * carried + incoming[k - 1].astype(jnp.float32), 0.0)
        o_ref[...] = carried
        for copy in copies + spans:
            copy.wait_send()

    return pl.pallas_call(
        kernel,
        out_shape=jax.ShapeDtypeStruct((entries, width), jnp.float32),
        in_specs=[VMEM] * 4,
        out_specs=VMEM,
        scratch_shapes=[
            pltpu.VMEM((entries, width), jnp.bfloat16),
            pltpu.VMEM((seq_count - 1, entries, width), jnp.bfloat16),
            pltpu.VMEM((8, width), jnp.float32),
            pltpu.VMEM((seq_count - 1, 8, width), jnp.float32),
            pltpu.SemaphoreType.DMA((2, seq_count - 1)),
            pltpu.SemaphoreType.DMA((2, seq_count - 1)),
        ],
        compiler_params=talking(number),
        cost_estimate=lasting(16),
        name="run_summary",
    )(steps, drives, coefficients, slopes)


def state_sweep(initial, steps, drives, inject, readout, slopes):
    rows, width = steps.shape
    entries = slopes.shape[0]
    length = math.gcd(rows, 32)
    group = math.gcd(length, 8)

    def kernel(
        init_ref, step_ref, drive_ref, inject_ref, read_ref, slope_ref, y_ref, before_ref, end_ref
    ):
        @pl.when(pl.program_id(0) == 0)
        def begin():
            end_ref[...] = init_ref[...]

        slope = slope_ref[...]

        def advance(position, state):
            for offset in range(group):
                t = position * group + offset
                before_ref[t] = state
                decays = jnp.exp2(step_ref[pl.ds(t, 1), :] * slope)
                drive = drive_ref[pl.ds(t, 1), :] * widen(inject_ref[t], width)
                state = state * decays + drive
                y_ref[pl.ds(t, 1), :] = jnp.sum(
                    state * widen(read_ref[t], width), axis=0, keepdims=True
                )
            return state

        end_ref[...] = lax.fori_loop(0, length // group, advance, end_ref[...])

    row_spec = pl.BlockSpec((length, width), lambda i: (i, 0))
    entry_spec = pl.BlockSpec((length, entries, LANES), lambda i: (i, 0, 0))
    fixed = pl.BlockSpec((entries, width), lambda i: (0, 0))
    return pl.pallas_call(
        kernel,
        grid=(rows // length,),
        out_shape=(
            jax.ShapeDtypeStruct((rows, width), jnp.float32),
            jax.ShapeDtypeStruct((rows, entries, width), jnp.float32),
            jax.ShapeDtypeStruct((entries, width), jnp.float32),
        ),
        in_specs=[fixed, row_spec, row_spec, entry_spec, entry_spec, fixed],
        out_specs=(
            row_spec,
            pl.BlockSpec((length, entries, width), lambda i: (i, 0, 0)),
            fixed,
        ),
        compiler_params=pltpu.CompilerParams(vmem_limit_bytes=LIMIT),
        cost_estimate=lasting(11),
        name="state_sweep",
    )(initial, steps, drives, inject, readout, slopes)


def adjoint_sweep(incoming, last_state, befores, steps, drives, inject, readout, upstream, slopes):
    rows, width = steps.shape
    entries = slopes.shape[0]
    length = math.gcd(rows, 32)
    group = math.gcd(length, 8)
    blocks = rows // length

    def kernel(
        in_ref,
        last_ref,
        before_ref,
        step_ref,
        drive_ref,
        inject_ref,
        read_ref,
        up_ref,
        slope_ref,
        through_ref,
        injected_ref,
        inject_out,
        read_out,
        rate_ref,
        adjoint_ref,
        state_ref,
    ):
        @pl.when(pl.program_id(0) == 0)
        def begin():
            adjoint_ref[...] = in_ref[...]
            state_ref[...] = last_ref[...]
            rate_ref[...] = jnp.zeros_like(rate_ref)

        slope = slope_ref[...]

        def retreat(position, carried):
            adjoint_in, rate = carried
            for offset in range(group):
                t = length - 1 - (position * group + offset)
                upper = up_ref[pl.ds(t, 1), :]
                step = step_ref[pl.ds(t, 1), :]
                adjoint = widen(read_ref[t], width) * upper + adjoint_in
                state = state_ref[...] if offset == 0 else before_ref[t + 1]
                read_out[t] = narrow(upper * state)
                adjoint_in = jnp.exp2(step * slope) * adjoint
                before = before_ref[t]
                through = adjoint_in * before
                rate = rate + through * step
                through_ref[pl.ds(t, 1), :] = jnp.sum(through * slope, axis=0, keepdims=True)
                injected_ref[pl.ds(t, 1), :] = jnp.sum(
                    adjoint * widen(inject_ref[t], width), axis=0, keepdims=True
                )
                inject_out[t] = narrow(adjoint * drive_ref[pl.ds(t, 1), :])
            state_ref[...] = before_ref[length - (position + 1) * group]
            return (adjoint_in, rate)

        adjoint_end, rate_end = lax.fori_loop(
            0, length // group, retreat, (adjoint_ref[...], rate_ref[...])
        )
        adjoint_ref[...] = adjoint_end
        rate_ref[...] = rate_end

    row_spec = pl.BlockSpec((length, width), lambda i: (blocks - 1 - i, 0))
    entry_spec = pl.BlockSpec((length, entries, LANES), lambda i: (blocks - 1 - i, 0, 0))
    fixed = pl.BlockSpec((entries, width), lambda i: (0, 0))
    wide = jax.ShapeDtypeStruct((rows, width), jnp.float32)
    partial = jax.ShapeDtypeStruct((rows, entries, LANES), jnp.float32)
    return pl.pallas_call(
        kernel,
        grid=(blocks,),
        out_shape=(
            wide,
            wide,
            partial,
            partial,
            jax.ShapeDtypeStruct((entries, width), jnp.float32),
        ),
        in_specs=[
            fixed,
            fixed,
            pl.BlockSpec((length, entries, width), lambda i: (blocks - 1 - i, 0, 0)),
            row_spec,
            row_spec,
            entry_spec,
            entry_spec,
            row_spec,
            fixed,
        ],
        out_specs=(row_spec, row_spec, entry_spec, entry_spec, fixed),
        scratch_shapes=[pltpu.VMEM((entries, width), jnp.float32)] * 2,
        compiler_params=pltpu.CompilerParams(vmem_limit_bytes=LIMIT),
        cost_estimate=lasting(15),
        name="adjoint_sweep",
    )(incoming, last_state, befores, steps, drives, inject, readout, upstream, slopes)


def over_rows(left, right):
    return lax.dot_general(left, right, (((0,), (0,)), ((), ())), preferred_element_type=jnp.float32)


def over_columns(left, right):
    return lax.dot_general(left, right, (((1,), (1,)), ((), ())), preferred_element_type=jnp.float32)


def stand_up(rows, target, shared_heads):
    count, width = rows.shape
    heads = width // HEAD_DIM
    group = heads // shared_heads
    turned = rows.astype(jnp.float32).T.astype(target.dtype)
    target[...] = jnp.zeros_like(target)
    for head in range(heads):
        shared = head // group
        target[shared * HEAD_DIM : (shared + 1) * HEAD_DIM, head * count : (head + 1) * count] = (
            turned[head * HEAD_DIM : (head + 1) * HEAD_DIM]
        )


def lie_down(upright, count, shared_heads):
    heads = upright.shape[1] // count
    group = heads // shared_heads
    blocks = []
    for head in range(heads):
        shared = head // group
        blocks.append(
            upright[
                shared * HEAD_DIM : (shared + 1) * HEAD_DIM, head * count : (head + 1) * count
            ]
        )
    return jnp.concatenate(blocks, axis=0).T


def hidden_bias(key_docs, query_docs, diagonal):
    key_count, query_count = key_docs.shape[0], query_docs.shape[1]
    shape = (key_count, query_count)
    earlier = lax.broadcasted_iota(jnp.int32, shape, 0) <= lax.broadcasted_iota(
        jnp.int32, shape, 1
    )
    bias = jnp.where(key_docs == query_docs, 0.0, masked_score)
    return jnp.where(jnp.logical_or(earlier, jnp.logical_not(diagonal)), bias, masked_score)


def attend(queries, both, key_docs, query_docs, number):
    rows, width = queries.shape
    key_width = both.shape[1] // 2
    shared_heads = key_width // HEAD_DIM
    heads = width // HEAD_DIM
    seq_count = lax.axis_size("seq")
    pairs = seq_count // 2
    scale = 0.125 * LOG2E

    def kernel(
        q_ref,
        x_ref,
        kd_ref,
        qd_ref,
        low_ref,
        att_ref,
        lse_ref,
        kv_ref,
        qt_ref,
        max_ref,
        sum_ref,
        send,
        recv,
        pass_send,
        pass_recv,
    ):
        me = lax.axis_index("seq")
        place = me % 2
        pair = me // 2
        partner, *others = pair_peers()
        meet([partner] + others)

        first = [
            send_to(x_ref, kv_ref.at[me], send.at[k], recv.at[k], others[k])
            for k in range(pairs - 1)
        ]
        across = send_to(x_ref, kv_ref.at[me], pass_send.at[0], pass_recv.at[0], partner)
        across.start()
        for copy in first:
            copy.start()
        kv_ref[me] = x_ref[...]
        stand_up(q_ref[...], qt_ref, shared_heads)

        def block(owner, own):
            keys = x_ref[:, :key_width] if own else kv_ref[owner, :, :key_width]
            values = x_ref[:, key_width:] if own else kv_ref[owner, :, key_width:]
            begin = pl.multiple_of(owner * rows, rows)
            bias = hidden_bias(kd_ref[pl.ds(begin, rows), :], qd_ref[...], own)
            for head in range(heads):
                columns = slice(head * rows, (head + 1) * rows)
                scores = product(keys, qt_ref[:, columns]) * scale + bias
                top = jnp.max(scores, axis=0, keepdims=True)
                if not own:
                    old = max_ref[:, columns]
                    top = jnp.maximum(top, old)
                weights = jnp.exp2(scores - top)
                total = jnp.sum(weights, axis=0, keepdims=True)
                weighted = over_rows(values, to_low(weights))
                if not own:
                    factor = jnp.exp2(old - top)
                    total = total + sum_ref[:, columns] * factor
                    weighted = weighted + att_ref[:, columns] * factor
                max_ref[:, columns] = top
                sum_ref[:, columns] = total
                att_ref[:, columns] = weighted

        def earlier(owner):
            @pl.when(owner < me)
            def visit():
                block(owner, False)

        block(me, True)
        for k in range(1, pairs):
            first[k - 1].wait_recv()
            origin = ((pair - k + pairs) % pairs) * 2 + place
            passed = send_to(
                kv_ref.at[origin], kv_ref.at[origin], pass_send.at[k], pass_recv.at[k], partner
            )
            passed.start()
            if k == 1:
                across.wait_recv()
                earlier(me + 1 - 2 * place)
            earlier(origin)

        @pl.loop(1, pairs)
        def arrived(k):
            origin = ((pair - k + pairs) % pairs) * 2 + place
            other = origin + 1 - 2 * place
            send_to(
                kv_ref.at[origin], kv_ref.at[origin], pass_send.at[k], pass_recv.at[k], partner
            ).wait_recv()
            earlier(other)

        att_ref[...] = att_ref[...] / sum_ref[...]
        lse_ref[...] = max_ref[...] + jnp.log2(sum_ref[...])
        low_ref[...] = to_low(lie_down(att_ref, rows, shared_heads))
        for copy in first + [across]:
            copy.wait_send()

        @pl.loop(1, pairs)
        def sent(k):
            origin = ((pair - k + pairs) % pairs) * 2 + place
            send_to(
                kv_ref.at[origin], kv_ref.at[origin], pass_send.at[k], pass_recv.at[k], partner
            ).wait_send()

    return pl.pallas_call(
        kernel,
        out_shape=(
            jax.ShapeDtypeStruct((rows, width), jnp.bfloat16),
            jax.ShapeDtypeStruct((key_width, heads * rows), jnp.float32),
            jax.ShapeDtypeStruct((1, heads * rows), jnp.float32),
            jax.ShapeDtypeStruct((seq_count,) + both.shape, both.dtype),
        ),
        in_specs=[VMEM] * 4,
        out_specs=(VMEM,) * 4,
        scratch_shapes=[
            pltpu.VMEM((key_width, heads * rows), jnp.bfloat16),
            pltpu.VMEM((1, heads * rows), jnp.float32),
            pltpu.VMEM((1, heads * rows), jnp.float32),
        ]
        + [pltpu.SemaphoreType.DMA((pairs,))] * 4,
        compiler_params=talking(number),
        cost_estimate=lasting(12),
        name="attend",
    )(queries, both, key_docs, query_docs)


def attend_back(own, queries, upstream, both_rows, key_docs, query_docs, attended, log_sum):
    rows, width = queries.shape
    total_rows = both_rows.shape[0]
    key_width = both_rows.shape[1] // 2
    shared_heads = key_width // HEAD_DIM
    heads = width // HEAD_DIM
    scale = 0.125 * LOG2E

    def kernel(
        own_ref, q_ref, up_ref, kv_ref, kd_ref, qd_ref, att_ref, lse_ref, qg_ref, kg_ref, vg_ref, qt_ref, ut_ref, acc_ref
    ):
        stand_up(q_ref[...], qt_ref, shared_heads)
        stand_up(up_ref[...], ut_ref, shared_heads)
        me = own_ref[0]
        delta = jnp.sum(ut_ref[...].astype(jnp.float32) * att_ref[...], axis=0, keepdims=True)
        acc_ref[...] = jnp.zeros_like(acc_ref)

        @pl.loop(me + 1, total_rows // rows)
        def later(position):
            begin = pl.multiple_of(position * rows, rows)
            kg_ref[pl.ds(begin, rows), :] = jnp.zeros((rows, key_width), jnp.bfloat16)
            vg_ref[pl.ds(begin, rows), :] = jnp.zeros((rows, key_width), jnp.bfloat16)

        @pl.loop(0, me + 1)
        def block(position):
            begin = pl.multiple_of(position * rows, rows)
            keys = kv_ref[pl.ds(begin, rows), :key_width]
            values = kv_ref[pl.ds(begin, rows), key_width:]
            bias = hidden_bias(kd_ref[pl.ds(begin, rows), :], qd_ref[...], position == me)
            key_grad = jnp.zeros((rows, key_width), jnp.float32)
            value_grad = jnp.zeros((rows, key_width), jnp.float32)
            for head in range(heads):
                columns = slice(head * rows, (head + 1) * rows)
                query = qt_ref[:, columns]
                upper = ut_ref[:, columns]
                probs = jnp.exp2(product(keys, query) * scale + bias - lse_ref[:, columns])
                value_grad = value_grad + over_columns(to_low(probs), upper)
                score_grad = to_low(probs * (product(values, upper) - delta[:, columns]))
                key_grad = key_grad + over_columns(score_grad, query)
                acc_ref[:, columns] += over_rows(keys, score_grad)
            kg_ref[pl.ds(begin, rows), :] = to_low(key_grad * 0.125)
            vg_ref[pl.ds(begin, rows), :] = to_low(value_grad)

        qg_ref[...] = to_low(lie_down(acc_ref, rows, shared_heads) * 0.125)

    return pl.pallas_call(
        kernel,
        out_shape=(
            jax.ShapeDtypeStruct((rows, width), jnp.bfloat16),
            jax.ShapeDtypeStruct((total_rows, key_width), jnp.bfloat16),
            jax.ShapeDtypeStruct((total_rows, key_width), jnp.bfloat16),
        ),
        in_specs=[pl.BlockSpec(memory_space=pltpu.SMEM)] + [VMEM] * 7,
        out_specs=(VMEM,) * 3,
        scratch_shapes=[
            pltpu.VMEM((key_width, heads * rows), jnp.bfloat16),
            pltpu.VMEM((key_width, heads * rows), jnp.bfloat16),
            pltpu.VMEM((key_width, heads * rows), jnp.float32),
        ],
        compiler_params=pltpu.CompilerParams(vmem_limit_bytes=LIMIT),
        cost_estimate=lasting(20),
        name="attend_back",
    )(own, queries, upstream, both_rows, key_docs, query_docs, attended, log_sum)


def body(
    tokens_in,
    cotangent,
    document_ids,
    expert_routes,
    norm_mixer,
    mixer_inner,
    mixer_gate,
    conv_taps,
    conv_bias,
    state_proj,
    step_proj,
    step_bias,
    decay_log,
    skip_gain,
    mixer_out,
    norm_ffn,
    ffn_gate,
    ffn_up,
    ffn_down,
    norm_attn,
    attn_query,
    attn_key,
    attn_value,
    attn_output,
    norm_moe,
    router,
    expert_gate,
    expert_up,
    expert_down,
):
    numbers = itertools.count()
    seq_count = lax.axis_size("seq")
    row_count = tokens_in.shape[0]
    total_rows = seq_count * row_count
    first_row = lax.axis_index("seq") * row_count
    last_row = first_row + row_count - 1

    me = lax.axis_index("seq")
    bit_count = seq_count.bit_length() - 1
    across_first = [0] + list(range(1, bit_count))
    along_first = [1, 0] + list(range(2, bit_count))

    def by_owner(values, bits):
        turned = values.transpose(0, 2, 1)
        own_rows = turned.shape[1] // seq_count
        order = [0]
        for bit in reversed(bits):
            order = order + [j + (1 << bit) for j in order]
        blocks = []
        for j in order:
            owner = me
            for bit in range(bit_count):
                if j >> bit & 1:
                    owner = owner + (1 << bit) * (1 - 2 * ((owner >> bit) & 1))
            blocks.append(lax.dynamic_slice_in_dim(turned, owner * own_rows, own_rows, 1))
        parts = []
        while len(blocks) > 1:
            half = len(blocks) // 2
            parts.append(jnp.concatenate(blocks[half:], axis=1) if half > 1 else blocks[half])
            blocks = blocks[:half]
        return parts + blocks, bits

    def begin_sum(*parts):
        flow = {"parts": parts, "bits": parts[0][0][1], "got": []}
        settle(flow)
        return flow

    def settle(flow):
        step = len(flow["got"])
        gradients = [
            jnp.einsum(
                "bdt,btf->bdf", rows[0][step], columns, preferred_element_type=jnp.float32
            )
            for rows, columns in flow["parts"]
        ]
        total = gradients[0] if len(gradients) == 1 else jnp.concatenate(gradients, axis=2)
        count = total.shape[1]
        first = count if step < len(flow["bits"]) else 0
        for got in flow["got"]:
            total = total + got[:, first : first + count].astype(jnp.float32)
        if step == len(flow["bits"]):
            flow["total"] = total
            return
        bit = flow["bits"][step]
        route = [(i, i ^ (1 << bit)) for i in range(seq_count)]
        flow["got"].append(lax.ppermute(to_low(total), "seq", route))

    def hold(values, *flows):
        if flows:
            tied = lax.optimization_barrier((values, *[flow["got"][-1] for flow in flows]))
            values = tied[0]
            for flow, got in zip(flows, tied[1:], strict=True):
                flow["got"][-1] = got
        return values

    def after(values, *flows):
        values = hold(values, *flows)
        for flow in flows:
            settle(flow)
        return values

    def finished(flow):
        while "total" not in flow:
            settle(flow)
        return flow["total"]

    def branch_sum(values):
        return head_sum(values, next(numbers), jnp.bfloat16, 4)

    local_docs = lax.dynamic_slice_in_dim(document_ids, first_row, row_count)
    reach = conv_taps.shape[0] - 1
    border = jnp.arange(reach, dtype=jnp.int32)
    docs_before = jnp.take(document_ids, jnp.maximum(first_row - reach + border, 0))
    docs_after = jnp.take(document_ids, jnp.minimum(first_row + row_count + border, total_rows - 1))
    docs_prior = jnp.concatenate([docs_before[reach - 1 :], local_docs[:-1]])
    retain = (local_docs == docs_prior).astype(jnp.float32)
    tokens = tokens_in.astype(jnp.float32)
    gain_mixer = norm_mixer.astype(jnp.float32)
    normed_one = to_low(rms_scale(tokens, gain_mixer))
    conv_in = to_low(product(normed_one, mixer_inner))
    gate_in = product(normed_one, mixer_gate)
    conv_edge = from_behind(conv_in[row_count - reach :], "seq", 1)
    extended = jnp.concatenate([conv_edge, conv_in]).astype(jnp.float32)
    docs_ext = jnp.concatenate([docs_before, local_docs])
    taps = conv_taps.astype(jnp.float32)
    conv_sum = conv_bias.astype(jnp.float32)[None, :]
    masks = []
    for offset in range(reach + 1):
        same_doc = (docs_ext[offset : offset + row_count] == local_docs).astype(jnp.float32)[
            :, None
        ]
        masks.append(same_doc)
        conv_sum = conv_sum + taps[offset] * extended[offset : offset + row_count] * same_doc
    activated = jax.nn.silu(conv_sum)
    act_low = to_low(activated)
    projected = head_sum(product(act_low, state_proj), next(numbers), jnp.float32, 1)
    rank_size = step_proj.shape[0]
    state_size = decay_log.shape[1]
    step_low = to_low(projected[:, :rank_size])
    inject = projected[:, rank_size : rank_size + state_size]
    readout = projected[:, rank_size + state_size :]
    step_pre = product(step_low, step_proj) + step_bias.astype(jnp.float32)
    step_dt = jax.nn.softplus(step_pre)
    decay_rate = jnp.exp(decay_log.astype(jnp.float32)).T
    slopes = -LOG2E * decay_rate
    steps = jnp.where(retain[:, None] > 0.0, step_dt, NEVER)
    drives = step_dt * activated
    inject_wide = spread(inject)
    readout_wide = spread(readout)
    state_in = run_summary(steps, drives, inject_wide, slopes, next(numbers), True)
    scanned, befores, state_out = state_sweep(
        state_in, steps, drives, inject_wide, readout_wide, slopes
    )
    skipping = skip_gain.astype(jnp.float32)
    mixed_state = scanned + skipping * activated
    gate_act = jax.nn.silu(gate_in)
    gated = to_low(mixed_state * gate_act)
    hidden_one = tokens + branch_sum(product(gated, mixer_out))
    gain_ffn = norm_ffn.astype(jnp.float32)
    normed_two = to_low(rms_scale(hidden_one, gain_ffn))
    gate_two = product(normed_two, ffn_gate)
    up_two = product(normed_two, ffn_up)
    ffn_act = to_low(jax.nn.silu(gate_two) * up_two)
    hidden_two = hidden_one + branch_sum(product(ffn_act, ffn_down))
    gain_attn = norm_attn.astype(jnp.float32)
    normed_three = to_low(rms_scale(hidden_two, gain_attn))
    queries = to_low(product(normed_three, attn_query))
    key_rows = to_low(product(normed_three, attn_key))
    value_rows = to_low(product(normed_three, attn_value))
    key_width = key_rows.shape[1]
    own_place = lax.axis_index("seq").reshape(1)
    key_docs = document_ids[:, None]
    query_docs = local_docs[None, :]
    attended_low, attended, log_sum, both_rows = attend(
        queries,
        jnp.concatenate([key_rows, value_rows], axis=1),
        key_docs,
        query_docs,
        next(numbers),
    )
    both_rows = both_rows.reshape(total_rows, -1)
    hidden_three = hidden_two + branch_sum(product(attended_low, attn_output))
    gain_moe = norm_moe.astype(jnp.float32)
    normed_four = to_low(rms_scale(hidden_three, gain_moe))
    logits = product(normed_four, router)
    expert_count = router.shape[1]
    experts = jnp.arange(expert_count, dtype=jnp.int32)
    named = (expert_routes[:, :, None] == experts).astype(jnp.float32)
    gate_weights = jax.nn.softmax(jnp.sum(named * logits[:, None, :], axis=2), axis=1)
    route_flat = expert_routes.reshape(-1)
    pair_count = route_flat.shape[0]
    pair_order = jnp.arange(pair_count, dtype=jnp.int32)
    earlier = (pair_order[None, :] < pair_order[:, None]) & (
        route_flat[None, :] == route_flat[:, None]
    )
    within = jnp.sum(earlier.astype(jnp.int32), axis=1)
    slot_index = (route_flat * CAP + within).reshape(row_count, 2)
    slots = jnp.arange(expert_count * CAP, dtype=jnp.int32)
    first_hit = slot_index[:, 0][None, :] == slots[:, None]
    second_hit = slot_index[:, 1][None, :] == slots[:, None]
    placing = (first_hit | second_hit).astype(jnp.bfloat16)
    slot_gates = jnp.sum(
        jnp.where(first_hit, gate_weights[:, 0][None, :], 0.0)
        + jnp.where(second_hit, gate_weights[:, 1][None, :], 0.0),
        axis=1,
    )
    expert_in = to_low(product(placing, normed_four)).reshape(expert_count, CAP, -1)
    slot_upstream = product(placing, cotangent)
    res_grad = to_low(slot_gates[:, None] * slot_upstream).reshape(expert_count, CAP, -1)
    gate_four = jnp.einsum(
        "ecd,edf->ecf", expert_in, expert_gate, preferred_element_type=jnp.float32
    )
    up_four = jnp.einsum("ecd,edf->ecf", expert_in, expert_up, preferred_element_type=jnp.float32)
    expert_act = to_low(jax.nn.silu(gate_four) * up_four)
    expert_res = jnp.einsum(
        "ecf,efd->ecd", expert_act, expert_down, preferred_element_type=jnp.float32
    ).reshape(expert_count * CAP, -1)
    upstream = cotangent.astype(jnp.float32)
    slot_dots = jnp.sum(expert_res * slot_upstream, axis=1)
    dots_part = jnp.stack(
        [
            jnp.sum(jnp.where(first_hit, slot_dots[:, None], 0.0), axis=0),
            jnp.sum(jnp.where(second_hit, slot_dots[:, None], 0.0), axis=0),
        ],
        axis=1,
    )
    combined = product(placing.T, to_low(slot_gates[:, None] * expert_res))
    act_back = to_low(
        jnp.einsum("ecd,efd->ecf", res_grad, expert_down, preferred_element_type=jnp.float32)
    ).astype(jnp.float32)
    gating_grad = to_low(act_back * up_four * silu_slope(gate_four))
    upward_grad = to_low(act_back * jax.nn.silu(gate_four))
    flow_expert_down = begin_sum((by_owner(res_grad, along_first), expert_act))
    expert_rows = by_owner(expert_in, across_first)
    flow_expert_in = begin_sum(
        (expert_rows, jnp.concatenate([gating_grad, upward_grad], axis=2))
    )
    slot_grads = (
        jnp.einsum("ecf,edf->ecd", gating_grad, expert_gate, preferred_element_type=jnp.float32)
        + jnp.einsum("ecf,edf->ecd", upward_grad, expert_up, preferred_element_type=jnp.float32)
    ).reshape(expert_count * CAP, -1)
    token_part = product(placing.T, to_low(slot_grads))
    model_width = tokens.shape[1]
    expert_sums = branch_sum(
        jnp.concatenate(
            [token_part, jnp.pad(dots_part, ((0, 0), (0, LANES - 2)))], axis=1
        )
    )
    normed_grad = expert_sums[:, :model_width]
    dots = expert_sums[:, model_width : model_width + 2]
    chosen_grad = gate_weights * (dots - jnp.sum(gate_weights * dots, axis=1, keepdims=True))
    logit_grad = jnp.sum(named * chosen_grad[:, :, None], axis=1)
    grad_router = exact_product(normed_four.astype(jnp.float32).T, logit_grad)
    normed_grad = normed_grad + exact_product(logit_grad, router.astype(jnp.float32).T)
    hidden_grad, grad_norm_moe = rms_back(hidden_three, gain_moe, normed_grad)
    three_grad = upstream + hidden_grad
    branch_grad = to_low(three_grad)
    attn_out_rows = by_owner(branch_grad[None], across_first)
    attended_grad = to_low(product(branch_grad, attn_output.T))
    query_grad, key_part, value_part = attend_back(
        own_place, queries, attended_grad, both_rows, key_docs, query_docs, attended, log_sum
    )
    key_part = hold(key_part, flow_expert_down, flow_expert_in)
    key_sum, value_sum, combined_sum = scatter_and_head_sum(
        [key_part, value_part], combined, next(numbers)
    )
    mixed_out = to_low(hidden_three + combined_sum)
    key_sum, attended_late = lax.optimization_barrier((key_sum, attended_low))
    key_sum = after(key_sum, flow_expert_down, flow_expert_in)
    key_grad = to_low(key_sum)
    value_grad = to_low(value_sum)
    flow_attn = begin_sum(
        (
            by_owner(normed_three[None], across_first),
            jnp.concatenate([query_grad, key_grad, value_grad], axis=1)[None],
        ),
        (attn_out_rows, attended_late[None]),
    )
    normed_part = (
        product(query_grad, attn_query.T)
        + product(key_grad, attn_key.T)
        + product(value_grad, attn_value.T)
    )
    normed_grad = branch_sum(normed_part)
    hidden_grad, grad_norm_attn = rms_back(hidden_two, gain_attn, normed_grad)
    two_grad = three_grad + hidden_grad
    branch_grad = to_low(two_grad)
    flow_ffn_down = begin_sum((by_owner(branch_grad[None], along_first), ffn_act[None]))
    ffn_back = to_low(product(branch_grad, ffn_down.T))
    ffn_back = after(ffn_back, flow_expert_down, flow_expert_in, flow_attn).astype(jnp.float32)
    feed_gate_grad = to_low(ffn_back * up_two * silu_slope(gate_two))
    feed_up_grad = to_low(ffn_back * jax.nn.silu(gate_two))
    feed_rows = by_owner(normed_two[None], across_first)
    flow_ffn_gate = begin_sum((feed_rows, feed_gate_grad[None]))
    normed_part = product(feed_gate_grad, ffn_gate.T) + product(feed_up_grad, ffn_up.T)
    normed_grad = branch_sum(normed_part)
    hidden_grad, grad_norm_ffn = rms_back(hidden_one, gain_ffn, normed_grad)
    one_grad = two_grad + hidden_grad
    branch_grad = to_low(one_grad)
    mixer_out_rows = by_owner(branch_grad[None], across_first)
    gated_grad = to_low(product(branch_grad, mixer_out.T)).astype(jnp.float32)
    scan_grad = gated_grad * gate_act
    gate_in_grad = to_low(gated_grad * mixed_state * silu_slope(gate_in))
    grad_skip_gain = jnp.sum(scan_grad * activated, axis=0)
    early_flows = (flow_expert_down, flow_expert_in, flow_attn, flow_ffn_down, flow_ffn_gate)
    scan_grad = hold(scan_grad, *early_flows)
    state_after = run_summary(steps, scan_grad, readout_wide, slopes, next(numbers), False)
    state_after, gate_grad_late, feed_up_late = lax.optimization_barrier(
        (state_after, gate_in_grad, feed_up_grad)
    )
    state_after = after(state_after, flow_attn, flow_ffn_down, flow_ffn_gate)
    flow_ffn_up = begin_sum((feed_rows, feed_up_late[None]))
    flow_mixer_gate = begin_sum((by_owner(normed_one[None], along_first), gate_grad_late[None]))
    through_sum, injected, inject_part, readout_part, rate_sum = adjoint_sweep(
        state_after,
        state_out,
        befores,
        steps,
        drives,
        inject_wide,
        readout_wide,
        scan_grad,
        slopes,
    )
    step_grad = LN2 * through_sum + activated * injected
    input_grad = step_dt * injected
    inject_grad = jnp.sum(inject_part, axis=2)
    readout_grad = jnp.sum(readout_part, axis=2)
    grad_decay_log = -rate_sum * decay_rate
    pre_grad = step_grad * jax.nn.sigmoid(step_pre)
    grad_step_bias = jnp.sum(pre_grad, axis=0)
    pre_low = to_low(pre_grad)
    grad_step_proj = product(step_low.T, pre_low)
    proj_part = jnp.concatenate([product(pre_low, step_proj.T), inject_grad, readout_grad], axis=1)
    proj_part, gated_late = lax.optimization_barrier((proj_part, gated))
    proj_part = after(proj_part, flow_ffn_down, flow_ffn_gate, flow_attn)
    flow_mixer_out = begin_sum((mixer_out_rows, gated_late[None]))
    proj_low = to_low(head_sum(proj_part, next(numbers), jnp.float32, 1))
    proj_low = after(proj_low, flow_ffn_up, flow_mixer_gate)
    grad_state_proj = product(act_low.T, proj_low)
    act_total = input_grad + skipping * scan_grad + product(proj_low, state_proj.T)
    conv_grad = act_total * silu_slope(conv_sum)
    conv_grad = after(conv_grad, flow_ffn_down, flow_ffn_gate)
    grad_conv_bias = jnp.sum(conv_grad, axis=0)
    after_edge = from_behind(conv_grad[:reach], "seq", -1)
    after_edge = after(after_edge, flow_mixer_out, flow_mixer_gate, flow_ffn_up)
    grad_ext = jnp.concatenate([conv_grad, after_edge])
    docs_next = jnp.concatenate([local_docs, docs_after])
    conv_in_grad = jnp.zeros_like(conv_grad)
    tap_rows = []
    for offset in range(reach + 1):
        tap_rows.append(
            jnp.sum(conv_grad * extended[offset : offset + row_count] * masks[offset], axis=0)
        )
        lead = reach - offset
        same_next = (docs_next[lead : lead + row_count] == local_docs).astype(jnp.float32)[:, None]
        conv_in_grad = conv_in_grad + taps[offset] * grad_ext[lead : lead + row_count] * same_next
    grad_conv_taps = jnp.stack(tap_rows)
    conv_low = to_low(conv_in_grad)
    inner_half = conv_low.shape[1] // 2
    grad_mixer_inner = to_low(product(normed_one.T, conv_low))
    normed_part = product(conv_low, mixer_inner.T) + product(gate_in_grad, mixer_gate.T)
    own_channels = grad_conv_bias.shape[0] // seq_count

    def cut(values, axis):
        values = jnp.moveaxis(values, axis, 0)
        return values.reshape(seq_count, -1)

    packed = jnp.concatenate(
        [
            cut(grad_norm_ffn, 0),
            cut(grad_norm_attn, 0),
            cut(grad_norm_moe, 0),
            cut(grad_router, 0),
            cut(grad_conv_taps, 1),
            cut(grad_conv_bias, 0),
            cut(grad_state_proj, 0),
            cut(grad_step_proj, 1),
            cut(grad_step_bias, 0),
            cut(grad_decay_log, 1),
            cut(grad_skip_gain, 0),
        ],
        axis=1,
    )
    spare = -packed.shape[1] % (16 * LANES)
    packed = to_low(jnp.pad(packed, ((0, 0), (0, spare)))).reshape(-1, LANES)
    packed = after(packed, flow_mixer_out)
    first_inner, second_inner, sum_packed, grad_tokens, grad_norm_mixer = last_sums(
        [grad_mixer_inner[:, :inner_half], grad_mixer_inner[:, inner_half:], packed],
        normed_part,
        tokens_in,
        gain_mixer[None, :],
        one_grad,
        next(numbers),
    )
    sum_attn = finished(flow_attn)[0]
    sum_expert_in = finished(flow_expert_in)
    expert_width = expert_gate.shape[2]
    sum_packed = sum_packed.reshape(-1)
    own_rows = model_width // seq_count
    taken = itertools.accumulate(
        [0]
        + [own_rows] * 3
        + [own_rows * expert_count]
        + [own_channels * (reach + 1), own_channels, own_channels * state_proj.shape[1]]
        + [own_channels * rank_size, own_channels, own_channels * state_size, own_channels]
    )
    bounds = list(taken)
    pieces = [sum_packed[low:high] for low, high in itertools.pairwise(bounds)]
    query_width = attn_query.shape[1]

    return (
        mixed_out,
        grad_tokens,
        lax.dynamic_slice_in_dim(grad_norm_mixer[0], me * own_rows, own_rows),
        jnp.concatenate([first_inner, second_inner], axis=1),
        finished(flow_mixer_gate)[0],
        pieces[4].reshape(own_channels, -1).T,
        pieces[5],
        pieces[6].reshape(own_channels, -1),
        pieces[7].reshape(own_channels, -1).T,
        pieces[8],
        pieces[9].reshape(own_channels, -1),
        pieces[10],
        finished(flow_mixer_out)[0].T,
        pieces[0],
        finished(flow_ffn_gate)[0],
        finished(flow_ffn_up)[0],
        finished(flow_ffn_down)[0].T,
        pieces[1],
        sum_attn[:, :query_width],
        sum_attn[:, query_width : query_width + key_width],
        sum_attn[:, query_width + key_width : query_width + 2 * key_width],
        sum_attn[:, query_width + 2 * key_width :].T,
        pieces[2],
        pieces[3].reshape(own_rows, -1),
        sum_expert_in[:, :, :expert_width],
        sum_expert_in[:, :, expert_width:],
        finished(flow_expert_down).transpose(0, 2, 1),
    )


def solution(mesh):
    in_specs = (
        P("seq", None),
        P("seq", None),
        P(),
        P("seq", None),
        P(),
        P(None, "head"),
        P(None, "head"),
        P(None, "head"),
        P("head"),
        P("head", None),
        P(None, "head"),
        P("head"),
        P("head", None),
        P("head"),
        P("head", None),
        P(),
        P(None, "head"),
        P(None, "head"),
        P("head", None),
        P(),
        P(None, "head"),
        P(None, "head"),
        P(None, "head"),
        P("head", None),
        P(),
        P(),
        P(None, None, "head"),
        P(None, None, "head"),
        P(None, "head", None),
    )
    out_specs = (
        P("seq", None),
        P("seq", None),
        P("seq"),
        P("seq", "head"),
        P("seq", "head"),
        P(None, ("head", "seq")),
        P(("head", "seq")),
        P(("head", "seq"), None),
        P(None, ("head", "seq")),
        P(("head", "seq")),
        P(("head", "seq"), None),
        P(("head", "seq")),
        P("head", "seq"),
        P("seq"),
        P("seq", "head"),
        P("seq", "head"),
        P("head", "seq"),
        P("seq"),
        P("seq", "head"),
        P("seq", "head"),
        P("seq", "head"),
        P("head", "seq"),
        P("seq"),
        P("seq", None),
        P(None, "seq", "head"),
        P(None, "seq", "head"),
        P(None, "head", "seq"),
    )
    return jax.shard_map(body, mesh=mesh, in_specs=in_specs, out_specs=out_specs, check_vma=False)
```

```python
import itertools
import math

import jax
import jax.numpy as jnp
from jax import lax
from jax.experimental import pallas as pl
from jax.experimental.pallas import tpu as pltpu
from jax.sharding import PartitionSpec as P

HEAD_DIM = 64
CAP = 160
LANES = 128
LOG2E = 1.4426950408889634
LN2 = 0.6931471805599453
NEVER = 1e30
MEBI = 1024 * 1024
MESH = pl.DeviceIdType.MESH
VMEM = pl.BlockSpec(memory_space=pltpu.VMEM)
ANY = pl.BlockSpec(memory_space=pl.ANY)


highest = lax.Precision.HIGHEST
epsilon = 1e-05
masked_score = -1e30


def from_behind(block, axis, distance):
    devices = range(lax.axis_size(axis))
    route = [(i - distance, i) for i in devices if i - distance in devices]
    return lax.ppermute(block, axis, route)


def to_low(values):
    return values.astype(jnp.bfloat16)


def product(left, right):
    return jnp.dot(left, right, preferred_element_type=jnp.float32)


def exact_product(left, right):
    return jnp.dot(left, right, precision=highest, preferred_element_type=jnp.float32)


def rms_scale(values, gain):
    return values * lax.rsqrt(jnp.mean(values * values, axis=-1, keepdims=True) + epsilon) * gain


def rms_back(values, gain, upstream):
    unused, pullback = jax.vjp(rms_scale, values, gain)
    return pullback(upstream)


def silu_slope(values):
    logistic = jax.nn.sigmoid(values)
    return logistic * (1.0 + values * (1.0 - logistic))


def meet(peers):
    barrier = pltpu.get_barrier_semaphore()
    for peer in peers:
        pl.semaphore_signal(barrier, inc=1, device_id=peer, device_id_type=MESH)
    pl.semaphore_wait(barrier, len(peers))


def send_to(source, target, send_sem, recv_sem, peer):
    return pltpu.make_async_remote_copy(
        src_ref=source,
        dst_ref=target,
        send_sem=send_sem,
        recv_sem=recv_sem,
        device_id=peer,
        device_id_type=MESH,
    )


def lasting(microseconds):
    return pl.CostEstimate(
        flops=int(microseconds * 1e3),
        bytes_accessed=int(microseconds * 1e3),
        transcendentals=0,
    )


def talking(number, mebibytes):
    return pltpu.CompilerParams(
        collective_id=number, has_side_effects=True, vmem_limit_bytes=mebibytes * MEBI
    )


def together(*jobs):
    waiting = list(jobs)
    while waiting:
        for job in list(waiting):
            if next(job, waiting) is waiting:
                waiting.remove(job)


def head_peers():
    seq = lax.axis_index("seq")
    head = lax.axis_index("head")
    return [(seq, head + 1 - 2 * (head % 2)), (seq, (head + 2) % 4)]


def head_scratch(rows, width, wire, pieces):
    return [pltpu.VMEM((rows // 2, width), wire)] * 4 + [
        pltpu.SemaphoreType.DMA((3, pieces)),
        pltpu.SemaphoreType.DMA((3, pieces)),
    ]


def head_job(x_ref, o_ref, scratch, wire, pieces):
    near_out, near_in, far_out, far_in, send, recv = scratch
    half = x_ref.shape[0] // 2
    step = half // pieces
    near, far = head_peers()
    core = lax.axis_index("head") % 2

    def rows_of(side, piece):
        return pl.ds(pl.multiple_of(side * half + piece * step, 8), step)

    first, second, third = [], [], []
    for piece in range(pieces):
        local = pl.ds(piece * step, step)
        near_out[local] = x_ref[rows_of(1 - core, piece)].astype(wire)
        first.append(
            send_to(
                near_out.at[local], near_in.at[local], send.at[0, piece], recv.at[0, piece], near
            )
        )
        first[-1].start()
    yield
    for piece in range(pieces):
        local = pl.ds(piece * step, step)
        first[piece].wait_recv()
        total = x_ref[rows_of(core, piece)] + near_in[local].astype(jnp.float32)
        far_out[local] = total.astype(wire)
        second.append(
            send_to(far_out.at[local], far_in.at[local], send.at[1, piece], recv.at[1, piece], far)
        )
        second[-1].start()
    yield
    for piece in range(pieces):
        local = pl.ds(piece * step, step)
        second[piece].wait_recv()
        whole = far_out[local].astype(jnp.float32) + far_in[local].astype(jnp.float32)
        o_ref[rows_of(core, piece)] = whole
        third.append(
            send_to(
                o_ref.at[rows_of(core, piece)],
                o_ref.at[rows_of(core, piece)],
                send.at[2, piece],
                recv.at[2, piece],
                near,
            )
        )
        third[-1].start()
    yield
    for copy in third:
        copy.wait_recv()
    for copy in first + second + third:
        copy.wait_send()


def head_sum(values, number, wire, pieces):
    rows, width = values.shape

    def kernel(x_ref, o_ref, *scratch):
        meet(head_peers())
        together(head_job(x_ref, o_ref, scratch, wire, pieces))

    return pl.pallas_call(
        kernel,
        out_shape=jax.ShapeDtypeStruct((rows, width), jnp.float32),
        in_specs=[VMEM],
        out_specs=VMEM,
        scratch_shapes=head_scratch(rows, width, wire, pieces),
        compiler_params=talking(number, 10),
        cost_estimate=lasting(6 + values.size // 40000),
        name="head_sum",
    )(values)


def pair_peers():
    seq = lax.axis_index("seq")
    head = lax.axis_index("head")
    pairs = lax.axis_size("seq") // 2
    place = seq % 2
    pair = seq // 2
    others = [(((pair + k) % pairs) * 2 + place, head) for k in range(1, pairs)]
    return [(seq + 1 - 2 * place, head)] + others


def scatter_shapes(arrays):
    seq_count = lax.axis_size("seq")
    return [(a.shape[0] // seq_count, a.shape[1]) for a in arrays]


def scatter_blocks(arrays):
    pairs = lax.axis_size("seq") // 2
    return [
        a.reshape(pairs, 2, shape[0], shape[1])
        for a, shape in zip(arrays, scatter_shapes(arrays), strict=True)
    ]


def scatter_scratch(shapes):
    pairs = lax.axis_size("seq") // 2
    count = len(shapes)
    return (
        [pltpu.VMEM((pairs,) + shape, jnp.bfloat16) for shape in shapes] * 2
        + [pltpu.VMEM((pairs - 1,) + shape, jnp.bfloat16) for shape in shapes]
        + [pltpu.SemaphoreType.DMA((count,))] * 3
        + [pltpu.SemaphoreType.DMA((count, pairs - 1))] * 2
    )


def scatter_job(takes, gives, scratch, shapes):
    count = len(takes)
    pairs = lax.axis_size("seq") // 2
    own, near, far = scratch[:count], scratch[count : 2 * count], scratch[2 * count : 3 * count]
    own_sem, near_send, near_recv, far_send, far_recv = scratch[3 * count :]
    seq = lax.axis_index("seq")
    place = seq % 2
    pair = seq // 2
    partner, *others = pair_peers()
    owners = [(pair + k) % pairs for k in range(1, pairs)]
    loads = [
        pltpu.make_async_copy(takes[i].at[:, place], own[i], own_sem.at[i]) for i in range(count)
    ]
    halves = [
        send_to(takes[i].at[:, 1 - place], near[i], near_send.at[i], near_recv.at[i], partner)
        for i in range(count)
    ]

    def launch(i):
        if i < count:
            halves[i].start()
            loads[i].start()

    sums = []

    def finish(i):
        for copy in sums[i]:
            copy.wait_recv()

        @pl.loop(0, shapes[i][0] // 16)
        def add(step):
            part = pl.ds(pl.multiple_of(step * 16, 16), 16)
            total = own[i][pair, part].astype(jnp.float32)
            for k in range(pairs - 1):
                total = total + far[i][k, part].astype(jnp.float32)
            gives[i][part] = total

    launch(0)
    launch(1)
    for i in range(count):
        yield
        halves[i].wait_recv()
        loads[i].wait()
        launch(i + 2)

        @pl.loop(0, pairs)
        def merge(block):
            @pl.loop(0, shapes[i][0] // 16)
            def add(step):
                part = pl.ds(pl.multiple_of(step * 16, 16), 16)
                total = own[i][block, part].astype(jnp.float32) + near[i][block, part].astype(
                    jnp.float32
                )
                own[i][block, part] = total.astype(jnp.bfloat16)

        sums.append(
            [
                send_to(
                    own[i].at[owners[k]],
                    far[i].at[k],
                    far_send.at[i, k],
                    far_recv.at[i, k],
                    others[k],
                )
                for k in range(pairs - 1)
            ]
        )
        for copy in sums[i]:
            copy.start()
        if i > 0:
            finish(i - 1)
    yield
    finish(count - 1)
    for copy in halves:
        copy.wait_send()
    for group in sums:
        for copy in group:
            copy.wait_send()


def scatter_and_head_sum(arrays, values, number):
    count = len(arrays)
    shapes = scatter_shapes(arrays)
    rows, width = values.shape
    spaces = scatter_scratch(shapes)

    def kernel(*refs):
        takes, x_ref = refs[:count], refs[count]
        gives, o_ref = refs[count + 1 : 2 * count + 1], refs[2 * count + 1]
        scratch = refs[2 * count + 2 :]
        meet(pair_peers() + head_peers())
        together(
            scatter_job(takes, gives, scratch[: len(spaces)], shapes),
            head_job(x_ref, o_ref, scratch[len(spaces) :], jnp.bfloat16, 4),
        )

    return pl.pallas_call(
        kernel,
        out_shape=[jax.ShapeDtypeStruct(shape, jnp.float32) for shape in shapes]
        + [jax.ShapeDtypeStruct((rows, width), jnp.float32)],
        in_specs=[ANY] * count + [VMEM],
        out_specs=[VMEM] * (count + 1),
        scratch_shapes=spaces + head_scratch(rows, width, jnp.bfloat16, 4),
        compiler_params=talking(number, 24),
        cost_estimate=lasting(20),
        name="scatter_and_head_sum",
    )(*scatter_blocks(arrays), values)


def last_sums(arrays, values, tokens, gain, upstream, number):
    count = len(arrays)
    shapes = scatter_shapes(arrays)
    rows, width = values.shape
    seq_count = lax.axis_size("seq")
    spaces = scatter_scratch(shapes)
    step = 16

    def kernel(*refs):
        takes = refs[:count]
        x_ref, token_ref, gain_ref, up_ref = refs[count : count + 4]
        gives = refs[count + 4 : 2 * count + 4]
        grad_ref, gain_out = refs[2 * count + 4 : 2 * count + 6]
        scratch = refs[2 * count + 6 :]
        total_ref, part_out, part_in, part_send, part_recv = scratch[-5:]
        seq = lax.axis_index("seq")
        head = lax.axis_index("head")
        peers = [((seq + k) % seq_count, head) for k in range(1, seq_count)]
        meet(peers + head_peers())

        def norm_job():
            yield from head_job(x_ref, total_ref, scratch[len(spaces) : -5], jnp.bfloat16, 4)

            def back(position, gained):
                part = pl.ds(pl.multiple_of(position * step, step), step)
                token = token_ref[part].astype(jnp.float32)
                scale = lax.rsqrt(jnp.mean(token * token, axis=1, keepdims=True) + epsilon)
                unit = token * scale
                given = total_ref[part]
                scaled = given * gain_ref[...]
                pull = jnp.mean(scaled * unit, axis=1, keepdims=True)
                grad_ref[part] = up_ref[part] + scale * (scaled - unit * pull)
                product_rows = given * unit
                return gained + product_rows[:8] + product_rows[8:]

            gained = lax.fori_loop(0, rows // step, back, jnp.zeros((8, width), jnp.float32))
            part_out[...] = jnp.sum(gained, axis=0, keepdims=True)
            copies = [
                send_to(part_out, part_in.at[k], part_send.at[k], part_recv.at[k], peers[k])
                for k in range(seq_count - 1)
            ]
            for copy in copies:
                copy.start()
            yield
            for copy in copies:
                copy.wait_recv()
            whole = part_out[...]
            for k in range(seq_count - 1):
                whole = whole + part_in[k]
            gain_out[...] = whole
            for copy in copies:
                copy.wait_send()

        together(norm_job(), scatter_job(takes, gives, scratch[: len(spaces)], shapes))

    return pl.pallas_call(
        kernel,
        out_shape=[jax.ShapeDtypeStruct(shape, jnp.float32) for shape in shapes]
        + [
            jax.ShapeDtypeStruct((rows, width), jnp.float32),
            jax.ShapeDtypeStruct((1, width), jnp.float32),
        ],
        in_specs=[ANY] * count + [VMEM] * 4,
        out_specs=[VMEM] * (count + 2),
        scratch_shapes=spaces
        + head_scratch(rows, width, jnp.bfloat16, 4)
        + [
            pltpu.VMEM((rows, width), jnp.float32),
            pltpu.VMEM((1, width), jnp.float32),
            pltpu.VMEM((seq_count - 1, 1, width), jnp.float32),
            pltpu.SemaphoreType.DMA((seq_count - 1,)),
            pltpu.SemaphoreType.DMA((seq_count - 1,)),
        ],
        compiler_params=talking(number, 28),
        cost_estimate=lasting(20),
        name="last_sums",
    )(*scatter_blocks(arrays), values, tokens, gain, upstream)


def widen(column_block, width):
    return jnp.concatenate([column_block] * (width // LANES), axis=-1)


def narrow(wide):
    width = wide.shape[-1]
    total = wide[:, :LANES]
    for place in range(1, width // LANES):
        total = total + wide[:, place * LANES : (place + 1) * LANES]
    return total


def spread(columns):
    return jnp.broadcast_to(columns[:, :, None], columns.shape + (LANES,))


def run_summary(steps, drives, coefficients, slopes, number, forward):
    rows, width = steps.shape
    entries = slopes.shape[0]
    seq_count = lax.axis_size("seq")
    group = math.gcd(rows, 8)

    def kernel(
        step_ref,
        drive_ref,
        coef_ref,
        slope_ref,
        o_ref,
        outgoing,
        incoming,
        span_out,
        span_in,
        send,
        recv,
    ):
        seq = lax.axis_index("seq")
        head = lax.axis_index("head")
        peers = [((seq + k) % seq_count, head) for k in range(1, seq_count)]
        meet(peers)
        slope = slope_ref[...]
        span_out[...] = jnp.broadcast_to(
            jnp.sum(step_ref[...], axis=0, keepdims=True), span_out.shape
        )
        spans = [
            send_to(span_out, span_in.at[k], send.at[1, k], recv.at[1, k], peers[k])
            for k in range(seq_count - 1)
        ]
        for copy in spans:
            copy.start()

        def advance(position, state):
            for offset in range(group):
                t = position * group + offset
                t = t if forward else rows - 1 - t
                decays = jnp.exp2(step_ref[pl.ds(t, 1), :] * slope)
                drive = drive_ref[pl.ds(t, 1), :] * widen(coef_ref[t], width)
                state = state * decays + drive if forward else (state + drive) * decays
            return state

        state = lax.fori_loop(0, rows // group, advance, jnp.zeros((entries, width), jnp.float32))
        outgoing[...] = state.astype(jnp.bfloat16)
        copies = [
            send_to(outgoing, incoming.at[k], send.at[0, k], recv.at[0, k], peers[k])
            for k in range(seq_count - 1)
        ]
        for copy in copies:
            copy.start()
        for copy in spans:
            copy.wait_recv()
        for copy in copies:
            copy.wait_recv()
        carried = jnp.zeros((entries, width), jnp.float32)
        order = range(seq_count - 1, 0, -1) if forward else range(1, seq_count)
        for k in order:
            known = seq - k >= 0 if forward else seq - k < 0
            whole = jnp.exp2(span_in[k - 1][:1] * slope)
            carried = jnp.where(known, whole * carried + incoming[k - 1].astype(jnp.float32), 0.0)
        o_ref[...] = carried
        for copy in copies + spans:
            copy.wait_send()

    return pl.pallas_call(
        kernel,
        out_shape=jax.ShapeDtypeStruct((entries, width), jnp.float32),
        in_specs=[VMEM] * 4,
        out_specs=VMEM,
        scratch_shapes=[
            pltpu.VMEM((entries, width), jnp.bfloat16),
            pltpu.VMEM((seq_count - 1, entries, width), jnp.bfloat16),
            pltpu.VMEM((8, width), jnp.float32),
            pltpu.VMEM((seq_count - 1, 8, width), jnp.float32),
            pltpu.SemaphoreType.DMA((2, seq_count - 1)),
            pltpu.SemaphoreType.DMA((2, seq_count - 1)),
        ],
        compiler_params=talking(number, 10),
        cost_estimate=lasting(16),
        name="run_summary",
    )(steps, drives, coefficients, slopes)


def state_sweep(initial, steps, drives, inject, readout, slopes):
    rows, width = steps.shape
    entries = slopes.shape[0]
    length = math.gcd(rows, 32)
    group = math.gcd(length, 8)

    def kernel(
        init_ref, step_ref, drive_ref, inject_ref, read_ref, slope_ref, y_ref, before_ref, end_ref
    ):
        @pl.when(pl.program_id(0) == 0)
        def begin():
            end_ref[...] = init_ref[...]

        slope = slope_ref[...]

        def advance(position, state):
            for offset in range(group):
                t = position * group + offset
                before_ref[t] = state
                decays = jnp.exp2(step_ref[pl.ds(t, 1), :] * slope)
                drive = drive_ref[pl.ds(t, 1), :] * widen(inject_ref[t], width)
                state = state * decays + drive
                y_ref[pl.ds(t, 1), :] = jnp.sum(
                    state * widen(read_ref[t], width), axis=0, keepdims=True
                )
            return state

        end_ref[...] = lax.fori_loop(0, length // group, advance, end_ref[...])

    row_spec = pl.BlockSpec((length, width), lambda i: (i, 0))
    entry_spec = pl.BlockSpec((length, entries, LANES), lambda i: (i, 0, 0))
    fixed = pl.BlockSpec((entries, width), lambda i: (0, 0))
    return pl.pallas_call(
        kernel,
        grid=(rows // length,),
        out_shape=(
            jax.ShapeDtypeStruct((rows, width), jnp.float32),
            pltpu.HBM((rows, entries, width), jnp.float32),
            jax.ShapeDtypeStruct((entries, width), jnp.float32),
        ),
        in_specs=[fixed, row_spec, row_spec, entry_spec, entry_spec, fixed],
        out_specs=(
            row_spec,
            pl.BlockSpec((length, entries, width), lambda i: (i, 0, 0)),
            fixed,
        ),
        compiler_params=pltpu.CompilerParams(vmem_limit_bytes=12 * MEBI),
        cost_estimate=lasting(11),
        name="state_sweep",
    )(initial, steps, drives, inject, readout, slopes)


def adjoint_sweep(incoming, last_state, befores, steps, drives, inject, readout, upstream, slopes):
    rows, width = steps.shape
    entries = slopes.shape[0]
    length = math.gcd(rows, 32)
    group = math.gcd(length, 8)
    blocks = rows // length

    def kernel(
        in_ref,
        last_ref,
        before_ref,
        step_ref,
        drive_ref,
        inject_ref,
        read_ref,
        up_ref,
        slope_ref,
        through_ref,
        injected_ref,
        inject_out,
        read_out,
        rate_ref,
        adjoint_ref,
        state_ref,
    ):
        @pl.when(pl.program_id(0) == 0)
        def begin():
            adjoint_ref[...] = in_ref[...]
            state_ref[...] = last_ref[...]
            rate_ref[...] = jnp.zeros_like(rate_ref)

        slope = slope_ref[...]

        def retreat(position, carried):
            adjoint_in, rate = carried
            for offset in range(group):
                t = length - 1 - (position * group + offset)
                upper = up_ref[pl.ds(t, 1), :]
                step = step_ref[pl.ds(t, 1), :]
                adjoint = widen(read_ref[t], width) * upper + adjoint_in
                state = state_ref[...] if offset == 0 else before_ref[t + 1]
                read_out[t] = narrow(upper * state)
                adjoint_in = jnp.exp2(step * slope) * adjoint
                before = before_ref[t]
                through = adjoint_in * before
                rate = rate + through * step
                through_ref[pl.ds(t, 1), :] = jnp.sum(through * slope, axis=0, keepdims=True)
                injected_ref[pl.ds(t, 1), :] = jnp.sum(
                    adjoint * widen(inject_ref[t], width), axis=0, keepdims=True
                )
                inject_out[t] = narrow(adjoint * drive_ref[pl.ds(t, 1), :])
            state_ref[...] = before_ref[length - (position + 1) * group]
            return (adjoint_in, rate)

        adjoint_end, rate_end = lax.fori_loop(
            0, length // group, retreat, (adjoint_ref[...], rate_ref[...])
        )
        adjoint_ref[...] = adjoint_end
        rate_ref[...] = rate_end

    row_spec = pl.BlockSpec((length, width), lambda i: (blocks - 1 - i, 0))
    entry_spec = pl.BlockSpec((length, entries, LANES), lambda i: (blocks - 1 - i, 0, 0))
    fixed = pl.BlockSpec((entries, width), lambda i: (0, 0))
    wide = jax.ShapeDtypeStruct((rows, width), jnp.float32)
    partial = jax.ShapeDtypeStruct((rows, entries, LANES), jnp.float32)
    return pl.pallas_call(
        kernel,
        grid=(blocks,),
        out_shape=(
            wide,
            wide,
            partial,
            partial,
            jax.ShapeDtypeStruct((entries, width), jnp.float32),
        ),
        in_specs=[
            fixed,
            fixed,
            pl.BlockSpec((length, entries, width), lambda i: (blocks - 1 - i, 0, 0)),
            row_spec,
            row_spec,
            entry_spec,
            entry_spec,
            row_spec,
            fixed,
        ],
        out_specs=(row_spec, row_spec, entry_spec, entry_spec, fixed),
        scratch_shapes=[pltpu.VMEM((entries, width), jnp.float32)] * 2,
        compiler_params=pltpu.CompilerParams(vmem_limit_bytes=14 * MEBI),
        cost_estimate=lasting(15),
        name="adjoint_sweep",
    )(
        incoming,
        last_state,
        pltpu.with_memory_space_constraint(befores, pltpu.HBM),
        steps,
        drives,
        inject,
        readout,
        upstream,
        slopes,
    )


def over_rows(left, right):
    return lax.dot_general(left, right, (((0,), (0,)), ((), ())), preferred_element_type=jnp.float32)


def over_columns(left, right):
    return lax.dot_general(left, right, (((1,), (1,)), ((), ())), preferred_element_type=jnp.float32)


def stand_up(rows, target, shared_heads):
    count, width = rows.shape
    heads = width // HEAD_DIM
    group = heads // shared_heads
    turned = rows.astype(jnp.float32).T.astype(target.dtype)
    target[...] = jnp.zeros_like(target)
    for head in range(heads):
        shared = head // group
        target[shared * HEAD_DIM : (shared + 1) * HEAD_DIM, head * count : (head + 1) * count] = (
            turned[head * HEAD_DIM : (head + 1) * HEAD_DIM]
        )


def lie_down(upright, count, shared_heads):
    heads = upright.shape[1] // count
    group = heads // shared_heads
    blocks = []
    for head in range(heads):
        shared = head // group
        blocks.append(
            upright[
                shared * HEAD_DIM : (shared + 1) * HEAD_DIM, head * count : (head + 1) * count
            ]
        )
    return jnp.concatenate(blocks, axis=0).T


def hidden_bias(key_docs, query_docs, diagonal):
    key_count, query_count = key_docs.shape[0], query_docs.shape[1]
    shape = (key_count, query_count)
    earlier = lax.broadcasted_iota(jnp.int32, shape, 0) <= lax.broadcasted_iota(
        jnp.int32, shape, 1
    )
    bias = jnp.where(key_docs == query_docs, 0.0, masked_score)
    return jnp.where(jnp.logical_or(earlier, jnp.logical_not(diagonal)), bias, masked_score)


def attend(queries, both, key_docs, query_docs, number):
    rows, width = queries.shape
    key_width = both.shape[1] // 2
    shared_heads = key_width // HEAD_DIM
    heads = width // HEAD_DIM
    seq_count = lax.axis_size("seq")
    pairs = seq_count // 2
    scale = 0.125 * LOG2E

    def kernel(
        q_ref,
        x_ref,
        kd_ref,
        qd_ref,
        low_ref,
        att_ref,
        lse_ref,
        kv_ref,
        qt_ref,
        max_ref,
        sum_ref,
        send,
        recv,
        pass_send,
        pass_recv,
    ):
        me = lax.axis_index("seq")
        place = me % 2
        pair = me // 2
        partner, *others = pair_peers()
        meet([partner] + others)

        first = [
            send_to(x_ref, kv_ref.at[me], send.at[k], recv.at[k], others[k])
            for k in range(pairs - 1)
        ]
        across = send_to(x_ref, kv_ref.at[me], pass_send.at[0], pass_recv.at[0], partner)
        across.start()
        for copy in first:
            copy.start()
        kv_ref[me] = x_ref[...]
        stand_up(q_ref[...], qt_ref, shared_heads)

        def block(owner, own):
            keys = x_ref[:, :key_width] if own else kv_ref[owner, :, :key_width]
            values = x_ref[:, key_width:] if own else kv_ref[owner, :, key_width:]
            begin = pl.multiple_of(owner * rows, rows)
            bias = hidden_bias(kd_ref[pl.ds(begin, rows), :], qd_ref[...], own)
            for head in range(heads):
                columns = slice(head * rows, (head + 1) * rows)
                scores = product(keys, qt_ref[:, columns]) * scale + bias
                top = jnp.max(scores, axis=0, keepdims=True)
                if not own:
                    old = max_ref[:, columns]
                    top = jnp.maximum(top, old)
                weights = jnp.exp2(scores - top)
                total = jnp.sum(weights, axis=0, keepdims=True)
                weighted = over_rows(values, to_low(weights))
                if not own:
                    factor = jnp.exp2(old - top)
                    total = total + sum_ref[:, columns] * factor
                    weighted = weighted + att_ref[:, columns] * factor
                max_ref[:, columns] = top
                sum_ref[:, columns] = total
                att_ref[:, columns] = weighted

        def earlier(owner):
            @pl.when(owner < me)
            def visit():
                block(owner, False)

        block(me, True)
        for k in range(1, pairs):
            first[k - 1].wait_recv()
            origin = ((pair - k + pairs) % pairs) * 2 + place
            passed = send_to(
                kv_ref.at[origin], kv_ref.at[origin], pass_send.at[k], pass_recv.at[k], partner
            )
            passed.start()
            if k == 1:
                across.wait_recv()
                earlier(me + 1 - 2 * place)
            earlier(origin)

        @pl.loop(1, pairs)
        def arrived(k):
            origin = ((pair - k + pairs) % pairs) * 2 + place
            other = origin + 1 - 2 * place
            send_to(
                kv_ref.at[origin], kv_ref.at[origin], pass_send.at[k], pass_recv.at[k], partner
            ).wait_recv()
            earlier(other)

        att_ref[...] = att_ref[...] / sum_ref[...]
        lse_ref[...] = max_ref[...] + jnp.log2(sum_ref[...])
        low_ref[...] = to_low(lie_down(att_ref, rows, shared_heads))
        for copy in first + [across]:
            copy.wait_send()

        @pl.loop(1, pairs)
        def sent(k):
            origin = ((pair - k + pairs) % pairs) * 2 + place
            send_to(
                kv_ref.at[origin], kv_ref.at[origin], pass_send.at[k], pass_recv.at[k], partner
            ).wait_send()

    return pl.pallas_call(
        kernel,
        out_shape=(
            jax.ShapeDtypeStruct((rows, width), jnp.bfloat16),
            jax.ShapeDtypeStruct((key_width, heads * rows), jnp.float32),
            jax.ShapeDtypeStruct((1, heads * rows), jnp.float32),
            jax.ShapeDtypeStruct((seq_count,) + both.shape, both.dtype),
        ),
        in_specs=[VMEM] * 4,
        out_specs=(VMEM,) * 4,
        scratch_shapes=[
            pltpu.VMEM((key_width, heads * rows), jnp.bfloat16),
            pltpu.VMEM((1, heads * rows), jnp.float32),
            pltpu.VMEM((1, heads * rows), jnp.float32),
        ]
        + [pltpu.SemaphoreType.DMA((pairs,))] * 4,
        compiler_params=talking(number, 24),
        cost_estimate=lasting(12),
        name="attend",
    )(queries, both, key_docs, query_docs)


def attend_back(own, queries, upstream, both_rows, key_docs, query_docs, attended, log_sum):
    rows, width = queries.shape
    total_rows = both_rows.shape[0]
    key_width = both_rows.shape[1] // 2
    shared_heads = key_width // HEAD_DIM
    heads = width // HEAD_DIM
    scale = 0.125 * LOG2E

    def kernel(
        own_ref, q_ref, up_ref, kv_ref, kd_ref, qd_ref, att_ref, lse_ref, qg_ref, kg_ref, vg_ref, qt_ref, ut_ref, acc_ref
    ):
        stand_up(q_ref[...], qt_ref, shared_heads)
        stand_up(up_ref[...], ut_ref, shared_heads)
        me = own_ref[0]
        delta = jnp.sum(ut_ref[...].astype(jnp.float32) * att_ref[...], axis=0, keepdims=True)
        acc_ref[...] = jnp.zeros_like(acc_ref)

        @pl.loop(me + 1, total_rows // rows)
        def later(position):
            begin = pl.multiple_of(position * rows, rows)
            kg_ref[pl.ds(begin, rows), :] = jnp.zeros((rows, key_width), jnp.bfloat16)
            vg_ref[pl.ds(begin, rows), :] = jnp.zeros((rows, key_width), jnp.bfloat16)

        @pl.loop(0, me + 1)
        def block(position):
            begin = pl.multiple_of(position * rows, rows)
            keys = kv_ref[pl.ds(begin, rows), :key_width]
            values = kv_ref[pl.ds(begin, rows), key_width:]
            bias = hidden_bias(kd_ref[pl.ds(begin, rows), :], qd_ref[...], position == me)
            key_grad = jnp.zeros((rows, key_width), jnp.float32)
            value_grad = jnp.zeros((rows, key_width), jnp.float32)
            for head in range(heads):
                columns = slice(head * rows, (head + 1) * rows)
                query = qt_ref[:, columns]
                upper = ut_ref[:, columns]
                probs = jnp.exp2(product(keys, query) * scale + bias - lse_ref[:, columns])
                value_grad = value_grad + over_columns(to_low(probs), upper)
                score_grad = to_low(probs * (product(values, upper) - delta[:, columns]))
                key_grad = key_grad + over_columns(score_grad, query)
                acc_ref[:, columns] += over_rows(keys, score_grad)
            kg_ref[pl.ds(begin, rows), :] = to_low(key_grad * 0.125)
            vg_ref[pl.ds(begin, rows), :] = to_low(value_grad)

        qg_ref[...] = to_low(lie_down(acc_ref, rows, shared_heads) * 0.125)

    return pl.pallas_call(
        kernel,
        out_shape=(
            jax.ShapeDtypeStruct((rows, width), jnp.bfloat16),
            jax.ShapeDtypeStruct((total_rows, key_width), jnp.bfloat16),
            jax.ShapeDtypeStruct((total_rows, key_width), jnp.bfloat16),
        ),
        in_specs=[pl.BlockSpec(memory_space=pltpu.SMEM)] + [VMEM] * 7,
        out_specs=(VMEM,) * 3,
        scratch_shapes=[
            pltpu.VMEM((key_width, heads * rows), jnp.bfloat16),
            pltpu.VMEM((key_width, heads * rows), jnp.bfloat16),
            pltpu.VMEM((key_width, heads * rows), jnp.float32),
        ],
        compiler_params=pltpu.CompilerParams(vmem_limit_bytes=28 * MEBI),
        cost_estimate=lasting(20),
        name="attend_back",
    )(own, queries, upstream, both_rows, key_docs, query_docs, attended, log_sum)


def body(
    tokens_in,
    cotangent,
    document_ids,
    expert_routes,
    norm_mixer,
    mixer_inner,
    mixer_gate,
    conv_taps,
    conv_bias,
    state_proj,
    step_proj,
    step_bias,
    decay_log,
    skip_gain,
    mixer_out,
    norm_ffn,
    ffn_gate,
    ffn_up,
    ffn_down,
    norm_attn,
    attn_query,
    attn_key,
    attn_value,
    attn_output,
    norm_moe,
    router,
    expert_gate,
    expert_up,
    expert_down,
):
    numbers = itertools.count()
    seq_count = lax.axis_size("seq")
    row_count = tokens_in.shape[0]
    total_rows = seq_count * row_count
    first_row = lax.axis_index("seq") * row_count
    last_row = first_row + row_count - 1

    me = lax.axis_index("seq")
    bit_count = seq_count.bit_length() - 1
    across_first = [0] + list(range(1, bit_count))
    along_first = [1, 0] + list(range(2, bit_count))

    def by_owner(values, bits):
        turned = values.transpose(0, 2, 1)
        own_rows = turned.shape[1] // seq_count
        order = [0]
        for bit in reversed(bits):
            order = order + [j + (1 << bit) for j in order]
        blocks = []
        for j in order:
            owner = me
            for bit in range(bit_count):
                if j >> bit & 1:
                    owner = owner + (1 << bit) * (1 - 2 * ((owner >> bit) & 1))
            blocks.append(lax.dynamic_slice_in_dim(turned, owner * own_rows, own_rows, 1))
        parts = []
        while len(blocks) > 1:
            half = len(blocks) // 2
            parts.append(jnp.concatenate(blocks[half:], axis=1) if half > 1 else blocks[half])
            blocks = blocks[:half]
        return parts + blocks, bits

    def begin_sum(*parts):
        flow = prepare_sum(*parts)
        send(flow)
        return flow

    def prepare_sum(*parts):
        flow = {"parts": parts, "bits": parts[0][0][1], "got": []}
        settle(flow)
        return flow

    def send(flow):
        bit = flow["bits"][len(flow["got"])]
        route = [(i, i ^ (1 << bit)) for i in range(seq_count)]
        flow["got"].append(lax.ppermute(flow["out"], "seq", route))

    def bind(values, *flows):
        tied = lax.optimization_barrier((values, *[flow["out"] for flow in flows]))
        for flow, out in zip(flows, tied[1:], strict=True):
            flow["out"] = out
        return tied[0]

    def settle(flow):
        step = len(flow["got"])
        gradients = [
            jnp.einsum(
                "bdt,btf->bdf", rows[0][step], columns, preferred_element_type=jnp.float32
            )
            for rows, columns in flow["parts"]
        ]
        total = gradients[0] if len(gradients) == 1 else jnp.concatenate(gradients, axis=2)
        count = total.shape[1]
        first = count if step < len(flow["bits"]) else 0
        for got in flow["got"]:
            total = total + got[:, first : first + count].astype(jnp.float32)
        if step == len(flow["bits"]):
            flow["total"] = total
            return
        flow["out"] = to_low(total)

    def hold(values, *flows):
        if flows:
            tied = lax.optimization_barrier((values, *[flow["got"][-1] for flow in flows]))
            values = tied[0]
            for flow, got in zip(flows, tied[1:], strict=True):
                flow["got"][-1] = got
        return values

    def after(values, *flows):
        values = hold(values, *flows)
        for flow in flows:
            settle(flow)
            if "total" not in flow:
                send(flow)
        return values

    def finished(flow):
        while "total" not in flow:
            settle(flow)
            if "total" not in flow:
                send(flow)
        return flow["total"]

    def branch_sum(values):
        return head_sum(values, next(numbers), jnp.bfloat16, 4)

    local_docs = lax.dynamic_slice_in_dim(document_ids, first_row, row_count)
    reach = conv_taps.shape[0] - 1
    border = jnp.arange(reach, dtype=jnp.int32)
    docs_before = jnp.take(document_ids, jnp.maximum(first_row - reach + border, 0))
    docs_after = jnp.take(document_ids, jnp.minimum(first_row + row_count + border, total_rows - 1))
    docs_prior = jnp.concatenate([docs_before[reach - 1 :], local_docs[:-1]])
    retain = (local_docs == docs_prior).astype(jnp.float32)
    tokens = tokens_in.astype(jnp.float32)
    gain_mixer = norm_mixer.astype(jnp.float32)
    normed_one = to_low(rms_scale(tokens, gain_mixer))
    conv_in = to_low(product(normed_one, mixer_inner))
    gate_in = product(normed_one, mixer_gate)
    conv_edge = from_behind(conv_in[row_count - reach :], "seq", 1)
    extended = jnp.concatenate([conv_edge, conv_in]).astype(jnp.float32)
    docs_ext = jnp.concatenate([docs_before, local_docs])
    taps = conv_taps.astype(jnp.float32)
    conv_sum = conv_bias.astype(jnp.float32)[None, :]
    masks = []
    for offset in range(reach + 1):
        same_doc = (docs_ext[offset : offset + row_count] == local_docs).astype(jnp.float32)[
            :, None
        ]
        masks.append(same_doc)
        conv_sum = conv_sum + taps[offset] * extended[offset : offset + row_count] * same_doc
    activated = jax.nn.silu(conv_sum)
    act_low = to_low(activated)
    projected = head_sum(product(act_low, state_proj), next(numbers), jnp.float32, 1)
    rank_size = step_proj.shape[0]
    state_size = decay_log.shape[1]
    step_low = to_low(projected[:, :rank_size])
    inject = projected[:, rank_size : rank_size + state_size]
    readout = projected[:, rank_size + state_size :]
    step_pre = product(step_low, step_proj) + step_bias.astype(jnp.float32)
    step_dt = jax.nn.softplus(step_pre)
    decay_rate = jnp.exp(decay_log.astype(jnp.float32)).T
    slopes = -LOG2E * decay_rate
    steps = jnp.where(retain[:, None] > 0.0, step_dt, NEVER)
    drives = step_dt * activated
    inject_wide = spread(inject)
    readout_wide = spread(readout)
    state_in = run_summary(steps, drives, inject_wide, slopes, next(numbers), True)
    scanned, befores, state_out = state_sweep(
        state_in, steps, drives, inject_wide, readout_wide, slopes
    )
    skipping = skip_gain.astype(jnp.float32)
    mixed_state = scanned + skipping * activated
    gate_act = jax.nn.silu(gate_in)
    gated = to_low(mixed_state * gate_act)
    hidden_one = tokens + branch_sum(product(gated, mixer_out))
    gain_ffn = norm_ffn.astype(jnp.float32)
    normed_two = to_low(rms_scale(hidden_one, gain_ffn))
    gate_two = product(normed_two, ffn_gate)
    up_two = product(normed_two, ffn_up)
    ffn_act = to_low(jax.nn.silu(gate_two) * up_two)
    hidden_two = hidden_one + branch_sum(product(ffn_act, ffn_down))
    gain_attn = norm_attn.astype(jnp.float32)
    normed_three = to_low(rms_scale(hidden_two, gain_attn))
    queries = to_low(product(normed_three, attn_query))
    key_rows = to_low(product(normed_three, attn_key))
    value_rows = to_low(product(normed_three, attn_value))
    key_width = key_rows.shape[1]
    own_place = lax.axis_index("seq").reshape(1)
    key_docs = document_ids[:, None]
    query_docs = local_docs[None, :]
    attended_low, attended, log_sum, both_rows = attend(
        queries,
        jnp.concatenate([key_rows, value_rows], axis=1),
        key_docs,
        query_docs,
        next(numbers),
    )
    both_rows = both_rows.reshape(total_rows, -1)
    hidden_three = hidden_two + branch_sum(product(attended_low, attn_output))
    gain_moe = norm_moe.astype(jnp.float32)
    normed_four = to_low(rms_scale(hidden_three, gain_moe))
    logits = product(normed_four, router)
    expert_count = router.shape[1]
    experts = jnp.arange(expert_count, dtype=jnp.int32)
    named = (expert_routes[:, :, None] == experts).astype(jnp.float32)
    gate_weights = jax.nn.softmax(jnp.sum(named * logits[:, None, :], axis=2), axis=1)
    route_flat = expert_routes.reshape(-1)
    pair_count = route_flat.shape[0]
    pair_order = jnp.arange(pair_count, dtype=jnp.int32)
    earlier = (pair_order[None, :] < pair_order[:, None]) & (
        route_flat[None, :] == route_flat[:, None]
    )
    within = jnp.sum(earlier.astype(jnp.int32), axis=1)
    slot_index = (route_flat * CAP + within).reshape(row_count, 2)
    slots = jnp.arange(expert_count * CAP, dtype=jnp.int32)
    first_hit = slot_index[:, 0][None, :] == slots[:, None]
    second_hit = slot_index[:, 1][None, :] == slots[:, None]
    placing = (first_hit | second_hit).astype(jnp.bfloat16)
    slot_gates = jnp.sum(
        jnp.where(first_hit, gate_weights[:, 0][None, :], 0.0)
        + jnp.where(second_hit, gate_weights[:, 1][None, :], 0.0),
        axis=1,
    )
    expert_in = to_low(product(placing, normed_four)).reshape(expert_count, CAP, -1)
    slot_upstream = product(placing, cotangent)
    res_grad = to_low(slot_gates[:, None] * slot_upstream).reshape(expert_count, CAP, -1)
    gate_four = jnp.einsum(
        "ecd,edf->ecf", expert_in, expert_gate, preferred_element_type=jnp.float32
    )
    up_four = jnp.einsum("ecd,edf->ecf", expert_in, expert_up, preferred_element_type=jnp.float32)
    expert_act = to_low(jax.nn.silu(gate_four) * up_four)
    expert_res = jnp.einsum(
        "ecf,efd->ecd", expert_act, expert_down, preferred_element_type=jnp.float32
    ).reshape(expert_count * CAP, -1)
    upstream = cotangent.astype(jnp.float32)
    slot_dots = jnp.sum(expert_res * slot_upstream, axis=1)
    dots_part = jnp.stack(
        [
            jnp.sum(jnp.where(first_hit, slot_dots[:, None], 0.0), axis=0),
            jnp.sum(jnp.where(second_hit, slot_dots[:, None], 0.0), axis=0),
        ],
        axis=1,
    )
    combined = product(placing.T, to_low(slot_gates[:, None] * expert_res))
    act_back = to_low(
        jnp.einsum("ecd,efd->ecf", res_grad, expert_down, preferred_element_type=jnp.float32)
    ).astype(jnp.float32)
    gating_grad = to_low(act_back * up_four * silu_slope(gate_four))
    upward_grad = to_low(act_back * jax.nn.silu(gate_four))
    flow_expert_down = begin_sum((by_owner(res_grad, along_first), expert_act))
    expert_rows = by_owner(expert_in, across_first)
    flow_expert_in = begin_sum(
        (expert_rows, jnp.concatenate([gating_grad, upward_grad], axis=2))
    )
    slot_grads = (
        jnp.einsum("ecf,edf->ecd", gating_grad, expert_gate, preferred_element_type=jnp.float32)
        + jnp.einsum("ecf,edf->ecd", upward_grad, expert_up, preferred_element_type=jnp.float32)
    ).reshape(expert_count * CAP, -1)
    token_part = product(placing.T, to_low(slot_grads))
    model_width = tokens.shape[1]
    expert_sums = branch_sum(
        jnp.concatenate(
            [token_part, jnp.pad(dots_part, ((0, 0), (0, LANES - 2)))], axis=1
        )
    )
    normed_grad = expert_sums[:, :model_width]
    dots = expert_sums[:, model_width : model_width + 2]
    chosen_grad = gate_weights * (dots - jnp.sum(gate_weights * dots, axis=1, keepdims=True))
    logit_grad = jnp.sum(named * chosen_grad[:, :, None], axis=1)
    grad_router = exact_product(normed_four.astype(jnp.float32).T, logit_grad)
    normed_grad = normed_grad + exact_product(logit_grad, router.astype(jnp.float32).T)
    hidden_grad, grad_norm_moe = rms_back(hidden_three, gain_moe, normed_grad)
    three_grad = upstream + hidden_grad
    branch_grad = to_low(three_grad)
    attn_out_rows = by_owner(branch_grad[None], across_first)
    attended_grad = to_low(product(branch_grad, attn_output.T))
    query_grad, key_part, value_part = attend_back(
        own_place, queries, attended_grad, both_rows, key_docs, query_docs, attended, log_sum
    )
    key_part = hold(key_part, flow_expert_down, flow_expert_in)
    key_sum, value_sum, combined_sum = scatter_and_head_sum(
        [key_part, value_part], combined, next(numbers)
    )
    mixed_out = to_low(hidden_three + combined_sum)
    key_sum, attended_late = lax.optimization_barrier((key_sum, attended_low))
    key_sum = after(key_sum, flow_expert_down, flow_expert_in)
    key_grad = to_low(key_sum)
    value_grad = to_low(value_sum)
    flow_attn = begin_sum(
        (
            by_owner(normed_three[None], across_first),
            jnp.concatenate([query_grad, key_grad, value_grad], axis=1)[None],
        ),
        (attn_out_rows, attended_late[None]),
    )
    normed_part = (
        product(query_grad, attn_query.T)
        + product(key_grad, attn_key.T)
        + product(value_grad, attn_value.T)
    )
    normed_grad = branch_sum(normed_part)
    hidden_grad, grad_norm_attn = rms_back(hidden_two, gain_attn, normed_grad)
    two_grad = three_grad + hidden_grad
    branch_grad = to_low(two_grad)
    flow_ffn_down = begin_sum((by_owner(branch_grad[None], along_first), ffn_act[None]))
    ffn_back = to_low(product(branch_grad, ffn_down.T))
    ffn_back = after(ffn_back, flow_expert_down, flow_expert_in, flow_attn).astype(jnp.float32)
    feed_gate_grad = to_low(ffn_back * up_two * silu_slope(gate_two))
    feed_up_grad = to_low(ffn_back * jax.nn.silu(gate_two))
    feed_rows = by_owner(normed_two[None], across_first)
    flow_ffn_gate = begin_sum((feed_rows, feed_gate_grad[None]))
    normed_part = product(feed_gate_grad, ffn_gate.T) + product(feed_up_grad, ffn_up.T)
    normed_grad = branch_sum(normed_part)
    hidden_grad, grad_norm_ffn = rms_back(hidden_one, gain_ffn, normed_grad)
    one_grad = two_grad + hidden_grad
    branch_grad = to_low(one_grad)
    mixer_out_rows = by_owner(branch_grad[None], across_first)
    gated_grad = to_low(product(branch_grad, mixer_out.T)).astype(jnp.float32)
    scan_grad = gated_grad * gate_act
    gate_in_grad = to_low(gated_grad * mixed_state * silu_slope(gate_in))
    grad_skip_gain = jnp.sum(scan_grad * activated, axis=0)
    early_flows = (flow_expert_down, flow_expert_in, flow_attn, flow_ffn_down, flow_ffn_gate)
    flow_ffn_up = prepare_sum((feed_rows, feed_up_grad[None]))
    flow_mixer_gate = prepare_sum((by_owner(normed_one[None], along_first), gate_in_grad[None]))
    flow_mixer_out = prepare_sum((mixer_out_rows, gated[None]))
    late_flows = (flow_ffn_up, flow_mixer_gate, flow_mixer_out)
    scan_grad = bind(scan_grad, *late_flows)
    scan_grad = hold(scan_grad, *early_flows)
    state_after = run_summary(steps, scan_grad, readout_wide, slopes, next(numbers), False)
    state_after = bind(state_after, *late_flows)
    state_after = after(state_after, flow_attn, flow_ffn_gate)
    send(flow_ffn_up)
    send(flow_mixer_gate)
    through_sum, injected, inject_part, readout_part, rate_sum = adjoint_sweep(
        state_after,
        state_out,
        befores,
        steps,
        drives,
        inject_wide,
        readout_wide,
        scan_grad,
        slopes,
    )
    step_grad = LN2 * through_sum + activated * injected
    input_grad = step_dt * injected
    inject_grad = jnp.sum(inject_part, axis=2)
    readout_grad = jnp.sum(readout_part, axis=2)
    grad_decay_log = -rate_sum * decay_rate
    pre_grad = step_grad * jax.nn.sigmoid(step_pre)
    grad_step_bias = jnp.sum(pre_grad, axis=0)
    pre_low = to_low(pre_grad)
    pre_low = bind(pre_low, flow_mixer_out)
    pre_low = after(pre_low, flow_ffn_up, flow_ffn_gate, flow_ffn_down, flow_attn)
    send(flow_mixer_out)
    grad_step_proj = product(pre_low.T, step_low)
    proj_part = jnp.concatenate([product(pre_low, step_proj.T), inject_grad, readout_grad], axis=1)
    proj_low = to_low(head_sum(proj_part, next(numbers), jnp.float32, 1))
    proj_low = after(proj_low, flow_mixer_gate, flow_ffn_down)
    grad_state_proj = product(act_low.T, proj_low)
    act_total = input_grad + skipping * scan_grad + product(proj_low, state_proj.T)
    conv_grad = act_total * silu_slope(conv_sum)
    conv_grad = after(conv_grad, flow_ffn_up, flow_mixer_out, flow_ffn_gate)
    grad_conv_bias = jnp.sum(conv_grad, axis=0)
    after_edge = from_behind(conv_grad[:reach], "seq", -1)
    after_edge = after(after_edge, flow_mixer_gate, flow_ffn_down)
    grad_ext = jnp.concatenate([conv_grad, after_edge])
    docs_next = jnp.concatenate([local_docs, docs_after])
    conv_in_grad = jnp.zeros_like(conv_grad)
    tap_rows = []
    for offset in range(reach + 1):
        tap_rows.append(
            jnp.sum(conv_grad * extended[offset : offset + row_count] * masks[offset], axis=0)
        )
        lead = reach - offset
        same_next = (docs_next[lead : lead + row_count] == local_docs).astype(jnp.float32)[:, None]
        conv_in_grad = conv_in_grad + taps[offset] * grad_ext[lead : lead + row_count] * same_next
    grad_conv_taps = jnp.stack(tap_rows)
    conv_low = to_low(conv_in_grad)
    inner_half = conv_low.shape[1] // 2
    grad_mixer_inner = to_low(product(normed_one.T, conv_low))
    normed_part = product(conv_low, mixer_inner.T) + product(gate_in_grad, mixer_gate.T)
    own_channels = grad_conv_bias.shape[0] // seq_count

    def cut(values):
        return values.reshape(seq_count, -1)

    channel_rows = jnp.concatenate(
        [grad_state_proj, jnp.pad(grad_step_proj, ((0, 0), (0, LANES - rank_size)))], axis=1
    )
    packed = jnp.concatenate(
        [
            cut(grad_decay_log.T),
            cut(grad_norm_ffn),
            cut(grad_norm_attn),
            cut(grad_norm_moe),
            cut(grad_router),
            cut(grad_conv_taps.T),
            cut(grad_conv_bias),
            cut(grad_step_bias),
            cut(grad_skip_gain),
        ],
        axis=1,
    )
    spare = -packed.shape[1] % (16 * LANES)
    packed = to_low(jnp.pad(packed, ((0, 0), (0, spare)))).reshape(-1, LANES)
    packed = after(packed, flow_mixer_out)
    first_inner, second_inner, sum_rows, sum_packed, grad_tokens, grad_norm_mixer = last_sums(
        [
            grad_mixer_inner[:, :inner_half],
            grad_mixer_inner[:, inner_half:],
            to_low(channel_rows),
            packed,
        ],
        normed_part,
        tokens_in,
        gain_mixer[None, :],
        one_grad,
        next(numbers),
    )
    sum_attn = finished(flow_attn)[0]
    sum_expert_in = finished(flow_expert_in)
    expert_width = expert_gate.shape[2]
    sum_packed = sum_packed.reshape(-1)
    own_rows = model_width // seq_count
    taken = itertools.accumulate(
        [0, own_channels * state_size]
        + [own_rows] * 3
        + [own_rows * expert_count, own_channels * (reach + 1)]
        + [own_channels] * 3
    )
    bounds = list(taken)
    pieces = [sum_packed[low:high] for low, high in itertools.pairwise(bounds)]
    query_width = attn_query.shape[1]

    return (
        mixed_out,
        grad_tokens,
        lax.dynamic_slice_in_dim(grad_norm_mixer[0], me * own_rows, own_rows),
        jnp.concatenate([first_inner, second_inner], axis=1),
        finished(flow_mixer_gate)[0],
        pieces[5].reshape(own_channels, -1).T,
        pieces[6],
        sum_rows[:, :LANES],
        sum_rows[:, LANES : LANES + rank_size].T,
        pieces[7],
        pieces[0].reshape(own_channels, -1),
        pieces[8],
        finished(flow_mixer_out)[0].T,
        pieces[1],
        finished(flow_ffn_gate)[0],
        finished(flow_ffn_up)[0],
        finished(flow_ffn_down)[0].T,
        pieces[2],
        sum_attn[:, :query_width],
        sum_attn[:, query_width : query_width + key_width],
        sum_attn[:, query_width + key_width : query_width + 2 * key_width],
        sum_attn[:, query_width + 2 * key_width :].T,
        pieces[3],
        pieces[4].reshape(own_rows, -1),
        sum_expert_in[:, :, :expert_width],
        sum_expert_in[:, :, expert_width:],
        finished(flow_expert_down).transpose(0, 2, 1),
    )


def solution(mesh):
    in_specs = (
        P("seq", None),
        P("seq", None),
        P(),
        P("seq", None),
        P(),
        P(None, "head"),
        P(None, "head"),
        P(None, "head"),
        P("head"),
        P("head", None),
        P(None, "head"),
        P("head"),
        P("head", None),
        P("head"),
        P("head", None),
        P(),
        P(None, "head"),
        P(None, "head"),
        P("head", None),
        P(),
        P(None, "head"),
        P(None, "head"),
        P(None, "head"),
        P("head", None),
        P(),
        P(),
        P(None, None, "head"),
        P(None, None, "head"),
        P(None, "head", None),
    )
    out_specs = (
        P("seq", None),
        P("seq", None),
        P("seq"),
        P("seq", "head"),
        P("seq", "head"),
        P(None, ("head", "seq")),
        P(("head", "seq")),
        P(("head", "seq"), None),
        P(None, ("head", "seq")),
        P(("head", "seq")),
        P(("head", "seq"), None),
        P(("head", "seq")),
        P("head", "seq"),
        P("seq"),
        P("seq", "head"),
        P("seq", "head"),
        P("head", "seq"),
        P("seq"),
        P("seq", "head"),
        P("seq", "head"),
        P("seq", "head"),
        P("head", "seq"),
        P("seq"),
        P("seq", None),
        P(None, "seq", "head"),
        P(None, "seq", "head"),
        P(None, "head", "seq"),
    )
    return jax.shard_map(body, mesh=mesh, in_specs=in_specs, out_specs=out_specs, check_vma=False)
```

```python
import itertools
import math

import jax
import jax.numpy as jnp
from jax import lax
from jax.experimental import pallas as pl
from jax.experimental.pallas import tpu as pltpu
from jax.sharding import PartitionSpec as P

HEAD_DIM = 64
CAP = 160
LANES = 128
LOG2E = 1.4426950408889634
LN2 = 0.6931471805599453
NEVER = 1e30
MEBI = 1024 * 1024
MESH = pl.DeviceIdType.MESH
VMEM = pl.BlockSpec(memory_space=pltpu.VMEM)
ANY = pl.BlockSpec(memory_space=pl.ANY)


highest = lax.Precision.HIGHEST
epsilon = 1e-05
masked_score = -1e30


def from_behind(block, axis, distance):
    devices = range(lax.axis_size(axis))
    route = [(i - distance, i) for i in devices if i - distance in devices]
    return lax.ppermute(block, axis, route)


def to_low(values):
    return values.astype(jnp.bfloat16)


def product(left, right):
    return jnp.dot(left, right, preferred_element_type=jnp.float32)


def exact_product(left, right):
    return jnp.dot(left, right, precision=highest, preferred_element_type=jnp.float32)


def rms_scale(values, gain):
    return values * lax.rsqrt(jnp.mean(values * values, axis=-1, keepdims=True) + epsilon) * gain


def rms_back(values, gain, upstream):
    unused, pullback = jax.vjp(rms_scale, values, gain)
    return pullback(upstream)


def silu_slope(values):
    logistic = jax.nn.sigmoid(values)
    return logistic * (1.0 + values * (1.0 - logistic))


def meet(peers):
    barrier = pltpu.get_barrier_semaphore()
    for peer in peers:
        pl.semaphore_signal(barrier, inc=1, device_id=peer, device_id_type=MESH)
    pl.semaphore_wait(barrier, len(peers))


def send_to(source, target, send_sem, recv_sem, peer):
    return pltpu.make_async_remote_copy(
        src_ref=source,
        dst_ref=target,
        send_sem=send_sem,
        recv_sem=recv_sem,
        device_id=peer,
        device_id_type=MESH,
    )


def lasting(microseconds):
    return pl.CostEstimate(
        flops=int(microseconds * 1e3),
        bytes_accessed=int(microseconds * 1e3),
        transcendentals=0,
    )


def talking(number, mebibytes):
    return pltpu.CompilerParams(
        collective_id=number, has_side_effects=True, vmem_limit_bytes=mebibytes * MEBI
    )


def together(*jobs):
    waiting = list(jobs)
    while waiting:
        for job in list(waiting):
            if next(job, waiting) is waiting:
                waiting.remove(job)


def head_peers():
    seq = lax.axis_index("seq")
    head = lax.axis_index("head")
    return [(seq, head + 1 - 2 * (head % 2)), (seq, (head + 2) % 4)]


def head_scratch(rows, width, wire, pieces):
    return [pltpu.VMEM((rows // 2, width), wire)] * 4 + [
        pltpu.SemaphoreType.DMA((3, pieces)),
        pltpu.SemaphoreType.DMA((3, pieces)),
    ]


def head_job(x_ref, o_ref, scratch, wire, pieces):
    near_out, near_in, far_out, far_in, send, recv = scratch
    half = x_ref.shape[0] // 2
    step = half // pieces
    near, far = head_peers()
    core = lax.axis_index("head") % 2

    def rows_of(side, piece):
        return pl.ds(pl.multiple_of(side * half + piece * step, 8), step)

    first, second, third = [], [], []
    for piece in range(pieces):
        local = pl.ds(piece * step, step)
        near_out[local] = x_ref[rows_of(1 - core, piece)].astype(wire)
        first.append(
            send_to(
                near_out.at[local], near_in.at[local], send.at[0, piece], recv.at[0, piece], near
            )
        )
        first[-1].start()
    yield
    for piece in range(pieces):
        local = pl.ds(piece * step, step)
        first[piece].wait_recv()
        total = x_ref[rows_of(core, piece)] + near_in[local].astype(jnp.float32)
        far_out[local] = total.astype(wire)
        second.append(
            send_to(far_out.at[local], far_in.at[local], send.at[1, piece], recv.at[1, piece], far)
        )
        second[-1].start()
    yield
    for piece in range(pieces):
        local = pl.ds(piece * step, step)
        second[piece].wait_recv()
        whole = far_out[local].astype(jnp.float32) + far_in[local].astype(jnp.float32)
        o_ref[rows_of(core, piece)] = whole
        third.append(
            send_to(
                o_ref.at[rows_of(core, piece)],
                o_ref.at[rows_of(core, piece)],
                send.at[2, piece],
                recv.at[2, piece],
                near,
            )
        )
        third[-1].start()
    yield
    for copy in third:
        copy.wait_recv()
    for copy in first + second + third:
        copy.wait_send()


def head_sum(values, number, wire, pieces):
    rows, width = values.shape

    def kernel(x_ref, o_ref, *scratch):
        meet(head_peers())
        together(head_job(x_ref, o_ref, scratch, wire, pieces))

    return pl.pallas_call(
        kernel,
        out_shape=jax.ShapeDtypeStruct((rows, width), jnp.float32),
        in_specs=[VMEM],
        out_specs=VMEM,
        scratch_shapes=head_scratch(rows, width, wire, pieces),
        compiler_params=talking(number, 10),
        cost_estimate=lasting(6 + values.size // 40000),
        name="head_sum",
    )(values)


def pair_peers():
    seq = lax.axis_index("seq")
    head = lax.axis_index("head")
    pairs = lax.axis_size("seq") // 2
    place = seq % 2
    pair = seq // 2
    others = [(((pair + k) % pairs) * 2 + place, head) for k in range(1, pairs)]
    return [(seq + 1 - 2 * place, head)] + others


def scatter_shapes(arrays):
    seq_count = lax.axis_size("seq")
    return [(a.shape[0] // seq_count, a.shape[1]) for a in arrays]


def scatter_blocks(arrays):
    pairs = lax.axis_size("seq") // 2
    return [
        a.reshape(pairs, 2, shape[0], shape[1])
        for a, shape in zip(arrays, scatter_shapes(arrays), strict=True)
    ]


def scatter_scratch(shapes):
    pairs = lax.axis_size("seq") // 2
    count = len(shapes)
    return (
        [pltpu.VMEM((pairs,) + shape, jnp.bfloat16) for shape in shapes] * 2
        + [pltpu.VMEM((pairs - 1,) + shape, jnp.bfloat16) for shape in shapes]
        + [pltpu.SemaphoreType.DMA((count,))] * 3
        + [pltpu.SemaphoreType.DMA((count, pairs - 1))] * 2
    )


def scatter_job(takes, gives, scratch, shapes):
    count = len(takes)
    pairs = lax.axis_size("seq") // 2
    own, near, far = scratch[:count], scratch[count : 2 * count], scratch[2 * count : 3 * count]
    own_sem, near_send, near_recv, far_send, far_recv = scratch[3 * count :]
    seq = lax.axis_index("seq")
    place = seq % 2
    pair = seq // 2
    partner, *others = pair_peers()
    owners = [(pair + k) % pairs for k in range(1, pairs)]
    loads = [
        pltpu.make_async_copy(takes[i].at[:, place], own[i], own_sem.at[i]) for i in range(count)
    ]
    halves = [
        send_to(takes[i].at[:, 1 - place], near[i], near_send.at[i], near_recv.at[i], partner)
        for i in range(count)
    ]

    def launch(i):
        if i < count:
            halves[i].start()
            loads[i].start()

    sums = []

    def finish(i):
        for copy in sums[i]:
            copy.wait_recv()

        @pl.loop(0, shapes[i][0] // 16)
        def add(step):
            part = pl.ds(pl.multiple_of(step * 16, 16), 16)
            total = own[i][pair, part].astype(jnp.float32)
            for k in range(pairs - 1):
                total = total + far[i][k, part].astype(jnp.float32)
            gives[i][part] = total

    launch(0)
    launch(1)
    for i in range(count):
        yield
        halves[i].wait_recv()
        loads[i].wait()
        launch(i + 2)

        @pl.loop(0, pairs)
        def merge(block):
            @pl.loop(0, shapes[i][0] // 16)
            def add(step):
                part = pl.ds(pl.multiple_of(step * 16, 16), 16)
                total = own[i][block, part].astype(jnp.float32) + near[i][block, part].astype(
                    jnp.float32
                )
                own[i][block, part] = total.astype(jnp.bfloat16)

        sums.append(
            [
                send_to(
                    own[i].at[owners[k]],
                    far[i].at[k],
                    far_send.at[i, k],
                    far_recv.at[i, k],
                    others[k],
                )
                for k in range(pairs - 1)
            ]
        )
        for copy in sums[i]:
            copy.start()
        if i > 0:
            finish(i - 1)
    yield
    finish(count - 1)
    for copy in halves:
        copy.wait_send()
    for group in sums:
        for copy in group:
            copy.wait_send()


def scatter_and_head_sum(arrays, values, number):
    count = len(arrays)
    shapes = scatter_shapes(arrays)
    rows, width = values.shape
    spaces = scatter_scratch(shapes)

    def kernel(*refs):
        takes, x_ref = refs[:count], refs[count]
        gives, o_ref = refs[count + 1 : 2 * count + 1], refs[2 * count + 1]
        scratch = refs[2 * count + 2 :]
        meet(pair_peers() + head_peers())
        together(
            scatter_job(takes, gives, scratch[: len(spaces)], shapes),
            head_job(x_ref, o_ref, scratch[len(spaces) :], jnp.bfloat16, 4),
        )

    return pl.pallas_call(
        kernel,
        out_shape=[jax.ShapeDtypeStruct(shape, jnp.float32) for shape in shapes]
        + [jax.ShapeDtypeStruct((rows, width), jnp.float32)],
        in_specs=[ANY] * count + [VMEM],
        out_specs=[VMEM] * (count + 1),
        scratch_shapes=spaces + head_scratch(rows, width, jnp.bfloat16, 4),
        compiler_params=talking(number, 24),
        cost_estimate=lasting(20),
        name="scatter_and_head_sum",
    )(*scatter_blocks(arrays), values)


def last_sums(arrays, values, tokens, gain, upstream, number):
    count = len(arrays)
    shapes = scatter_shapes(arrays)
    rows, width = values.shape
    seq_count = lax.axis_size("seq")
    spaces = scatter_scratch(shapes)
    step = 16

    def kernel(*refs):
        takes = refs[:count]
        x_ref, token_ref, gain_ref, up_ref = refs[count : count + 4]
        gives = refs[count + 4 : 2 * count + 4]
        grad_ref, gain_out = refs[2 * count + 4 : 2 * count + 6]
        scratch = refs[2 * count + 6 :]
        total_ref, part_out, part_in, part_send, part_recv = scratch[-5:]
        seq = lax.axis_index("seq")
        head = lax.axis_index("head")
        peers = [((seq + k) % seq_count, head) for k in range(1, seq_count)]
        meet(peers + head_peers())

        def norm_job():
            yield from head_job(x_ref, total_ref, scratch[len(spaces) : -5], jnp.bfloat16, 4)

            def back(position, gained):
                part = pl.ds(pl.multiple_of(position * step, step), step)
                token = token_ref[part].astype(jnp.float32)
                scale = lax.rsqrt(jnp.mean(token * token, axis=1, keepdims=True) + epsilon)
                unit = token * scale
                given = total_ref[part]
                scaled = given * gain_ref[...]
                pull = jnp.mean(scaled * unit, axis=1, keepdims=True)
                grad_ref[part] = up_ref[part] + scale * (scaled - unit * pull)
                product_rows = given * unit
                return gained + product_rows[:8] + product_rows[8:]

            gained = lax.fori_loop(0, rows // step, back, jnp.zeros((8, width), jnp.float32))
            part_out[...] = jnp.sum(gained, axis=0, keepdims=True)
            copies = [
                send_to(part_out, part_in.at[k], part_send.at[k], part_recv.at[k], peers[k])
                for k in range(seq_count - 1)
            ]
            for copy in copies:
                copy.start()
            yield
            for copy in copies:
                copy.wait_recv()
            whole = part_out[...]
            for k in range(seq_count - 1):
                whole = whole + part_in[k]
            gain_out[...] = whole
            for copy in copies:
                copy.wait_send()

        together(norm_job(), scatter_job(takes, gives, scratch[: len(spaces)], shapes))

    return pl.pallas_call(
        kernel,
        out_shape=[jax.ShapeDtypeStruct(shape, jnp.float32) for shape in shapes]
        + [
            jax.ShapeDtypeStruct((rows, width), jnp.float32),
            jax.ShapeDtypeStruct((1, width), jnp.float32),
        ],
        in_specs=[ANY] * count + [VMEM] * 4,
        out_specs=[VMEM] * (count + 2),
        scratch_shapes=spaces
        + head_scratch(rows, width, jnp.bfloat16, 4)
        + [
            pltpu.VMEM((rows, width), jnp.float32),
            pltpu.VMEM((1, width), jnp.float32),
            pltpu.VMEM((seq_count - 1, 1, width), jnp.float32),
            pltpu.SemaphoreType.DMA((seq_count - 1,)),
            pltpu.SemaphoreType.DMA((seq_count - 1,)),
        ],
        compiler_params=talking(number, 28),
        cost_estimate=lasting(20),
        name="last_sums",
    )(*scatter_blocks(arrays), values, tokens, gain, upstream)


def widen(column_block, width):
    return jnp.concatenate([column_block] * (width // LANES), axis=-1)


def narrow(wide):
    width = wide.shape[-1]
    total = wide[:, :LANES]
    for place in range(1, width // LANES):
        total = total + wide[:, place * LANES : (place + 1) * LANES]
    return total


def spread(columns):
    return jnp.broadcast_to(columns[:, :, None], columns.shape + (LANES,))


def run_summary(steps, drives, coefficients, slopes, number, forward):
    rows, width = steps.shape
    entries = slopes.shape[0]
    seq_count = lax.axis_size("seq")
    group = math.gcd(rows, 8)

    def kernel(
        step_ref,
        drive_ref,
        coef_ref,
        slope_ref,
        o_ref,
        outgoing,
        incoming,
        span_out,
        span_in,
        send,
        recv,
    ):
        seq = lax.axis_index("seq")
        head = lax.axis_index("head")
        peers = [((seq + k) % seq_count, head) for k in range(1, seq_count)]
        meet(peers)
        slope = slope_ref[...]
        span_out[...] = jnp.broadcast_to(
            jnp.sum(step_ref[...], axis=0, keepdims=True), span_out.shape
        )
        spans = [
            send_to(span_out, span_in.at[k], send.at[1, k], recv.at[1, k], peers[k])
            for k in range(seq_count - 1)
        ]
        for copy in spans:
            copy.start()

        def advance(position, state):
            for offset in range(group):
                t = position * group + offset
                t = t if forward else rows - 1 - t
                decays = jnp.exp2(step_ref[pl.ds(t, 1), :] * slope)
                drive = drive_ref[pl.ds(t, 1), :] * widen(coef_ref[t], width)
                state = state * decays + drive if forward else (state + drive) * decays
            return state

        state = lax.fori_loop(0, rows // group, advance, jnp.zeros((entries, width), jnp.float32))
        outgoing[...] = state.astype(jnp.bfloat16)
        copies = [
            send_to(outgoing, incoming.at[k], send.at[0, k], recv.at[0, k], peers[k])
            for k in range(seq_count - 1)
        ]
        for copy in copies:
            copy.start()
        for copy in spans:
            copy.wait_recv()
        for copy in copies:
            copy.wait_recv()
        carried = jnp.zeros((entries, width), jnp.float32)
        order = range(seq_count - 1, 0, -1) if forward else range(1, seq_count)
        for k in order:
            known = seq - k >= 0 if forward else seq - k < 0
            whole = jnp.exp2(span_in[k - 1][:1] * slope)
            carried = jnp.where(known, whole * carried + incoming[k - 1].astype(jnp.float32), 0.0)
        o_ref[...] = carried
        for copy in copies + spans:
            copy.wait_send()

    return pl.pallas_call(
        kernel,
        out_shape=jax.ShapeDtypeStruct((entries, width), jnp.float32),
        in_specs=[VMEM] * 4,
        out_specs=VMEM,
        scratch_shapes=[
            pltpu.VMEM((entries, width), jnp.bfloat16),
            pltpu.VMEM((seq_count - 1, entries, width), jnp.bfloat16),
            pltpu.VMEM((8, width), jnp.float32),
            pltpu.VMEM((seq_count - 1, 8, width), jnp.float32),
            pltpu.SemaphoreType.DMA((2, seq_count - 1)),
            pltpu.SemaphoreType.DMA((2, seq_count - 1)),
        ],
        compiler_params=talking(number, 10),
        cost_estimate=lasting(16),
        name="run_summary",
    )(steps, drives, coefficients, slopes)


def state_sweep(initial, steps, drives, inject, readout, slopes):
    rows, width = steps.shape
    entries = slopes.shape[0]
    length = math.gcd(rows, 32)
    group = math.gcd(length, 8)

    def kernel(
        init_ref, step_ref, drive_ref, inject_ref, read_ref, slope_ref, y_ref, before_ref, end_ref
    ):
        @pl.when(pl.program_id(0) == 0)
        def begin():
            end_ref[...] = init_ref[...]

        slope = slope_ref[...]

        def advance(position, state):
            for offset in range(group):
                t = position * group + offset
                before_ref[t] = state
                decays = jnp.exp2(step_ref[pl.ds(t, 1), :] * slope)
                drive = drive_ref[pl.ds(t, 1), :] * widen(inject_ref[t], width)
                state = state * decays + drive
                y_ref[pl.ds(t, 1), :] = jnp.sum(
                    state * widen(read_ref[t], width), axis=0, keepdims=True
                )
            return state

        end_ref[...] = lax.fori_loop(0, length // group, advance, end_ref[...])

    row_spec = pl.BlockSpec((length, width), lambda i: (i, 0))
    entry_spec = pl.BlockSpec((length, entries, LANES), lambda i: (i, 0, 0))
    fixed = pl.BlockSpec((entries, width), lambda i: (0, 0))
    return pl.pallas_call(
        kernel,
        grid=(rows // length,),
        out_shape=(
            jax.ShapeDtypeStruct((rows, width), jnp.float32),
            pltpu.HBM((rows, entries, width), jnp.float32),
            jax.ShapeDtypeStruct((entries, width), jnp.float32),
        ),
        in_specs=[fixed, row_spec, row_spec, entry_spec, entry_spec, fixed],
        out_specs=(
            row_spec,
            pl.BlockSpec((length, entries, width), lambda i: (i, 0, 0)),
            fixed,
        ),
        compiler_params=pltpu.CompilerParams(vmem_limit_bytes=12 * MEBI),
        cost_estimate=lasting(11),
        name="state_sweep",
    )(initial, steps, drives, inject, readout, slopes)


def adjoint_sweep(incoming, last_state, befores, steps, drives, inject, readout, upstream, slopes):
    rows, width = steps.shape
    entries = slopes.shape[0]
    length = math.gcd(rows, 32)
    group = math.gcd(length, 8)
    blocks = rows // length

    def kernel(
        in_ref,
        last_ref,
        before_ref,
        step_ref,
        drive_ref,
        inject_ref,
        read_ref,
        up_ref,
        slope_ref,
        through_ref,
        injected_ref,
        inject_out,
        read_out,
        rate_ref,
        adjoint_ref,
        state_ref,
    ):
        @pl.when(pl.program_id(0) == 0)
        def begin():
            adjoint_ref[...] = in_ref[...]
            state_ref[...] = last_ref[...]
            rate_ref[...] = jnp.zeros_like(rate_ref)

        slope = slope_ref[...]

        def retreat(position, carried):
            adjoint_in, rate = carried
            for offset in range(group):
                t = length - 1 - (position * group + offset)
                upper = up_ref[pl.ds(t, 1), :]
                step = step_ref[pl.ds(t, 1), :]
                adjoint = widen(read_ref[t], width) * upper + adjoint_in
                state = state_ref[...] if offset == 0 else before_ref[t + 1]
                read_out[t] = narrow(upper * state)
                adjoint_in = jnp.exp2(step * slope) * adjoint
                before = before_ref[t]
                through = adjoint_in * before
                rate = rate + through * step
                through_ref[pl.ds(t, 1), :] = jnp.sum(through * slope, axis=0, keepdims=True)
                injected_ref[pl.ds(t, 1), :] = jnp.sum(
                    adjoint * widen(inject_ref[t], width), axis=0, keepdims=True
                )
                inject_out[t] = narrow(adjoint * drive_ref[pl.ds(t, 1), :])
            state_ref[...] = before_ref[length - (position + 1) * group]
            return (adjoint_in, rate)

        adjoint_end, rate_end = lax.fori_loop(
            0, length // group, retreat, (adjoint_ref[...], rate_ref[...])
        )
        adjoint_ref[...] = adjoint_end
        rate_ref[...] = rate_end

    row_spec = pl.BlockSpec((length, width), lambda i: (blocks - 1 - i, 0))
    entry_spec = pl.BlockSpec((length, entries, LANES), lambda i: (blocks - 1 - i, 0, 0))
    fixed = pl.BlockSpec((entries, width), lambda i: (0, 0))
    wide = jax.ShapeDtypeStruct((rows, width), jnp.float32)
    partial = jax.ShapeDtypeStruct((rows, entries, LANES), jnp.float32)
    return pl.pallas_call(
        kernel,
        grid=(blocks,),
        out_shape=(
            wide,
            wide,
            partial,
            partial,
            jax.ShapeDtypeStruct((entries, width), jnp.float32),
        ),
        in_specs=[
            fixed,
            fixed,
            pl.BlockSpec((length, entries, width), lambda i: (blocks - 1 - i, 0, 0)),
            row_spec,
            row_spec,
            entry_spec,
            entry_spec,
            row_spec,
            fixed,
        ],
        out_specs=(row_spec, row_spec, entry_spec, entry_spec, fixed),
        scratch_shapes=[pltpu.VMEM((entries, width), jnp.float32)] * 2,
        compiler_params=pltpu.CompilerParams(vmem_limit_bytes=14 * MEBI),
        cost_estimate=lasting(15),
        name="adjoint_sweep",
    )(
        incoming,
        last_state,
        pltpu.with_memory_space_constraint(befores, pltpu.HBM),
        steps,
        drives,
        inject,
        readout,
        upstream,
        slopes,
    )


def over_rows(left, right):
    return lax.dot_general(left, right, (((0,), (0,)), ((), ())), preferred_element_type=jnp.float32)


def over_columns(left, right):
    return lax.dot_general(left, right, (((1,), (1,)), ((), ())), preferred_element_type=jnp.float32)


def stand_up(rows, target, shared_heads):
    count, width = rows.shape
    heads = width // HEAD_DIM
    group = heads // shared_heads
    turned = rows.astype(jnp.float32).T.astype(target.dtype)
    target[...] = jnp.zeros_like(target)
    for head in range(heads):
        shared = head // group
        target[shared * HEAD_DIM : (shared + 1) * HEAD_DIM, head * count : (head + 1) * count] = (
            turned[head * HEAD_DIM : (head + 1) * HEAD_DIM]
        )


def lie_down(upright, count, shared_heads):
    heads = upright.shape[1] // count
    group = heads // shared_heads
    blocks = []
    for head in range(heads):
        shared = head // group
        blocks.append(
            upright[
                shared * HEAD_DIM : (shared + 1) * HEAD_DIM, head * count : (head + 1) * count
            ]
        )
    return jnp.concatenate(blocks, axis=0).T


def hidden_bias(key_docs, query_docs, diagonal):
    key_count, query_count = key_docs.shape[0], query_docs.shape[1]
    shape = (key_count, query_count)
    earlier = lax.broadcasted_iota(jnp.int32, shape, 0) <= lax.broadcasted_iota(
        jnp.int32, shape, 1
    )
    bias = jnp.where(key_docs == query_docs, 0.0, masked_score)
    return jnp.where(jnp.logical_or(earlier, jnp.logical_not(diagonal)), bias, masked_score)


def attend(queries, both, key_docs, query_docs, number):
    rows, width = queries.shape
    key_width = both.shape[1] // 2
    shared_heads = key_width // HEAD_DIM
    heads = width // HEAD_DIM
    seq_count = lax.axis_size("seq")
    pairs = seq_count // 2
    scale = 0.125 * LOG2E

    def kernel(
        q_ref,
        x_ref,
        kd_ref,
        qd_ref,
        low_ref,
        att_ref,
        lse_ref,
        kv_ref,
        qt_ref,
        max_ref,
        sum_ref,
        send,
        recv,
        pass_send,
        pass_recv,
    ):
        me = lax.axis_index("seq")
        place = me % 2
        pair = me // 2
        partner, *others = pair_peers()
        meet([partner] + others)

        first = [
            send_to(x_ref, kv_ref.at[me], send.at[k], recv.at[k], others[k])
            for k in range(pairs - 1)
        ]
        across = send_to(x_ref, kv_ref.at[me], pass_send.at[0], pass_recv.at[0], partner)
        across.start()
        for copy in first:
            copy.start()
        kv_ref[me] = x_ref[...]
        stand_up(q_ref[...], qt_ref, shared_heads)

        def block(owner, own):
            keys = x_ref[:, :key_width] if own else kv_ref[owner, :, :key_width]
            values = x_ref[:, key_width:] if own else kv_ref[owner, :, key_width:]
            begin = pl.multiple_of(owner * rows, rows)
            bias = hidden_bias(kd_ref[pl.ds(begin, rows), :], qd_ref[...], own)
            for head in range(heads):
                columns = slice(head * rows, (head + 1) * rows)
                scores = product(keys, qt_ref[:, columns]) * scale + bias
                top = jnp.max(scores, axis=0, keepdims=True)
                if not own:
                    old = max_ref[:, columns]
                    top = jnp.maximum(top, old)
                weights = jnp.exp2(scores - top)
                total = jnp.sum(weights, axis=0, keepdims=True)
                weighted = over_rows(values, to_low(weights))
                if not own:
                    factor = jnp.exp2(old - top)
                    total = total + sum_ref[:, columns] * factor
                    weighted = weighted + att_ref[:, columns] * factor
                max_ref[:, columns] = top
                sum_ref[:, columns] = total
                att_ref[:, columns] = weighted

        def earlier(owner):
            @pl.when(owner < me)
            def visit():
                block(owner, False)

        block(me, True)
        for k in range(1, pairs):
            first[k - 1].wait_recv()
            origin = ((pair - k + pairs) % pairs) * 2 + place
            passed = send_to(
                kv_ref.at[origin], kv_ref.at[origin], pass_send.at[k], pass_recv.at[k], partner
            )
            passed.start()
            if k == 1:
                across.wait_recv()
                earlier(me + 1 - 2 * place)
            earlier(origin)

        @pl.loop(1, pairs)
        def arrived(k):
            origin = ((pair - k + pairs) % pairs) * 2 + place
            other = origin + 1 - 2 * place
            send_to(
                kv_ref.at[origin], kv_ref.at[origin], pass_send.at[k], pass_recv.at[k], partner
            ).wait_recv()
            earlier(other)

        att_ref[...] = att_ref[...] / sum_ref[...]
        lse_ref[...] = max_ref[...] + jnp.log2(sum_ref[...])
        low_ref[...] = to_low(lie_down(att_ref, rows, shared_heads))
        for copy in first + [across]:
            copy.wait_send()

        @pl.loop(1, pairs)
        def sent(k):
            origin = ((pair - k + pairs) % pairs) * 2 + place
            send_to(
                kv_ref.at[origin], kv_ref.at[origin], pass_send.at[k], pass_recv.at[k], partner
            ).wait_send()

    return pl.pallas_call(
        kernel,
        out_shape=(
            jax.ShapeDtypeStruct((rows, width), jnp.bfloat16),
            jax.ShapeDtypeStruct((key_width, heads * rows), jnp.float32),
            jax.ShapeDtypeStruct((1, heads * rows), jnp.float32),
            jax.ShapeDtypeStruct((seq_count,) + both.shape, both.dtype),
        ),
        in_specs=[VMEM] * 4,
        out_specs=(VMEM,) * 4,
        scratch_shapes=[
            pltpu.VMEM((key_width, heads * rows), jnp.bfloat16),
            pltpu.VMEM((1, heads * rows), jnp.float32),
            pltpu.VMEM((1, heads * rows), jnp.float32),
        ]
        + [pltpu.SemaphoreType.DMA((pairs,))] * 4,
        compiler_params=talking(number, 24),
        cost_estimate=lasting(12),
        name="attend",
    )(queries, both, key_docs, query_docs)


def attend_back(own, queries, upstream, both_rows, key_docs, query_docs, attended, log_sum):
    rows, width = queries.shape
    total_rows = both_rows.shape[0]
    key_width = both_rows.shape[1] // 2
    shared_heads = key_width // HEAD_DIM
    heads = width // HEAD_DIM
    scale = 0.125 * LOG2E

    def kernel(
        own_ref, q_ref, up_ref, kv_ref, kd_ref, qd_ref, att_ref, lse_ref, qg_ref, kg_ref, vg_ref, qt_ref, ut_ref, acc_ref
    ):
        stand_up(q_ref[...], qt_ref, shared_heads)
        stand_up(up_ref[...], ut_ref, shared_heads)
        me = own_ref[0]
        delta = jnp.sum(ut_ref[...].astype(jnp.float32) * att_ref[...], axis=0, keepdims=True)
        acc_ref[...] = jnp.zeros_like(acc_ref)

        @pl.loop(me + 1, total_rows // rows)
        def later(position):
            begin = pl.multiple_of(position * rows, rows)
            kg_ref[pl.ds(begin, rows), :] = jnp.zeros((rows, key_width), jnp.bfloat16)
            vg_ref[pl.ds(begin, rows), :] = jnp.zeros((rows, key_width), jnp.bfloat16)

        @pl.loop(0, me + 1)
        def block(position):
            begin = pl.multiple_of(position * rows, rows)
            keys = kv_ref[pl.ds(begin, rows), :key_width]
            values = kv_ref[pl.ds(begin, rows), key_width:]
            bias = hidden_bias(kd_ref[pl.ds(begin, rows), :], qd_ref[...], position == me)
            key_grad = jnp.zeros((rows, key_width), jnp.float32)
            value_grad = jnp.zeros((rows, key_width), jnp.float32)
            for head in range(heads):
                columns = slice(head * rows, (head + 1) * rows)
                query = qt_ref[:, columns]
                upper = ut_ref[:, columns]
                probs = jnp.exp2(product(keys, query) * scale + bias - lse_ref[:, columns])
                value_grad = value_grad + over_columns(to_low(probs), upper)
                score_grad = to_low(probs * (product(values, upper) - delta[:, columns]))
                key_grad = key_grad + over_columns(score_grad, query)
                acc_ref[:, columns] += over_rows(keys, score_grad)
            kg_ref[pl.ds(begin, rows), :] = to_low(key_grad * 0.125)
            vg_ref[pl.ds(begin, rows), :] = to_low(value_grad)

        qg_ref[...] = to_low(lie_down(acc_ref, rows, shared_heads) * 0.125)

    return pl.pallas_call(
        kernel,
        out_shape=(
            jax.ShapeDtypeStruct((rows, width), jnp.bfloat16),
            jax.ShapeDtypeStruct((total_rows, key_width), jnp.bfloat16),
            jax.ShapeDtypeStruct((total_rows, key_width), jnp.bfloat16),
        ),
        in_specs=[pl.BlockSpec(memory_space=pltpu.SMEM)] + [VMEM] * 7,
        out_specs=(VMEM,) * 3,
        scratch_shapes=[
            pltpu.VMEM((key_width, heads * rows), jnp.bfloat16),
            pltpu.VMEM((key_width, heads * rows), jnp.bfloat16),
            pltpu.VMEM((key_width, heads * rows), jnp.float32),
        ],
        compiler_params=pltpu.CompilerParams(vmem_limit_bytes=28 * MEBI),
        cost_estimate=lasting(20),
        name="attend_back",
    )(own, queries, upstream, both_rows, key_docs, query_docs, attended, log_sum)


def body(
    tokens_in,
    cotangent,
    document_ids,
    expert_routes,
    norm_mixer,
    mixer_inner,
    mixer_gate,
    conv_taps,
    conv_bias,
    state_proj,
    step_proj,
    step_bias,
    decay_log,
    skip_gain,
    mixer_out,
    norm_ffn,
    ffn_gate,
    ffn_up,
    ffn_down,
    norm_attn,
    attn_query,
    attn_key,
    attn_value,
    attn_output,
    norm_moe,
    router,
    expert_gate,
    expert_up,
    expert_down,
):
    numbers = itertools.count()
    seq_count = lax.axis_size("seq")
    row_count = tokens_in.shape[0]
    total_rows = seq_count * row_count
    first_row = lax.axis_index("seq") * row_count
    last_row = first_row + row_count - 1

    me = lax.axis_index("seq")
    bit_count = seq_count.bit_length() - 1
    across_first = [0] + list(range(1, bit_count))
    along_first = [1, 0] + list(range(2, bit_count))

    def by_owner(values, bits):
        turned = values.transpose(0, 2, 1)
        own_rows = turned.shape[1] // seq_count
        order = [0]
        for bit in reversed(bits):
            order = order + [j + (1 << bit) for j in order]
        blocks = []
        for j in order:
            owner = me
            for bit in range(bit_count):
                if j >> bit & 1:
                    owner = owner + (1 << bit) * (1 - 2 * ((owner >> bit) & 1))
            blocks.append(lax.dynamic_slice_in_dim(turned, owner * own_rows, own_rows, 1))
        half = len(blocks) // 2
        return (
            jnp.concatenate(blocks[half:], axis=1),
            jnp.concatenate(blocks[:half], axis=1),
        ), bits

    def over_tokens(rows, columns):
        if rows.shape[0] == 1:
            return product(rows[0], columns[0])[None]
        return jnp.einsum("bdt,btf->bdf", rows, columns, preferred_element_type=jnp.float32)

    def begin_sum(*parts):
        flow = prepare_sum(*parts)
        send(flow)
        return flow

    def prepare_sum(*parts):
        flow = {"parts": parts, "bits": parts[0][0][1], "got": []}
        settle(flow)
        return flow

    def send(flow):
        bit = flow["bits"][len(flow["got"])]
        route = [(i, i ^ (1 << bit)) for i in range(seq_count)]
        flow["got"].append(lax.ppermute(flow["out"], "seq", route))

    def bind(values, *flows):
        tied = lax.optimization_barrier((values, *[flow["out"] for flow in flows]))
        for flow, out in zip(flows, tied[1:], strict=True):
            flow["out"] = out
        return tied[0]

    def settle(flow):
        step = len(flow["got"])
        if step < 2:
            gradients = [over_tokens(rows[0][step], columns) for rows, columns in flow["parts"]]
            total = gradients[0] if len(gradients) == 1 else jnp.concatenate(gradients, axis=2)
            if step == 0:
                flow["out"] = to_low(total)
                return
            flow["own"] = total + flow["got"][0].astype(jnp.float32)
        count = flow["own"].shape[1] >> (step - 1)
        half = count // 2
        last = step == len(flow["bits"])
        part = slice(0, count) if last else slice(half, count)
        total = flow["own"][:, part]
        for got in flow["got"][1:]:
            total = total + got[:, part].astype(jnp.float32)
        flow["total" if last else "out"] = total if last else to_low(total)

    def hold(values, *flows):
        if flows:
            tied = lax.optimization_barrier((values, *[flow["got"][-1] for flow in flows]))
            values = tied[0]
            for flow, got in zip(flows, tied[1:], strict=True):
                flow["got"][-1] = got
        return values

    def after(values, *flows):
        values = hold(values, *flows)
        for flow in flows:
            settle(flow)
            if "total" not in flow:
                send(flow)
        return values

    def finished(flow):
        while "total" not in flow:
            settle(flow)
            if "total" not in flow:
                send(flow)
        return flow["total"]

    def branch_sum(values):
        return head_sum(values, next(numbers), jnp.bfloat16, 4)

    local_docs = lax.dynamic_slice_in_dim(document_ids, first_row, row_count)
    reach = conv_taps.shape[0] - 1
    border = jnp.arange(reach, dtype=jnp.int32)
    docs_before = jnp.take(document_ids, jnp.maximum(first_row - reach + border, 0))
    docs_after = jnp.take(document_ids, jnp.minimum(first_row + row_count + border, total_rows - 1))
    docs_prior = jnp.concatenate([docs_before[reach - 1 :], local_docs[:-1]])
    retain = (local_docs == docs_prior).astype(jnp.float32)
    tokens = tokens_in.astype(jnp.float32)
    gain_mixer = norm_mixer.astype(jnp.float32)
    normed_one = to_low(rms_scale(tokens, gain_mixer))
    conv_in = to_low(product(normed_one, mixer_inner))
    gate_in = product(normed_one, mixer_gate)
    conv_edge = from_behind(conv_in[row_count - reach :], "seq", 1)
    extended = jnp.concatenate([conv_edge, conv_in]).astype(jnp.float32)
    docs_ext = jnp.concatenate([docs_before, local_docs])
    taps = conv_taps.astype(jnp.float32)
    conv_sum = conv_bias.astype(jnp.float32)[None, :]
    masks = []
    for offset in range(reach + 1):
        same_doc = (docs_ext[offset : offset + row_count] == local_docs).astype(jnp.float32)[
            :, None
        ]
        masks.append(same_doc)
        conv_sum = conv_sum + taps[offset] * extended[offset : offset + row_count] * same_doc
    activated = jax.nn.silu(conv_sum)
    act_low = to_low(activated)
    projected = head_sum(product(act_low, state_proj), next(numbers), jnp.float32, 1)
    rank_size = step_proj.shape[0]
    state_size = decay_log.shape[1]
    step_low = to_low(projected[:, :rank_size])
    inject = projected[:, rank_size : rank_size + state_size]
    readout = projected[:, rank_size + state_size :]
    step_pre = product(step_low, step_proj) + step_bias.astype(jnp.float32)
    step_dt = jax.nn.softplus(step_pre)
    decay_rate = jnp.exp(decay_log.astype(jnp.float32)).T
    slopes = -LOG2E * decay_rate
    steps = jnp.where(retain[:, None] > 0.0, step_dt, NEVER)
    drives = step_dt * activated
    inject_wide = spread(inject)
    readout_wide = spread(readout)
    state_in = run_summary(steps, drives, inject_wide, slopes, next(numbers), True)
    scanned, befores, state_out = state_sweep(
        state_in, steps, drives, inject_wide, readout_wide, slopes
    )
    skipping = skip_gain.astype(jnp.float32)
    mixed_state = scanned + skipping * activated
    gate_act = jax.nn.silu(gate_in)
    gated = to_low(mixed_state * gate_act)
    hidden_one = tokens + branch_sum(product(gated, mixer_out))
    gain_ffn = norm_ffn.astype(jnp.float32)
    normed_two = to_low(rms_scale(hidden_one, gain_ffn))
    gate_two = product(normed_two, ffn_gate)
    up_two = product(normed_two, ffn_up)
    ffn_act = to_low(jax.nn.silu(gate_two) * up_two)
    hidden_two = hidden_one + branch_sum(product(ffn_act, ffn_down))
    gain_attn = norm_attn.astype(jnp.float32)
    normed_three = to_low(rms_scale(hidden_two, gain_attn))
    queries = to_low(product(normed_three, attn_query))
    key_rows = to_low(product(normed_three, attn_key))
    value_rows = to_low(product(normed_three, attn_value))
    key_width = key_rows.shape[1]
    own_place = lax.axis_index("seq").reshape(1)
    key_docs = document_ids[:, None]
    query_docs = local_docs[None, :]
    attended_low, attended, log_sum, both_rows = attend(
        queries,
        jnp.concatenate([key_rows, value_rows], axis=1),
        key_docs,
        query_docs,
        next(numbers),
    )
    both_rows = both_rows.reshape(total_rows, -1)
    hidden_three = hidden_two + branch_sum(product(attended_low, attn_output))
    gain_moe = norm_moe.astype(jnp.float32)
    normed_four = to_low(rms_scale(hidden_three, gain_moe))
    logits = product(normed_four, router)
    expert_count = router.shape[1]
    experts = jnp.arange(expert_count, dtype=jnp.int32)
    named = (expert_routes[:, :, None] == experts).astype(jnp.float32)
    gate_weights = jax.nn.softmax(jnp.sum(named * logits[:, None, :], axis=2), axis=1)
    route_flat = expert_routes.reshape(-1)
    pair_count = route_flat.shape[0]
    pair_order = jnp.arange(pair_count, dtype=jnp.int32)
    earlier = (pair_order[None, :] < pair_order[:, None]) & (
        route_flat[None, :] == route_flat[:, None]
    )
    within = jnp.sum(earlier.astype(jnp.int32), axis=1)
    slot_index = (route_flat * CAP + within).reshape(row_count, 2)
    slots = jnp.arange(expert_count * CAP, dtype=jnp.int32)
    first_hit = slot_index[:, 0][None, :] == slots[:, None]
    second_hit = slot_index[:, 1][None, :] == slots[:, None]
    placing = (first_hit | second_hit).astype(jnp.bfloat16)
    slot_gates = jnp.sum(
        jnp.where(first_hit, gate_weights[:, 0][None, :], 0.0)
        + jnp.where(second_hit, gate_weights[:, 1][None, :], 0.0),
        axis=1,
    )
    expert_in = to_low(product(placing, normed_four)).reshape(expert_count, CAP, -1)
    slot_upstream = product(placing, cotangent)
    res_grad = to_low(slot_gates[:, None] * slot_upstream).reshape(expert_count, CAP, -1)
    gate_four = jnp.einsum(
        "ecd,edf->ecf", expert_in, expert_gate, preferred_element_type=jnp.float32
    )
    up_four = jnp.einsum("ecd,edf->ecf", expert_in, expert_up, preferred_element_type=jnp.float32)
    expert_act = to_low(jax.nn.silu(gate_four) * up_four)
    expert_res = jnp.einsum(
        "ecf,efd->ecd", expert_act, expert_down, preferred_element_type=jnp.float32
    ).reshape(expert_count * CAP, -1)
    upstream = cotangent.astype(jnp.float32)
    slot_dots = jnp.sum(expert_res * slot_upstream, axis=1)
    dots_part = jnp.stack(
        [
            jnp.sum(jnp.where(first_hit, slot_dots[:, None], 0.0), axis=0),
            jnp.sum(jnp.where(second_hit, slot_dots[:, None], 0.0), axis=0),
        ],
        axis=1,
    )
    combined = product(placing.T, to_low(slot_gates[:, None] * expert_res))
    act_back = to_low(
        jnp.einsum("ecd,efd->ecf", res_grad, expert_down, preferred_element_type=jnp.float32)
    ).astype(jnp.float32)
    gating_grad = to_low(act_back * up_four * silu_slope(gate_four))
    upward_grad = to_low(act_back * jax.nn.silu(gate_four))
    flow_expert_down = begin_sum((by_owner(res_grad, along_first), expert_act))
    expert_rows = by_owner(expert_in, across_first)
    flow_expert_in = begin_sum(
        (expert_rows, jnp.concatenate([gating_grad, upward_grad], axis=2))
    )
    slot_grads = (
        jnp.einsum("ecf,edf->ecd", gating_grad, expert_gate, preferred_element_type=jnp.float32)
        + jnp.einsum("ecf,edf->ecd", upward_grad, expert_up, preferred_element_type=jnp.float32)
    ).reshape(expert_count * CAP, -1)
    token_part = product(placing.T, to_low(slot_grads))
    model_width = tokens.shape[1]
    expert_sums = branch_sum(
        jnp.concatenate(
            [token_part, jnp.pad(dots_part, ((0, 0), (0, LANES - 2)))], axis=1
        )
    )
    normed_grad = expert_sums[:, :model_width]
    dots = expert_sums[:, model_width : model_width + 2]
    chosen_grad = gate_weights * (dots - jnp.sum(gate_weights * dots, axis=1, keepdims=True))
    logit_grad = jnp.sum(named * chosen_grad[:, :, None], axis=1)
    grad_router = exact_product(normed_four.astype(jnp.float32).T, logit_grad)
    normed_grad = normed_grad + exact_product(logit_grad, router.astype(jnp.float32).T)
    hidden_grad, grad_norm_moe = rms_back(hidden_three, gain_moe, normed_grad)
    three_grad = upstream + hidden_grad
    branch_grad = to_low(three_grad)
    attn_out_rows = by_owner(branch_grad[None], across_first)
    attended_grad = to_low(product(branch_grad, attn_output.T))
    query_grad, key_part, value_part = attend_back(
        own_place, queries, attended_grad, both_rows, key_docs, query_docs, attended, log_sum
    )
    key_part = hold(key_part, flow_expert_down)
    key_sum, value_sum, combined_sum = scatter_and_head_sum(
        [key_part, value_part], combined, next(numbers)
    )
    mixed_out = to_low(hidden_three + combined_sum)
    key_sum, attended_late = lax.optimization_barrier((key_sum, attended_low))
    key_sum = after(key_sum, flow_expert_down, flow_expert_in)
    key_grad = to_low(key_sum)
    value_grad = to_low(value_sum)
    flow_attn = begin_sum(
        (
            by_owner(normed_three[None], across_first),
            jnp.concatenate([query_grad, key_grad, value_grad], axis=1)[None],
        ),
        (attn_out_rows, attended_late[None]),
    )
    normed_part = (
        product(query_grad, attn_query.T)
        + product(key_grad, attn_key.T)
        + product(value_grad, attn_value.T)
    )
    normed_grad = branch_sum(normed_part)
    hidden_grad, grad_norm_attn = rms_back(hidden_two, gain_attn, normed_grad)
    two_grad = three_grad + hidden_grad
    branch_grad = to_low(two_grad)
    flow_ffn_down = begin_sum((by_owner(branch_grad[None], along_first), ffn_act[None]))
    ffn_back = to_low(product(branch_grad, ffn_down.T))
    ffn_back = after(ffn_back, flow_expert_down, flow_expert_in, flow_attn).astype(jnp.float32)
    feed_gate_grad = to_low(ffn_back * up_two * silu_slope(gate_two))
    feed_up_grad = to_low(ffn_back * jax.nn.silu(gate_two))
    feed_rows = by_owner(normed_two[None], across_first)
    flow_ffn_gate = begin_sum((feed_rows, feed_gate_grad[None]))
    normed_part = product(feed_gate_grad, ffn_gate.T) + product(feed_up_grad, ffn_up.T)
    normed_grad = branch_sum(normed_part)
    hidden_grad, grad_norm_ffn = rms_back(hidden_one, gain_ffn, normed_grad)
    one_grad = two_grad + hidden_grad
    branch_grad = to_low(one_grad)
    mixer_out_rows = by_owner(branch_grad[None], across_first)
    gated_grad = to_low(product(branch_grad, mixer_out.T)).astype(jnp.float32)
    scan_grad = gated_grad * gate_act
    gate_in_grad = to_low(gated_grad * mixed_state * silu_slope(gate_in))
    grad_skip_gain = jnp.sum(scan_grad * activated, axis=0)
    early_flows = (flow_expert_down, flow_expert_in, flow_attn, flow_ffn_down, flow_ffn_gate)
    flow_ffn_up = prepare_sum((feed_rows, feed_up_grad[None]))
    flow_mixer_gate = prepare_sum((by_owner(normed_one[None], along_first), gate_in_grad[None]))
    flow_mixer_out = prepare_sum((mixer_out_rows, gated[None]))
    late_flows = (flow_ffn_up, flow_mixer_gate, flow_mixer_out)
    scan_grad = bind(scan_grad, *late_flows)
    scan_grad = hold(scan_grad, *early_flows)
    state_after = run_summary(steps, scan_grad, readout_wide, slopes, next(numbers), False)
    state_after = bind(state_after, *late_flows)
    state_after = after(state_after, flow_attn, flow_ffn_gate)
    send(flow_ffn_up)
    send(flow_mixer_gate)
    through_sum, injected, inject_part, readout_part, rate_sum = adjoint_sweep(
        state_after,
        state_out,
        befores,
        steps,
        drives,
        inject_wide,
        readout_wide,
        scan_grad,
        slopes,
    )
    step_grad = LN2 * through_sum + activated * injected
    input_grad = step_dt * injected
    inject_grad = jnp.sum(inject_part, axis=2)
    readout_grad = jnp.sum(readout_part, axis=2)
    grad_decay_log = -rate_sum * decay_rate
    pre_grad = step_grad * jax.nn.sigmoid(step_pre)
    grad_step_bias = jnp.sum(pre_grad, axis=0)
    pre_low = to_low(pre_grad)
    pre_low = bind(pre_low, flow_mixer_out)
    pre_low = after(pre_low, flow_ffn_up, flow_ffn_gate, flow_ffn_down, flow_attn)
    send(flow_mixer_out)
    grad_step_proj = product(pre_low.T, step_low)
    proj_part = jnp.concatenate([product(pre_low, step_proj.T), inject_grad, readout_grad], axis=1)
    proj_low = to_low(head_sum(proj_part, next(numbers), jnp.float32, 1))
    proj_low = after(proj_low, flow_mixer_gate, flow_ffn_down)
    grad_state_proj = product(act_low.T, proj_low)
    act_total = input_grad + skipping * scan_grad + product(proj_low, state_proj.T)
    conv_grad = act_total * silu_slope(conv_sum)
    conv_grad = after(conv_grad, flow_ffn_up, flow_mixer_out, flow_ffn_gate)
    grad_conv_bias = jnp.sum(conv_grad, axis=0)
    after_edge = from_behind(conv_grad[:reach], "seq", -1)
    after_edge = after(after_edge, flow_ffn_down)
    grad_ext = jnp.concatenate([conv_grad, after_edge])
    docs_next = jnp.concatenate([local_docs, docs_after])
    conv_in_grad = jnp.zeros_like(conv_grad)
    tap_rows = []
    for offset in range(reach + 1):
        tap_rows.append(
            jnp.sum(conv_grad * extended[offset : offset + row_count] * masks[offset], axis=0)
        )
        lead = reach - offset
        same_next = (docs_next[lead : lead + row_count] == local_docs).astype(jnp.float32)[:, None]
        conv_in_grad = conv_in_grad + taps[offset] * grad_ext[lead : lead + row_count] * same_next
    grad_conv_taps = jnp.stack(tap_rows)
    conv_low = to_low(conv_in_grad)
    inner_half = conv_low.shape[1] // 2
    grad_mixer_inner = to_low(product(normed_one.T, conv_low))
    normed_part = product(conv_low, mixer_inner.T) + product(gate_in_grad, mixer_gate.T)
    own_channels = grad_conv_bias.shape[0] // seq_count

    def cut(values):
        return values.reshape(seq_count, -1)

    channel_rows = jnp.concatenate(
        [grad_state_proj, jnp.pad(grad_step_proj, ((0, 0), (0, LANES - rank_size)))], axis=1
    )
    packed = jnp.concatenate(
        [
            cut(grad_decay_log.T),
            cut(grad_norm_ffn),
            cut(grad_norm_attn),
            cut(grad_norm_moe),
            cut(grad_router),
            cut(grad_conv_taps.T),
            cut(grad_conv_bias),
            cut(grad_step_bias),
            cut(grad_skip_gain),
        ],
        axis=1,
    )
    spare = -packed.shape[1] % (16 * LANES)
    packed = to_low(jnp.pad(packed, ((0, 0), (0, spare)))).reshape(-1, LANES)
    packed = after(packed, flow_mixer_out, flow_mixer_gate)
    first_inner, second_inner, sum_rows, sum_packed, grad_tokens, grad_norm_mixer = last_sums(
        [
            grad_mixer_inner[:, :inner_half],
            grad_mixer_inner[:, inner_half:],
            to_low(channel_rows),
            packed,
        ],
        normed_part,
        tokens_in,
        gain_mixer[None, :],
        one_grad,
        next(numbers),
    )
    sum_attn = finished(flow_attn)[0]
    sum_expert_in = finished(flow_expert_in)
    expert_width = expert_gate.shape[2]
    sum_packed = sum_packed.reshape(-1)
    own_rows = model_width // seq_count
    taken = itertools.accumulate(
        [0, own_channels * state_size]
        + [own_rows] * 3
        + [own_rows * expert_count, own_channels * (reach + 1)]
        + [own_channels] * 3
    )
    bounds = list(taken)
    pieces = [sum_packed[low:high] for low, high in itertools.pairwise(bounds)]
    query_width = attn_query.shape[1]

    return (
        mixed_out,
        grad_tokens,
        lax.dynamic_slice_in_dim(grad_norm_mixer[0], me * own_rows, own_rows),
        jnp.concatenate([first_inner, second_inner], axis=1),
        finished(flow_mixer_gate)[0],
        pieces[5].reshape(own_channels, -1).T,
        pieces[6],
        sum_rows[:, :LANES],
        sum_rows[:, LANES : LANES + rank_size].T,
        pieces[7],
        pieces[0].reshape(own_channels, -1),
        pieces[8],
        finished(flow_mixer_out)[0].T,
        pieces[1],
        finished(flow_ffn_gate)[0],
        finished(flow_ffn_up)[0],
        finished(flow_ffn_down)[0].T,
        pieces[2],
        sum_attn[:, :query_width],
        sum_attn[:, query_width : query_width + key_width],
        sum_attn[:, query_width + key_width : query_width + 2 * key_width],
        sum_attn[:, query_width + 2 * key_width :].T,
        pieces[3],
        pieces[4].reshape(own_rows, -1),
        sum_expert_in[:, :, :expert_width],
        sum_expert_in[:, :, expert_width:],
        finished(flow_expert_down).transpose(0, 2, 1),
    )


def solution(mesh):
    in_specs = (
        P("seq", None),
        P("seq", None),
        P(),
        P("seq", None),
        P(),
        P(None, "head"),
        P(None, "head"),
        P(None, "head"),
        P("head"),
        P("head", None),
        P(None, "head"),
        P("head"),
        P("head", None),
        P("head"),
        P("head", None),
        P(),
        P(None, "head"),
        P(None, "head"),
        P("head", None),
        P(),
        P(None, "head"),
        P(None, "head"),
        P(None, "head"),
        P("head", None),
        P(),
        P(),
        P(None, None, "head"),
        P(None, None, "head"),
        P(None, "head", None),
    )
    out_specs = (
        P("seq", None),
        P("seq", None),
        P("seq"),
        P("seq", "head"),
        P("seq", "head"),
        P(None, ("head", "seq")),
        P(("head", "seq")),
        P(("head", "seq"), None),
        P(None, ("head", "seq")),
        P(("head", "seq")),
        P(("head", "seq"), None),
        P(("head", "seq")),
        P("head", "seq"),
        P("seq"),
        P("seq", "head"),
        P("seq", "head"),
        P("head", "seq"),
        P("seq"),
        P("seq", "head"),
        P("seq", "head"),
        P("seq", "head"),
        P("head", "seq"),
        P("seq"),
        P("seq", None),
        P(None, "seq", "head"),
        P(None, "seq", "head"),
        P(None, "head", "seq"),
    )
    return jax.shard_map(body, mesh=mesh, in_specs=in_specs, out_specs=out_specs, check_vma=False)
```

```python
import itertools
import math

import jax
import jax.numpy as jnp
from jax import lax
from jax.experimental import pallas as pl
from jax.experimental.pallas import tpu as pltpu
from jax.sharding import PartitionSpec as P

HEAD_DIM = 64
CAP = 160
LANES = 128
LOG2E = 1.4426950408889634
LN2 = 0.6931471805599453
NEVER = 1e30
MEBI = 1024 * 1024
MESH = pl.DeviceIdType.MESH
VMEM = pl.BlockSpec(memory_space=pltpu.VMEM)
ANY = pl.BlockSpec(memory_space=pl.ANY)


highest = lax.Precision.HIGHEST
epsilon = 1e-05
masked_score = -1e30


def from_behind(block, axis, distance):
    devices = range(lax.axis_size(axis))
    route = [(i - distance, i) for i in devices if i - distance in devices]
    return lax.ppermute(block, axis, route)


def to_low(values):
    return values.astype(jnp.bfloat16)


def product(left, right):
    return jnp.dot(left, right, preferred_element_type=jnp.float32)


def exact_product(left, right):
    return jnp.dot(left, right, precision=highest, preferred_element_type=jnp.float32)


def rms_scale(values, gain):
    return values * lax.rsqrt(jnp.mean(values * values, axis=-1, keepdims=True) + epsilon) * gain


def rms_back(values, gain, upstream):
    unused, pullback = jax.vjp(rms_scale, values, gain)
    return pullback(upstream)


def silu_slope(values):
    logistic = jax.nn.sigmoid(values)
    return logistic * (1.0 + values * (1.0 - logistic))


def meet(peers):
    barrier = pltpu.get_barrier_semaphore()
    for peer in peers:
        pl.semaphore_signal(barrier, inc=1, device_id=peer, device_id_type=MESH)
    pl.semaphore_wait(barrier, len(peers))


def send_to(source, target, send_sem, recv_sem, peer):
    return pltpu.make_async_remote_copy(
        src_ref=source,
        dst_ref=target,
        send_sem=send_sem,
        recv_sem=recv_sem,
        device_id=peer,
        device_id_type=MESH,
    )


def lasting(microseconds):
    return pl.CostEstimate(
        flops=int(microseconds * 1e3),
        bytes_accessed=int(microseconds * 1e3),
        transcendentals=0,
    )


def talking(number, mebibytes):
    return pltpu.CompilerParams(
        collective_id=number, has_side_effects=True, vmem_limit_bytes=mebibytes * MEBI
    )


def together(*jobs):
    waiting = list(jobs)
    while waiting:
        for job in list(waiting):
            if next(job, waiting) is waiting:
                waiting.remove(job)


def head_peers():
    seq = lax.axis_index("seq")
    head = lax.axis_index("head")
    return [(seq, head + 1 - 2 * (head % 2)), (seq, (head + 2) % 4)]


def head_scratch(rows, width, wire, pieces):
    return [pltpu.VMEM((rows // 2, width), wire)] * 4 + [
        pltpu.SemaphoreType.DMA((3, pieces)),
        pltpu.SemaphoreType.DMA((3, pieces)),
    ]


def head_job(x_ref, o_ref, scratch, wire, pieces):
    near_out, near_in, far_out, far_in, send, recv = scratch
    half = x_ref.shape[0] // 2
    step = half // pieces
    near, far = head_peers()
    core = lax.axis_index("head") % 2

    def rows_of(side, piece):
        return pl.ds(pl.multiple_of(side * half + piece * step, 8), step)

    first, second, third = [], [], []
    for piece in range(pieces):
        local = pl.ds(piece * step, step)
        near_out[local] = x_ref[rows_of(1 - core, piece)].astype(wire)
        first.append(
            send_to(
                near_out.at[local], near_in.at[local], send.at[0, piece], recv.at[0, piece], near
            )
        )
        first[-1].start()
    yield
    for piece in range(pieces):
        local = pl.ds(piece * step, step)
        first[piece].wait_recv()
        total = x_ref[rows_of(core, piece)] + near_in[local].astype(jnp.float32)
        far_out[local] = total.astype(wire)
        second.append(
            send_to(far_out.at[local], far_in.at[local], send.at[1, piece], recv.at[1, piece], far)
        )
        second[-1].start()
    yield
    for piece in range(pieces):
        local = pl.ds(piece * step, step)
        second[piece].wait_recv()
        whole = far_out[local].astype(jnp.float32) + far_in[local].astype(jnp.float32)
        o_ref[rows_of(core, piece)] = whole
        third.append(
            send_to(
                o_ref.at[rows_of(core, piece)],
                o_ref.at[rows_of(core, piece)],
                send.at[2, piece],
                recv.at[2, piece],
                near,
            )
        )
        third[-1].start()
    yield
    for copy in third:
        copy.wait_recv()
    for copy in first + second + third:
        copy.wait_send()


def head_sum(values, number, wire, pieces):
    rows, width = values.shape

    def kernel(x_ref, o_ref, *scratch):
        meet(head_peers())
        together(head_job(x_ref, o_ref, scratch, wire, pieces))

    return pl.pallas_call(
        kernel,
        out_shape=jax.ShapeDtypeStruct((rows, width), jnp.float32),
        in_specs=[VMEM],
        out_specs=VMEM,
        scratch_shapes=head_scratch(rows, width, wire, pieces),
        compiler_params=talking(number, 10),
        cost_estimate=lasting(6 + values.size // 40000),
        name="head_sum",
    )(values)


def pair_peers():
    seq = lax.axis_index("seq")
    head = lax.axis_index("head")
    pairs = lax.axis_size("seq") // 2
    place = seq % 2
    pair = seq // 2
    others = [(((pair + k) % pairs) * 2 + place, head) for k in range(1, pairs)]
    return [(seq + 1 - 2 * place, head)] + others


def scatter_shapes(arrays):
    seq_count = lax.axis_size("seq")
    return [(a.shape[0] // seq_count, a.shape[1]) for a in arrays]


def scatter_blocks(arrays):
    pairs = lax.axis_size("seq") // 2
    return [
        a.reshape(pairs, 2, shape[0], shape[1])
        for a, shape in zip(arrays, scatter_shapes(arrays), strict=True)
    ]


def scatter_scratch(shapes):
    pairs = lax.axis_size("seq") // 2
    count = len(shapes)
    return (
        [pltpu.VMEM((pairs,) + shape, jnp.bfloat16) for shape in shapes] * 2
        + [pltpu.VMEM((pairs - 1,) + shape, jnp.bfloat16) for shape in shapes]
        + [pltpu.SemaphoreType.DMA((count,))] * 3
        + [pltpu.SemaphoreType.DMA((count, pairs - 1))] * 2
    )


def scatter_job(takes, gives, scratch, shapes):
    count = len(takes)
    pairs = lax.axis_size("seq") // 2
    own, near, far = scratch[:count], scratch[count : 2 * count], scratch[2 * count : 3 * count]
    own_sem, near_send, near_recv, far_send, far_recv = scratch[3 * count :]
    seq = lax.axis_index("seq")
    place = seq % 2
    pair = seq // 2
    partner, *others = pair_peers()
    owners = [(pair + k) % pairs for k in range(1, pairs)]
    loads = [
        pltpu.make_async_copy(takes[i].at[:, place], own[i], own_sem.at[i]) for i in range(count)
    ]
    halves = [
        send_to(takes[i].at[:, 1 - place], near[i], near_send.at[i], near_recv.at[i], partner)
        for i in range(count)
    ]

    def launch(i):
        if i < count:
            halves[i].start()
            loads[i].start()

    sums = []

    def finish(i):
        for copy in sums[i]:
            copy.wait_recv()

        @pl.loop(0, shapes[i][0] // 16)
        def add(step):
            part = pl.ds(pl.multiple_of(step * 16, 16), 16)
            total = own[i][pair, part].astype(jnp.float32)
            for k in range(pairs - 1):
                total = total + far[i][k, part].astype(jnp.float32)
            gives[i][part] = total

    launch(0)
    launch(1)
    for i in range(count):
        yield
        halves[i].wait_recv()
        loads[i].wait()
        launch(i + 2)

        @pl.loop(0, pairs)
        def merge(block):
            @pl.loop(0, shapes[i][0] // 16)
            def add(step):
                part = pl.ds(pl.multiple_of(step * 16, 16), 16)
                total = own[i][block, part].astype(jnp.float32) + near[i][block, part].astype(
                    jnp.float32
                )
                own[i][block, part] = total.astype(jnp.bfloat16)

        sums.append(
            [
                send_to(
                    own[i].at[owners[k]],
                    far[i].at[k],
                    far_send.at[i, k],
                    far_recv.at[i, k],
                    others[k],
                )
                for k in range(pairs - 1)
            ]
        )
        for copy in sums[i]:
            copy.start()
        if i > 0:
            finish(i - 1)
    yield
    finish(count - 1)
    for copy in halves:
        copy.wait_send()
    for group in sums:
        for copy in group:
            copy.wait_send()


def scatter_and_head_sum(arrays, values, number):
    count = len(arrays)
    shapes = scatter_shapes(arrays)
    rows, width = values.shape
    spaces = scatter_scratch(shapes)

    def kernel(*refs):
        takes, x_ref = refs[:count], refs[count]
        gives, o_ref = refs[count + 1 : 2 * count + 1], refs[2 * count + 1]
        scratch = refs[2 * count + 2 :]
        meet(pair_peers() + head_peers())
        together(
            scatter_job(takes, gives, scratch[: len(spaces)], shapes),
            head_job(x_ref, o_ref, scratch[len(spaces) :], jnp.bfloat16, 4),
        )

    return pl.pallas_call(
        kernel,
        out_shape=[jax.ShapeDtypeStruct(shape, jnp.float32) for shape in shapes]
        + [jax.ShapeDtypeStruct((rows, width), jnp.float32)],
        in_specs=[ANY] * count + [VMEM],
        out_specs=[VMEM] * (count + 1),
        scratch_shapes=spaces + head_scratch(rows, width, jnp.bfloat16, 4),
        compiler_params=talking(number, 24),
        cost_estimate=lasting(20),
        name="scatter_and_head_sum",
    )(*scatter_blocks(arrays), values)


def last_sums(arrays, values, tokens, gain, upstream, number):
    count = len(arrays)
    shapes = scatter_shapes(arrays)
    rows, width = values.shape
    seq_count = lax.axis_size("seq")
    spaces = scatter_scratch(shapes)
    step = 16

    def kernel(*refs):
        takes = refs[:count]
        x_ref, token_ref, gain_ref, up_ref = refs[count : count + 4]
        gives = refs[count + 4 : 2 * count + 4]
        grad_ref, gain_out = refs[2 * count + 4 : 2 * count + 6]
        scratch = refs[2 * count + 6 :]
        total_ref, part_out, part_in, part_send, part_recv = scratch[-5:]
        seq = lax.axis_index("seq")
        head = lax.axis_index("head")
        peers = [((seq + k) % seq_count, head) for k in range(1, seq_count)]
        meet(peers + head_peers())

        def norm_job():
            yield from head_job(x_ref, total_ref, scratch[len(spaces) : -5], jnp.bfloat16, 4)

            def back(position, gained):
                part = pl.ds(pl.multiple_of(position * step, step), step)
                token = token_ref[part].astype(jnp.float32)
                scale = lax.rsqrt(jnp.mean(token * token, axis=1, keepdims=True) + epsilon)
                unit = token * scale
                given = total_ref[part]
                scaled = given * gain_ref[...]
                pull = jnp.mean(scaled * unit, axis=1, keepdims=True)
                grad_ref[part] = up_ref[part] + scale * (scaled - unit * pull)
                product_rows = given * unit
                return gained + product_rows[:8] + product_rows[8:]

            gained = lax.fori_loop(0, rows // step, back, jnp.zeros((8, width), jnp.float32))
            part_out[...] = jnp.sum(gained, axis=0, keepdims=True)
            copies = [
                send_to(part_out, part_in.at[k], part_send.at[k], part_recv.at[k], peers[k])
                for k in range(seq_count - 1)
            ]
            for copy in copies:
                copy.start()
            yield
            for copy in copies:
                copy.wait_recv()
            whole = part_out[...]
            for k in range(seq_count - 1):
                whole = whole + part_in[k]
            gain_out[...] = whole
            for copy in copies:
                copy.wait_send()

        together(norm_job(), scatter_job(takes, gives, scratch[: len(spaces)], shapes))

    return pl.pallas_call(
        kernel,
        out_shape=[jax.ShapeDtypeStruct(shape, jnp.float32) for shape in shapes]
        + [
            jax.ShapeDtypeStruct((rows, width), jnp.float32),
            jax.ShapeDtypeStruct((1, width), jnp.float32),
        ],
        in_specs=[ANY] * count + [VMEM] * 4,
        out_specs=[VMEM] * (count + 2),
        scratch_shapes=spaces
        + head_scratch(rows, width, jnp.bfloat16, 4)
        + [
            pltpu.VMEM((rows, width), jnp.float32),
            pltpu.VMEM((1, width), jnp.float32),
            pltpu.VMEM((seq_count - 1, 1, width), jnp.float32),
            pltpu.SemaphoreType.DMA((seq_count - 1,)),
            pltpu.SemaphoreType.DMA((seq_count - 1,)),
        ],
        compiler_params=talking(number, 28),
        cost_estimate=lasting(20),
        name="last_sums",
    )(*scatter_blocks(arrays), values, tokens, gain, upstream)


def widen(column_block, width):
    return jnp.concatenate([column_block] * (width // LANES), axis=-1)


def narrow(wide):
    width = wide.shape[-1]
    total = wide[:, :LANES]
    for place in range(1, width // LANES):
        total = total + wide[:, place * LANES : (place + 1) * LANES]
    return total


def spread(columns):
    return jnp.broadcast_to(columns[:, :, None], columns.shape + (LANES,))


def run_summary(steps, drives, coefficients, slopes, number, forward):
    rows, width = steps.shape
    entries = slopes.shape[0]
    seq_count = lax.axis_size("seq")
    group = math.gcd(rows, 8)

    def kernel(
        step_ref,
        drive_ref,
        coef_ref,
        slope_ref,
        o_ref,
        outgoing,
        incoming,
        span_out,
        span_in,
        send,
        recv,
    ):
        seq = lax.axis_index("seq")
        head = lax.axis_index("head")
        peers = [((seq + k) % seq_count, head) for k in range(1, seq_count)]
        meet(peers)
        slope = slope_ref[...]
        span_out[...] = jnp.broadcast_to(
            jnp.sum(step_ref[...], axis=0, keepdims=True), span_out.shape
        )
        spans = [
            send_to(span_out, span_in.at[k], send.at[1, k], recv.at[1, k], peers[k])
            for k in range(seq_count - 1)
        ]
        for copy in spans:
            copy.start()

        def advance(position, state):
            for offset in range(group):
                t = position * group + offset
                t = t if forward else rows - 1 - t
                decays = jnp.exp2(step_ref[pl.ds(t, 1), :] * slope)
                drive = drive_ref[pl.ds(t, 1), :] * widen(coef_ref[t], width)
                state = state * decays + drive if forward else (state + drive) * decays
            return state

        state = lax.fori_loop(0, rows // group, advance, jnp.zeros((entries, width), jnp.float32))
        outgoing[...] = state.astype(jnp.bfloat16)
        copies = [
            send_to(outgoing, incoming.at[k], send.at[0, k], recv.at[0, k], peers[k])
            for k in range(seq_count - 1)
        ]
        for copy in copies:
            copy.start()
        for copy in spans:
            copy.wait_recv()
        for copy in copies:
            copy.wait_recv()
        carried = jnp.zeros((entries, width), jnp.float32)
        order = range(seq_count - 1, 0, -1) if forward else range(1, seq_count)
        for k in order:
            known = seq - k >= 0 if forward else seq - k < 0
            whole = jnp.exp2(span_in[k - 1][:1] * slope)
            carried = jnp.where(known, whole * carried + incoming[k - 1].astype(jnp.float32), 0.0)
        o_ref[...] = carried
        for copy in copies + spans:
            copy.wait_send()

    return pl.pallas_call(
        kernel,
        out_shape=jax.ShapeDtypeStruct((entries, width), jnp.float32),
        in_specs=[VMEM] * 4,
        out_specs=VMEM,
        scratch_shapes=[
            pltpu.VMEM((entries, width), jnp.bfloat16),
            pltpu.VMEM((seq_count - 1, entries, width), jnp.bfloat16),
            pltpu.VMEM((8, width), jnp.float32),
            pltpu.VMEM((seq_count - 1, 8, width), jnp.float32),
            pltpu.SemaphoreType.DMA((2, seq_count - 1)),
            pltpu.SemaphoreType.DMA((2, seq_count - 1)),
        ],
        compiler_params=talking(number, 10),
        cost_estimate=lasting(16),
        name="run_summary",
    )(steps, drives, coefficients, slopes)


def state_sweep(initial, steps, drives, inject, readout, slopes):
    rows, width = steps.shape
    entries = slopes.shape[0]
    length = math.gcd(rows, 32)
    group = math.gcd(length, 8)

    def kernel(
        init_ref, step_ref, drive_ref, inject_ref, read_ref, slope_ref, y_ref, before_ref, end_ref
    ):
        @pl.when(pl.program_id(0) == 0)
        def begin():
            end_ref[...] = init_ref[...]

        slope = slope_ref[...]

        def advance(position, state):
            for offset in range(group):
                t = position * group + offset
                before_ref[t] = state
                decays = jnp.exp2(step_ref[pl.ds(t, 1), :] * slope)
                drive = drive_ref[pl.ds(t, 1), :] * widen(inject_ref[t], width)
                state = state * decays + drive
                y_ref[pl.ds(t, 1), :] = jnp.sum(
                    state * widen(read_ref[t], width), axis=0, keepdims=True
                )
            return state

        end_ref[...] = lax.fori_loop(0, length // group, advance, end_ref[...])

    row_spec = pl.BlockSpec((length, width), lambda i: (i, 0))
    entry_spec = pl.BlockSpec((length, entries, LANES), lambda i: (i, 0, 0))
    fixed = pl.BlockSpec((entries, width), lambda i: (0, 0))
    return pl.pallas_call(
        kernel,
        grid=(rows // length,),
        out_shape=(
            jax.ShapeDtypeStruct((rows, width), jnp.float32),
            pltpu.HBM((rows, entries, width), jnp.float32),
            jax.ShapeDtypeStruct((entries, width), jnp.float32),
        ),
        in_specs=[fixed, row_spec, row_spec, entry_spec, entry_spec, fixed],
        out_specs=(
            row_spec,
            pl.BlockSpec((length, entries, width), lambda i: (i, 0, 0)),
            fixed,
        ),
        compiler_params=pltpu.CompilerParams(vmem_limit_bytes=12 * MEBI),
        cost_estimate=lasting(11),
        name="state_sweep",
    )(initial, steps, drives, inject, readout, slopes)


def adjoint_sweep(incoming, last_state, befores, steps, drives, inject, readout, upstream, slopes):
    rows, width = steps.shape
    entries = slopes.shape[0]
    length = math.gcd(rows, 32)
    group = math.gcd(length, 8)
    blocks = rows // length

    def kernel(
        in_ref,
        last_ref,
        before_ref,
        step_ref,
        drive_ref,
        inject_ref,
        read_ref,
        up_ref,
        slope_ref,
        through_ref,
        injected_ref,
        inject_out,
        read_out,
        rate_ref,
        adjoint_ref,
        state_ref,
    ):
        @pl.when(pl.program_id(0) == 0)
        def begin():
            adjoint_ref[...] = in_ref[...]
            state_ref[...] = last_ref[...]
            rate_ref[...] = jnp.zeros_like(rate_ref)

        slope = slope_ref[...]

        def retreat(position, carried):
            adjoint_in, rate = carried
            for offset in range(group):
                t = length - 1 - (position * group + offset)
                upper = up_ref[pl.ds(t, 1), :]
                step = step_ref[pl.ds(t, 1), :]
                adjoint = widen(read_ref[t], width) * upper + adjoint_in
                state = state_ref[...] if offset == 0 else before_ref[t + 1]
                read_out[t] = narrow(upper * state)
                adjoint_in = jnp.exp2(step * slope) * adjoint
                before = before_ref[t]
                through = adjoint_in * before
                rate = rate + through * step
                through_ref[pl.ds(t, 1), :] = jnp.sum(through * slope, axis=0, keepdims=True)
                injected_ref[pl.ds(t, 1), :] = jnp.sum(
                    adjoint * widen(inject_ref[t], width), axis=0, keepdims=True
                )
                inject_out[t] = narrow(adjoint * drive_ref[pl.ds(t, 1), :])
            state_ref[...] = before_ref[length - (position + 1) * group]
            return (adjoint_in, rate)

        adjoint_end, rate_end = lax.fori_loop(
            0, length // group, retreat, (adjoint_ref[...], rate_ref[...])
        )
        adjoint_ref[...] = adjoint_end
        rate_ref[...] = rate_end

    row_spec = pl.BlockSpec((length, width), lambda i: (blocks - 1 - i, 0))
    entry_spec = pl.BlockSpec((length, entries, LANES), lambda i: (blocks - 1 - i, 0, 0))
    fixed = pl.BlockSpec((entries, width), lambda i: (0, 0))
    wide = jax.ShapeDtypeStruct((rows, width), jnp.float32)
    partial = jax.ShapeDtypeStruct((rows, entries, LANES), jnp.float32)
    return pl.pallas_call(
        kernel,
        grid=(blocks,),
        out_shape=(
            wide,
            wide,
            partial,
            partial,
            jax.ShapeDtypeStruct((entries, width), jnp.float32),
        ),
        in_specs=[
            fixed,
            fixed,
            pl.BlockSpec((length, entries, width), lambda i: (blocks - 1 - i, 0, 0)),
            row_spec,
            row_spec,
            entry_spec,
            entry_spec,
            row_spec,
            fixed,
        ],
        out_specs=(row_spec, row_spec, entry_spec, entry_spec, fixed),
        scratch_shapes=[pltpu.VMEM((entries, width), jnp.float32)] * 2,
        compiler_params=pltpu.CompilerParams(vmem_limit_bytes=14 * MEBI),
        cost_estimate=lasting(15),
        name="adjoint_sweep",
    )(
        incoming,
        last_state,
        pltpu.with_memory_space_constraint(befores, pltpu.HBM),
        steps,
        drives,
        inject,
        readout,
        upstream,
        slopes,
    )


def over_rows(left, right):
    return lax.dot_general(left, right, (((0,), (0,)), ((), ())), preferred_element_type=jnp.float32)


def over_columns(left, right):
    return lax.dot_general(left, right, (((1,), (1,)), ((), ())), preferred_element_type=jnp.float32)


def stand_up(rows, target, shared_heads):
    count, width = rows.shape
    heads = width // HEAD_DIM
    group = heads // shared_heads
    turned = rows.astype(jnp.float32).T.astype(target.dtype)
    target[...] = jnp.zeros_like(target)
    for head in range(heads):
        shared = head // group
        target[shared * HEAD_DIM : (shared + 1) * HEAD_DIM, head * count : (head + 1) * count] = (
            turned[head * HEAD_DIM : (head + 1) * HEAD_DIM]
        )


def lie_down(upright, count, shared_heads):
    heads = upright.shape[1] // count
    group = heads // shared_heads
    blocks = []
    for head in range(heads):
        shared = head // group
        blocks.append(
            upright[
                shared * HEAD_DIM : (shared + 1) * HEAD_DIM, head * count : (head + 1) * count
            ]
        )
    return jnp.concatenate(blocks, axis=0).T


def hidden_bias(key_docs, query_docs, diagonal):
    key_count, query_count = key_docs.shape[0], query_docs.shape[1]
    shape = (key_count, query_count)
    earlier = lax.broadcasted_iota(jnp.int32, shape, 0) <= lax.broadcasted_iota(
        jnp.int32, shape, 1
    )
    bias = jnp.where(key_docs == query_docs, 0.0, masked_score)
    return jnp.where(jnp.logical_or(earlier, jnp.logical_not(diagonal)), bias, masked_score)


def attend(queries, both, key_docs, query_docs, number):
    rows, width = queries.shape
    key_width = both.shape[1] // 2
    shared_heads = key_width // HEAD_DIM
    heads = width // HEAD_DIM
    seq_count = lax.axis_size("seq")
    pairs = seq_count // 2
    scale = 0.125 * LOG2E

    def kernel(
        q_ref,
        x_ref,
        kd_ref,
        qd_ref,
        low_ref,
        att_ref,
        lse_ref,
        kv_ref,
        qt_ref,
        max_ref,
        sum_ref,
        send,
        recv,
        pass_send,
        pass_recv,
    ):
        me = lax.axis_index("seq")
        place = me % 2
        pair = me // 2
        partner, *others = pair_peers()
        meet([partner] + others)

        first = [
            send_to(x_ref, kv_ref.at[me], send.at[k], recv.at[k], others[k])
            for k in range(pairs - 1)
        ]
        across = send_to(x_ref, kv_ref.at[me], pass_send.at[0], pass_recv.at[0], partner)
        across.start()
        for copy in first:
            copy.start()
        kv_ref[me] = x_ref[...]
        stand_up(q_ref[...], qt_ref, shared_heads)

        def block(owner, own):
            keys = x_ref[:, :key_width] if own else kv_ref[owner, :, :key_width]
            values = x_ref[:, key_width:] if own else kv_ref[owner, :, key_width:]
            begin = pl.multiple_of(owner * rows, rows)
            bias = hidden_bias(kd_ref[pl.ds(begin, rows), :], qd_ref[...], own)
            for head in range(heads):
                columns = slice(head * rows, (head + 1) * rows)
                scores = product(keys, qt_ref[:, columns]) * scale + bias
                top = jnp.max(scores, axis=0, keepdims=True)
                if not own:
                    old = max_ref[:, columns]
                    top = jnp.maximum(top, old)
                weights = jnp.exp2(scores - top)
                total = jnp.sum(weights, axis=0, keepdims=True)
                weighted = over_rows(values, to_low(weights))
                if not own:
                    factor = jnp.exp2(old - top)
                    total = total + sum_ref[:, columns] * factor
                    weighted = weighted + att_ref[:, columns] * factor
                max_ref[:, columns] = top
                sum_ref[:, columns] = total
                att_ref[:, columns] = weighted

        def earlier(owner):
            @pl.when(owner < me)
            def visit():
                block(owner, False)

        block(me, True)
        for k in range(1, pairs):
            first[k - 1].wait_recv()
            origin = ((pair - k + pairs) % pairs) * 2 + place
            passed = send_to(
                kv_ref.at[origin], kv_ref.at[origin], pass_send.at[k], pass_recv.at[k], partner
            )
            passed.start()
            if k == 1:
                across.wait_recv()
                earlier(me + 1 - 2 * place)
            earlier(origin)

        @pl.loop(1, pairs)
        def arrived(k):
            origin = ((pair - k + pairs) % pairs) * 2 + place
            other = origin + 1 - 2 * place
            send_to(
                kv_ref.at[origin], kv_ref.at[origin], pass_send.at[k], pass_recv.at[k], partner
            ).wait_recv()
            earlier(other)

        att_ref[...] = att_ref[...] / sum_ref[...]
        lse_ref[...] = max_ref[...] + jnp.log2(sum_ref[...])
        low_ref[...] = to_low(lie_down(att_ref, rows, shared_heads))
        for copy in first + [across]:
            copy.wait_send()

        @pl.loop(1, pairs)
        def sent(k):
            origin = ((pair - k + pairs) % pairs) * 2 + place
            send_to(
                kv_ref.at[origin], kv_ref.at[origin], pass_send.at[k], pass_recv.at[k], partner
            ).wait_send()

    return pl.pallas_call(
        kernel,
        out_shape=(
            jax.ShapeDtypeStruct((rows, width), jnp.bfloat16),
            jax.ShapeDtypeStruct((key_width, heads * rows), jnp.float32),
            jax.ShapeDtypeStruct((1, heads * rows), jnp.float32),
            jax.ShapeDtypeStruct((seq_count,) + both.shape, both.dtype),
        ),
        in_specs=[VMEM] * 4,
        out_specs=(VMEM,) * 4,
        scratch_shapes=[
            pltpu.VMEM((key_width, heads * rows), jnp.bfloat16),
            pltpu.VMEM((1, heads * rows), jnp.float32),
            pltpu.VMEM((1, heads * rows), jnp.float32),
        ]
        + [pltpu.SemaphoreType.DMA((pairs,))] * 4,
        compiler_params=talking(number, 24),
        cost_estimate=lasting(12),
        name="attend",
    )(queries, both, key_docs, query_docs)


def attend_back(own, queries, upstream, both_rows, key_docs, query_docs, attended, log_sum):
    rows, width = queries.shape
    total_rows = both_rows.shape[0]
    key_width = both_rows.shape[1] // 2
    shared_heads = key_width // HEAD_DIM
    heads = width // HEAD_DIM
    scale = 0.125 * LOG2E

    def kernel(
        own_ref, q_ref, up_ref, kv_ref, kd_ref, qd_ref, att_ref, lse_ref, qg_ref, kg_ref, vg_ref, qt_ref, ut_ref, acc_ref
    ):
        stand_up(q_ref[...], qt_ref, shared_heads)
        stand_up(up_ref[...], ut_ref, shared_heads)
        me = own_ref[0]
        delta = jnp.sum(ut_ref[...].astype(jnp.float32) * att_ref[...], axis=0, keepdims=True)
        acc_ref[...] = jnp.zeros_like(acc_ref)

        @pl.loop(me + 1, total_rows // rows)
        def later(position):
            begin = pl.multiple_of(position * rows, rows)
            kg_ref[pl.ds(begin, rows), :] = jnp.zeros((rows, key_width), jnp.bfloat16)
            vg_ref[pl.ds(begin, rows), :] = jnp.zeros((rows, key_width), jnp.bfloat16)

        @pl.loop(0, me + 1)
        def block(position):
            begin = pl.multiple_of(position * rows, rows)
            keys = kv_ref[pl.ds(begin, rows), :key_width]
            values = kv_ref[pl.ds(begin, rows), key_width:]
            bias = hidden_bias(kd_ref[pl.ds(begin, rows), :], qd_ref[...], position == me)
            key_grad = jnp.zeros((rows, key_width), jnp.float32)
            value_grad = jnp.zeros((rows, key_width), jnp.float32)
            for head in range(heads):
                columns = slice(head * rows, (head + 1) * rows)
                query = qt_ref[:, columns]
                upper = ut_ref[:, columns]
                probs = jnp.exp2(product(keys, query) * scale + bias - lse_ref[:, columns])
                value_grad = value_grad + over_columns(to_low(probs), upper)
                score_grad = to_low(probs * (product(values, upper) - delta[:, columns]))
                key_grad = key_grad + over_columns(score_grad, query)
                acc_ref[:, columns] += over_rows(keys, score_grad)
            kg_ref[pl.ds(begin, rows), :] = to_low(key_grad * 0.125)
            vg_ref[pl.ds(begin, rows), :] = to_low(value_grad)

        qg_ref[...] = to_low(lie_down(acc_ref, rows, shared_heads) * 0.125)

    return pl.pallas_call(
        kernel,
        out_shape=(
            jax.ShapeDtypeStruct((rows, width), jnp.bfloat16),
            jax.ShapeDtypeStruct((total_rows, key_width), jnp.bfloat16),
            jax.ShapeDtypeStruct((total_rows, key_width), jnp.bfloat16),
        ),
        in_specs=[pl.BlockSpec(memory_space=pltpu.SMEM)] + [VMEM] * 7,
        out_specs=(VMEM,) * 3,
        scratch_shapes=[
            pltpu.VMEM((key_width, heads * rows), jnp.bfloat16),
            pltpu.VMEM((key_width, heads * rows), jnp.bfloat16),
            pltpu.VMEM((key_width, heads * rows), jnp.float32),
        ],
        compiler_params=pltpu.CompilerParams(vmem_limit_bytes=28 * MEBI),
        cost_estimate=lasting(20),
        name="attend_back",
    )(own, queries, upstream, both_rows, key_docs, query_docs, attended, log_sum)


def body(
    tokens_in,
    cotangent,
    document_ids,
    expert_routes,
    norm_mixer,
    mixer_inner,
    mixer_gate,
    conv_taps,
    conv_bias,
    state_proj,
    step_proj,
    step_bias,
    decay_log,
    skip_gain,
    mixer_out,
    norm_ffn,
    ffn_gate,
    ffn_up,
    ffn_down,
    norm_attn,
    attn_query,
    attn_key,
    attn_value,
    attn_output,
    norm_moe,
    router,
    expert_gate,
    expert_up,
    expert_down,
):
    numbers = itertools.count()
    seq_count = lax.axis_size("seq")
    row_count = tokens_in.shape[0]
    total_rows = seq_count * row_count
    first_row = lax.axis_index("seq") * row_count
    last_row = first_row + row_count - 1

    me = lax.axis_index("seq")
    bit_count = seq_count.bit_length() - 1
    across_first = [0] + list(range(1, bit_count))
    along_first = [1, 0] + list(range(2, bit_count))

    def by_owner(values, bits):
        turned = values.transpose(0, 2, 1)
        own_rows = turned.shape[1] // seq_count
        order = [0]
        for bit in reversed(bits):
            order = order + [j + (1 << bit) for j in order]
        blocks = []
        for j in order:
            owner = me
            for bit in range(bit_count):
                if j >> bit & 1:
                    owner = owner + (1 << bit) * (1 - 2 * ((owner >> bit) & 1))
            blocks.append(lax.dynamic_slice_in_dim(turned, owner * own_rows, own_rows, 1))
        half = len(blocks) // 2
        return (
            jnp.concatenate(blocks[half:], axis=1),
            jnp.concatenate(blocks[:half], axis=1),
        ), bits

    def over_tokens(rows, columns):
        if rows.shape[0] == 1:
            return product(rows[0], columns[0])[None]
        return jnp.einsum("bdt,btf->bdf", rows, columns, preferred_element_type=jnp.float32)

    def begin_sum(*parts):
        flow = prepare_sum(*parts)
        send(flow)
        return flow

    def prepare_sum(*parts):
        flow = {"parts": parts, "bits": parts[0][0][1], "got": []}
        settle(flow)
        return flow

    def send(flow):
        bit = flow["bits"][len(flow["got"])]
        route = [(i, i ^ (1 << bit)) for i in range(seq_count)]
        flow["got"].append(lax.ppermute(flow["out"], "seq", route))

    def bind(values, *flows):
        tied = lax.optimization_barrier((values, *[flow["out"] for flow in flows]))
        for flow, out in zip(flows, tied[1:], strict=True):
            flow["out"] = out
        return tied[0]

    def settle(flow):
        step = len(flow["got"])
        if step < 2:
            gradients = [over_tokens(rows[0][step], columns) for rows, columns in flow["parts"]]
            total = gradients[0] if len(gradients) == 1 else jnp.concatenate(gradients, axis=2)
            if step == 0:
                flow["out"] = to_low(total)
                return
            flow["own"] = total + flow["got"][0].astype(jnp.float32)
        count = flow["own"].shape[1] >> (step - 1)
        half = count // 2
        last = step == len(flow["bits"])
        part = slice(0, count) if last else slice(half, count)
        total = flow["own"][:, part]
        for got in flow["got"][1:]:
            total = total + got[:, part].astype(jnp.float32)
        flow["total" if last else "out"] = total if last else to_low(total)

    def hold(values, *flows):
        if flows:
            tied = lax.optimization_barrier((values, *[flow["got"][-1] for flow in flows]))
            values = tied[0]
            for flow, got in zip(flows, tied[1:], strict=True):
                flow["got"][-1] = got
        return values

    def after(values, *flows):
        values = hold(values, *flows)
        for flow in flows:
            settle(flow)
            if "total" not in flow:
                send(flow)
        return values

    def finished(flow):
        while "total" not in flow:
            settle(flow)
            if "total" not in flow:
                send(flow)
        return flow["total"]

    def branch_sum(values):
        return head_sum(values, next(numbers), jnp.bfloat16, 4)

    local_docs = lax.dynamic_slice_in_dim(document_ids, first_row, row_count)
    reach = conv_taps.shape[0] - 1
    border = jnp.arange(reach, dtype=jnp.int32)
    docs_before = jnp.take(document_ids, jnp.maximum(first_row - reach + border, 0))
    docs_after = jnp.take(document_ids, jnp.minimum(first_row + row_count + border, total_rows - 1))
    docs_prior = jnp.concatenate([docs_before[reach - 1 :], local_docs[:-1]])
    retain = (local_docs == docs_prior).astype(jnp.float32)
    tokens = tokens_in.astype(jnp.float32)
    gain_mixer = norm_mixer.astype(jnp.float32)
    normed_one = to_low(rms_scale(tokens, gain_mixer))
    conv_in = to_low(product(normed_one, mixer_inner))
    gate_in = product(normed_one, mixer_gate)
    conv_edge = from_behind(conv_in[row_count - reach :], "seq", 1)
    extended = jnp.concatenate([conv_edge, conv_in]).astype(jnp.float32)
    docs_ext = jnp.concatenate([docs_before, local_docs])
    taps = conv_taps.astype(jnp.float32)
    conv_sum = conv_bias.astype(jnp.float32)[None, :]
    masks = []
    for offset in range(reach + 1):
        same_doc = (docs_ext[offset : offset + row_count] == local_docs).astype(jnp.float32)[
            :, None
        ]
        masks.append(same_doc)
        conv_sum = conv_sum + taps[offset] * extended[offset : offset + row_count] * same_doc
    activated = jax.nn.silu(conv_sum)
    act_low = to_low(activated)
    projected = head_sum(product(act_low, state_proj), next(numbers), jnp.float32, 1)
    rank_size = step_proj.shape[0]
    state_size = decay_log.shape[1]
    step_low = to_low(projected[:, :rank_size])
    inject = projected[:, rank_size : rank_size + state_size]
    readout = projected[:, rank_size + state_size :]
    step_pre = product(step_low, step_proj) + step_bias.astype(jnp.float32)
    step_dt = jax.nn.softplus(step_pre)
    decay_rate = jnp.exp(decay_log.astype(jnp.float32)).T
    slopes = -LOG2E * decay_rate
    steps = jnp.where(retain[:, None] > 0.0, step_dt, NEVER)
    drives = step_dt * activated
    inject_wide = spread(inject)
    readout_wide = spread(readout)
    state_in = run_summary(steps, drives, inject_wide, slopes, next(numbers), True)
    scanned, befores, state_out = state_sweep(
        state_in, steps, drives, inject_wide, readout_wide, slopes
    )
    skipping = skip_gain.astype(jnp.float32)
    mixed_state = scanned + skipping * activated
    gate_act = jax.nn.silu(gate_in)
    gated = to_low(mixed_state * gate_act)
    hidden_one = tokens + branch_sum(product(gated, mixer_out))
    gain_ffn = norm_ffn.astype(jnp.float32)
    normed_two = to_low(rms_scale(hidden_one, gain_ffn))
    gate_two = product(normed_two, ffn_gate)
    up_two = product(normed_two, ffn_up)
    ffn_act = to_low(jax.nn.silu(gate_two) * up_two)
    hidden_two = hidden_one + branch_sum(product(ffn_act, ffn_down))
    gain_attn = norm_attn.astype(jnp.float32)
    normed_three = to_low(rms_scale(hidden_two, gain_attn))
    queries = to_low(product(normed_three, attn_query))
    key_rows = to_low(product(normed_three, attn_key))
    value_rows = to_low(product(normed_three, attn_value))
    key_width = key_rows.shape[1]
    own_place = lax.axis_index("seq").reshape(1)
    key_docs = document_ids[:, None]
    query_docs = local_docs[None, :]
    attended_low, attended, log_sum, both_rows = attend(
        queries,
        jnp.concatenate([key_rows, value_rows], axis=1),
        key_docs,
        query_docs,
        next(numbers),
    )
    both_rows = both_rows.reshape(total_rows, -1)
    hidden_three = hidden_two + branch_sum(product(attended_low, attn_output))
    gain_moe = norm_moe.astype(jnp.float32)
    normed_four = to_low(rms_scale(hidden_three, gain_moe))
    logits = product(normed_four, router)
    expert_count = router.shape[1]
    experts = jnp.arange(expert_count, dtype=jnp.int32)
    named = (expert_routes[:, :, None] == experts).astype(jnp.float32)
    lead = jnp.sum((named[:, 0] - named[:, 1]) * logits, axis=1, keepdims=True)
    gate_weights = jax.nn.sigmoid(jnp.concatenate([lead, -lead], axis=1))
    route_flat = expert_routes.reshape(-1)
    pair_count = route_flat.shape[0]
    pair_order = jnp.arange(pair_count, dtype=jnp.int32)
    earlier = (pair_order[None, :] < pair_order[:, None]) & (
        route_flat[None, :] == route_flat[:, None]
    )
    within = jnp.sum(earlier.astype(jnp.int32), axis=1)
    slot_index = (route_flat * CAP + within).reshape(row_count, 2)
    slots = jnp.arange(expert_count * CAP, dtype=jnp.int32)
    first_hit = slot_index[:, 0][None, :] == slots[:, None]
    second_hit = slot_index[:, 1][None, :] == slots[:, None]
    placing = (first_hit | second_hit).astype(jnp.bfloat16)
    slot_gates = jnp.sum(
        jnp.where(first_hit, gate_weights[:, 0][None, :], 0.0)
        + jnp.where(second_hit, gate_weights[:, 1][None, :], 0.0),
        axis=1,
    )
    expert_in = to_low(product(placing, normed_four)).reshape(expert_count, CAP, -1)
    slot_upstream = product(placing, cotangent)
    res_grad = to_low(slot_gates[:, None] * slot_upstream).reshape(expert_count, CAP, -1)
    gate_four = jnp.einsum(
        "ecd,edf->ecf", expert_in, expert_gate, preferred_element_type=jnp.float32
    )
    up_four = jnp.einsum("ecd,edf->ecf", expert_in, expert_up, preferred_element_type=jnp.float32)
    expert_act = to_low(jax.nn.silu(gate_four) * up_four)
    expert_res = jnp.einsum(
        "ecf,efd->ecd", expert_act, expert_down, preferred_element_type=jnp.float32
    ).reshape(expert_count * CAP, -1)
    upstream = cotangent.astype(jnp.float32)
    slot_dots = jnp.sum(expert_res * slot_upstream, axis=1)
    dots_part = jnp.stack(
        [
            jnp.sum(jnp.where(first_hit, slot_dots[:, None], 0.0), axis=0),
            jnp.sum(jnp.where(second_hit, slot_dots[:, None], 0.0), axis=0),
        ],
        axis=1,
    )
    combined = product(placing.T, to_low(slot_gates[:, None] * expert_res))
    act_back = to_low(
        jnp.einsum("ecd,efd->ecf", res_grad, expert_down, preferred_element_type=jnp.float32)
    ).astype(jnp.float32)
    gating_grad = to_low(act_back * up_four * silu_slope(gate_four))
    upward_grad = to_low(act_back * jax.nn.silu(gate_four))
    flow_expert_down = begin_sum((by_owner(res_grad, along_first), expert_act))
    expert_rows = by_owner(expert_in, across_first)
    flow_expert_in = begin_sum(
        (expert_rows, jnp.concatenate([gating_grad, upward_grad], axis=2))
    )
    slot_grads = (
        jnp.einsum("ecf,edf->ecd", gating_grad, expert_gate, preferred_element_type=jnp.float32)
        + jnp.einsum("ecf,edf->ecd", upward_grad, expert_up, preferred_element_type=jnp.float32)
    ).reshape(expert_count * CAP, -1)
    token_part = product(placing.T, to_low(slot_grads))
    model_width = tokens.shape[1]
    expert_sums = branch_sum(
        jnp.concatenate(
            [token_part, jnp.pad(dots_part, ((0, 0), (0, LANES - 2)))], axis=1
        )
    )
    normed_grad = expert_sums[:, :model_width]
    dots = expert_sums[:, model_width : model_width + 2]
    chosen_grad = gate_weights * (dots - jnp.sum(gate_weights * dots, axis=1, keepdims=True))
    logit_grad = jnp.sum(named * chosen_grad[:, :, None], axis=1)
    grad_router = exact_product(normed_four.astype(jnp.float32).T, logit_grad)
    normed_grad = normed_grad + exact_product(logit_grad, router.astype(jnp.float32).T)
    hidden_grad, grad_norm_moe = rms_back(hidden_three, gain_moe, normed_grad)
    three_grad = upstream + hidden_grad
    branch_grad = to_low(three_grad)
    attn_out_rows = by_owner(branch_grad[None], across_first)
    attended_grad = to_low(product(branch_grad, attn_output.T))
    query_grad, key_part, value_part = attend_back(
        own_place, queries, attended_grad, both_rows, key_docs, query_docs, attended, log_sum
    )
    key_part = hold(key_part, flow_expert_down)
    key_sum, value_sum, combined_sum = scatter_and_head_sum(
        [key_part, value_part], combined, next(numbers)
    )
    mixed_out = to_low(hidden_three + combined_sum)
    key_sum, attended_late = lax.optimization_barrier((key_sum, attended_low))
    key_sum = after(key_sum, flow_expert_down, flow_expert_in)
    key_grad = to_low(key_sum)
    value_grad = to_low(value_sum)
    flow_attn = begin_sum(
        (
            by_owner(normed_three[None], across_first),
            jnp.concatenate([query_grad, key_grad, value_grad], axis=1)[None],
        ),
        (attn_out_rows, attended_late[None]),
    )
    normed_part = (
        product(query_grad, attn_query.T)
        + product(key_grad, attn_key.T)
        + product(value_grad, attn_value.T)
    )
    normed_grad = branch_sum(normed_part)
    hidden_grad, grad_norm_attn = rms_back(hidden_two, gain_attn, normed_grad)
    two_grad = three_grad + hidden_grad
    branch_grad = to_low(two_grad)
    flow_ffn_down = begin_sum((by_owner(branch_grad[None], along_first), ffn_act[None]))
    ffn_back = to_low(product(branch_grad, ffn_down.T))
    ffn_back = after(ffn_back, flow_expert_down, flow_expert_in, flow_attn).astype(jnp.float32)
    feed_gate_grad = to_low(ffn_back * up_two * silu_slope(gate_two))
    feed_up_grad = to_low(ffn_back * jax.nn.silu(gate_two))
    feed_rows = by_owner(normed_two[None], across_first)
    flow_ffn_gate = begin_sum((feed_rows, feed_gate_grad[None]))
    normed_part = product(feed_gate_grad, ffn_gate.T) + product(feed_up_grad, ffn_up.T)
    normed_grad = branch_sum(normed_part)
    hidden_grad, grad_norm_ffn = rms_back(hidden_one, gain_ffn, normed_grad)
    one_grad = two_grad + hidden_grad
    branch_grad = to_low(one_grad)
    mixer_out_rows = by_owner(branch_grad[None], across_first)
    gated_grad = to_low(product(branch_grad, mixer_out.T)).astype(jnp.float32)
    scan_grad = gated_grad * gate_act
    gate_in_grad = to_low(gated_grad * mixed_state * silu_slope(gate_in))
    grad_skip_gain = jnp.sum(scan_grad * activated, axis=0)
    early_flows = (flow_expert_down, flow_expert_in, flow_attn, flow_ffn_down, flow_ffn_gate)
    flow_ffn_up = prepare_sum((feed_rows, feed_up_grad[None]))
    flow_mixer_gate = prepare_sum((by_owner(normed_one[None], along_first), gate_in_grad[None]))
    flow_mixer_out = prepare_sum((mixer_out_rows, gated[None]))
    late_flows = (flow_ffn_up, flow_mixer_gate, flow_mixer_out)
    scan_grad = bind(scan_grad, *late_flows)
    scan_grad = hold(scan_grad, *early_flows)
    state_after = run_summary(steps, scan_grad, readout_wide, slopes, next(numbers), False)
    state_after = bind(state_after, *late_flows)
    state_after = after(state_after, flow_attn, flow_ffn_gate)
    send(flow_ffn_up)
    send(flow_mixer_gate)
    through_sum, injected, inject_part, readout_part, rate_sum = adjoint_sweep(
        state_after,
        state_out,
        befores,
        steps,
        drives,
        inject_wide,
        readout_wide,
        scan_grad,
        slopes,
    )
    step_grad = LN2 * through_sum + activated * injected
    input_grad = step_dt * injected
    inject_grad = jnp.sum(inject_part, axis=2)
    readout_grad = jnp.sum(readout_part, axis=2)
    grad_decay_log = -rate_sum * decay_rate
    pre_grad = step_grad * jax.nn.sigmoid(step_pre)
    grad_step_bias = jnp.sum(pre_grad, axis=0)
    pre_low = to_low(pre_grad)
    pre_low = bind(pre_low, flow_mixer_out)
    pre_low = after(pre_low, flow_ffn_up, flow_ffn_gate, flow_ffn_down, flow_attn)
    send(flow_mixer_out)
    grad_step_proj = product(pre_low.T, step_low)
    proj_part = jnp.concatenate([product(pre_low, step_proj.T), inject_grad, readout_grad], axis=1)
    proj_low = to_low(head_sum(proj_part, next(numbers), jnp.float32, 1))
    proj_low = after(proj_low, flow_mixer_gate, flow_ffn_down)
    grad_state_proj = product(act_low.T, proj_low)
    act_total = input_grad + skipping * scan_grad + product(proj_low, state_proj.T)
    conv_grad = act_total * silu_slope(conv_sum)
    conv_grad = after(conv_grad, flow_ffn_up, flow_mixer_out, flow_ffn_gate)
    grad_conv_bias = jnp.sum(conv_grad, axis=0)
    after_edge = from_behind(conv_grad[:reach], "seq", -1)
    after_edge = after(after_edge, flow_ffn_down)
    grad_ext = jnp.concatenate([conv_grad, after_edge])
    docs_next = jnp.concatenate([local_docs, docs_after])
    conv_in_grad = jnp.zeros_like(conv_grad)
    tap_rows = []
    for offset in range(reach + 1):
        tap_rows.append(
            jnp.sum(conv_grad * extended[offset : offset + row_count] * masks[offset], axis=0)
        )
        lead = reach - offset
        same_next = (docs_next[lead : lead + row_count] == local_docs).astype(jnp.float32)[:, None]
        conv_in_grad = conv_in_grad + taps[offset] * grad_ext[lead : lead + row_count] * same_next
    grad_conv_taps = jnp.stack(tap_rows)
    conv_low = to_low(conv_in_grad)
    inner_half = conv_low.shape[1] // 2
    grad_mixer_inner = to_low(product(normed_one.T, conv_low))
    normed_part = product(conv_low, mixer_inner.T) + product(gate_in_grad, mixer_gate.T)
    own_channels = grad_conv_bias.shape[0] // seq_count

    def cut(values):
        return values.reshape(seq_count, -1)

    channel_rows = jnp.concatenate(
        [grad_state_proj, jnp.pad(grad_step_proj, ((0, 0), (0, LANES - rank_size)))], axis=1
    )
    packed = jnp.concatenate(
        [
            cut(grad_decay_log.T),
            cut(grad_norm_ffn),
            cut(grad_norm_attn),
            cut(grad_norm_moe),
            cut(grad_router),
            cut(grad_conv_taps.T),
            cut(grad_conv_bias),
            cut(grad_step_bias),
            cut(grad_skip_gain),
        ],
        axis=1,
    )
    spare = -packed.shape[1] % (16 * LANES)
    packed = to_low(jnp.pad(packed, ((0, 0), (0, spare)))).reshape(-1, LANES)
    packed = after(packed, flow_mixer_out, flow_mixer_gate)
    first_inner, second_inner, sum_rows, sum_packed, grad_tokens, grad_norm_mixer = last_sums(
        [
            grad_mixer_inner[:, :inner_half],
            grad_mixer_inner[:, inner_half:],
            to_low(channel_rows),
            packed,
        ],
        normed_part,
        tokens_in,
        gain_mixer[None, :],
        one_grad,
        next(numbers),
    )
    sum_attn = finished(flow_attn)[0]
    sum_expert_in = finished(flow_expert_in)
    expert_width = expert_gate.shape[2]
    sum_packed = sum_packed.reshape(-1)
    own_rows = model_width // seq_count
    taken = itertools.accumulate(
        [0, own_channels * state_size]
        + [own_rows] * 3
        + [own_rows * expert_count, own_channels * (reach + 1)]
        + [own_channels] * 3
    )
    bounds = list(taken)
    pieces = [sum_packed[low:high] for low, high in itertools.pairwise(bounds)]
    query_width = attn_query.shape[1]

    return (
        mixed_out,
        grad_tokens,
        lax.dynamic_slice_in_dim(grad_norm_mixer[0], me * own_rows, own_rows),
        jnp.concatenate([first_inner, second_inner], axis=1),
        finished(flow_mixer_gate)[0],
        pieces[5].reshape(own_channels, -1).T,
        pieces[6],
        sum_rows[:, :LANES],
        sum_rows[:, LANES : LANES + rank_size].T,
        pieces[7],
        pieces[0].reshape(own_channels, -1),
        pieces[8],
        finished(flow_mixer_out)[0].T,
        pieces[1],
        finished(flow_ffn_gate)[0],
        finished(flow_ffn_up)[0],
        finished(flow_ffn_down)[0].T,
        pieces[2],
        sum_attn[:, :query_width],
        sum_attn[:, query_width : query_width + key_width],
        sum_attn[:, query_width + key_width : query_width + 2 * key_width],
        sum_attn[:, query_width + 2 * key_width :].T,
        pieces[3],
        pieces[4].reshape(own_rows, -1),
        sum_expert_in[:, :, :expert_width],
        sum_expert_in[:, :, expert_width:],
        finished(flow_expert_down).transpose(0, 2, 1),
    )


def solution(mesh):
    in_specs = (
        P("seq", None),
        P("seq", None),
        P(),
        P("seq", None),
        P(),
        P(None, "head"),
        P(None, "head"),
        P(None, "head"),
        P("head"),
        P("head", None),
        P(None, "head"),
        P("head"),
        P("head", None),
        P("head"),
        P("head", None),
        P(),
        P(None, "head"),
        P(None, "head"),
        P("head", None),
        P(),
        P(None, "head"),
        P(None, "head"),
        P(None, "head"),
        P("head", None),
        P(),
        P(),
        P(None, None, "head"),
        P(None, None, "head"),
        P(None, "head", None),
    )
    out_specs = (
        P("seq", None),
        P("seq", None),
        P("seq"),
        P("seq", "head"),
        P("seq", "head"),
        P(None, ("head", "seq")),
        P(("head", "seq")),
        P(("head", "seq"), None),
        P(None, ("head", "seq")),
        P(("head", "seq")),
        P(("head", "seq"), None),
        P(("head", "seq")),
        P("head", "seq"),
        P("seq"),
        P("seq", "head"),
        P("seq", "head"),
        P("head", "seq"),
        P("seq"),
        P("seq", "head"),
        P("seq", "head"),
        P("seq", "head"),
        P("head", "seq"),
        P("seq"),
        P("seq", None),
        P(None, "seq", "head"),
        P(None, "seq", "head"),
        P(None, "head", "seq"),
    )
    return jax.shard_map(body, mesh=mesh, in_specs=in_specs, out_specs=out_specs, check_vma=False)
```

```python
import itertools
import math

import jax
import jax.numpy as jnp
from jax import lax
from jax.experimental import pallas as pl
from jax.experimental.pallas import tpu as pltpu
from jax.sharding import PartitionSpec as P

HEAD_DIM = 64
CAP = 160
LANES = 128
LOG2E = 1.4426950408889634
LN2 = 0.6931471805599453
NEVER = 1e30
MEBI = 1024 * 1024
MESH = pl.DeviceIdType.MESH
VMEM = pl.BlockSpec(memory_space=pltpu.VMEM)
ANY = pl.BlockSpec(memory_space=pl.ANY)


highest = lax.Precision.HIGHEST
epsilon = 1e-05
masked_score = -1e30


def from_behind(block, axis, distance):
    devices = range(lax.axis_size(axis))
    route = [(i - distance, i) for i in devices if i - distance in devices]
    return lax.ppermute(block, axis, route)


def to_low(values):
    return values.astype(jnp.bfloat16)


def product(left, right):
    return jnp.dot(left, right, preferred_element_type=jnp.float32)


def exact_product(left, right):
    return jnp.dot(left, right, precision=highest, preferred_element_type=jnp.float32)


def rms_scale(values, gain):
    return values * lax.rsqrt(jnp.mean(values * values, axis=-1, keepdims=True) + epsilon) * gain


def rms_back(values, gain, upstream):
    unused, pullback = jax.vjp(rms_scale, values, gain)
    return pullback(upstream)


def silu_slope(values):
    logistic = jax.nn.sigmoid(values)
    return logistic * (1.0 + values * (1.0 - logistic))


def meet(peers):
    barrier = pltpu.get_barrier_semaphore()
    for peer in peers:
        pl.semaphore_signal(barrier, inc=1, device_id=peer, device_id_type=MESH)
    pl.semaphore_wait(barrier, len(peers))


def send_to(source, target, send_sem, recv_sem, peer):
    return pltpu.make_async_remote_copy(
        src_ref=source,
        dst_ref=target,
        send_sem=send_sem,
        recv_sem=recv_sem,
        device_id=peer,
        device_id_type=MESH,
    )


def lasting(microseconds):
    return pl.CostEstimate(
        flops=int(microseconds * 1e3),
        bytes_accessed=int(microseconds * 1e3),
        transcendentals=0,
    )


def talking(number, mebibytes):
    return pltpu.CompilerParams(
        collective_id=number, has_side_effects=True, vmem_limit_bytes=mebibytes * MEBI
    )


def together(*jobs):
    waiting = list(jobs)
    while waiting:
        for job in list(waiting):
            if next(job, waiting) is waiting:
                waiting.remove(job)


def head_peers():
    seq = lax.axis_index("seq")
    head = lax.axis_index("head")
    return [(seq, head + 1 - 2 * (head % 2)), (seq, (head + 2) % 4)]


def head_scratch(rows, width, wire, pieces):
    return [pltpu.VMEM((rows // 2, width), wire)] * 4 + [
        pltpu.SemaphoreType.DMA((3, pieces)),
        pltpu.SemaphoreType.DMA((3, pieces)),
    ]


def head_job(x_ref, o_ref, scratch, wire, pieces):
    near_out, near_in, far_out, far_in, send, recv = scratch
    half = x_ref.shape[0] // 2
    step = half // pieces
    near, far = head_peers()
    core = lax.axis_index("head") % 2

    def rows_of(side, piece):
        return pl.ds(pl.multiple_of(side * half + piece * step, 8), step)

    first, second, third = [], [], []
    for piece in range(pieces):
        local = pl.ds(piece * step, step)
        near_out[local] = x_ref[rows_of(1 - core, piece)].astype(wire)
        first.append(
            send_to(
                near_out.at[local], near_in.at[local], send.at[0, piece], recv.at[0, piece], near
            )
        )
        first[-1].start()
    yield
    for piece in range(pieces):
        local = pl.ds(piece * step, step)
        first[piece].wait_recv()
        total = x_ref[rows_of(core, piece)] + near_in[local].astype(jnp.float32)
        far_out[local] = total.astype(wire)
        second.append(
            send_to(far_out.at[local], far_in.at[local], send.at[1, piece], recv.at[1, piece], far)
        )
        second[-1].start()
    yield
    for piece in range(pieces):
        local = pl.ds(piece * step, step)
        second[piece].wait_recv()
        whole = far_out[local].astype(jnp.float32) + far_in[local].astype(jnp.float32)
        o_ref[rows_of(core, piece)] = whole
        third.append(
            send_to(
                o_ref.at[rows_of(core, piece)],
                o_ref.at[rows_of(core, piece)],
                send.at[2, piece],
                recv.at[2, piece],
                near,
            )
        )
        third[-1].start()
    yield
    for copy in third:
        copy.wait_recv()
    for copy in first + second + third:
        copy.wait_send()


def head_sum(values, number, wire, pieces):
    rows, width = values.shape

    def kernel(x_ref, o_ref, *scratch):
        meet(head_peers())
        together(head_job(x_ref, o_ref, scratch, wire, pieces))

    return pl.pallas_call(
        kernel,
        out_shape=jax.ShapeDtypeStruct((rows, width), jnp.float32),
        in_specs=[VMEM],
        out_specs=VMEM,
        scratch_shapes=head_scratch(rows, width, wire, pieces),
        compiler_params=talking(number, 10),
        cost_estimate=lasting(6 + values.size // 40000),
        name="head_sum",
    )(values)


def pair_peers():
    seq = lax.axis_index("seq")
    head = lax.axis_index("head")
    pairs = lax.axis_size("seq") // 2
    place = seq % 2
    pair = seq // 2
    others = [(((pair + k) % pairs) * 2 + place, head) for k in range(1, pairs)]
    return [(seq + 1 - 2 * place, head)] + others


def level_count():
    return lax.axis_size("seq").bit_length() - 1


def level_peers():
    seq = lax.axis_index("seq")
    head = lax.axis_index("head")
    bits = [1 << level for level in range(level_count())]
    return [(seq + bit * (1 - 2 * ((seq // bit) % 2)), head) for bit in bits]


def scatter_shapes(arrays):
    seq_count = lax.axis_size("seq")
    return [(a.shape[0] // seq_count, a.shape[1]) for a in arrays]


def scatter_blocks(arrays):
    half = lax.axis_size("seq") // 2
    return [
        a.reshape(half, 2, shape[0], shape[1])
        for a, shape in zip(arrays, scatter_shapes(arrays), strict=True)
    ]


def scatter_scratch(shapes):
    half = lax.axis_size("seq") // 2
    levels = level_count()
    count = len(shapes)
    spaces = []
    for shape in shapes:
        for level in range(levels):
            spaces.append(pltpu.VMEM((half >> level,) + shape, jnp.bfloat16))
        for level in range(levels - 1):
            spaces.append(pltpu.VMEM((half >> level + 1, 2) + shape, jnp.bfloat16))
    return (
        spaces
        + [pltpu.SemaphoreType.DMA((count, half))]
        + [pltpu.SemaphoreType.DMA((count, levels))] * 2
    )


def scatter_job(takes, gives, scratch, shapes):
    count = len(takes)
    levels = level_count()
    half = lax.axis_size("seq") // 2
    own_sem, send, recv = scratch[-3:]
    per_array = 2 * levels - 1
    got = [scratch[i * per_array : i * per_array + levels] for i in range(count)]
    kept = [scratch[i * per_array + levels : (i + 1) * per_array] for i in range(count)]
    seq = lax.axis_index("seq")
    bits = [(seq // (1 << level)) % 2 for level in range(levels)]
    peers = level_peers()

    def exchange(i, level):
        source = takes[i] if level == 0 else kept[i][level - 1]
        return send_to(
            source.at[:, 1 - bits[level]],
            got[i][level],
            send.at[i, level],
            recv.at[i, level],
            peers[level],
        )

    loads = [
        [
            pltpu.make_async_copy(
                takes[i].at[j, bits[0]], kept[i][0].at[j // 2, j % 2], own_sem.at[i, j]
            )
            for j in range(half)
        ]
        for i in range(count)
    ]
    sent = []

    def launch(i, level):
        copy = exchange(i, level)
        copy.start()
        sent.append(copy)
        if level == 0:
            for load in loads[i]:
                load.start()

    def merge(i, level):
        exchange(i, level).wait_recv()
        if level == 0:
            for load in loads[i]:
                load.wait()

        @pl.loop(0, half >> level)
        def blocks(j):
            @pl.loop(0, shapes[i][0] // 16)
            def add(step):
                part = pl.ds(pl.multiple_of(step * 16, 16), 16)
                if level == 0:
                    mine = kept[i][0][j // 2, j % 2, part]
                else:
                    mine = kept[i][level - 1][j, bits[level], part]
                total = mine.astype(jnp.float32) + got[i][level][j, part].astype(jnp.float32)
                if level == levels - 1:
                    gives[i][part] = total
                else:
                    kept[i][level][j // 2, j % 2, part] = total.astype(jnp.bfloat16)

    launch(0, 0)
    if count > 1:
        launch(1, 0)
    for turn in range(count + levels - 1):
        for level in range(levels):
            i = turn - level
            if 0 <= i < count:
                yield
                merge(i, level)
                if level == 0 and i + 2 < count:
                    launch(i + 2, 0)
                if level + 1 < levels:
                    launch(i, level + 1)
    for copy in sent:
        copy.wait_send()


def scatter_and_head_sum(arrays, values, number):
    count = len(arrays)
    shapes = scatter_shapes(arrays)
    rows, width = values.shape
    spaces = scatter_scratch(shapes)

    def kernel(*refs):
        takes, x_ref = refs[:count], refs[count]
        gives, o_ref = refs[count + 1 : 2 * count + 1], refs[2 * count + 1]
        scratch = refs[2 * count + 2 :]
        meet(level_peers() + head_peers())
        together(
            scatter_job(takes, gives, scratch[: len(spaces)], shapes),
            head_job(x_ref, o_ref, scratch[len(spaces) :], jnp.bfloat16, 4),
        )

    return pl.pallas_call(
        kernel,
        out_shape=[jax.ShapeDtypeStruct(shape, jnp.float32) for shape in shapes]
        + [jax.ShapeDtypeStruct((rows, width), jnp.float32)],
        in_specs=[ANY] * count + [VMEM],
        out_specs=[VMEM] * (count + 1),
        scratch_shapes=spaces + head_scratch(rows, width, jnp.bfloat16, 4),
        compiler_params=talking(number, 24),
        cost_estimate=lasting(20),
        name="scatter_and_head_sum",
    )(*scatter_blocks(arrays), values)


def last_sums(arrays, values, tokens, gain, upstream, number):
    count = len(arrays)
    shapes = scatter_shapes(arrays)
    rows, width = values.shape
    seq_count = lax.axis_size("seq")
    spaces = scatter_scratch(shapes)
    step = 16

    def kernel(*refs):
        takes = refs[:count]
        x_ref, token_ref, gain_ref, up_ref = refs[count : count + 4]
        gives = refs[count + 4 : 2 * count + 4]
        grad_ref, gain_out = refs[2 * count + 4 : 2 * count + 6]
        scratch = refs[2 * count + 6 :]
        total_ref, part_out, part_in, part_send, part_recv = scratch[-5:]
        seq = lax.axis_index("seq")
        head = lax.axis_index("head")
        peers = [((seq + k) % seq_count, head) for k in range(1, seq_count)]
        meet(peers + head_peers())

        def norm_job():
            yield from head_job(x_ref, total_ref, scratch[len(spaces) : -5], jnp.bfloat16, 4)

            def back(position, gained):
                part = pl.ds(pl.multiple_of(position * step, step), step)
                token = token_ref[part].astype(jnp.float32)
                scale = lax.rsqrt(jnp.mean(token * token, axis=1, keepdims=True) + epsilon)
                unit = token * scale
                given = total_ref[part]
                scaled = given * gain_ref[...]
                pull = jnp.mean(scaled * unit, axis=1, keepdims=True)
                grad_ref[part] = up_ref[part] + scale * (scaled - unit * pull)
                product_rows = given * unit
                return gained + product_rows[:8] + product_rows[8:]

            gained = lax.fori_loop(0, rows // step, back, jnp.zeros((8, width), jnp.float32))
            part_out[...] = jnp.sum(gained, axis=0, keepdims=True)
            copies = [
                send_to(part_out, part_in.at[k], part_send.at[k], part_recv.at[k], peers[k])
                for k in range(seq_count - 1)
            ]
            for copy in copies:
                copy.start()
            yield
            for copy in copies:
                copy.wait_recv()
            whole = part_out[...]
            for k in range(seq_count - 1):
                whole = whole + part_in[k]
            gain_out[...] = whole
            for copy in copies:
                copy.wait_send()

        together(norm_job(), scatter_job(takes, gives, scratch[: len(spaces)], shapes))

    return pl.pallas_call(
        kernel,
        out_shape=[jax.ShapeDtypeStruct(shape, jnp.float32) for shape in shapes]
        + [
            jax.ShapeDtypeStruct((rows, width), jnp.float32),
            jax.ShapeDtypeStruct((1, width), jnp.float32),
        ],
        in_specs=[ANY] * count + [VMEM] * 4,
        out_specs=[VMEM] * (count + 2),
        scratch_shapes=spaces
        + head_scratch(rows, width, jnp.bfloat16, 4)
        + [
            pltpu.VMEM((rows, width), jnp.float32),
            pltpu.VMEM((1, width), jnp.float32),
            pltpu.VMEM((seq_count - 1, 1, width), jnp.float32),
            pltpu.SemaphoreType.DMA((seq_count - 1,)),
            pltpu.SemaphoreType.DMA((seq_count - 1,)),
        ],
        compiler_params=talking(number, 28),
        cost_estimate=lasting(20),
        name="last_sums",
    )(*scatter_blocks(arrays), values, tokens, gain, upstream)


def widen(column_block, width):
    return jnp.concatenate([column_block] * (width // LANES), axis=-1)


def narrow(wide):
    width = wide.shape[-1]
    total = wide[:, :LANES]
    for place in range(1, width // LANES):
        total = total + wide[:, place * LANES : (place + 1) * LANES]
    return total


def spread(columns):
    return jnp.broadcast_to(columns[:, :, None], columns.shape + (LANES,))


def run_summary(steps, drives, coefficients, slopes, number, forward):
    rows, width = steps.shape
    entries = slopes.shape[0]
    seq_count = lax.axis_size("seq")
    group = math.gcd(rows, 8)

    def kernel(
        step_ref,
        drive_ref,
        coef_ref,
        slope_ref,
        o_ref,
        outgoing,
        incoming,
        span_out,
        span_in,
        send,
        recv,
    ):
        seq = lax.axis_index("seq")
        head = lax.axis_index("head")
        peers = [((seq + k) % seq_count, head) for k in range(1, seq_count)]
        meet(peers)
        slope = slope_ref[...]
        span_out[...] = jnp.broadcast_to(
            jnp.sum(step_ref[...], axis=0, keepdims=True), span_out.shape
        )
        spans = [
            send_to(span_out, span_in.at[k], send.at[1, k], recv.at[1, k], peers[k])
            for k in range(seq_count - 1)
        ]
        for copy in spans:
            copy.start()

        def advance(position, state):
            for offset in range(group):
                t = position * group + offset
                t = t if forward else rows - 1 - t
                decays = jnp.exp2(step_ref[pl.ds(t, 1), :] * slope)
                drive = drive_ref[pl.ds(t, 1), :] * widen(coef_ref[t], width)
                state = state * decays + drive if forward else (state + drive) * decays
            return state

        state = lax.fori_loop(0, rows // group, advance, jnp.zeros((entries, width), jnp.float32))
        outgoing[...] = state.astype(jnp.bfloat16)
        copies = [
            send_to(outgoing, incoming.at[k], send.at[0, k], recv.at[0, k], peers[k])
            for k in range(seq_count - 1)
        ]
        for copy in copies:
            copy.start()
        for copy in spans:
            copy.wait_recv()
        for copy in copies:
            copy.wait_recv()
        carried = jnp.zeros((entries, width), jnp.float32)
        order = range(seq_count - 1, 0, -1) if forward else range(1, seq_count)
        for k in order:
            known = seq - k >= 0 if forward else seq - k < 0
            whole = jnp.exp2(span_in[k - 1][:1] * slope)
            carried = jnp.where(known, whole * carried + incoming[k - 1].astype(jnp.float32), 0.0)
        o_ref[...] = carried
        for copy in copies + spans:
            copy.wait_send()

    return pl.pallas_call(
        kernel,
        out_shape=jax.ShapeDtypeStruct((entries, width), jnp.float32),
        in_specs=[VMEM] * 4,
        out_specs=VMEM,
        scratch_shapes=[
            pltpu.VMEM((entries, width), jnp.bfloat16),
            pltpu.VMEM((seq_count - 1, entries, width), jnp.bfloat16),
            pltpu.VMEM((8, width), jnp.float32),
            pltpu.VMEM((seq_count - 1, 8, width), jnp.float32),
            pltpu.SemaphoreType.DMA((2, seq_count - 1)),
            pltpu.SemaphoreType.DMA((2, seq_count - 1)),
        ],
        compiler_params=talking(number, 10),
        cost_estimate=lasting(16),
        name="run_summary",
    )(steps, drives, coefficients, slopes)


def state_sweep(initial, steps, drives, inject, readout, slopes):
    rows, width = steps.shape
    entries = slopes.shape[0]
    length = math.gcd(rows, 32)
    group = math.gcd(length, 8)

    def kernel(
        init_ref, step_ref, drive_ref, inject_ref, read_ref, slope_ref, y_ref, before_ref, end_ref
    ):
        @pl.when(pl.program_id(0) == 0)
        def begin():
            end_ref[...] = init_ref[...]

        slope = slope_ref[...]

        def advance(position, state):
            for offset in range(group):
                t = position * group + offset
                before_ref[t] = state
                decays = jnp.exp2(step_ref[pl.ds(t, 1), :] * slope)
                drive = drive_ref[pl.ds(t, 1), :] * widen(inject_ref[t], width)
                state = state * decays + drive
                y_ref[pl.ds(t, 1), :] = jnp.sum(
                    state * widen(read_ref[t], width), axis=0, keepdims=True
                )
            return state

        end_ref[...] = lax.fori_loop(0, length // group, advance, end_ref[...])

    row_spec = pl.BlockSpec((length, width), lambda i: (i, 0))
    entry_spec = pl.BlockSpec((length, entries, LANES), lambda i: (i, 0, 0))
    fixed = pl.BlockSpec((entries, width), lambda i: (0, 0))
    return pl.pallas_call(
        kernel,
        grid=(rows // length,),
        out_shape=(
            jax.ShapeDtypeStruct((rows, width), jnp.float32),
            pltpu.HBM((rows, entries, width), jnp.float32),
            jax.ShapeDtypeStruct((entries, width), jnp.float32),
        ),
        in_specs=[fixed, row_spec, row_spec, entry_spec, entry_spec, fixed],
        out_specs=(
            row_spec,
            pl.BlockSpec((length, entries, width), lambda i: (i, 0, 0)),
            fixed,
        ),
        compiler_params=pltpu.CompilerParams(vmem_limit_bytes=12 * MEBI),
        cost_estimate=lasting(11),
        name="state_sweep",
    )(initial, steps, drives, inject, readout, slopes)


def adjoint_sweep(incoming, last_state, befores, steps, drives, inject, readout, upstream, slopes):
    rows, width = steps.shape
    entries = slopes.shape[0]
    length = math.gcd(rows, 32)
    group = math.gcd(length, 8)
    blocks = rows // length

    def kernel(
        in_ref,
        last_ref,
        before_ref,
        step_ref,
        drive_ref,
        inject_ref,
        read_ref,
        up_ref,
        slope_ref,
        through_ref,
        injected_ref,
        inject_out,
        read_out,
        rate_ref,
        adjoint_ref,
        state_ref,
    ):
        @pl.when(pl.program_id(0) == 0)
        def begin():
            adjoint_ref[...] = in_ref[...]
            state_ref[...] = last_ref[...]
            rate_ref[...] = jnp.zeros_like(rate_ref)

        slope = slope_ref[...]

        def retreat(position, carried):
            adjoint_in, rate = carried
            for offset in range(group):
                t = length - 1 - (position * group + offset)
                upper = up_ref[pl.ds(t, 1), :]
                step = step_ref[pl.ds(t, 1), :]
                adjoint = widen(read_ref[t], width) * upper + adjoint_in
                state = state_ref[...] if offset == 0 else before_ref[t + 1]
                read_out[t] = narrow(upper * state)
                adjoint_in = jnp.exp2(step * slope) * adjoint
                before = before_ref[t]
                through = adjoint_in * before
                rate = rate + through * step
                through_ref[pl.ds(t, 1), :] = jnp.sum(through * slope, axis=0, keepdims=True)
                injected_ref[pl.ds(t, 1), :] = jnp.sum(
                    adjoint * widen(inject_ref[t], width), axis=0, keepdims=True
                )
                inject_out[t] = narrow(adjoint * drive_ref[pl.ds(t, 1), :])
            state_ref[...] = before_ref[length - (position + 1) * group]
            return (adjoint_in, rate)

        adjoint_end, rate_end = lax.fori_loop(
            0, length // group, retreat, (adjoint_ref[...], rate_ref[...])
        )
        adjoint_ref[...] = adjoint_end
        rate_ref[...] = rate_end

    row_spec = pl.BlockSpec((length, width), lambda i: (blocks - 1 - i, 0))
    entry_spec = pl.BlockSpec((length, entries, LANES), lambda i: (blocks - 1 - i, 0, 0))
    fixed = pl.BlockSpec((entries, width), lambda i: (0, 0))
    wide = jax.ShapeDtypeStruct((rows, width), jnp.float32)
    partial = jax.ShapeDtypeStruct((rows, entries, LANES), jnp.float32)
    return pl.pallas_call(
        kernel,
        grid=(blocks,),
        out_shape=(
            wide,
            wide,
            partial,
            partial,
            jax.ShapeDtypeStruct((entries, width), jnp.float32),
        ),
        in_specs=[
            fixed,
            fixed,
            pl.BlockSpec((length, entries, width), lambda i: (blocks - 1 - i, 0, 0)),
            row_spec,
            row_spec,
            entry_spec,
            entry_spec,
            row_spec,
            fixed,
        ],
        out_specs=(row_spec, row_spec, entry_spec, entry_spec, fixed),
        scratch_shapes=[pltpu.VMEM((entries, width), jnp.float32)] * 2,
        compiler_params=pltpu.CompilerParams(vmem_limit_bytes=14 * MEBI),
        cost_estimate=lasting(15),
        name="adjoint_sweep",
    )(
        incoming,
        last_state,
        pltpu.with_memory_space_constraint(befores, pltpu.HBM),
        steps,
        drives,
        inject,
        readout,
        upstream,
        slopes,
    )


def over_rows(left, right):
    return lax.dot_general(left, right, (((0,), (0,)), ((), ())), preferred_element_type=jnp.float32)


def over_columns(left, right):
    return lax.dot_general(left, right, (((1,), (1,)), ((), ())), preferred_element_type=jnp.float32)


def stand_up(rows, target, shared_heads):
    count, width = rows.shape
    heads = width // HEAD_DIM
    group = heads // shared_heads
    turned = rows.astype(jnp.float32).T.astype(target.dtype)
    target[...] = jnp.zeros_like(target)
    for head in range(heads):
        shared = head // group
        target[shared * HEAD_DIM : (shared + 1) * HEAD_DIM, head * count : (head + 1) * count] = (
            turned[head * HEAD_DIM : (head + 1) * HEAD_DIM]
        )


def lie_down(upright, count, shared_heads):
    heads = upright.shape[1] // count
    group = heads // shared_heads
    blocks = []
    for head in range(heads):
        shared = head // group
        blocks.append(
            upright[
                shared * HEAD_DIM : (shared + 1) * HEAD_DIM, head * count : (head + 1) * count
            ]
        )
    return jnp.concatenate(blocks, axis=0).T


def hidden_bias(key_docs, query_docs, diagonal):
    key_count, query_count = key_docs.shape[0], query_docs.shape[1]
    shape = (key_count, query_count)
    earlier = lax.broadcasted_iota(jnp.int32, shape, 0) <= lax.broadcasted_iota(
        jnp.int32, shape, 1
    )
    bias = jnp.where(key_docs == query_docs, 0.0, masked_score)
    return jnp.where(jnp.logical_or(earlier, jnp.logical_not(diagonal)), bias, masked_score)


def attend(queries, both, key_docs, query_docs, number):
    rows, width = queries.shape
    key_width = both.shape[1] // 2
    shared_heads = key_width // HEAD_DIM
    heads = width // HEAD_DIM
    seq_count = lax.axis_size("seq")
    pairs = seq_count // 2
    scale = 0.125 * LOG2E

    def kernel(
        q_ref,
        x_ref,
        kd_ref,
        qd_ref,
        low_ref,
        att_ref,
        lse_ref,
        kv_ref,
        qt_ref,
        max_ref,
        sum_ref,
        send,
        recv,
        pass_send,
        pass_recv,
    ):
        me = lax.axis_index("seq")
        place = me % 2
        pair = me // 2
        partner, *others = pair_peers()
        meet([partner] + others)

        first = [
            send_to(x_ref, kv_ref.at[me], send.at[k], recv.at[k], others[k])
            for k in range(pairs - 1)
        ]
        across = send_to(x_ref, kv_ref.at[me], pass_send.at[0], pass_recv.at[0], partner)
        across.start()
        for copy in first:
            copy.start()
        kv_ref[me] = x_ref[...]
        stand_up(q_ref[...], qt_ref, shared_heads)

        def block(owner, own):
            keys = x_ref[:, :key_width] if own else kv_ref[owner, :, :key_width]
            values = x_ref[:, key_width:] if own else kv_ref[owner, :, key_width:]
            begin = pl.multiple_of(owner * rows, rows)
            bias = hidden_bias(kd_ref[pl.ds(begin, rows), :], qd_ref[...], own)
            for head in range(heads):
                columns = slice(head * rows, (head + 1) * rows)
                scores = product(keys, qt_ref[:, columns]) * scale + bias
                top = jnp.max(scores, axis=0, keepdims=True)
                if not own:
                    old = max_ref[:, columns]
                    top = jnp.maximum(top, old)
                weights = jnp.exp2(scores - top)
                total = jnp.sum(weights, axis=0, keepdims=True)
                weighted = over_rows(values, to_low(weights))
                if not own:
                    factor = jnp.exp2(old - top)
                    total = total + sum_ref[:, columns] * factor
                    weighted = weighted + att_ref[:, columns] * factor
                max_ref[:, columns] = top
                sum_ref[:, columns] = total
                att_ref[:, columns] = weighted

        def earlier(owner):
            @pl.when(owner < me)
            def visit():
                block(owner, False)

        block(me, True)
        for k in range(1, pairs):
            first[k - 1].wait_recv()
            origin = ((pair - k + pairs) % pairs) * 2 + place
            passed = send_to(
                kv_ref.at[origin], kv_ref.at[origin], pass_send.at[k], pass_recv.at[k], partner
            )
            passed.start()
            if k == 1:
                across.wait_recv()
                earlier(me + 1 - 2 * place)
            earlier(origin)

        @pl.loop(1, pairs)
        def arrived(k):
            origin = ((pair - k + pairs) % pairs) * 2 + place
            other = origin + 1 - 2 * place
            send_to(
                kv_ref.at[origin], kv_ref.at[origin], pass_send.at[k], pass_recv.at[k], partner
            ).wait_recv()
            earlier(other)

        att_ref[...] = att_ref[...] / sum_ref[...]
        lse_ref[...] = max_ref[...] + jnp.log2(sum_ref[...])
        low_ref[...] = to_low(lie_down(att_ref, rows, shared_heads))
        for copy in first + [across]:
            copy.wait_send()

        @pl.loop(1, pairs)
        def sent(k):
            origin = ((pair - k + pairs) % pairs) * 2 + place
            send_to(
                kv_ref.at[origin], kv_ref.at[origin], pass_send.at[k], pass_recv.at[k], partner
            ).wait_send()

    return pl.pallas_call(
        kernel,
        out_shape=(
            jax.ShapeDtypeStruct((rows, width), jnp.bfloat16),
            jax.ShapeDtypeStruct((key_width, heads * rows), jnp.float32),
            jax.ShapeDtypeStruct((1, heads * rows), jnp.float32),
            jax.ShapeDtypeStruct((seq_count,) + both.shape, both.dtype),
        ),
        in_specs=[VMEM] * 4,
        out_specs=(VMEM,) * 4,
        scratch_shapes=[
            pltpu.VMEM((key_width, heads * rows), jnp.bfloat16),
            pltpu.VMEM((1, heads * rows), jnp.float32),
            pltpu.VMEM((1, heads * rows), jnp.float32),
        ]
        + [pltpu.SemaphoreType.DMA((pairs,))] * 4,
        compiler_params=talking(number, 24),
        cost_estimate=lasting(12),
        name="attend",
    )(queries, both, key_docs, query_docs)


def attend_back(own, queries, upstream, both_rows, key_docs, query_docs, attended, log_sum):
    rows, width = queries.shape
    total_rows = both_rows.shape[0]
    key_width = both_rows.shape[1] // 2
    shared_heads = key_width // HEAD_DIM
    heads = width // HEAD_DIM
    scale = 0.125 * LOG2E

    def kernel(
        own_ref, q_ref, up_ref, kv_ref, kd_ref, qd_ref, att_ref, lse_ref, qg_ref, kg_ref, vg_ref, qt_ref, ut_ref, acc_ref
    ):
        stand_up(q_ref[...], qt_ref, shared_heads)
        stand_up(up_ref[...], ut_ref, shared_heads)
        me = own_ref[0]
        delta = jnp.sum(ut_ref[...].astype(jnp.float32) * att_ref[...], axis=0, keepdims=True)
        acc_ref[...] = jnp.zeros_like(acc_ref)

        @pl.loop(me + 1, total_rows // rows)
        def later(position):
            begin = pl.multiple_of(position * rows, rows)
            kg_ref[pl.ds(begin, rows), :] = jnp.zeros((rows, key_width), jnp.bfloat16)
            vg_ref[pl.ds(begin, rows), :] = jnp.zeros((rows, key_width), jnp.bfloat16)

        @pl.loop(0, me + 1)
        def block(position):
            begin = pl.multiple_of(position * rows, rows)
            keys = kv_ref[pl.ds(begin, rows), :key_width]
            values = kv_ref[pl.ds(begin, rows), key_width:]
            bias = hidden_bias(kd_ref[pl.ds(begin, rows), :], qd_ref[...], position == me)
            key_grad = jnp.zeros((rows, key_width), jnp.float32)
            value_grad = jnp.zeros((rows, key_width), jnp.float32)
            for head in range(heads):
                columns = slice(head * rows, (head + 1) * rows)
                query = qt_ref[:, columns]
                upper = ut_ref[:, columns]
                probs = jnp.exp2(product(keys, query) * scale + bias - lse_ref[:, columns])
                value_grad = value_grad + over_columns(to_low(probs), upper)
                score_grad = to_low(probs * (product(values, upper) - delta[:, columns]))
                key_grad = key_grad + over_columns(score_grad, query)
                acc_ref[:, columns] += over_rows(keys, score_grad)
            kg_ref[pl.ds(begin, rows), :] = to_low(key_grad * 0.125)
            vg_ref[pl.ds(begin, rows), :] = to_low(value_grad)

        qg_ref[...] = to_low(lie_down(acc_ref, rows, shared_heads) * 0.125)

    return pl.pallas_call(
        kernel,
        out_shape=(
            jax.ShapeDtypeStruct((rows, width), jnp.bfloat16),
            jax.ShapeDtypeStruct((total_rows, key_width), jnp.bfloat16),
            jax.ShapeDtypeStruct((total_rows, key_width), jnp.bfloat16),
        ),
        in_specs=[pl.BlockSpec(memory_space=pltpu.SMEM)] + [VMEM] * 7,
        out_specs=(VMEM,) * 3,
        scratch_shapes=[
            pltpu.VMEM((key_width, heads * rows), jnp.bfloat16),
            pltpu.VMEM((key_width, heads * rows), jnp.bfloat16),
            pltpu.VMEM((key_width, heads * rows), jnp.float32),
        ],
        compiler_params=pltpu.CompilerParams(vmem_limit_bytes=28 * MEBI),
        cost_estimate=lasting(20),
        name="attend_back",
    )(own, queries, upstream, both_rows, key_docs, query_docs, attended, log_sum)


def body(
    tokens_in,
    cotangent,
    document_ids,
    expert_routes,
    norm_mixer,
    mixer_inner,
    mixer_gate,
    conv_taps,
    conv_bias,
    state_proj,
    step_proj,
    step_bias,
    decay_log,
    skip_gain,
    mixer_out,
    norm_ffn,
    ffn_gate,
    ffn_up,
    ffn_down,
    norm_attn,
    attn_query,
    attn_key,
    attn_value,
    attn_output,
    norm_moe,
    router,
    expert_gate,
    expert_up,
    expert_down,
):
    numbers = itertools.count()
    seq_count = lax.axis_size("seq")
    row_count = tokens_in.shape[0]
    total_rows = seq_count * row_count
    first_row = lax.axis_index("seq") * row_count
    last_row = first_row + row_count - 1

    me = lax.axis_index("seq")
    bit_count = seq_count.bit_length() - 1
    across_first = [0] + list(range(1, bit_count))
    along_first = [1, 0] + list(range(2, bit_count))

    def by_owner(values, bits):
        turned = values.transpose(0, 2, 1)
        own_rows = turned.shape[1] // seq_count
        order = [0]
        for bit in reversed(bits):
            order = order + [j + (1 << bit) for j in order]
        blocks = []
        for j in order:
            owner = me
            for bit in range(bit_count):
                if j >> bit & 1:
                    owner = owner + (1 << bit) * (1 - 2 * ((owner >> bit) & 1))
            blocks.append(lax.dynamic_slice_in_dim(turned, owner * own_rows, own_rows, 1))
        half = len(blocks) // 2
        return (
            jnp.concatenate(blocks[half:], axis=1),
            jnp.concatenate(blocks[:half], axis=1),
        ), bits

    def over_tokens(rows, columns):
        if rows.shape[0] == 1:
            return product(rows[0], columns[0])[None]
        return jnp.einsum("bdt,btf->bdf", rows, columns, preferred_element_type=jnp.float32)

    def begin_sum(*parts):
        flow = prepare_sum(*parts)
        send(flow)
        return flow

    def prepare_sum(*parts):
        flow = {"parts": parts, "bits": parts[0][0][1], "got": []}
        settle(flow)
        return flow

    def send(flow):
        bit = flow["bits"][len(flow["got"])]
        route = [(i, i ^ (1 << bit)) for i in range(seq_count)]
        flow["got"].append(lax.ppermute(flow["out"], "seq", route))

    def bind(values, *flows):
        tied = lax.optimization_barrier((values, *[flow["out"] for flow in flows]))
        for flow, out in zip(flows, tied[1:], strict=True):
            flow["out"] = out
        return tied[0]

    def settle(flow):
        step = len(flow["got"])
        if step < 2:
            gradients = [over_tokens(rows[0][step], columns) for rows, columns in flow["parts"]]
            total = gradients[0] if len(gradients) == 1 else jnp.concatenate(gradients, axis=2)
            if step == 0:
                flow["out"] = to_low(total)
                return
            flow["own"] = total + flow["got"][0].astype(jnp.float32)
        count = flow["own"].shape[1] >> (step - 1)
        half = count // 2
        last = step == len(flow["bits"])
        part = slice(0, count) if last else slice(half, count)
        total = flow["own"][:, part]
        for got in flow["got"][1:]:
            total = total + got[:, part].astype(jnp.float32)
        flow["total" if last else "out"] = total if last else to_low(total)

    def hold(values, *flows):
        if flows:
            tied = lax.optimization_barrier((values, *[flow["got"][-1] for flow in flows]))
            values = tied[0]
            for flow, got in zip(flows, tied[1:], strict=True):
                flow["got"][-1] = got
        return values

    def after(values, *flows):
        values = hold(values, *flows)
        for flow in flows:
            settle(flow)
            if "total" not in flow:
                send(flow)
        return values

    def finished(flow):
        while "total" not in flow:
            settle(flow)
            if "total" not in flow:
                send(flow)
        return flow["total"]

    def branch_sum(values):
        return head_sum(values, next(numbers), jnp.bfloat16, 4)

    local_docs = lax.dynamic_slice_in_dim(document_ids, first_row, row_count)
    reach = conv_taps.shape[0] - 1
    border = jnp.arange(reach, dtype=jnp.int32)
    docs_before = jnp.take(document_ids, jnp.maximum(first_row - reach + border, 0))
    docs_after = jnp.take(document_ids, jnp.minimum(first_row + row_count + border, total_rows - 1))
    docs_prior = jnp.concatenate([docs_before[reach - 1 :], local_docs[:-1]])
    retain = (local_docs == docs_prior).astype(jnp.float32)
    tokens = tokens_in.astype(jnp.float32)
    gain_mixer = norm_mixer.astype(jnp.float32)
    normed_one = to_low(rms_scale(tokens, gain_mixer))
    conv_in = to_low(product(normed_one, mixer_inner))
    gate_in = product(normed_one, mixer_gate)
    conv_edge = from_behind(conv_in[row_count - reach :], "seq", 1)
    extended = jnp.concatenate([conv_edge, conv_in]).astype(jnp.float32)
    docs_ext = jnp.concatenate([docs_before, local_docs])
    taps = conv_taps.astype(jnp.float32)
    conv_sum = conv_bias.astype(jnp.float32)[None, :]
    masks = []
    for offset in range(reach + 1):
        same_doc = (docs_ext[offset : offset + row_count] == local_docs).astype(jnp.float32)[
            :, None
        ]
        masks.append(same_doc)
        conv_sum = conv_sum + taps[offset] * extended[offset : offset + row_count] * same_doc
    activated = jax.nn.silu(conv_sum)
    act_low = to_low(activated)
    projected = head_sum(product(act_low, state_proj), next(numbers), jnp.float32, 1)
    rank_size = step_proj.shape[0]
    state_size = decay_log.shape[1]
    step_low = to_low(projected[:, :rank_size])
    inject = projected[:, rank_size : rank_size + state_size]
    readout = projected[:, rank_size + state_size :]
    step_pre = product(step_low, step_proj) + step_bias.astype(jnp.float32)
    step_dt = jax.nn.softplus(step_pre)
    decay_rate = jnp.exp(decay_log.astype(jnp.float32)).T
    slopes = -LOG2E * decay_rate
    steps = jnp.where(retain[:, None] > 0.0, step_dt, NEVER)
    drives = step_dt * activated
    inject_wide = spread(inject)
    readout_wide = spread(readout)
    state_in = run_summary(steps, drives, inject_wide, slopes, next(numbers), True)
    scanned, befores, state_out = state_sweep(
        state_in, steps, drives, inject_wide, readout_wide, slopes
    )
    skipping = skip_gain.astype(jnp.float32)
    mixed_state = scanned + skipping * activated
    gate_act = jax.nn.silu(gate_in)
    gated = to_low(mixed_state * gate_act)
    hidden_one = tokens + branch_sum(product(gated, mixer_out))
    gain_ffn = norm_ffn.astype(jnp.float32)
    normed_two = to_low(rms_scale(hidden_one, gain_ffn))
    gate_two = product(normed_two, ffn_gate)
    up_two = product(normed_two, ffn_up)
    ffn_act = to_low(jax.nn.silu(gate_two) * up_two)
    hidden_two = hidden_one + branch_sum(product(ffn_act, ffn_down))
    gain_attn = norm_attn.astype(jnp.float32)
    normed_three = to_low(rms_scale(hidden_two, gain_attn))
    queries = to_low(product(normed_three, attn_query))
    key_rows = to_low(product(normed_three, attn_key))
    value_rows = to_low(product(normed_three, attn_value))
    key_width = key_rows.shape[1]
    own_place = lax.axis_index("seq").reshape(1)
    key_docs = document_ids[:, None]
    query_docs = local_docs[None, :]
    attended_low, attended, log_sum, both_rows = attend(
        queries,
        jnp.concatenate([key_rows, value_rows], axis=1),
        key_docs,
        query_docs,
        next(numbers),
    )
    both_rows = both_rows.reshape(total_rows, -1)
    hidden_three = hidden_two + branch_sum(product(attended_low, attn_output))
    gain_moe = norm_moe.astype(jnp.float32)
    normed_four = to_low(rms_scale(hidden_three, gain_moe))
    logits = product(normed_four, router)
    expert_count = router.shape[1]
    experts = jnp.arange(expert_count, dtype=jnp.int32)
    named = (expert_routes[:, :, None] == experts).astype(jnp.float32)
    lead = jnp.sum((named[:, 0] - named[:, 1]) * logits, axis=1, keepdims=True)
    gate_weights = jax.nn.sigmoid(jnp.concatenate([lead, -lead], axis=1))
    route_flat = expert_routes.reshape(-1)
    pair_count = route_flat.shape[0]
    pair_order = jnp.arange(pair_count, dtype=jnp.int32)
    earlier = (pair_order[None, :] < pair_order[:, None]) & (
        route_flat[None, :] == route_flat[:, None]
    )
    within = jnp.sum(earlier.astype(jnp.int32), axis=1)
    slot_index = (route_flat * CAP + within).reshape(row_count, 2)
    slots = jnp.arange(expert_count * CAP, dtype=jnp.int32)
    first_hit = slot_index[:, 0][None, :] == slots[:, None]
    second_hit = slot_index[:, 1][None, :] == slots[:, None]
    placing = (first_hit | second_hit).astype(jnp.bfloat16)
    slot_gates = jnp.sum(
        jnp.where(first_hit, gate_weights[:, 0][None, :], 0.0)
        + jnp.where(second_hit, gate_weights[:, 1][None, :], 0.0),
        axis=1,
    )
    expert_in = to_low(product(placing, normed_four)).reshape(expert_count, CAP, -1)
    slot_upstream = product(placing, cotangent)
    res_grad = to_low(slot_gates[:, None] * slot_upstream).reshape(expert_count, CAP, -1)
    gate_four = jnp.einsum(
        "ecd,edf->ecf", expert_in, expert_gate, preferred_element_type=jnp.float32
    )
    up_four = jnp.einsum("ecd,edf->ecf", expert_in, expert_up, preferred_element_type=jnp.float32)
    expert_act = to_low(jax.nn.silu(gate_four) * up_four)
    expert_res = jnp.einsum(
        "ecf,efd->ecd", expert_act, expert_down, preferred_element_type=jnp.float32
    ).reshape(expert_count * CAP, -1)
    upstream = cotangent.astype(jnp.float32)
    slot_dots = jnp.sum(expert_res * slot_upstream, axis=1)
    dots_part = jnp.stack(
        [
            jnp.sum(jnp.where(first_hit, slot_dots[:, None], 0.0), axis=0),
            jnp.sum(jnp.where(second_hit, slot_dots[:, None], 0.0), axis=0),
        ],
        axis=1,
    )
    combined = product(placing.T, to_low(slot_gates[:, None] * expert_res))
    act_back = to_low(
        jnp.einsum("ecd,efd->ecf", res_grad, expert_down, preferred_element_type=jnp.float32)
    ).astype(jnp.float32)
    gating_grad = to_low(act_back * up_four * silu_slope(gate_four))
    upward_grad = to_low(act_back * jax.nn.silu(gate_four))
    flow_expert_down = begin_sum((by_owner(res_grad, along_first), expert_act))
    expert_rows = by_owner(expert_in, across_first)
    flow_expert_in = begin_sum(
        (expert_rows, jnp.concatenate([gating_grad, upward_grad], axis=2))
    )
    slot_grads = (
        jnp.einsum("ecf,edf->ecd", gating_grad, expert_gate, preferred_element_type=jnp.float32)
        + jnp.einsum("ecf,edf->ecd", upward_grad, expert_up, preferred_element_type=jnp.float32)
    ).reshape(expert_count * CAP, -1)
    token_part = product(placing.T, to_low(slot_grads))
    model_width = tokens.shape[1]
    expert_sums = branch_sum(
        jnp.concatenate(
            [token_part, jnp.pad(dots_part, ((0, 0), (0, LANES - 2)))], axis=1
        )
    )
    normed_grad = expert_sums[:, :model_width]
    dots = expert_sums[:, model_width : model_width + 2]
    chosen_grad = gate_weights * (dots - jnp.sum(gate_weights * dots, axis=1, keepdims=True))
    logit_grad = jnp.sum(named * chosen_grad[:, :, None], axis=1)
    grad_router = exact_product(normed_four.astype(jnp.float32).T, logit_grad)
    normed_grad = normed_grad + exact_product(logit_grad, router.astype(jnp.float32).T)
    hidden_grad, grad_norm_moe = rms_back(hidden_three, gain_moe, normed_grad)
    three_grad = upstream + hidden_grad
    branch_grad = to_low(three_grad)
    attn_out_rows = by_owner(branch_grad[None], across_first)
    attended_grad = to_low(product(branch_grad, attn_output.T))
    query_grad, key_part, value_part = attend_back(
        own_place, queries, attended_grad, both_rows, key_docs, query_docs, attended, log_sum
    )
    key_part = hold(key_part, flow_expert_down)
    key_sum, value_sum, combined_sum = scatter_and_head_sum(
        [key_part, value_part], combined, next(numbers)
    )
    mixed_out = to_low(hidden_three + combined_sum)
    key_sum, attended_late = lax.optimization_barrier((key_sum, attended_low))
    key_sum = after(key_sum, flow_expert_down, flow_expert_in)
    key_grad = to_low(key_sum)
    value_grad = to_low(value_sum)
    flow_attn = begin_sum(
        (
            by_owner(normed_three[None], across_first),
            jnp.concatenate([query_grad, key_grad, value_grad], axis=1)[None],
        ),
        (attn_out_rows, attended_late[None]),
    )
    normed_part = (
        product(query_grad, attn_query.T)
        + product(key_grad, attn_key.T)
        + product(value_grad, attn_value.T)
    )
    normed_grad = branch_sum(normed_part)
    hidden_grad, grad_norm_attn = rms_back(hidden_two, gain_attn, normed_grad)
    two_grad = three_grad + hidden_grad
    branch_grad = to_low(two_grad)
    flow_ffn_down = begin_sum((by_owner(branch_grad[None], along_first), ffn_act[None]))
    ffn_back = to_low(product(branch_grad, ffn_down.T))
    ffn_back = after(ffn_back, flow_expert_down, flow_expert_in, flow_attn).astype(jnp.float32)
    feed_gate_grad = to_low(ffn_back * up_two * silu_slope(gate_two))
    feed_up_grad = to_low(ffn_back * jax.nn.silu(gate_two))
    feed_rows = by_owner(normed_two[None], across_first)
    flow_ffn_gate = begin_sum((feed_rows, feed_gate_grad[None]))
    normed_part = product(feed_gate_grad, ffn_gate.T) + product(feed_up_grad, ffn_up.T)
    normed_grad = branch_sum(normed_part)
    hidden_grad, grad_norm_ffn = rms_back(hidden_one, gain_ffn, normed_grad)
    one_grad = two_grad + hidden_grad
    branch_grad = to_low(one_grad)
    mixer_out_rows = by_owner(branch_grad[None], across_first)
    gated_grad = to_low(product(branch_grad, mixer_out.T)).astype(jnp.float32)
    scan_grad = gated_grad * gate_act
    gate_in_grad = to_low(gated_grad * mixed_state * silu_slope(gate_in))
    grad_skip_gain = jnp.sum(scan_grad * activated, axis=0)
    early_flows = (flow_expert_down, flow_expert_in, flow_attn, flow_ffn_down, flow_ffn_gate)
    flow_ffn_up = prepare_sum((feed_rows, feed_up_grad[None]))
    flow_mixer_gate = prepare_sum((by_owner(normed_one[None], along_first), gate_in_grad[None]))
    flow_mixer_out = prepare_sum((mixer_out_rows, gated[None]))
    late_flows = (flow_ffn_up, flow_mixer_gate, flow_mixer_out)
    scan_grad = bind(scan_grad, *late_flows)
    scan_grad = hold(scan_grad, *early_flows)
    state_after = run_summary(steps, scan_grad, readout_wide, slopes, next(numbers), False)
    state_after = bind(state_after, *late_flows)
    state_after = after(state_after, flow_attn, flow_ffn_gate)
    send(flow_ffn_up)
    send(flow_mixer_gate)
    through_sum, injected, inject_part, readout_part, rate_sum = adjoint_sweep(
        state_after,
        state_out,
        befores,
        steps,
        drives,
        inject_wide,
        readout_wide,
        scan_grad,
        slopes,
    )
    step_grad = LN2 * through_sum + activated * injected
    input_grad = step_dt * injected
    inject_grad = jnp.sum(inject_part, axis=2)
    readout_grad = jnp.sum(readout_part, axis=2)
    grad_decay_log = -rate_sum * decay_rate
    pre_grad = step_grad * jax.nn.sigmoid(step_pre)
    grad_step_bias = jnp.sum(pre_grad, axis=0)
    pre_low = to_low(pre_grad)
    pre_low = bind(pre_low, flow_mixer_out)
    pre_low = after(pre_low, flow_ffn_up, flow_ffn_gate, flow_ffn_down, flow_attn)
    send(flow_mixer_out)
    grad_step_proj = product(pre_low.T, step_low)
    proj_part = jnp.concatenate([product(pre_low, step_proj.T), inject_grad, readout_grad], axis=1)
    proj_low = to_low(head_sum(proj_part, next(numbers), jnp.float32, 1))
    proj_low = after(proj_low, flow_mixer_gate, flow_ffn_down)
    grad_state_proj = product(act_low.T, proj_low)
    act_total = input_grad + skipping * scan_grad + product(proj_low, state_proj.T)
    conv_grad = act_total * silu_slope(conv_sum)
    conv_grad = after(conv_grad, flow_ffn_up, flow_mixer_out, flow_ffn_gate)
    grad_conv_bias = jnp.sum(conv_grad, axis=0)
    after_edge = from_behind(conv_grad[:reach], "seq", -1)
    after_edge = after(after_edge, flow_ffn_down)
    grad_ext = jnp.concatenate([conv_grad, after_edge])
    docs_next = jnp.concatenate([local_docs, docs_after])
    conv_in_grad = jnp.zeros_like(conv_grad)
    tap_rows = []
    for offset in range(reach + 1):
        tap_rows.append(
            jnp.sum(conv_grad * extended[offset : offset + row_count] * masks[offset], axis=0)
        )
        lead = reach - offset
        same_next = (docs_next[lead : lead + row_count] == local_docs).astype(jnp.float32)[:, None]
        conv_in_grad = conv_in_grad + taps[offset] * grad_ext[lead : lead + row_count] * same_next
    grad_conv_taps = jnp.stack(tap_rows)
    conv_low = to_low(conv_in_grad)
    inner_half = conv_low.shape[1] // 2
    grad_mixer_inner = to_low(product(normed_one.T, conv_low))
    normed_part = product(conv_low, mixer_inner.T) + product(gate_in_grad, mixer_gate.T)
    own_channels = grad_conv_bias.shape[0] // seq_count

    def cut(values):
        return values.reshape(seq_count, -1)

    channel_rows = jnp.concatenate(
        [grad_state_proj, jnp.pad(grad_step_proj, ((0, 0), (0, LANES - rank_size)))], axis=1
    )
    packed = jnp.concatenate(
        [
            cut(grad_decay_log.T),
            cut(grad_norm_ffn),
            cut(grad_norm_attn),
            cut(grad_norm_moe),
            cut(grad_router),
            cut(grad_conv_taps.T),
            cut(grad_conv_bias),
            cut(grad_step_bias),
            cut(grad_skip_gain),
        ],
        axis=1,
    )
    spare = -packed.shape[1] % (16 * LANES)
    packed = to_low(jnp.pad(packed, ((0, 0), (0, spare)))).reshape(-1, LANES)
    packed = after(packed, flow_mixer_out, flow_mixer_gate)
    first_inner, second_inner, sum_rows, sum_packed, grad_tokens, grad_norm_mixer = last_sums(
        [
            grad_mixer_inner[:, :inner_half],
            grad_mixer_inner[:, inner_half:],
            to_low(channel_rows),
            packed,
        ],
        normed_part,
        tokens_in,
        gain_mixer[None, :],
        one_grad,
        next(numbers),
    )
    sum_attn = finished(flow_attn)[0]
    sum_expert_in = finished(flow_expert_in)
    expert_width = expert_gate.shape[2]
    sum_packed = sum_packed.reshape(-1)
    own_rows = model_width // seq_count
    taken = itertools.accumulate(
        [0, own_channels * state_size]
        + [own_rows] * 3
        + [own_rows * expert_count, own_channels * (reach + 1)]
        + [own_channels] * 3
    )
    bounds = list(taken)
    pieces = [sum_packed[low:high] for low, high in itertools.pairwise(bounds)]
    query_width = attn_query.shape[1]

    return (
        mixed_out,
        grad_tokens,
        lax.dynamic_slice_in_dim(grad_norm_mixer[0], me * own_rows, own_rows),
        jnp.concatenate([first_inner, second_inner], axis=1),
        finished(flow_mixer_gate)[0],
        pieces[5].reshape(own_channels, -1).T,
        pieces[6],
        sum_rows[:, :LANES],
        sum_rows[:, LANES : LANES + rank_size].T,
        pieces[7],
        pieces[0].reshape(own_channels, -1),
        pieces[8],
        finished(flow_mixer_out)[0].T,
        pieces[1],
        finished(flow_ffn_gate)[0],
        finished(flow_ffn_up)[0],
        finished(flow_ffn_down)[0].T,
        pieces[2],
        sum_attn[:, :query_width],
        sum_attn[:, query_width : query_width + key_width],
        sum_attn[:, query_width + key_width : query_width + 2 * key_width],
        sum_attn[:, query_width + 2 * key_width :].T,
        pieces[3],
        pieces[4].reshape(own_rows, -1),
        sum_expert_in[:, :, :expert_width],
        sum_expert_in[:, :, expert_width:],
        finished(flow_expert_down).transpose(0, 2, 1),
    )


def solution(mesh):
    in_specs = (
        P("seq", None),
        P("seq", None),
        P(),
        P("seq", None),
        P(),
        P(None, "head"),
        P(None, "head"),
        P(None, "head"),
        P("head"),
        P("head", None),
        P(None, "head"),
        P("head"),
        P("head", None),
        P("head"),
        P("head", None),
        P(),
        P(None, "head"),
        P(None, "head"),
        P("head", None),
        P(),
        P(None, "head"),
        P(None, "head"),
        P(None, "head"),
        P("head", None),
        P(),
        P(),
        P(None, None, "head"),
        P(None, None, "head"),
        P(None, "head", None),
    )
    out_specs = (
        P("seq", None),
        P("seq", None),
        P("seq"),
        P("seq", "head"),
        P("seq", "head"),
        P(None, ("head", "seq")),
        P(("head", "seq")),
        P(("head", "seq"), None),
        P(None, ("head", "seq")),
        P(("head", "seq")),
        P(("head", "seq"), None),
        P(("head", "seq")),
        P("head", "seq"),
        P("seq"),
        P("seq", "head"),
        P("seq", "head"),
        P("head", "seq"),
        P("seq"),
        P("seq", "head"),
        P("seq", "head"),
        P("seq", "head"),
        P("head", "seq"),
        P("seq"),
        P("seq", None),
        P(None, "seq", "head"),
        P(None, "seq", "head"),
        P(None, "head", "seq"),
    )
    return jax.shard_map(body, mesh=mesh, in_specs=in_specs, out_specs=out_specs, check_vma=False)
```
